32 devices in a mesh: seq: 16 (over z, y, core), fsdp: 2 (over x).
Axes of the slice: x: 2, y: 2, z: 4, core: 2. Of those that a mesh axis runs over, the one named last changes fastest.
Arguments:
- tokens: bfloat16 [2, 4096, 2048], P('fsdp', 'seq'), may hold values from -6 to 6
- per_layer: bfloat16 [2, 4096, 256], P('fsdp', 'seq'), may hold values from -6 to 6
- teacher: bfloat16 [2, 4096, 2048], P('fsdp', 'seq'), may hold values from -6 to 6
- cont_lengths: int32 [2, 4], replicated, may hold values from 257 to 512, as said below
- w_query: bfloat16 [2048, 2048], P(('seq', 'fsdp')), may hold values from -0.125 to 0.125
- w_kv: bfloat16 [2048, 1024], P(('seq', 'fsdp')), may hold values from -0.125 to 0.125
- w_out: bfloat16 [2048, 2048], P(('seq', 'fsdp')), may hold values from -0.125 to 0.125
- laurel_left: bfloat16 [2048, 64], P(('seq', 'fsdp')), may hold values from -0.125 to 0.125
- laurel_right: bfloat16 [64, 2048], P(None, ('seq', 'fsdp')), may hold values from -0.75 to 0.75
- pl_gate: bfloat16 [2048, 256], P(('seq', 'fsdp')), may hold values from -0.125 to 0.125
- pl_proj: bfloat16 [256, 2048], P(('seq', 'fsdp')), may hold values from -0.375 to 0.375
- norm_gains: bfloat16 [6, 2048], P(None, ('seq', 'fsdp')), may hold values from 0.25 to 1.75
- head_gains: bfloat16 [2, 256], P(None, ('seq', 'fsdp')), may hold values from 0.29882812 to 0.5
- ffn_weight: bfloat16 [8192, 3, 2048], P(('seq', 'fsdp')), may hold values from -0.125 to 0.125
Outputs:
- block_out: float32 [2, 4096, 2048], P('fsdp', 'seq')
- match_loss: float32 [], replicated
- d_tokens: float32 [2, 4096, 2048], P('fsdp', 'seq')
- d_per_layer: float32 [2, 4096, 256], P('fsdp', 'seq')
- d_w_query: float32 [2048, 2048], P(('seq', 'fsdp'))
- d_w_kv: float32 [2048, 1024], P(('seq', 'fsdp'))
- d_w_out: float32 [2048, 2048], P(('seq', 'fsdp'))
- d_laurel_left: float32 [2048, 64], P(('seq', 'fsdp'))
- d_laurel_right: float32 [64, 2048], P(None, ('seq', 'fsdp'))
- d_pl_gate: float32 [2048, 256], P(('seq', 'fsdp'))
- d_pl_proj: float32 [256, 2048], P(('seq', 'fsdp'))
- d_norm_gains: float32 [6, 2048], P(None, ('seq', 'fsdp'))
- d_head_gains: float32 [2, 256], P(None, ('seq', 'fsdp'))
- d_ffn_weight: float32 [8192, 3, 2048], P(('seq', 'fsdp'))
The draws below stay inside these ranges and needn't reach their ends.
Inputs may be any that keep to these rules, and one draw needn't show every extreme that they name: `cont_lengths`: in every group some continuation has all 512 slots valid.
All inputs are finite; a program needn't handle non-finite values.
Results may differ from the reference program's by a relative error of at most 0.02.
Values may be sent and summed in bfloat16 or wider, within the bound.
A program may use at most 512 MiB of HBM per device.

```python
import math
import jax
import jax.numpy as jnp
from jax import lax

D = 2048
HEADS = 8
KV_HEADS = 2
HEAD = 256
FF = 8192
RANK = 64
PLD = 256
WINDOW = 512
CONT_LEN = 512
GROUPS = 2
GTOK = 4096
PROMPT = 2048
NCONT = 4
TOKENS = 8192


def draw_cont_lengths(key, part):
    key = jax.random.fold_in(key, 7)
    first_key, second_key = jax.random.split(key)
    lengths = jax.random.randint(first_key, (GROUPS, NCONT), CONT_LEN // 2 + 1, CONT_LEN + 1)
    longest = jax.random.randint(second_key, (GROUPS, 1), 0, NCONT)
    lengths = jnp.where(jnp.arange(NCONT)[None, :] == longest, CONT_LEN, lengths)
    return lengths.astype(jnp.int32)


def level_of(own_key, extent, cuts, least, top_value):
    factor_of = 1.0
    for axis_at, shards_of in cuts:
        steps = jax.random.uniform(jax.random.fold_in(jax.random.fold_in(own_key, 6), axis_at), (shards_of,), jnp.float32, least / len(cuts), top_value / len(cuts))
        factor_of = factor_of * jnp.repeat(jnp.exp(steps), extent[axis_at] // shards_of).reshape((-1,) + (1,) * (len(extent) - 1 - axis_at))
    return factor_of


def centred(own_key, dims, deviation, limit, pieces=(), kind=jnp.bfloat16):
    array = deviation * jax.random.normal(own_key, dims, jnp.float32)
    if pieces:
        array = array * level_of(own_key, dims, pieces, -0.22, 0.18)
    return jnp.clip(array, -limit, limit).astype(kind)


def setup_inputs(seed: int = 0) -> dict:
    arg_keys = jax.random.split(jax.random.key(seed), 15)
    tokens = centred(arg_keys[0], (GROUPS, GTOK, D), 1.0, 6.0, ((0, 2), (1, 16)))
    per_layer = centred(arg_keys[1], (GROUPS, GTOK, PLD), 1.0, 6.0, ((0, 2), (1, 16)))
    teacher = centred(arg_keys[2], (GROUPS, GTOK, D), 1.0, 6.0, ((0, 2), (1, 16)))
    cont_lengths = draw_cont_lengths(jax.random.fold_in(arg_keys[14], 71), 0)
    w_query = centred(arg_keys[4], (D, HEADS * HEAD), D ** -0.5, 0.125, ((0, 32),))
    w_kv = centred(arg_keys[5], (D, 2 * KV_HEADS * HEAD), D ** -0.5, 0.125, ((0, 32),))
    w_out = centred(arg_keys[6], (HEADS * HEAD, D), (HEADS * HEAD) ** -0.5, 0.125, ((0, 32),))
    laurel_left = centred(arg_keys[7], (D, RANK), D ** -0.5, 0.125, ((0, 32),))
    laurel_right = centred(arg_keys[8], (RANK, D), RANK ** -0.5, 0.75, ((1, 32),))
    pl_gate = centred(arg_keys[9], (D, PLD), D ** -0.5, 0.125, ((0, 32),))
    pl_proj = centred(arg_keys[10], (PLD, D), PLD ** -0.5, 0.375, ((0, 32),))
    norm_gains = jnp.clip(1.0 + 0.15 * jax.random.normal(arg_keys[11], (6, D), jnp.float32), 0.25, 1.75).astype(jnp.bfloat16)
    head_gains = jnp.clip(0.29882812 + 0.20117188 * jax.random.uniform(arg_keys[12], (2, HEAD), jnp.float32) ** level_of(arg_keys[12], (2, HEAD), ((1, 32),), -0.2, 0.2), 0.29882812, 0.5).astype(jnp.bfloat16)
    ffn_weight = centred(arg_keys[13], (FF, 3, D), D ** -0.5, 0.125, ((0, 32),))
    return dict(tokens=tokens, per_layer=per_layer, teacher=teacher, cont_lengths=cont_lengths, w_query=w_query, w_kv=w_kv, w_out=w_out, laurel_left=laurel_left, laurel_right=laurel_right, pl_gate=pl_gate, pl_proj=pl_proj, norm_gains=norm_gains, head_gains=head_gains, ffn_weight=ffn_weight)


@jax.custom_vjp
def low(v):
    return lax.optimization_barrier(v.astype(jnp.bfloat16)).astype(jnp.float32)

@jax.custom_vjp
def low_back(v):
    return v

def low_keep(v):
    return (low(v), None)

def low_pass(kept, grad):
    return (grad,)

def back_keep(v):
    return (v, None)

def back_low(kept, grad):
    return (low(grad),)
low.defvjp(low_keep, low_pass)
low_back.defvjp(back_keep, back_low)
EPSILON = 1e-06
INV_SQRT2 = 0.7071067811865476
ROPE_BASE = 10000.0

def matmul(left, right):
    return jnp.dot(left, right, precision=lax.Precision.HIGHEST, preferred_element_type=jnp.float32)

def rms_norm(values, gain):
    return values * lax.rsqrt(lax.optimization_barrier(jnp.mean(values * values, axis=-1, keepdims=True)) + EPSILON) * gain

def plain_norm(values):
    return values * lax.rsqrt(lax.optimization_barrier(jnp.mean(values * values, axis=-1, keepdims=True)) + EPSILON)

def rotate(values, places):
    half_dim = values.shape[-1] // 2
    freqs = jnp.exp(jnp.arange(half_dim, dtype=jnp.float32) * (-2.0 * math.log(ROPE_BASE) / values.shape[-1]))
    angles = places.astype(jnp.float32)[:, None, None] * freqs
    cosine = jnp.cos(angles)
    sine = jnp.sin(angles)
    first = values[..., :half_dim]
    second = values[..., half_dim:]
    return jnp.concatenate([first * cosine - second * sine, second * cosine + first * sine], -1)

def attention(query_low, key_low, value_low, places):
    kv_shape = (KV_HEADS, HEAD)

    def stream(values):
        prompt_part = values[:PROMPT]
        cont_part = values[PROMPT:].reshape((NCONT, CONT_LEN) + kv_shape)
        tail_part = jnp.broadcast_to(prompt_part[PROMPT - WINDOW:], (NCONT, WINDOW) + kv_shape)
        joined = jnp.concatenate([tail_part, cont_part], 1).reshape((NCONT * (WINDOW + CONT_LEN),) + kv_shape)
        return jnp.concatenate([jnp.zeros((WINDOW,) + kv_shape, jnp.float32), prompt_part, joined], 0)
    key_stream = stream(key_low)
    value_stream = stream(value_low)
    cont_places = jnp.arange(PROMPT - WINDOW, PROMPT + CONT_LEN, dtype=jnp.int32)
    place_stream = jnp.concatenate([jnp.arange(-WINDOW, PROMPT, dtype=jnp.int32), jnp.tile(cont_places, NCONT)])
    blocks = GTOK // WINDOW
    query_starts = jnp.arange(blocks, dtype=jnp.int32) * WINDOW
    relative = query_starts - PROMPT
    key_starts = jnp.where(query_starts < PROMPT, query_starts, WINDOW + PROMPT + relative // CONT_LEN * (WINDOW + CONT_LEN) + relative % CONT_LEN).astype(jnp.int32)
    group_heads = HEADS // KV_HEADS

    def one_block(block_args):
        query_block, key_start, query_places = block_args
        keys = lax.dynamic_slice_in_dim(key_stream, key_start, 2 * WINDOW, 0)
        values = lax.dynamic_slice_in_dim(value_stream, key_start, 2 * WINDOW, 0)
        key_places = lax.dynamic_slice_in_dim(place_stream, key_start, 2 * WINDOW, 0)
        grouped = query_block.reshape(WINDOW, KV_HEADS, group_heads, HEAD)
        scores = jnp.einsum('qgjd,kgd->gjqk', grouped, keys, precision=lax.Precision.HIGHEST)
        scores = low_back(scores)
        visible = (key_places[None, :] <= query_places[:, None]) & (query_places[:, None] - key_places[None, :] < WINDOW) & (key_places[None, :] >= 0)
        masked = jnp.where(visible, scores, -1e+30)
        probs = low(jax.nn.softmax(masked, axis=-1))
        context = jnp.einsum('gjqk,kgd->qgjd', probs, values, precision=lax.Precision.HIGHEST)
        return context.reshape(WINDOW, HEADS * HEAD)
    outputs = lax.map(jax.checkpoint(one_block), (query_low.reshape(blocks, WINDOW, HEADS, HEAD), key_starts, places.reshape(blocks, WINDOW)))
    return outputs.reshape(GTOK, HEADS * HEAD)

def layer_forward(states, layer_in, places, wq, wkv, wo, lleft, lright, plg, plp, gains, head_gain, ffw):
    row_count = states.shape[0]
    normed = rms_norm(states, gains[0])
    normed_low = low(normed)
    query_raw = low_back(matmul(normed_low, wq))
    kv_raw = low_back(matmul(normed_low, wkv))
    queries = rotate(rms_norm(query_raw.reshape(row_count, HEADS, HEAD), head_gain[0]), places)
    keys = rotate(rms_norm(kv_raw[:, :KV_HEADS * HEAD].reshape(row_count, KV_HEADS, HEAD), head_gain[1]), places)
    values = plain_norm(kv_raw[:, KV_HEADS * HEAD:].reshape(row_count, KV_HEADS, HEAD))
    context = attention(low(queries), low(keys), low(values), places)
    context_low = low(low_back(context))
    attn_raw = low_back(matmul(context_low, wo))
    attn_out = rms_norm(attn_raw, gains[1])
    laurel_mid = low(low_back(matmul(normed_low, lleft)))
    laurel_raw = low_back(matmul(laurel_mid, lright))
    mixed = (states + attn_out + normed + rms_norm(laurel_raw, gains[2])) * INV_SQRT2
    ffn_in = low(rms_norm(mixed, gains[3]))
    gate = low_back(matmul(ffn_in, ffw[:, 0, :].T))
    upward = low_back(matmul(ffn_in, ffw[:, 1, :].T))
    hidden = low(jax.nn.gelu(gate, approximate=True) * upward)
    down_out = low_back(matmul(hidden, ffw[:, 2, :]))
    after_ffn = mixed + rms_norm(down_out, gains[4])
    after_low = low(after_ffn)
    pl_raw = low_back(matmul(after_low, plg))
    pl_mid = low(jax.nn.gelu(pl_raw, approximate=True) * layer_in)
    pl_out = low_back(matmul(pl_mid, plp))
    return after_ffn + rms_norm(pl_out, gains[5])

def reference(tokens, per_layer, teacher, cont_lengths, w_query, w_kv, w_out, laurel_left, laurel_right, pl_gate, pl_proj, norm_gains, head_gains, ffn_weight):
    indices = jnp.arange(GTOK, dtype=jnp.int32)
    offset_in = indices - PROMPT
    places = jnp.where(indices < PROMPT, indices, PROMPT + offset_in % CONT_LEN).astype(jnp.int32)
    cont_ids = offset_in // CONT_LEN

    def forward(states, layer_in, wq, wkv, wo, lleft, lright, plg, plp, gains, head_gain, ffw):

        def one_group(group_args):
            group_states, group_in = group_args
            return layer_forward(group_states, group_in, places, wq, wkv, wo, lleft, lright, plg, plp, gains, head_gain, ffw)
        return lax.map(jax.checkpoint(one_group), (states, layer_in))
    primals = tuple((value.astype(jnp.float32) for value in (tokens, per_layer, w_query, w_kv, w_out, laurel_left, laurel_right, pl_gate, pl_proj, norm_gains, head_gains, ffn_weight)))
    outputs, backward = jax.vjp(forward, *primals)
    lens_tok = lax.optimization_barrier(jnp.sum(jnp.where(cont_ids[None, :, None] == jnp.arange(NCONT, dtype=jnp.int32)[None, None, :], cont_lengths[:, None, :], 0), axis=-1))
    valid = (indices[None, :] < PROMPT) | (offset_in[None, :] % CONT_LEN < lens_tok)
    weight_mask = valid.astype(jnp.float32)
    count = jnp.sum(weight_mask)
    errors = outputs - teacher.astype(jnp.float32)
    match_loss = jnp.sum(weight_mask[..., None] * errors * errors) / (2.0 * D * count)
    cotangent = weight_mask[..., None] * errors * (TOKENS / count)
    grads = backward(cotangent)
    return (outputs, match_loss, grads[0], grads[1], grads[2], grads[3], grads[4], grads[5], grads[6], grads[7], grads[8], grads[9], grads[10], grads[11])
```

```python
import math

import jax
import jax.numpy as jnp
from jax import lax
from jax.sharding import Mesh, PartitionSpec as P

D = 2048
HEADS = 8
KV_HEADS = 2
HEAD = 256
WINDOW = 512
CONT_LEN = 512
RANK = 64
PLD = 256

EPSILON = 1e-06
INV_SQRT2 = 0.7071067811865476
ROPE_BASE = 10000.0
BF16 = jnp.bfloat16
F32 = jnp.float32


def rms_norm(values, gain):
    return values * lax.rsqrt(jnp.mean(values * values, axis=-1, keepdims=True) + EPSILON) * gain


def plain_norm(values):
    return values * lax.rsqrt(jnp.mean(values * values, axis=-1, keepdims=True) + EPSILON)


def rotate(values, places):
    half_dim = values.shape[-1] // 2
    freqs = jnp.exp(
        jnp.arange(half_dim, dtype=F32) * (-2.0 * math.log(ROPE_BASE) / values.shape[-1])
    )
    angles = places.astype(F32)[:, None, None] * freqs
    cosine = jnp.cos(angles)
    sine = jnp.sin(angles)
    first = values[..., :half_dim]
    second = values[..., half_dim:]
    return jnp.concatenate([first * cosine - second * sine, second * cosine + first * sine], -1)


def gelu_tanh(values):
    return jax.nn.gelu(values, approximate=True)


def gated_product(gate_in, up_in):
    return gelu_tanh(gate_in) * up_in


def full_dot(left, right):
    return jnp.dot(left, right, preferred_element_type=F32)


def left_dot(left, right):
    return lax.dot_general(left, right, (((0,), (0,)), ((), ())), preferred_element_type=F32)


def right_dot(left, right):
    return lax.dot_general(left, right, (((1,), (1,)), ((), ())), preferred_element_type=F32)


def ring_order(n):
    return list(range(0, n, 2)) + list(range(n - 1, 0, -2))


def ring_pairs(n, by):
    order = ring_order(n)
    return [(order[i], order[(i + by) % n]) for i in range(n)]


def ring(value, by):
    return lax.ppermute(value, "zy", ring_pairs(lax.axis_size("zy"), by))


def swap(value, axis):
    return lax.ppermute(value, axis, [(0, 1), (1, 0)])


def rows_of_four(own):
    pair = jnp.concatenate([own, swap(own, "fsdp")], 0)
    return jnp.concatenate([pair, swap(pair, "core")], 0)


def sum_of_four(partial):
    count = partial.shape[0] // 4
    low = partial[2 * count :].astype(BF16)
    pair = partial[: 2 * count] + swap(low, "core").astype(F32)
    low = pair[count:].astype(BF16)
    return pair[:count] + swap(low, "fsdp").astype(F32)


def body(
    tokens,
    per_layer,
    teacher,
    cont_lengths,
    w_query,
    w_kv,
    w_out,
    laurel_left,
    laurel_right,
    pl_gate,
    pl_proj,
    norm_gains,
    head_gains,
    ffn_weight,
):
    states = tokens[0].astype(F32)
    layer_in = per_layer[0].astype(F32)
    target = teacher[0].astype(F32)
    row_count = states.shape[0]
    chips = lax.axis_size("zy")
    seq_count = 2 * chips
    group_count = lax.axis_size("fsdp")
    shards = seq_count * group_count
    chip = lax.axis_index("zy")
    core = lax.axis_index("core")
    seq_index = chip * 2 + core
    group_index = lax.axis_index("fsdp")
    half_point = seq_count // 2
    prompt_len = half_point * row_count
    cont_shards = CONT_LEN // row_count
    cont_count = prompt_len // CONT_LEN
    is_cont = seq_index >= half_point
    rel_index = seq_index - half_point
    local_shard = jnp.where(is_cont, rel_index % cont_shards, 0)
    cont_index = jnp.where(is_cont, rel_index // cont_shards, 0)
    first_place = jnp.where(is_cont, prompt_len + local_shard * row_count, seq_index * row_count)
    row_range = jnp.arange(row_count, dtype=jnp.int32)
    places = first_place + row_range
    group_lengths = jnp.sum(
        jnp.where(
            jnp.arange(group_count, dtype=jnp.int32)[:, None] == group_index, cont_lengths, 0
        ),
        axis=0,
    )
    my_length = jnp.sum(
        jnp.where(jnp.arange(cont_count, dtype=jnp.int32) == cont_index, group_lengths, 0)
    )
    valid = jnp.logical_or(
        jnp.logical_not(is_cont), local_shard * row_count + row_range < my_length
    )
    weight_mask = valid.astype(F32)
    count = F32(group_count * prompt_len) + jnp.sum(cont_lengths).astype(F32)
    total_slots = float(row_count * seq_count * group_count)
    ring_pos = jnp.where(chip % 2 == 0, chip // 2, chips - 1 - chip // 2)

    def ring_owner(offset):
        spot = (ring_pos + offset + chips) % chips
        return jnp.where(spot < chips // 2, 2 * spot, 2 * (chips - 1 - spot) + 1)

    shard_rows = w_query.shape[0]
    key_cols = KV_HEADS * HEAD
    proj_cols = pl_proj.shape[0] * D // shard_rows
    misc_cols = RANK
    head_part = head_gains.reshape(-1, 1)
    misc = jnp.concatenate(
        [
            norm_gains.T,
            jnp.pad(head_part, ((0, shard_rows - head_part.shape[0]), (0, 0))),
            jnp.zeros((shard_rows, misc_cols - 7), BF16),
        ],
        1,
    )
    pack_a = jnp.concatenate([w_query, w_kv, laurel_left, misc], 1)
    pack_b = jnp.concatenate(
        [w_out, pl_gate, pl_proj.reshape(shard_rows, proj_cols), laurel_right.T], 1
    )
    all_axes = ("zy", "core", "fsdp")
    full_a = lax.all_gather(pack_a, all_axes, axis=0, tiled=True)
    full_b = lax.all_gather(pack_b, all_axes, axis=0, tiled=True)
    wq = full_a[:, :D]
    wkv = full_a[:, D : D + 2 * key_cols]
    lleft = full_a[:, D + 2 * key_cols : D + 2 * key_cols + RANK]
    misc_full = full_a[:, D + 2 * key_cols + RANK :]
    gains = misc_full[:, :6].T.astype(F32)
    head_n = head_gains.shape[1]
    head_gain = (
        misc_full[:, 6]
        .reshape(shards, shard_rows)[:, : 2 * head_n]
        .reshape(shards, 2, head_n)
        .transpose(1, 0, 2)
        .reshape(2, HEAD)
        .astype(F32)
    )
    wo = full_b[:, :D]
    plg = full_b[:, D : D + PLD]
    plp = full_b[:, D + PLD : D + PLD + proj_cols].reshape(PLD, D)
    lright = full_b[:, D + PLD + proj_cols :].T

    units = ffn_weight.shape[0]
    half = units // 2
    kinds = [ffn_weight[:, kind] for kind in range(3)]
    ups = [[w[:half] for w in kinds]]
    downs = [[w[half:] for w in kinds]]
    for _ in range(1, chips):
        ups.append([ring(w, 1) for w in ups[-1]])
        downs.append([ring(w, -1) for w in downs[-1]])
    parts = []
    first = 0
    while first < chips:
        length = max(1, (chips - first) // 2)
        parts.append(list(range(first, first + length)))
        first += length
    part_weights = [
        [
            jnp.concatenate([half_w for k in part for half_w in (ups[k][kind], downs[k][kind])], 0)
            for kind in range(3)
        ]
        for part in parts
    ]

    normed = rms_norm(states, gains[0])
    normed_low = normed.astype(BF16)
    query_raw = full_dot(normed_low, wq)
    kv_raw = full_dot(normed_low, wkv)

    def prepare(q_input, k_input, v_input, q_gain, k_gain):
        q_heads = rotate(rms_norm(q_input.reshape(row_count, HEADS, HEAD), q_gain), places)
        k_heads = rotate(rms_norm(k_input.reshape(row_count, KV_HEADS, HEAD), k_gain), places)
        v_heads = plain_norm(v_input.reshape(row_count, KV_HEADS, HEAD))
        return (q_heads, k_heads, v_heads)

    (queries, keys_new, values_new), prepare_back = jax.vjp(
        prepare, query_raw, kv_raw[:, :key_cols], kv_raw[:, key_cols:], head_gain[0], head_gain[1]
    )
    query_low = queries.astype(BF16)
    kv_own = jnp.concatenate(
        [
            keys_new.reshape(row_count, key_cols).astype(BF16),
            values_new.reshape(row_count, key_cols).astype(BF16),
        ],
        1,
    )

    mid = chips // 2
    chain = [(i, i + 1) for i in range(mid - 1)] + [(mid - 1, mid + 1)]
    kv_before = jnp.where(
        chip == mid,
        lax.ppermute(kv_own, "zy", [(mid - 1, mid)]),
        lax.ppermute(kv_own, "zy", chain),
    )
    spans = []
    span = 2
    while span < mid:
        spans.append(span)
        span *= 2
    for span in spans:
        moved = lax.ppermute(
            kv_before, "zy", [(mid + i, mid + i + span) for i in range(min(span, mid - span))]
        )
        fresh = jnp.logical_and(chip >= mid + span, chip < mid + 2 * span)
        kv_before = jnp.where(fresh, moved, kv_before)
    kv_other = swap(jnp.where(core == 0, kv_own, kv_before), "core")
    keys_all = jnp.concatenate([kv_before, kv_other, kv_own], 0)
    key_len = keys_all.shape[0]
    key_places = first_place - 2 * row_count + jnp.arange(key_len, dtype=jnp.int32)
    visible = (
        (key_places[None, :] <= places[:, None])
        & (places[:, None] - key_places[None, :] < WINDOW)
        & (key_places[None, :] >= 0)
    )
    group_heads = HEADS // KV_HEADS
    query_grouped = query_low.reshape(row_count, KV_HEADS, group_heads, HEAD)
    key_heads = keys_all[:, :key_cols].reshape(key_len, KV_HEADS, HEAD)
    value_heads = keys_all[:, key_cols:].reshape(key_len, KV_HEADS, HEAD)

    def masked_scores():
        scores = jnp.einsum(
            "qgjd,kgd->gjqk", query_grouped, key_heads, preferred_element_type=F32
        )
        return jnp.where(visible, scores, -1e30)

    scores_fwd = masked_scores()
    top_score = jnp.max(scores_fwd, axis=-1, keepdims=True)
    expo = jnp.exp(scores_fwd - top_score)
    totals = jnp.sum(expo, axis=-1, keepdims=True)
    probs = expo / totals
    log_total = top_score + jnp.log(totals)
    probs_low = probs.astype(BF16)
    context = jnp.einsum("gjqk,kgd->qgjd", probs_low, value_heads, preferred_element_type=F32)
    context_low = context.reshape(row_count, HEADS * HEAD).astype(BF16)
    attn_raw = full_dot(context_low, wo)
    attn_out = rms_norm(attn_raw, gains[1])
    laurel_mid = full_dot(normed_low, lleft).astype(BF16)
    laurel_raw = full_dot(laurel_mid, lright)
    mixed = (states + attn_out + normed + rms_norm(laurel_raw, gains[2])) * INV_SQRT2
    ffn_in = rms_norm(mixed, gains[3]).astype(BF16)

    ffn_rows = rows_of_four(ffn_in)
    gates, uppers, hiddens = [], [], []
    running = None
    for weights in part_weights:
        gate = right_dot(ffn_rows, weights[0])
        upper = right_dot(ffn_rows, weights[1])
        hidden = gated_product(gate, upper).astype(BF16)
        term = full_dot(hidden, weights[2])
        running = term if running is None else running + term
        gates.append(gate)
        uppers.append(upper)
        hiddens.append(hidden)
    down_out = sum_of_four(running)
    after_ffn = mixed + rms_norm(down_out, gains[4])
    after_low = after_ffn.astype(BF16)
    pl_raw = full_dot(after_low, plg)
    pl_act = gelu_tanh(pl_raw)
    pl_mid = (pl_act * layer_in).astype(BF16)
    pl_out = full_dot(pl_mid, plp)
    result = after_ffn + rms_norm(pl_out, gains[5])
    errors = result - target
    squares = jnp.sum(weight_mask[:, None] * errors * errors)

    grad_out = weight_mask[:, None] * errors * (total_slots / count)
    unused, pl_norm_back = jax.vjp(rms_norm, pl_out, gains[5])
    grad_pl_out, grad_g5 = pl_norm_back(grad_out)
    grad_pl_low = grad_pl_out.astype(BF16)
    grad_plp = left_dot(pl_mid, grad_pl_low)
    grad_pl_mid = right_dot(grad_pl_low, plp)
    grad_layer_in = grad_pl_mid * pl_act
    unused, gelu_back = jax.vjp(gelu_tanh, pl_raw)
    grad_pl_raw = gelu_back(grad_pl_mid * layer_in)[0].astype(BF16)
    grad_plg = left_dot(after_low, grad_pl_raw)
    grad_after = grad_out + right_dot(grad_pl_raw, plg)
    unused, down_norm_back = jax.vjp(rms_norm, down_out, gains[4])
    grad_down, grad_g4 = down_norm_back(grad_after)
    grad_down_low = grad_down.astype(BF16)

    grad_down_rows = rows_of_four(grad_down_low)
    grad_gates, grad_uppers = [], []
    running = None
    for weights, gate, upper in zip(part_weights, gates, uppers):
        unused, act_back = jax.vjp(gated_product, gate, upper)
        grad_gate, grad_upper = act_back(right_dot(grad_down_rows, weights[2]))
        grad_gates.append(grad_gate.astype(BF16))
        grad_uppers.append(grad_upper.astype(BF16))
        term = full_dot(grad_gates[-1], weights[0]) + full_dot(grad_uppers[-1], weights[1])
        running = term if running is None else running + term
    grad_ffn_in = sum_of_four(running)

    def unit_grads(k):
        for part, gg, gu, hid in zip(parts, grad_gates, grad_uppers, hiddens):
            if k in part:
                at = (k - part[0]) * units
                cut = slice(at, at + units)
                return [
                    left_dot(gg[:, cut], ffn_rows),
                    left_dot(gu[:, cut], ffn_rows),
                    left_dot(hid[:, cut], grad_down_rows),
                ]

    up_sums, down_sums = None, None
    for k in list(range(1, chips)) + [0]:
        terms = unit_grads(k)
        if up_sums is None:
            up_sums = [t[:half] for t in terms]
            down_sums = [t[half:] for t in terms]
        else:
            up_sums = [
                ring(s.astype(BF16), 1).astype(F32) + t[:half] for s, t in zip(up_sums, terms)
            ]
            down_sums = [
                ring(s.astype(BF16), -1).astype(F32) + t[half:] for s, t in zip(down_sums, terms)
            ]
    grad_ffn = jnp.stack(
        [jnp.concatenate([a, b], 0) for a, b in zip(up_sums, down_sums)], 1
    )

    unused, mix_norm_back = jax.vjp(rms_norm, mixed, gains[3])
    grad_mixed_norm, grad_g3 = mix_norm_back(grad_ffn_in)
    grad_scaled = (grad_after + grad_mixed_norm) * INV_SQRT2
    unused, laurel_norm_back = jax.vjp(rms_norm, laurel_raw, gains[2])
    grad_laurel, grad_g2 = laurel_norm_back(grad_scaled)
    grad_laurel_low = grad_laurel.astype(BF16)
    grad_lright_t = left_dot(grad_laurel_low, laurel_mid)
    grad_mid_low = right_dot(grad_laurel_low, lright).astype(BF16)
    grad_lleft = left_dot(normed_low, grad_mid_low)
    unused, attn_norm_back = jax.vjp(rms_norm, attn_raw, gains[1])
    grad_attn, grad_g1 = attn_norm_back(grad_scaled)
    grad_attn_low = grad_attn.astype(BF16)
    grad_wo = left_dot(context_low, grad_attn_low)
    grad_context = (
        right_dot(grad_attn_low, wo).astype(BF16).reshape(row_count, KV_HEADS, group_heads, HEAD)
    )
    probs_again = jnp.exp(masked_scores() - log_total)
    grad_probs = jnp.einsum(
        "qgjd,kgd->gjqk", grad_context, value_heads, preferred_element_type=F32
    )
    grad_scores = (
        probs_again * (grad_probs - jnp.sum(probs_again * grad_probs, axis=-1, keepdims=True))
    ).astype(BF16)
    grad_queries = jnp.einsum("gjqk,kgd->qgjd", grad_scores, key_heads, preferred_element_type=F32)
    grad_keys = jnp.einsum(
        "gjqk,qgjd->kgd", grad_scores, query_grouped, preferred_element_type=F32
    )
    grad_values = jnp.einsum(
        "gjqk,qgjd->kgd", probs_again.astype(BF16), grad_context, preferred_element_type=F32
    )
    grad_kv = jnp.concatenate(
        [grad_keys.reshape(key_len, key_cols), grad_values.reshape(key_len, key_cols)], 1
    )
    grad_before = grad_kv[:row_count]
    grad_own = grad_kv[2 * row_count :]
    returned = swap(grad_kv[row_count : 2 * row_count].astype(BF16), "core").astype(F32)
    grad_own = grad_own + jnp.where(core == 0, returned, 0.0)
    grad_before = grad_before + jnp.where(core == 0, 0.0, returned)
    for span in reversed(spans):
        back = [(mid + i + span, mid + i) for i in range(min(span, mid - span))]
        grad_before = grad_before + lax.ppermute(grad_before.astype(BF16), "zy", back).astype(F32)
    before_low = grad_before.astype(BF16)
    grad_own = (
        grad_own
        + lax.ppermute(before_low, "zy", [(b, a) for a, b in chain]).astype(F32)
        + lax.ppermute(before_low, "zy", [(mid, mid - 1)]).astype(F32)
    )
    grad_query_raw, grad_key_raw, grad_value_raw, grad_hq, grad_hk = prepare_back(
        (
            grad_queries.reshape(row_count, HEADS, HEAD),
            grad_own[:, :key_cols].reshape(row_count, KV_HEADS, HEAD),
            grad_own[:, key_cols:].reshape(row_count, KV_HEADS, HEAD),
        )
    )
    grad_query_low = grad_query_raw.astype(BF16)
    grad_kv_low = jnp.concatenate([grad_key_raw, grad_value_raw], 1).astype(BF16)
    grad_wq = left_dot(normed_low, grad_query_low)
    grad_wkv = left_dot(normed_low, grad_kv_low)
    grad_normed = (
        grad_scaled
        + right_dot(grad_mid_low, lleft)
        + right_dot(grad_query_low, wq)
        + right_dot(grad_kv_low, wkv)
    )
    unused, input_norm_back = jax.vjp(rms_norm, states, gains[0])
    grad_states, grad_g0 = input_norm_back(grad_normed)
    grad_tokens = grad_scaled + grad_states

    def scatter_sum(full):
        cols = full.shape[1]
        blocks = full.reshape(chips, 2, group_count, shard_rows, cols)
        mine = lax.dynamic_index_in_dim(blocks, core, 1, keepdims=False)
        other = lax.dynamic_index_in_dim(blocks, 1 - core, 1, keepdims=False)
        blocks = mine + swap(other.astype(BF16), "core").astype(F32)
        mine = lax.dynamic_index_in_dim(blocks, group_index, 1, keepdims=False)
        other = lax.dynamic_index_in_dim(blocks, 1 - group_index, 1, keepdims=False)
        blocks = mine + swap(other.astype(BF16), "fsdp").astype(F32)
        mid_row = shard_rows // 2
        up_sum, down_sum = None, None
        for k in list(range(1, chips)) + [0]:
            up_term = lax.dynamic_index_in_dim(blocks, ring_owner(-k), 0, False)[:mid_row]
            down_term = lax.dynamic_index_in_dim(blocks, ring_owner(k), 0, False)[mid_row:]
            if up_sum is None:
                up_sum, down_sum = up_term, down_term
            else:
                up_sum = ring(up_sum.astype(BF16), 1).astype(F32) + up_term
                down_sum = ring(down_sum.astype(BF16), -1).astype(F32) + down_term
        return jnp.concatenate([up_sum, down_sum], 0)

    head_back = jnp.stack([grad_hq, grad_hk]).reshape(2, shards, head_n).transpose(1, 0, 2)
    head_back = head_back.reshape(shards, 2 * head_n)
    head_back = jnp.pad(head_back, ((0, 0), (0, shard_rows - 2 * head_n))).reshape(-1, 1)
    gains_back = jnp.stack([grad_g0, grad_g1, grad_g2, grad_g3, grad_g4, grad_g5], 1)
    misc_back = jnp.concatenate(
        [gains_back, head_back, jnp.zeros((D, misc_cols - 7), F32)], 1
    )
    sums_b = scatter_sum(
        jnp.concatenate(
            [grad_wo, grad_plg, grad_plp.reshape(D, proj_cols), grad_lright_t], 1
        )
    )
    sums_a = scatter_sum(jnp.concatenate([grad_wq, grad_wkv, grad_lleft, misc_back], 1))

    total = jnp.broadcast_to(squares, (8, 128))
    total = total + swap(total, "core")
    total = total + swap(total, "fsdp")
    span = 1
    while span < chips:
        total = total + lax.ppermute(total, "zy", [(i, i ^ span) for i in range(chips)])
        span *= 2
    match_loss = total[0, 0] / (2.0 * D * count)

    misc_out = sums_a[:, D + 2 * key_cols + RANK :]
    return (
        result[None],
        match_loss,
        grad_tokens[None],
        grad_layer_in[None],
        sums_a[:, :D],
        sums_a[:, D : D + 2 * key_cols],
        sums_b[:, :D],
        sums_a[:, D + 2 * key_cols : D + 2 * key_cols + RANK],
        sums_b[:, D + PLD + proj_cols :].T,
        sums_b[:, D : D + PLD],
        sums_b[:, D + PLD : D + PLD + proj_cols].reshape(pl_proj.shape),
        misc_out[:, :6].T,
        misc_out[: 2 * head_n, 6].reshape(2, head_n),
        grad_ffn,
    )


def solution(mesh):
    seq, fsdp = mesh.shape["seq"], mesh.shape["fsdp"]
    fine = Mesh(mesh.devices.reshape(seq // 2, 2, fsdp), ("zy", "core", "fsdp"))
    rows = P("fsdp", ("zy", "core"), None)
    split = ("zy", "core", "fsdp")
    weights = (
        P(split, None),
        P(split, None),
        P(split, None),
        P(split, None),
        P(None, split),
        P(split, None),
        P(split, None),
        P(None, split),
        P(None, split),
        P(split, None, None),
    )
    return jax.shard_map(
        body,
        mesh=fine,
        in_specs=(rows, rows, rows, P()) + weights,
        out_specs=(rows, P(), rows, rows) + weights,
        check_vma=False,
    )
```

```python
import functools
import math

import jax
import jax.numpy as jnp
from jax import lax
from jax.experimental import pallas as pl
from jax.experimental.pallas import tpu as pltpu
from jax.sharding import Mesh, PartitionSpec as P

D = 2048
HEADS = 8
KV_HEADS = 2
HEAD = 256
WINDOW = 512
CONT_LEN = 512
RANK = 64
PLD = 256

EPSILON = 1e-06
INV_SQRT2 = 0.7071067811865476
ROPE_BASE = 10000.0
BF16 = jnp.bfloat16
F32 = jnp.float32


def rms_norm(values, gain):
    return values * lax.rsqrt(jnp.mean(values * values, axis=-1, keepdims=True) + EPSILON) * gain


def plain_norm(values):
    return values * lax.rsqrt(jnp.mean(values * values, axis=-1, keepdims=True) + EPSILON)


def rotate(values, places):
    half_dim = values.shape[-1] // 2
    freqs = jnp.exp(
        jnp.arange(half_dim, dtype=F32) * (-2.0 * math.log(ROPE_BASE) / values.shape[-1])
    )
    angles = places.astype(F32)[:, None, None] * freqs
    cosine = jnp.cos(angles)
    sine = jnp.sin(angles)
    first = values[..., :half_dim]
    second = values[..., half_dim:]
    return jnp.concatenate([first * cosine - second * sine, second * cosine + first * sine], -1)


def gelu_tanh(values):
    return jax.nn.gelu(values, approximate=True)


def gated_product(gate_in, up_in):
    return gelu_tanh(gate_in) * up_in


def full_dot(left, right):
    return jnp.dot(left, right, preferred_element_type=F32)


def left_dot(left, right):
    return lax.dot_general(left, right, (((0,), (0,)), ((), ())), preferred_element_type=F32)


def right_dot(left, right):
    return lax.dot_general(left, right, (((1,), (1,)), ((), ())), preferred_element_type=F32)


def ring_order(n):
    return list(range(0, n, 2)) + list(range(n - 1, 0, -2))


def ring_pairs(n, by):
    order = ring_order(n)
    return [(order[i], order[(i + by) % n]) for i in range(n)]


def ring(value, by):
    return lax.ppermute(value, "zy", ring_pairs(lax.axis_size("zy"), by))


def swap(value, axis):
    return lax.ppermute(value, axis, [(0, 1), (1, 0)])


MESH = pl.DeviceIdType.MESH


def ring_chip(spot, chips):
    spot = lax.rem(spot, chips)
    return jnp.where(spot < chips // 2, 2 * spot, 2 * (chips - 1 - spot) + 1)


def ring_spot(chip, chips):
    return jnp.where(lax.rem(chip, 2) == 0, chip // 2, chips - 1 - chip // 2)


def gather_kernel(chips, streams, shard, full, ring_send, ring_recv, x_send, x_recv, core_send, core_recv, own_sem):
    chip = lax.axis_index("zy")
    core = lax.axis_index("core")
    side = lax.axis_index("fsdp")
    spot = ring_spot(chip, chips)
    rows = shard.shape[0]

    def neighbour(by):
        return {"zy": ring_chip(spot + chips + by, chips)}

    other_core = {"core": 1 - core}
    other_side = {"fsdp": 1 - side}

    barrier = pltpu.get_barrier_semaphore()
    for peer in (neighbour(1), neighbour(-1), other_core, other_side):
        pl.semaphore_signal(barrier, inc=1, device_id=peer, device_id_type=MESH)
    pl.semaphore_wait(barrier, 4)

    def place(owner, its_core, its_side, stream):
        row = ((owner * 2 + its_core) * 2 + its_side) * rows
        return full.at[pl.ds(pl.multiple_of(row, rows), rows), pl.ds(stream[0], stream[1])]

    def owner_at(step, stream):
        return ring_chip(spot + chips - stream[2] * step, chips)

    def send(src, dst, sems, at, peer):
        return pltpu.make_async_remote_copy(
            src_ref=src,
            dst_ref=dst,
            send_sem=sems[0].at[at],
            recv_sem=sems[1].at[at],
            device_id=peer,
            device_id_type=MESH,
        )

    ring_sems, x_sems, core_sems = (ring_send, ring_recv), (x_send, x_recv), (core_send, core_recv)

    def ring_copy(number, away, step, src=None):
        stream = streams[number]
        its_side = 1 - side if away else side
        spot_ref = place(owner_at(step, stream), core, its_side, stream)
        return send(src if src is not None else spot_ref, spot_ref, ring_sems, (number, away, step), neighbour(stream[2]))

    def ring_arrival(number, away, step):
        stream = streams[number]
        its_side = 1 - side if away else side
        spot_ref = place(owner_at(step, stream), core, its_side, stream)
        return send(spot_ref, spot_ref, ring_sems, (number, away, step - 1), neighbour(stream[2]))

    def x_copy(number, step, its_side, src=None):
        stream = streams[number]
        spot_ref = place(owner_at(step, stream), core, its_side, stream)
        return send(src if src is not None else spot_ref, spot_ref, x_sems, (number, step), other_side)

    def core_copy(number, away, step, its_core, src=None):
        stream = streams[number]
        its_side = 1 - side if away else side
        spot_ref = place(owner_at(step, stream), its_core, its_side, stream)
        return send(src if src is not None else spot_ref, spot_ref, core_sems, (number, away, step), other_core)

    def cut(stream):
        return shard.at[:, pl.ds(stream[0], stream[1])]

    own_row = ((chip * 2 + core) * 2 + side) * rows
    own = pltpu.make_async_copy(
        shard, full.at[pl.ds(pl.multiple_of(own_row, rows), rows), :], own_sem
    )
    own.start()
    numbers = range(len(streams))
    for number in numbers:
        if streams[number][3]:
            x_copy(number, 0, side, cut(streams[number])).start()
    for number in numbers:
        ring_copy(number, 0, 0, cut(streams[number])).start()
    for number in numbers:
        if not streams[number][3]:
            x_copy(number, 0, side, cut(streams[number])).start()
    for number in numbers:
        core_copy(number, 0, 0, core, cut(streams[number])).start()
    for number in numbers:
        if streams[number][3]:
            x_copy(number, 0, 1 - side).wait_recv()
            ring_copy(number, 1, 0).start()
            core_copy(number, 1, 0, core).start()

    def turn(step, carry):
        for number in numbers:
            aways = (0, 1) if streams[number][3] else (0,)
            for away in aways:
                ring_arrival(number, away, step).wait_recv()

                @pl.when(step < chips - 1)
                def _(number=number, away=away):
                    ring_copy(number, away, step).start()

                core_copy(number, away, step, core).start()
            if not streams[number][3]:
                x_copy(number, step, side).start()
        for number in numbers:
            if not streams[number][3]:
                x_copy(number, step - 1, 1 - side).wait_recv()
                core_copy(number, 1, step - 1, core).start()
        return carry

    lax.fori_loop(1, chips, turn, 0)
    for number in numbers:
        if not streams[number][3]:
            x_copy(number, chips - 1, 1 - side).wait_recv()
            core_copy(number, 1, chips - 1, core).start()
    own.wait()

    def drain(step, carry):
        for number in numbers:
            first = streams[number][3]
            for away in (0, 1):
                core_copy(number, away, step, 1 - core).wait_recv()
                core_copy(number, away, step, core).wait_send()
                if first or not away:

                    @pl.when(step < chips - 1)
                    def _(number=number, away=away):
                        ring_copy(number, away, step).wait_send()

            if not first:
                x_copy(number, step, side).wait_send()
        return carry

    lax.fori_loop(0, chips, drain, 0)
    for number in numbers:
        if streams[number][3]:
            x_copy(number, 0, side).wait_send()


def gather_all(shard, chips):
    rows, cols = shard.shape
    tiles = cols // 128
    first = int(round(tiles * 0.43)) // 2 * 2
    rest = tiles - first
    bounds = [0, first // 2, first, first + rest // 2, tiles]
    streams = tuple(
        (128 * bounds[i], 128 * (bounds[i + 1] - bounds[i]), 1 if i % 2 == 0 else -1, i < 2)
        for i in range(4)
    )
    dma = pltpu.SemaphoreType.DMA
    return pl.pallas_call(
        functools.partial(gather_kernel, chips, streams),
        out_shape=jax.ShapeDtypeStruct((rows * 4 * chips, cols), shard.dtype),
        in_specs=[pl.BlockSpec(memory_space=pl.ANY)],
        out_specs=pl.BlockSpec(memory_space=pl.ANY),
        scratch_shapes=[
            dma((4, 2, chips)),
            dma((4, 2, chips)),
            dma((4, chips)),
            dma((4, chips)),
            dma((4, 2, chips)),
            dma((4, 2, chips)),
            dma,
        ],
        compiler_params=pltpu.CompilerParams(collective_id=0, has_side_effects=True),
        cost_estimate=pl.CostEstimate(
            flops=0, bytes_accessed=2 * rows * 4 * chips * cols * 2, transcendentals=0
        ),
        name="gather_all",
    )(shard)


def sum_kernel(chips, streams, counts, *refs):
    arrays, outs, held, core_in, ring_in, x_in, sems = refs_of(counts, refs)
    load_sem, core_send, core_recv, ring_send, ring_recv, x_send, x_recv = sems
    chip = lax.axis_index("zy")
    core = lax.axis_index("core")
    side = lax.axis_index("fsdp")
    spot = ring_spot(chip, chips)
    far = 1 - side

    def neighbour(by):
        return {"zy": ring_chip(spot + chips + by, chips)}

    other_core = {"core": 1 - core}
    other_side = {"fsdp": 1 - side}
    barrier = pltpu.get_barrier_semaphore()
    for peer in (neighbour(1), neighbour(-1), other_core, other_side):
        pl.semaphore_signal(barrier, inc=1, device_id=peer, device_id_type=MESH)
    pl.semaphore_wait(barrier, 4)

    numbers = range(len(streams))

    def owner_at(number, turn):
        return ring_chip(spot + 2 * chips - streams[number][3] * turn, chips)

    def cols(number):
        return pl.ds(streams[number][1], streams[number][2])

    def remote(src, dst, send, recv, peer):
        return pltpu.make_async_remote_copy(
            src_ref=src, dst_ref=dst, send_sem=send, recv_sem=recv, device_id=peer, device_id_type=MESH
        )

    def core_copy(number, turn):
        owner = owner_at(number, turn)
        array = streams[number][0]
        return remote(
            arrays[array].at[owner, 1 - core, :, :, cols(number)],
            core_in[array].at[owner, :, :, cols(number)],
            core_send.at[number, turn - 1],
            core_recv.at[number, turn - 1],
            other_core,
        )

    def x_copy(number, turn):
        array = streams[number][0]
        first = streams[number][4]
        slot = turn - 1 if first else 0
        return remote(
            held[array].at[owner_at(number, turn), far, :, cols(number)],
            x_in[number].at[slot],
            x_send.at[number, slot],
            x_recv.at[number, slot],
            other_side,
        )

    def ring_copy(number, turn):
        array = streams[number][0]
        owner = owner_at(number, turn)
        if streams[number][4]:
            src = held[array].at[owner, pl.ds(side, 1), :, cols(number)]
        else:
            src = held[array].at[owner, :, :, cols(number)]
        return remote(
            src,
            ring_in[number].at[turn - 1],
            ring_send.at[number, turn - 1],
            ring_recv.at[number, turn - 1],
            neighbour(streams[number][3]),
        )

    loads = [
        pltpu.make_async_copy(arrays[i].at[:, core], held[i], load_sem.at[i])
        for i in range(len(arrays))
    ]

    def send_cores(turn, carry):
        for number in numbers:
            core_copy(number, turn).start()
        return carry

    lax.fori_loop(1, 2, send_cores, 0)
    for load in loads:
        load.start()
    lax.fori_loop(2, chips + 1, send_cores, 0)
    for load in loads:
        load.wait()

    def add_cores(number, turn):
        array = streams[number][0]
        owner = owner_at(number, turn)
        core_copy(number, turn).wait_recv()
        for its_side in range(2):
            held[array][owner, its_side, :, cols(number)] = (
                held[array][owner, its_side, :, cols(number)].astype(F32)
                + core_in[array][owner, its_side, :, cols(number)].astype(F32)
            ).astype(BF16)

    def begin(turn):
        for number in numbers:
            if streams[number][4]:
                add_cores(number, turn)
                x_copy(number, turn).start()

    begin(1)

    def round_trip(turn, carry):
        @pl.when(turn < chips)
        def _():
            begin(turn + 1)

        for number in numbers:
            array = streams[number][0]
            owner = owner_at(number, turn)
            if not streams[number][4]:
                add_cores(number, turn)

                @pl.when(turn > 1)
                def _(number=number, array=array, owner=owner):
                    ring_copy(number, turn - 1).wait_recv()
                    for its_side in range(2):
                        held[array][owner, its_side, :, cols(number)] = (
                            held[array][owner, its_side, :, cols(number)].astype(F32)
                            + ring_in[number][turn - 2, its_side].astype(F32)
                        ).astype(BF16)

                @pl.when(turn < chips)
                def _(number=number):
                    ring_copy(number, turn).start()

        for number in numbers:
            array = streams[number][0]
            owner = owner_at(number, turn)
            if streams[number][4]:
                x_copy(number, turn).wait_recv()

                @pl.when(turn == 1)
                def _(number=number, array=array, owner=owner):
                    held[array][owner, side, :, cols(number)] = (
                        held[array][owner, side, :, cols(number)].astype(F32)
                        + x_in[number][turn - 1].astype(F32)
                    ).astype(BF16)

                @pl.when(turn > 1)
                def _(number=number, array=array, owner=owner):
                    ring_copy(number, turn - 1).wait_recv()
                    total = (
                        held[array][owner, side, :, cols(number)].astype(F32)
                        + x_in[number][turn - 1].astype(F32)
                        + ring_in[number][turn - 2, 0].astype(F32)
                    )
                    held[array][owner, side, :, cols(number)] = total.astype(BF16)

                    @pl.when(turn == chips)
                    def _():
                        outs[array][:, cols(number)] = total

                @pl.when(turn < chips)
                def _(number=number):
                    ring_copy(number, turn).start()

        return carry

    lax.fori_loop(1, chips + 1, round_trip, 0)
    for number in numbers:
        if not streams[number][4]:
            x_copy(number, chips).start()
    for number in numbers:
        array = streams[number][0]
        if not streams[number][4]:
            x_copy(number, chips).wait_recv()
            outs[array][:, cols(number)] = held[array][chip, side, :, cols(number)].astype(
                F32
            ) + x_in[number][0].astype(F32)

    def drain(turn, carry):
        for number in numbers:
            core_copy(number, turn).wait_send()
            if streams[number][4]:
                x_copy(number, turn).wait_send()

            @pl.when(turn < chips)
            def _(number=number):
                ring_copy(number, turn).wait_send()

        return carry

    lax.fori_loop(1, chips + 1, drain, 0)
    for number in numbers:
        if not streams[number][4]:
            x_copy(number, chips).wait_send()


def refs_of(counts, refs):
    groups, at = [], 0
    for count in counts:
        groups.append(refs[at : at + count])
        at += count
    return groups


def sum_all(arrays, firsts, chips):
    rows = arrays[0].shape[0] // (4 * chips)
    streams = []
    for i, (array, first) in enumerate(zip(arrays, firsts)):
        width = array.shape[1]
        left = width // 256 * 128
        streams.append((i, 0, left, 1, first))
        streams.append((i, left, width - left, -1, first))
    streams = tuple(sorted(streams, key=lambda stream: stream[4]))
    count, number = len(arrays), len(streams)
    dma = pltpu.SemaphoreType.DMA
    vmem = pltpu.VMEM
    scratch = (
        [vmem((chips, 2, rows, a.shape[1]), BF16) for a in arrays]
        + [vmem((chips, 2, rows, a.shape[1]), BF16) for a in arrays]
        + [vmem((chips - 1, 1 if first else 2, rows, width), BF16) for _, _, width, _, first in streams]
        + [vmem((chips if first else 1, rows, width), BF16) for _, _, width, _, first in streams]
        + [dma((count,))]
        + [dma((number, chips)) for _ in range(6)]
    )
    return pl.pallas_call(
        functools.partial(
            sum_kernel, chips, streams, (count, count, count, count, number, number, 7)
        ),
        out_shape=[jax.ShapeDtypeStruct((rows, a.shape[1]), F32) for a in arrays],
        in_specs=[pl.BlockSpec(memory_space=pl.ANY)] * count,
        out_specs=[pl.BlockSpec(memory_space=pltpu.VMEM)] * count,
        scratch_shapes=scratch,
        compiler_params=pltpu.CompilerParams(
            collective_id=1, has_side_effects=True, vmem_limit_bytes=56 << 20
        ),
        cost_estimate=pl.CostEstimate(
            flops=0, bytes_accessed=sum(2 * a.size for a in arrays), transcendentals=0
        ),
        name="sum_all",
    )(*[a.reshape(chips, 2, 2, rows, a.shape[1]) for a in arrays])


def tie(*values):
    return lax.optimization_barrier(values)


def shares(total, count):
    return [total // count + (1 if i < total % count else 0) for i in range(count)]


def rows_of_four(own):
    pair = jnp.concatenate([own, swap(own, "fsdp")], 0)
    return jnp.concatenate([pair, swap(pair, "core")], 0)


def sum_of_four(partial):
    count = partial.shape[0] // 4
    low = partial[2 * count :].astype(BF16)
    pair = partial[: 2 * count] + swap(low, "core").astype(F32)
    low = pair[count:].astype(BF16)
    return pair[:count] + swap(low, "fsdp").astype(F32)


def body(
    tokens,
    per_layer,
    teacher,
    cont_lengths,
    w_query,
    w_kv,
    w_out,
    laurel_left,
    laurel_right,
    pl_gate,
    pl_proj,
    norm_gains,
    head_gains,
    ffn_weight,
):
    states = tokens[0].astype(F32)
    layer_in = per_layer[0].astype(F32)
    target = teacher[0].astype(F32)
    row_count = states.shape[0]
    chips = lax.axis_size("zy")
    seq_count = 2 * chips
    group_count = lax.axis_size("fsdp")
    shards = seq_count * group_count
    chip = lax.axis_index("zy")
    core = lax.axis_index("core")
    seq_index = chip * 2 + core
    group_index = lax.axis_index("fsdp")
    half_point = seq_count // 2
    prompt_len = half_point * row_count
    cont_shards = CONT_LEN // row_count
    cont_count = prompt_len // CONT_LEN
    is_cont = seq_index >= half_point
    rel_index = seq_index - half_point
    local_shard = jnp.where(is_cont, rel_index % cont_shards, 0)
    cont_index = jnp.where(is_cont, rel_index // cont_shards, 0)
    first_place = jnp.where(is_cont, prompt_len + local_shard * row_count, seq_index * row_count)
    row_range = jnp.arange(row_count, dtype=jnp.int32)
    places = first_place + row_range
    group_lengths = jnp.sum(
        jnp.where(
            jnp.arange(group_count, dtype=jnp.int32)[:, None] == group_index, cont_lengths, 0
        ),
        axis=0,
    )
    my_length = jnp.sum(
        jnp.where(jnp.arange(cont_count, dtype=jnp.int32) == cont_index, group_lengths, 0)
    )
    valid = jnp.logical_or(
        jnp.logical_not(is_cont), local_shard * row_count + row_range < my_length
    )
    weight_mask = valid.astype(F32)
    count = F32(group_count * prompt_len) + jnp.sum(cont_lengths).astype(F32)
    total_slots = float(row_count * seq_count * group_count)
    shard_rows = w_query.shape[0]
    key_cols = KV_HEADS * HEAD
    proj_cols = pl_proj.shape[0] * D // shard_rows
    misc_cols = RANK
    head_part = head_gains.reshape(-1, 1)
    misc = jnp.concatenate(
        [
            norm_gains.T,
            jnp.pad(head_part, ((0, shard_rows - head_part.shape[0]), (0, 0))),
            jnp.zeros((shard_rows, misc_cols - 7), BF16),
        ],
        1,
    )
    pack = jnp.concatenate(
        [
            w_query,
            w_kv,
            laurel_left,
            misc,
            pl_gate,
            pl_proj.reshape(shard_rows, proj_cols),
            w_out,
            laurel_right.T,
            jnp.zeros((shard_rows, 128 - RANK), BF16),
        ],
        1,
    )

    units = ffn_weight.shape[0]
    half = units // 2
    by_kind = ffn_weight.transpose(1, 0, 2)
    ups, downs = [by_kind[:, :half]], [by_kind[:, half:]]
    stage_steps = shares(chips - 1, 7)

    def pass_on(stage):
        for _ in range(stage_steps[stage]):
            ups.append(ring(ups[-1], 1))
            downs.append(ring(downs[-1], -1))

    def stage_end(values):
        (ups[-1], downs[-1]), values = tie((ups[-1], downs[-1]), values)
        return values

    pass_on(0)
    full = stage_end(gather_all(pack, chips))
    pass_on(1)
    at = 0
    pieces = []
    for width in (D, 2 * key_cols, RANK, misc_cols, PLD, proj_cols, D, RANK):
        pieces.append(full[:, at : at + width])
        at += width
    wq, wkv, lleft, misc_full, plg, plp, wo, lright = pieces
    plp = plp.reshape(PLD, D)
    lright = lright.T
    gains = misc_full[:, :6].T.astype(F32)
    head_n = head_gains.shape[1]
    head_gain = (
        misc_full[:, 6]
        .reshape(shards, shard_rows)[:, : 2 * head_n]
        .reshape(shards, 2, head_n)
        .transpose(1, 0, 2)
        .reshape(2, HEAD)
        .astype(F32)
    )

    normed = rms_norm(states, gains[0])
    normed_low = normed.astype(BF16)
    query_raw = full_dot(normed_low, wq)
    kv_raw = full_dot(normed_low, wkv)

    def prepare(q_input, k_input, v_input, q_gain, k_gain):
        q_heads = rotate(rms_norm(q_input.reshape(row_count, HEADS, HEAD), q_gain), places)
        k_heads = rotate(rms_norm(k_input.reshape(row_count, KV_HEADS, HEAD), k_gain), places)
        v_heads = plain_norm(v_input.reshape(row_count, KV_HEADS, HEAD))
        return (q_heads, k_heads, v_heads)

    (queries, keys_new, values_new), prepare_back = jax.vjp(
        prepare, query_raw, kv_raw[:, :key_cols], kv_raw[:, key_cols:], head_gain[0], head_gain[1]
    )
    query_low = queries.astype(BF16)
    kv_own = jnp.concatenate(
        [
            keys_new.reshape(row_count, key_cols).astype(BF16),
            values_new.reshape(row_count, key_cols).astype(BF16),
        ],
        1,
    )

    query_low, kv_own = stage_end((query_low, kv_own))
    pass_on(2)

    mid = chips // 2
    chain = [(i, i + 1) for i in range(mid - 1)] + [(mid - 1, mid + 1)]
    kv_before = jnp.where(
        chip == mid,
        lax.ppermute(kv_own, "zy", [(mid - 1, mid)]),
        lax.ppermute(kv_own, "zy", chain),
    )
    spans = []
    span = 2
    while span < mid:
        spans.append(span)
        span *= 2
    for span in spans:
        moved = lax.ppermute(
            kv_before, "zy", [(mid + i, mid + i + span) for i in range(min(span, mid - span))]
        )
        fresh = jnp.logical_and(chip >= mid + span, chip < mid + 2 * span)
        kv_before = jnp.where(fresh, moved, kv_before)
    kv_other = swap(jnp.where(core == 0, kv_own, kv_before), "core")
    keys_all = jnp.concatenate([kv_before, kv_other, kv_own], 0)
    keys_all = stage_end(keys_all)
    pass_on(3)
    key_len = keys_all.shape[0]
    key_places = first_place - 2 * row_count + jnp.arange(key_len, dtype=jnp.int32)
    visible = (
        (key_places[None, :] <= places[:, None])
        & (places[:, None] - key_places[None, :] < WINDOW)
        & (key_places[None, :] >= 0)
    )
    group_heads = HEADS // KV_HEADS
    query_grouped = query_low.reshape(row_count, KV_HEADS, group_heads, HEAD)
    key_heads = keys_all[:, :key_cols].reshape(key_len, KV_HEADS, HEAD)
    value_heads = keys_all[:, key_cols:].reshape(key_len, KV_HEADS, HEAD)

    def masked_scores():
        scores = jnp.einsum(
            "qgjd,kgd->gjqk", query_grouped, key_heads, preferred_element_type=F32
        )
        return jnp.where(visible, scores, -1e30)

    scores_fwd = masked_scores()
    top_score = jnp.max(scores_fwd, axis=-1, keepdims=True)
    expo = jnp.exp(scores_fwd - top_score)
    totals = jnp.sum(expo, axis=-1, keepdims=True)
    probs = expo / totals
    log_total = top_score + jnp.log(totals)
    probs_low = probs.astype(BF16)
    context = jnp.einsum("gjqk,kgd->qgjd", probs_low, value_heads, preferred_element_type=F32)
    context_low = context.reshape(row_count, HEADS * HEAD).astype(BF16)
    attn_raw = full_dot(context_low, wo)
    attn_out = rms_norm(attn_raw, gains[1])
    laurel_mid = full_dot(normed_low, lleft).astype(BF16)
    laurel_raw = full_dot(laurel_mid, lright)
    mixed = (states + attn_out + normed + rms_norm(laurel_raw, gains[2])) * INV_SQRT2
    ffn_in = rms_norm(mixed, gains[3]).astype(BF16)

    ffn_in = stage_end(ffn_in)
    pass_on(4)
    ffn_rows = stage_end(rows_of_four(ffn_in))
    gates, uppers, hiddens, part_weights, parts = [], [], [], [], []
    running = None

    def forward_part(running, first, last):
        weights = [
            jnp.concatenate([w[kind] for k in range(first, last) for w in (ups[k], downs[k])], 0)
            for kind in range(3)
        ]
        gate = right_dot(ffn_rows, weights[0])
        upper = right_dot(ffn_rows, weights[1])
        hidden = gated_product(gate, upper).astype(BF16)
        term = full_dot(hidden, weights[2])
        gates.append(gate)
        uppers.append(upper)
        hiddens.append(hidden)
        part_weights.append(weights)
        parts.append(range(first, last))
        return term if running is None else running + term

    here = len(ups)
    pass_on(5)
    cut_a = max(1, here * 2 // 3)
    running = stage_end(forward_part(None, 0, cut_a))
    here = len(ups)
    pass_on(6)
    running = forward_part(running, cut_a, here)
    if here < chips:
        running = stage_end(running)
        running = forward_part(running, here, chips)
    down_out = sum_of_four(running)
    after_ffn = mixed + rms_norm(down_out, gains[4])
    after_low = after_ffn.astype(BF16)
    pl_raw = full_dot(after_low, plg)
    pl_act = gelu_tanh(pl_raw)
    pl_mid = (pl_act * layer_in).astype(BF16)
    pl_out = full_dot(pl_mid, plp)
    result = after_ffn + rms_norm(pl_out, gains[5])
    errors = result - target
    squares = jnp.sum(weight_mask[:, None] * errors * errors)

    grad_out = weight_mask[:, None] * errors * (total_slots / count)
    unused, pl_norm_back = jax.vjp(rms_norm, pl_out, gains[5])
    grad_pl_out, grad_g5 = pl_norm_back(grad_out)
    grad_pl_low = grad_pl_out.astype(BF16)
    grad_plp = left_dot(pl_mid, grad_pl_low)
    grad_pl_mid = right_dot(grad_pl_low, plp)
    grad_layer_in = grad_pl_mid * pl_act
    unused, gelu_back = jax.vjp(gelu_tanh, pl_raw)
    grad_pl_raw = gelu_back(grad_pl_mid * layer_in)[0].astype(BF16)
    grad_plg = left_dot(after_low, grad_pl_raw)
    grad_after = grad_out + right_dot(grad_pl_raw, plg)
    unused, down_norm_back = jax.vjp(rms_norm, down_out, gains[4])
    grad_down, grad_g4 = down_norm_back(grad_after)
    grad_down_low = grad_down.astype(BF16)

    grad_down_rows = rows_of_four(grad_down_low)
    grad_gates, grad_uppers = [], []

    def backward_part(number):
        unused, act_back = jax.vjp(gated_product, gates[number], uppers[number])
        grad_gate, grad_upper = act_back(right_dot(grad_down_rows, part_weights[number][2]))
        return grad_gate.astype(BF16), grad_upper.astype(BF16)

    def unit_grads(k):
        for part, (gg, gu), hid in zip(parts, grad_parts, hiddens):
            if k in part:
                at = (k - part[0]) * units
                up_cut, down_cut = slice(at, at + half), slice(at + half, at + units)
                return (
                    left_dot(jnp.concatenate([gg[:, up_cut], gu[:, up_cut]], 1), ffn_rows),
                    left_dot(jnp.concatenate([gg[:, down_cut], gu[:, down_cut]], 1), ffn_rows),
                    left_dot(hid[:, at : at + units], grad_down_rows),
                )

    def add_terms(arrived, terms):
        halves = (terms[0], terms[2][:half], terms[1], terms[2][half:])
        if arrived is None:
            return halves
        return tuple(a.astype(F32) + t for a, t in zip(arrived, halves))

    order = list(range(1, chips)) + [0]
    ring_steps = shares(chips - 1, 7)
    done = 0
    sums = None

    def move(sums):
        low = [s.astype(BF16) for s in sums]
        return [ring(low[0], 1), ring(low[1], 1), ring(low[2], -1), ring(low[3], -1)]

    def beside(stage, work):
        nonlocal done, sums
        values = None
        for step in range(ring_steps[stage]):
            arrived = move(sums)
            done += 1
            terms = unit_grads(order[done])
            if step == 0:
                values = work()
            arrived, terms, values = tie(arrived, terms, values)
            sums = add_terms(arrived, terms)
        return work() if values is None else values

    grad_parts = [backward_part(0)]
    sums = add_terms(None, unit_grads(order[0]))

    def work():
        return [backward_part(number) for number in range(1, len(parts))]

    grad_parts += beside(0, work)

    def work():
        running = None
        for weights, (gg, gu) in zip(part_weights, grad_parts):
            term = full_dot(gg, weights[0]) + full_dot(gu, weights[1])
            running = term if running is None else running + term
        return running

    running = beside(1, work)
    grad_ffn_in = beside(2, lambda: sum_of_four(running))
    def work():
        unused, mix_norm_back = jax.vjp(rms_norm, mixed, gains[3])
        grad_mixed_norm, grad_g3 = mix_norm_back(grad_ffn_in)
        grad_scaled = (grad_after + grad_mixed_norm) * INV_SQRT2
        unused, laurel_norm_back = jax.vjp(rms_norm, laurel_raw, gains[2])
        grad_laurel, grad_g2 = laurel_norm_back(grad_scaled)
        grad_laurel_low = grad_laurel.astype(BF16)
        grad_lright_t = left_dot(grad_laurel_low, laurel_mid)
        grad_mid_low = right_dot(grad_laurel_low, lright).astype(BF16)
        grad_lleft = left_dot(normed_low, grad_mid_low)
        unused, attn_norm_back = jax.vjp(rms_norm, attn_raw, gains[1])
        grad_attn, grad_g1 = attn_norm_back(grad_scaled)
        grad_attn_low = grad_attn.astype(BF16)
        grad_wo = left_dot(context_low, grad_attn_low)
        grad_context = right_dot(grad_attn_low, wo).astype(BF16)
        return (
            grad_context,
            grad_scaled,
            grad_wo,
            grad_lleft,
            grad_lright_t,
            grad_mid_low,
            (grad_g1, grad_g2, grad_g3),
        )

    (
        grad_context,
        grad_scaled,
        grad_wo,
        grad_lleft,
        grad_lright_t,
        grad_mid_low,
        (grad_g1, grad_g2, grad_g3),
    ) = beside(3, work)
    grad_context = grad_context.reshape(row_count, KV_HEADS, group_heads, HEAD)

    def work():
        probs_again = jnp.exp(masked_scores() - log_total)
        grad_probs = jnp.einsum(
            "qgjd,kgd->gjqk", grad_context, value_heads, preferred_element_type=F32
        )
        grad_scores = (
            probs_again * (grad_probs - jnp.sum(probs_again * grad_probs, axis=-1, keepdims=True))
        ).astype(BF16)
        grad_queries = jnp.einsum("gjqk,kgd->qgjd", grad_scores, key_heads, preferred_element_type=F32)
        grad_keys = jnp.einsum(
            "gjqk,qgjd->kgd", grad_scores, query_grouped, preferred_element_type=F32
        )
        grad_values = jnp.einsum(
            "gjqk,qgjd->kgd", probs_again.astype(BF16), grad_context, preferred_element_type=F32
        )
        grad_kv = jnp.concatenate(
            [grad_keys.reshape(key_len, key_cols), grad_values.reshape(key_len, key_cols)], 1
        )
        return grad_queries, grad_kv

    grad_queries, grad_kv = beside(4, work)

    def work():
        grad_before = grad_kv[:row_count]
        grad_own = grad_kv[2 * row_count :]
        returned = swap(grad_kv[row_count : 2 * row_count].astype(BF16), "core").astype(F32)
        grad_own = grad_own + jnp.where(core == 0, returned, 0.0)
        grad_before = grad_before + jnp.where(core == 0, 0.0, returned)
        for span in reversed(spans):
            back = [(mid + i + span, mid + i) for i in range(min(span, mid - span))]
            grad_before = grad_before + lax.ppermute(grad_before.astype(BF16), "zy", back).astype(F32)
        before_low = grad_before.astype(BF16)
        grad_own = (
            grad_own
            + lax.ppermute(before_low, "zy", [(b, a) for a, b in chain]).astype(F32)
            + lax.ppermute(before_low, "zy", [(mid, mid - 1)]).astype(F32)
        )
        return grad_own

    grad_own = beside(5, work)
    def work():
        grad_query_raw, grad_key_raw, grad_value_raw, grad_hq, grad_hk = prepare_back(
            (
                grad_queries.reshape(row_count, HEADS, HEAD),
                grad_own[:, :key_cols].reshape(row_count, KV_HEADS, HEAD),
                grad_own[:, key_cols:].reshape(row_count, KV_HEADS, HEAD),
            )
        )
        grad_query_low = grad_query_raw.astype(BF16)
        grad_kv_low = jnp.concatenate([grad_key_raw, grad_value_raw], 1).astype(BF16)
        grad_wq = left_dot(normed_low, grad_query_low)
        grad_wkv = left_dot(normed_low, grad_kv_low)
        grad_normed = (
            grad_scaled
            + right_dot(grad_mid_low, lleft)
            + right_dot(grad_query_low, wq)
            + right_dot(grad_kv_low, wkv)
        )
        unused, input_norm_back = jax.vjp(rms_norm, states, gains[0])
        grad_states, grad_g0 = input_norm_back(grad_normed)
        grad_tokens = grad_scaled + grad_states
        return grad_tokens, grad_wq, grad_wkv, grad_g0, grad_hq, grad_hk

    grad_tokens, grad_wq, grad_wkv, grad_g0, grad_hq, grad_hk = beside(6, work)
    up_pair, up_down, down_pair, down_down = sums
    grad_ffn = jnp.stack(
        [
            jnp.concatenate([up_pair[:half], down_pair[:half]], 0),
            jnp.concatenate([up_pair[half:], down_pair[half:]], 0),
            jnp.concatenate([up_down, down_down], 0),
        ],
        1,
    )

    head_back = jnp.stack([grad_hq, grad_hk]).reshape(2, shards, head_n).transpose(1, 0, 2)
    head_back = head_back.reshape(shards, 2 * head_n)
    head_back = jnp.pad(head_back, ((0, 0), (0, shard_rows - 2 * head_n))).reshape(-1, 1)
    gains_back = jnp.stack([grad_g0, grad_g1, grad_g2, grad_g3, grad_g4, grad_g5], 1)
    misc_back = jnp.concatenate(
        [gains_back, head_back, jnp.zeros((D, misc_cols - 7), F32)], 1
    )
    rest_back = jnp.concatenate(
        [
            grad_lleft,
            misc_back,
            grad_plg,
            grad_plp.reshape(D, proj_cols),
            grad_lright_t,
            jnp.zeros((D, 128 - RANK), F32),
        ],
        1,
    )
    sums_wq, sums_wkv, sums_wo, sums_rest = sum_all(
        [g.astype(BF16) for g in (grad_wq, grad_wkv, grad_wo, rest_back)],
        (False, False, True, True),
        chips,
    )
    at = 0
    rest = []
    for width in (RANK, misc_cols, PLD, proj_cols, RANK):
        rest.append(sums_rest[:, at : at + width])
        at += width

    total = jnp.broadcast_to(squares, (8, 128))
    total = total + swap(total, "core")
    total = total + swap(total, "fsdp")
    span = 1
    while span < chips:
        total = total + lax.ppermute(total, "zy", [(i, i ^ span) for i in range(chips)])
        span *= 2
    match_loss = total[0, 0] / (2.0 * D * count)

    return (
        result[None],
        match_loss,
        grad_tokens[None],
        grad_layer_in[None],
        sums_wq,
        sums_wkv,
        sums_wo,
        rest[0],
        rest[4].T,
        rest[2],
        rest[3].reshape(pl_proj.shape),
        rest[1][:, :6].T,
        rest[1][: 2 * head_n, 6].reshape(2, head_n),
        grad_ffn,
    )


def solution(mesh):
    seq, fsdp = mesh.shape["seq"], mesh.shape["fsdp"]
    fine = Mesh(mesh.devices.reshape(seq // 2, 2, fsdp), ("zy", "core", "fsdp"))
    rows = P("fsdp", ("zy", "core"), None)
    split = ("zy", "core", "fsdp")
    weights = (
        P(split, None),
        P(split, None),
        P(split, None),
        P(split, None),
        P(None, split),
        P(split, None),
        P(split, None),
        P(None, split),
        P(None, split),
        P(split, None, None),
    )
    return jax.shard_map(
        body,
        mesh=fine,
        in_specs=(rows, rows, rows, P()) + weights,
        out_specs=(rows, P(), rows, rows) + weights,
        check_vma=False,
    )
```

```python
import functools
import math

import jax
import jax.numpy as jnp
from jax import lax
from jax.experimental import pallas as pl
from jax.experimental.pallas import tpu as pltpu
from jax.sharding import Mesh, PartitionSpec as P

D = 2048
HEADS = 8
KV_HEADS = 2
HEAD = 256
WINDOW = 512
CONT_LEN = 512
RANK = 64
PLD = 256

EPSILON = 1e-06
INV_SQRT2 = 0.7071067811865476
ROPE_BASE = 10000.0
BF16 = jnp.bfloat16
F32 = jnp.float32


def rms_norm(values, gain):
    return values * lax.rsqrt(jnp.mean(values * values, axis=-1, keepdims=True) + EPSILON) * gain


def gelu_tanh(values):
    return jax.nn.gelu(values, approximate=True)


def gated_product(gate_in, up_in):
    return gelu_tanh(gate_in) * up_in


def full_dot(left, right):
    return jnp.dot(left, right, preferred_element_type=F32)


def left_dot(left, right):
    return lax.dot_general(left, right, (((0,), (0,)), ((), ())), preferred_element_type=F32)


def right_dot(left, right):
    return lax.dot_general(left, right, (((1,), (1,)), ((), ())), preferred_element_type=F32)


def ring_order(n):
    return list(range(0, n, 2)) + list(range(n - 1, 0, -2))


def ring_pairs(n, by):
    order = ring_order(n)
    return [(order[i], order[(i + by) % n]) for i in range(n)]


def ring(value, by):
    return lax.ppermute(value, "zy", ring_pairs(lax.axis_size("zy"), by))


def swap(value, axis):
    return lax.ppermute(value, axis, [(0, 1), (1, 0)])


MESH = pl.DeviceIdType.MESH


def ring_chip(spot, chips):
    spot = lax.rem(spot, chips)
    return jnp.where(spot < chips // 2, 2 * spot, 2 * (chips - 1 - spot) + 1)


def ring_spot(chip, chips):
    return jnp.where(lax.rem(chip, 2) == 0, chip // 2, chips - 1 - chip // 2)


def gather_kernel(chips, streams, shard, full, ring_send, ring_recv, x_send, x_recv, core_send, core_recv, own_sem):
    chip = lax.axis_index("zy")
    core = lax.axis_index("core")
    side = lax.axis_index("fsdp")
    spot = ring_spot(chip, chips)
    rows = shard.shape[0]

    def neighbour(by):
        return {"zy": ring_chip(spot + chips + by, chips)}

    other_core = {"core": 1 - core}
    other_side = {"fsdp": 1 - side}

    barrier = pltpu.get_barrier_semaphore()
    for peer in (neighbour(1), neighbour(-1), other_core, other_side):
        pl.semaphore_signal(barrier, inc=1, device_id=peer, device_id_type=MESH)
    pl.semaphore_wait(barrier, 4)

    def place(owner, its_core, its_side, stream):
        row = ((owner * 2 + its_core) * 2 + its_side) * rows
        return full.at[pl.ds(pl.multiple_of(row, rows), rows), pl.ds(stream[0], stream[1])]

    def owner_at(step, stream):
        return ring_chip(spot + chips - stream[2] * step, chips)

    def send(src, dst, sems, at, peer):
        return pltpu.make_async_remote_copy(
            src_ref=src,
            dst_ref=dst,
            send_sem=sems[0].at[at],
            recv_sem=sems[1].at[at],
            device_id=peer,
            device_id_type=MESH,
        )

    ring_sems, x_sems, core_sems = (ring_send, ring_recv), (x_send, x_recv), (core_send, core_recv)

    def ring_copy(number, away, step, src=None):
        stream = streams[number]
        its_side = 1 - side if away else side
        spot_ref = place(owner_at(step, stream), core, its_side, stream)
        return send(src if src is not None else spot_ref, spot_ref, ring_sems, (number, away, step), neighbour(stream[2]))

    def ring_arrival(number, away, step):
        stream = streams[number]
        its_side = 1 - side if away else side
        spot_ref = place(owner_at(step, stream), core, its_side, stream)
        return send(spot_ref, spot_ref, ring_sems, (number, away, step - 1), neighbour(stream[2]))

    def x_copy(number, step, its_side, src=None):
        stream = streams[number]
        spot_ref = place(owner_at(step, stream), core, its_side, stream)
        return send(src if src is not None else spot_ref, spot_ref, x_sems, (number, step), other_side)

    def core_copy(number, away, step, its_core, src=None):
        stream = streams[number]
        its_side = 1 - side if away else side
        spot_ref = place(owner_at(step, stream), its_core, its_side, stream)
        return send(src if src is not None else spot_ref, spot_ref, core_sems, (number, away, step), other_core)

    def cut(stream):
        return shard.at[:, pl.ds(stream[0], stream[1])]

    own_row = ((chip * 2 + core) * 2 + side) * rows
    own = pltpu.make_async_copy(
        shard, full.at[pl.ds(pl.multiple_of(own_row, rows), rows), :], own_sem
    )
    own.start()
    numbers = range(len(streams))
    for number in numbers:
        if streams[number][3]:
            x_copy(number, 0, side, cut(streams[number])).start()
    for number in numbers:
        ring_copy(number, 0, 0, cut(streams[number])).start()
    for number in numbers:
        if not streams[number][3]:
            x_copy(number, 0, side, cut(streams[number])).start()
    for number in numbers:
        core_copy(number, 0, 0, core, cut(streams[number])).start()
    for number in numbers:
        if streams[number][3]:
            x_copy(number, 0, 1 - side).wait_recv()
            ring_copy(number, 1, 0).start()
            core_copy(number, 1, 0, core).start()

    def turn(step, carry):
        for number in numbers:
            aways = (0, 1) if streams[number][3] else (0,)
            for away in aways:
                ring_arrival(number, away, step).wait_recv()

                @pl.when(step < chips - 1)
                def _(number=number, away=away):
                    ring_copy(number, away, step).start()

                core_copy(number, away, step, core).start()
            if not streams[number][3]:
                x_copy(number, step, side).start()
        for number in numbers:
            if not streams[number][3]:
                x_copy(number, step - 1, 1 - side).wait_recv()
                core_copy(number, 1, step - 1, core).start()
        return carry

    lax.fori_loop(1, chips, turn, 0)
    for number in numbers:
        if not streams[number][3]:
            x_copy(number, chips - 1, 1 - side).wait_recv()
            core_copy(number, 1, chips - 1, core).start()
    own.wait()

    def drain(step, carry):
        for number in numbers:
            first = streams[number][3]
            for away in (0, 1):
                core_copy(number, away, step, 1 - core).wait_recv()
                core_copy(number, away, step, core).wait_send()
                if first or not away:

                    @pl.when(step < chips - 1)
                    def _(number=number, away=away):
                        ring_copy(number, away, step).wait_send()

            if not first:
                x_copy(number, step, side).wait_send()
        return carry

    lax.fori_loop(0, chips, drain, 0)
    for number in numbers:
        if streams[number][3]:
            x_copy(number, 0, side).wait_send()


def gather_all(shard, chips):
    rows, cols = shard.shape
    tiles = cols // 128
    first = int(round(tiles * 0.43)) // 2 * 2
    rest = tiles - first
    bounds = [0, first // 2, first, first + rest // 2, tiles]
    streams = tuple(
        (128 * bounds[i], 128 * (bounds[i + 1] - bounds[i]), 1 if i % 2 == 0 else -1, i < 2)
        for i in range(4)
    )
    dma = pltpu.SemaphoreType.DMA
    return pl.pallas_call(
        functools.partial(gather_kernel, chips, streams),
        out_shape=jax.ShapeDtypeStruct((rows * 4 * chips, cols), shard.dtype),
        in_specs=[pl.BlockSpec(memory_space=pl.ANY)],
        out_specs=pl.BlockSpec(memory_space=pl.ANY),
        scratch_shapes=[
            dma((4, 2, chips)),
            dma((4, 2, chips)),
            dma((4, chips)),
            dma((4, chips)),
            dma((4, 2, chips)),
            dma((4, 2, chips)),
            dma,
        ],
        compiler_params=pltpu.CompilerParams(collective_id=0, has_side_effects=True),
        cost_estimate=pl.CostEstimate(
            flops=0, bytes_accessed=2 * rows * 4 * chips * cols * 2, transcendentals=0
        ),
        name="gather_all",
    )(shard)


def sum_kernel(chips, streams, counts, *refs):
    arrays, (tile,), outs, (tile_out,), held, core_in, ring_in, x_in, tiles, sems = refs_of(counts, refs)
    load_sem, core_send, core_recv, ring_send, ring_recv, x_send, x_recv, tile_send, tile_recv = sems
    tile_pairs, tile_ring = tiles
    chip = lax.axis_index("zy")
    core = lax.axis_index("core")
    side = lax.axis_index("fsdp")
    spot = ring_spot(chip, chips)
    far = 1 - side

    def neighbour(by):
        return {"zy": ring_chip(spot + chips + by, chips)}

    other_core = {"core": 1 - core}
    other_side = {"fsdp": 1 - side}
    barrier = pltpu.get_barrier_semaphore()
    for peer in (neighbour(1), neighbour(-1), other_core, other_side):
        pl.semaphore_signal(barrier, inc=1, device_id=peer, device_id_type=MESH)
    pl.semaphore_wait(barrier, 4)

    numbers = range(len(streams))

    def owner_at(number, turn):
        return ring_chip(spot + 2 * chips - streams[number][3] * turn, chips)

    def cols(number):
        return pl.ds(streams[number][1], streams[number][2])

    def remote(src, dst, send, recv, peer):
        return pltpu.make_async_remote_copy(
            src_ref=src, dst_ref=dst, send_sem=send, recv_sem=recv, device_id=peer, device_id_type=MESH
        )

    def core_copy(number, turn):
        owner = owner_at(number, turn)
        array = streams[number][0]
        return remote(
            arrays[array].at[owner, 1 - core, :, :, cols(number)],
            core_in[array].at[owner, :, :, cols(number)],
            core_send.at[number, turn - 1],
            core_recv.at[number, turn - 1],
            other_core,
        )

    def x_copy(number, turn):
        array = streams[number][0]
        first = streams[number][4]
        slot = turn - 1 if first else 0
        return remote(
            held[array].at[owner_at(number, turn), far, :, cols(number)],
            x_in[number].at[slot],
            x_send.at[number, slot],
            x_recv.at[number, slot],
            other_side,
        )

    def ring_copy(number, turn):
        array = streams[number][0]
        owner = owner_at(number, turn)
        if streams[number][4]:
            src = held[array].at[owner, pl.ds(side, 1), :, cols(number)]
        else:
            src = held[array].at[owner, :, :, cols(number)]
        return remote(
            src,
            ring_in[number].at[turn - 1],
            ring_send.at[number, turn - 1],
            ring_recv.at[number, turn - 1],
            neighbour(streams[number][3]),
        )

    loads = [
        pltpu.make_async_copy(arrays[i].at[:, core], held[i], load_sem.at[i])
        for i in range(len(arrays))
    ]

    def send_cores(turn, carry):
        for number in numbers:
            core_copy(number, turn).start()
        return carry

    def tile_copy(src, dst, number, peer):
        return remote(src, dst, tile_send.at[number], tile_recv.at[number], peer)

    def tile_turn(turn):
        spot_ref = tile_ring.at[ring_chip(spot + 2 * chips - turn + 1, chips)]
        return tile_copy(spot_ref, spot_ref, turn + 1, neighbour(1))

    def tile_arrival(turn):
        spot_ref = tile_ring.at[ring_chip(spot + 2 * chips - turn, chips)]
        return tile_copy(spot_ref, spot_ref, turn + 1, neighbour(1))

    tile_copy(tile, tile_pairs.at[0], 0, other_core).start()
    lax.fori_loop(1, 2, send_cores, 0)
    for load in loads:
        load.start()
    tile_copy(tile, tile_pairs.at[0], 0, other_core).wait()
    tile_pairs[1] = tile[...] + tile_pairs[0]
    tile_copy(tile_pairs.at[1], tile_pairs.at[2], 1, other_side).start()
    lax.fori_loop(2, chips + 1, send_cores, 0)
    for load in loads:
        load.wait()

    def add_cores(number, turn):
        array = streams[number][0]
        owner = owner_at(number, turn)
        core_copy(number, turn).wait_recv()
        for its_side in range(2):
            held[array][owner, its_side, :, cols(number)] = (
                held[array][owner, its_side, :, cols(number)].astype(F32)
                + core_in[array][owner, its_side, :, cols(number)].astype(F32)
            ).astype(BF16)

    def begin(turn):
        for number in numbers:
            if streams[number][4]:
                add_cores(number, turn)
                x_copy(number, turn).start()

    begin(1)
    tile_copy(tile_pairs.at[1], tile_pairs.at[2], 1, other_side).wait()
    tile_ring[chip] = tile_pairs[1] + tile_pairs[2]

    def round_trip(turn, carry):
        @pl.when(turn > 1)
        def _():
            tile_arrival(turn - 1).wait_recv()

        @pl.when(turn < chips)
        def _():
            tile_turn(turn).start()

        @pl.when(turn < chips)
        def _():
            begin(turn + 1)

        for number in numbers:
            array = streams[number][0]
            owner = owner_at(number, turn)
            if not streams[number][4]:
                add_cores(number, turn)

                @pl.when(turn > 1)
                def _(number=number, array=array, owner=owner):
                    ring_copy(number, turn - 1).wait_recv()
                    for its_side in range(2):
                        held[array][owner, its_side, :, cols(number)] = (
                            held[array][owner, its_side, :, cols(number)].astype(F32)
                            + ring_in[number][turn - 2, its_side].astype(F32)
                        ).astype(BF16)

                @pl.when(turn < chips)
                def _(number=number):
                    ring_copy(number, turn).start()

        for number in numbers:
            array = streams[number][0]
            owner = owner_at(number, turn)
            if streams[number][4]:
                x_copy(number, turn).wait_recv()

                @pl.when(turn == 1)
                def _(number=number, array=array, owner=owner):
                    held[array][owner, side, :, cols(number)] = (
                        held[array][owner, side, :, cols(number)].astype(F32)
                        + x_in[number][turn - 1].astype(F32)
                    ).astype(BF16)

                @pl.when(turn > 1)
                def _(number=number, array=array, owner=owner):
                    ring_copy(number, turn - 1).wait_recv()
                    total = (
                        held[array][owner, side, :, cols(number)].astype(F32)
                        + x_in[number][turn - 1].astype(F32)
                        + ring_in[number][turn - 2, 0].astype(F32)
                    )
                    held[array][owner, side, :, cols(number)] = total.astype(BF16)

                    @pl.when(turn == chips)
                    def _():
                        outs[array][:, cols(number)] = total

                @pl.when(turn < chips)
                def _(number=number):
                    ring_copy(number, turn).start()

        return carry

    lax.fori_loop(1, chips + 1, round_trip, 0)
    for number in numbers:
        if not streams[number][4]:
            x_copy(number, chips).start()
    tile_out[...] = lax.fori_loop(1, chips, lambda i, total: total + tile_ring[i], tile_ring[0])
    for number in numbers:
        array = streams[number][0]
        if not streams[number][4]:
            x_copy(number, chips).wait_recv()
            outs[array][:, cols(number)] = held[array][chip, side, :, cols(number)].astype(
                F32
            ) + x_in[number][0].astype(F32)

    def drain(turn, carry):
        for number in numbers:
            core_copy(number, turn).wait_send()
            if streams[number][4]:
                x_copy(number, turn).wait_send()

            @pl.when(turn < chips)
            def _(number=number):
                ring_copy(number, turn).wait_send()

        @pl.when(turn < chips)
        def _():
            tile_turn(turn).wait_send()

        return carry

    lax.fori_loop(1, chips + 1, drain, 0)
    for number in numbers:
        if not streams[number][4]:
            x_copy(number, chips).wait_send()


def refs_of(counts, refs):
    groups, at = [], 0
    for count in counts:
        groups.append(refs[at : at + count])
        at += count
    return groups


def sum_all(arrays, firsts, tile, chips):
    rows = arrays[0].shape[0] // (4 * chips)
    streams = []
    for i, (array, first) in enumerate(zip(arrays, firsts)):
        width = array.shape[1]
        left = width // 256 * 128
        streams.append((i, 0, left, 1, first))
        streams.append((i, left, width - left, -1, first))
    streams = tuple(sorted(streams, key=lambda stream: stream[4]))
    count, number = len(arrays), len(streams)
    dma = pltpu.SemaphoreType.DMA
    vmem = pltpu.VMEM
    scratch = (
        [vmem((chips, 2, rows, a.shape[1]), BF16) for a in arrays]
        + [vmem((chips, 2, rows, a.shape[1]), BF16) for a in arrays]
        + [vmem((chips - 1, 1 if first else 2, rows, width), BF16) for _, _, width, _, first in streams]
        + [vmem((chips if first else 1, rows, width), BF16) for _, _, width, _, first in streams]
        + [vmem((3, 8, 128), F32), vmem((chips, 8, 128), F32)]
        + [dma((count,))]
        + [dma((number, chips)) for _ in range(6)]
        + [dma((chips + 1,)) for _ in range(2)]
    )
    return pl.pallas_call(
        functools.partial(
            sum_kernel, chips, streams, (count, 1, count, 1, count, count, number, number, 2, 9)
        ),
        out_shape=[jax.ShapeDtypeStruct((rows, a.shape[1]), F32) for a in arrays]
        + [jax.ShapeDtypeStruct((8, 128), F32)],
        in_specs=[pl.BlockSpec(memory_space=pl.ANY)] * count + [pl.BlockSpec(memory_space=pltpu.VMEM)],
        out_specs=[pl.BlockSpec(memory_space=pltpu.VMEM)] * (count + 1),
        scratch_shapes=scratch,
        compiler_params=pltpu.CompilerParams(
            collective_id=1, has_side_effects=True, vmem_limit_bytes=56 << 20
        ),
        cost_estimate=pl.CostEstimate(
            flops=0, bytes_accessed=sum(2 * a.size for a in arrays), transcendentals=0
        ),
        name="sum_all",
    )(*[a.reshape(chips, 2, 2, rows, a.shape[1]) for a in arrays], tile)


LITTLE = pl.CostEstimate(flops=0, bytes_accessed=1024, transcendentals=0)
VMEM_LIMIT = 56 << 20


def whole(shape):
    return pl.BlockSpec(shape, lambda *_: (0,) * len(shape))


def piece(kernel, name, grid, in_specs, out_specs, out_shapes, scratch=()):
    return pl.pallas_call(
        kernel,
        grid=grid,
        in_specs=in_specs,
        out_specs=out_specs,
        out_shape=[jax.ShapeDtypeStruct(shape, dtype) for shape, dtype in out_shapes],
        scratch_shapes=list(scratch),
        compiler_params=pltpu.CompilerParams(vmem_limit_bytes=VMEM_LIMIT),
        cost_estimate=LITTLE,
        name=name,
    )


def inverse_rms(values):
    return lax.rsqrt(jnp.mean(values * values, axis=-1, keepdims=True) + EPSILON)


def norm_back(values, gain, grad):
    scale = inverse_rms(values)
    scaled = grad * gain
    mean = jnp.mean(values * scaled, axis=-1, keepdims=True)
    back = scale * scaled - values * (scale * scale * scale * mean)
    return back, jnp.sum(grad * (values * scale), axis=0, keepdims=True)


def qkv_kernel(tokens, gains, head_gain, cosine, sine, weight, low, raw, new):
    at = pl.program_id(0)

    @pl.when(at == 0)
    def _():
        states = tokens[...].astype(F32)
        low[...] = (states * inverse_rms(states) * gains[0:1]).astype(BF16)

    out = full_dot(low[...], weight[...])
    raw[...] = out
    plain = out * inverse_rms(out)
    values = plain * jnp.where(at < HEADS, head_gain[0:1], head_gain[1:2])
    half = HEAD // 2
    first, second = values[:, :half], values[:, half:]
    turned = jnp.concatenate(
        [first * cosine[...] - second * sine[...], second * cosine[...] + first * sine[...]], 1
    )
    new[...] = jnp.where(at < HEADS + KV_HEADS, turned, plain).astype(BF16)


def make_qkv(tokens, gains, head_gain, cosine, sine, full):
    rows = tokens.shape[0]
    heads = HEADS + 2 * KV_HEADS
    return piece(
        qkv_kernel,
        "make_qkv",
        (heads,),
        [
            whole((rows, D)),
            whole(gains.shape),
            whole((2, HEAD)),
            whole(cosine.shape),
            whole(sine.shape),
            pl.BlockSpec((D, HEAD), lambda i: (0, HEADS + i)),
        ],
        [
            whole((rows, D)),
            pl.BlockSpec((rows, HEAD), lambda i: (0, i)),
            pl.BlockSpec((rows, HEAD), lambda i: (0, i)),
        ],
        [((rows, D), BF16), ((rows, heads * HEAD), F32), ((rows, heads * HEAD), BF16)],
    )(tokens, gains, head_gain, cosine, sine, full)


def softmax_of(query, key, visible):
    scores = jnp.where(visible > 0.0, right_dot(query, key), -1e30)
    expo = jnp.exp(scores - jnp.max(scores, axis=-1, keepdims=True))
    return expo / jnp.sum(expo, axis=-1, keepdims=True)


def attend_kernel(
    tokens, gains, low, query, key, value, visible, w_out, lleft, lright,
    context, attn_raw, mixed, ffn_in, mid,
):
    at = pl.program_id(0)
    probs = softmax_of(query[...], key[...], visible[...]).astype(BF16)
    here = full_dot(probs, value[...]).astype(BF16)
    context[...] = here
    term = full_dot(here, w_out[...])

    @pl.when(at == 0)
    def _():
        attn_raw[...] = term

    @pl.when(at > 0)
    def _():
        attn_raw[...] += term

    @pl.when(at == HEADS - 1)
    def _():
        states = tokens[...].astype(F32)
        raw = attn_raw[...]
        total = states + raw * inverse_rms(raw) * gains[1:2]
        total = total + states * inverse_rms(states) * gains[0:1]
        mid[...] = full_dot(low[...], lleft[...]).astype(BF16)
        laurel = right_dot(mid[...], lright[...])
        total = (total + laurel * inverse_rms(laurel) * gains[2:3]) * INV_SQRT2
        mixed[...] = total
        ffn_in[...] = (total * inverse_rms(total) * gains[3:4]).astype(BF16)


def attend(tokens, gains, low, qkv, keys_all, visible, full):
    rows = tokens.shape[0]
    seen = keys_all.shape[0]
    group = HEADS // KV_HEADS
    side = 128
    left_at, right_at = full.shape[1] // side - 2, full.shape[1] // side - 1
    return piece(
        attend_kernel,
        "attend",
        (HEADS,),
        [
            whole((rows, D)),
            whole(gains.shape),
            whole((rows, D)),
            pl.BlockSpec((rows, HEAD), lambda i: (0, i)),
            pl.BlockSpec((seen, HEAD), lambda i: (0, i // group)),
            pl.BlockSpec((seen, HEAD), lambda i: (0, KV_HEADS + i // group)),
            whole((rows, seen)),
            pl.BlockSpec((HEAD, D), lambda i: (i, 0)),
            pl.BlockSpec((D, side), lambda i: (0, left_at)),
            pl.BlockSpec((D, side), lambda i: (0, right_at)),
        ],
        [
            pl.BlockSpec((rows, HEAD), lambda i: (0, i)),
            whole((rows, D)),
            whole((rows, D)),
            whole((rows, D)),
            whole((rows, side)),
        ],
        [
            ((rows, HEADS * HEAD), BF16),
            ((rows, D), F32),
            ((rows, D), F32),
            ((rows, D), BF16),
            ((rows, side), BF16),
        ],
    )(tokens, gains, low, qkv, keys_all, keys_all, visible, full, full, full)


def load_weights(weights, held, sems):
    copies, at = [], 0
    for number, ref in enumerate(weights):
        count = ref.shape[1]
        copies.append(pltpu.make_async_copy(ref, held.at[:, pl.ds(at, count)], sems.at[number]))
        at += count
    return copies


UNIT_BLOCK = 256


def ffn_forward_kernel(count, add, *refs):
    weights, refs = refs[:count], refs[count:]
    if add:
        before, refs = refs[0], refs[1:]
    rows, total, gate, upper, hidden, held, sems = refs
    copies = load_weights(weights, held, sems)

    @pl.when(pl.program_id(0) == 0)
    def _():
        for copy in copies:
            copy.start()
        for copy in copies:
            copy.wait()

    here = rows[...]
    running = before[...] if add else None
    for first in range(0, held.shape[1], UNIT_BLOCK):
        cut = slice(first, first + UNIT_BLOCK)
        gate_in = right_dot(here, held[0, cut])
        upper_in = right_dot(here, held[1, cut])
        low = gated_product(gate_in, upper_in).astype(BF16)
        gate[:, cut] = gate_in
        upper[:, cut] = upper_in
        hidden[:, cut] = low
        term = full_dot(low, held[2, cut])
        running = term if running is None else running + term
    total[...] = running


def ffn_forward(rows, before, weights):
    many, step = rows.shape[0], 256
    units = sum(w.shape[1] for w in weights)
    by_row = lambda width: pl.BlockSpec((step, width), lambda i: (i, 0))
    add = before is not None
    return piece(
        functools.partial(ffn_forward_kernel, len(weights), add),
        "ffn_forward",
        (many // step,),
        [pl.BlockSpec(memory_space=pl.ANY)] * len(weights) + [by_row(D)] * (1 + add),
        [by_row(D), by_row(units), by_row(units), by_row(units)],
        [((many, D), F32), ((many, units), F32), ((many, units), F32), ((many, units), BF16)],
        [pltpu.VMEM((3, units, D), BF16), pltpu.SemaphoreType.DMA((len(weights),))],
    )(*weights, *([before] if add else []), rows)


def ffn_backward_kernel(count, widths, add, *refs):
    weights, refs = refs[:count], refs[count:]
    if add:
        before, refs = refs[0], refs[1:]
    number = len(widths)
    rows, refs = refs[0], refs[1:]
    gates, uppers, refs = refs[:number], refs[number : 2 * number], refs[2 * number :]
    total, refs = refs[0], refs[1:]
    grad_gates, grad_uppers, (held, sems) = refs[:number], refs[number : 2 * number], refs[2 * number :]
    copies = load_weights(weights, held, sems)

    @pl.when(pl.program_id(0) == 0)
    def _():
        for copy in copies:
            copy.start()
        for copy in copies:
            copy.wait()

    here = rows[...]
    running = before[...] if add else None
    at = 0
    for gate, upper, grad_gate, grad_upper, width in zip(gates, uppers, grad_gates, grad_uppers, widths):
        for first in range(0, width, UNIT_BLOCK):
            cut = slice(first, first + UNIT_BLOCK)
            held_cut = slice(at + first, at + first + UNIT_BLOCK)
            unused, act_back = jax.vjp(gated_product, gate[:, cut], upper[:, cut])
            back_gate, back_upper = act_back(right_dot(here, held[2, held_cut]))
            low_gate, low_upper = back_gate.astype(BF16), back_upper.astype(BF16)
            grad_gate[:, cut] = low_gate
            grad_upper[:, cut] = low_upper
            term = full_dot(low_gate, held[0, held_cut]) + full_dot(low_upper, held[1, held_cut])
            running = term if running is None else running + term
        at += width
    total[...] = running


def ffn_backward(rows, before, weights, gates, uppers):
    many, step = rows.shape[0], 256
    widths = tuple(gate.shape[1] for gate in gates)
    by_row = lambda width: pl.BlockSpec((step, width), lambda i: (i, 0))
    add = before is not None
    blocks = [by_row(width) for width in widths]
    lows = [((many, width), BF16) for width in widths]
    total, *grads = piece(
        functools.partial(ffn_backward_kernel, len(weights), widths, add),
        "ffn_backward",
        (many // step,),
        [pl.BlockSpec(memory_space=pl.ANY)] * len(weights) + [by_row(D)] * (1 + add) + blocks * 2,
        [by_row(D)] + blocks * 2,
        [((many, D), F32)] + lows * 2,
        [pltpu.VMEM((3, sum(widths), D), BF16), pltpu.SemaphoreType.DMA((len(weights),))],
    )(*weights, *([before] if add else []), rows, *gates, *uppers)
    return total, list(zip(grads[: len(widths)], grads[len(widths) :]))


def unit_grads_kernel(grad_gate, grad_upper, hidden, rows, down_rows, out):
    out[0] = left_dot(grad_gate[...], rows[...])
    out[1] = left_dot(grad_upper[...], rows[...])
    out[2] = left_dot(hidden[...], down_rows[...])


def unit_grads_of(at, units, grad_gate, grad_upper, hidden, rows, down_rows):
    if units % 128:
        cut = slice(at * units, (at + 1) * units)
        return jnp.stack(
            [
                left_dot(grad_gate[:, cut], rows),
                left_dot(grad_upper[:, cut], rows),
                left_dot(hidden[:, cut], down_rows),
            ]
        )
    many, width = rows.shape[0], 512
    narrow = pl.BlockSpec((many, units), lambda i: (0, at))
    wide = pl.BlockSpec((many, width), lambda i: (0, i))
    return piece(
        unit_grads_kernel,
        "unit_grads",
        (D // width,),
        [narrow, narrow, narrow, wide, wide],
        [pl.BlockSpec((3, units, width), lambda i: (0, 0, i))],
        [((3, units, D), F32)],
    )(grad_gate, grad_upper, hidden, rows, down_rows)[0]


def attend_back_kernel(
    gains, grad_in, grad_after, mixed, attn_raw, mid, low, lleft, lright, w_out, context, query, key, value, visible,
    grad_mixed, grad_mid, grad_gains, grad_left, grad_right, grad_w_out, grad_query, grad_key, grad_value,
    grad_attn,
):
    at = pl.program_id(0)

    @pl.when(at == 0)
    def _():
        back, gain_3 = norm_back(mixed[...], gains[3:4], grad_in[...])
        total = (grad_after[...] + back) * INV_SQRT2
        grad_mixed[...] = total
        back, gain_2 = norm_back(right_dot(mid[...], lright[...]), gains[2:3], total)
        back_low = back.astype(BF16)
        grad_right[...] = left_dot(back_low, mid[...])
        mid_low = full_dot(back_low, lright[...]).astype(BF16)
        grad_mid[...] = mid_low
        grad_left[...] = left_dot(low[...], mid_low)
        back, gain_1 = norm_back(attn_raw[...], gains[1:2], total)
        grad_attn[...] = back.astype(BF16)
        grad_gains[...] = jnp.concatenate(
            [gain_1, gain_2, gain_3, jnp.zeros((5, D), F32)], 0
        )

    grad_context = right_dot(grad_attn[...], w_out[...]).astype(BF16)
    grad_w_out[...] = left_dot(context[...], grad_attn[...]).astype(BF16)
    probs = softmax_of(query[...], key[...], visible[...])
    grad_probs = right_dot(grad_context, value[...])
    inner = jnp.sum(probs * grad_probs, axis=-1, keepdims=True)
    grad_scores = (probs * (grad_probs - inner)).astype(BF16)
    grad_query[...] = full_dot(grad_scores, key[...])
    key_term = left_dot(grad_scores, query[...])
    value_term = left_dot(probs.astype(BF16), grad_context)
    group = HEADS // KV_HEADS

    @pl.when(lax.rem(at, group) == 0)
    def _():
        grad_key[...] = key_term
        grad_value[...] = value_term

    @pl.when(lax.rem(at, group) > 0)
    def _():
        grad_key[...] += key_term
        grad_value[...] += value_term


def attend_back(gains, grad_in, grad_after, mixed, attn_raw, mid, low, full, context, qkv, keys_all, visible):
    rows = low.shape[0]
    seen = keys_all.shape[0]
    group = HEADS // KV_HEADS
    side = 128
    left_at, right_at = full.shape[1] // side - 2, full.shape[1] // side - 1
    head = pl.BlockSpec((rows, HEAD), lambda i: (0, i))
    once = lambda shape: pl.BlockSpec(shape, lambda i: (0, 0), pipeline_mode=pl.Buffered(1))
    return piece(
        attend_back_kernel,
        "attend_back",
        (HEADS,),
        [
            whole(gains.shape),
            once((rows, D)),
            once((rows, D)),
            once((rows, D)),
            once((rows, D)),
            whole((rows, side)),
            whole((rows, D)),
            pl.BlockSpec((D, side), lambda i: (0, left_at)),
            pl.BlockSpec((D, side), lambda i: (0, right_at)),
            pl.BlockSpec((HEAD, D), lambda i: (i, 0)),
            head,
            head,
            pl.BlockSpec((seen, HEAD), lambda i: (0, i // group)),
            pl.BlockSpec((seen, HEAD), lambda i: (0, KV_HEADS + i // group)),
            whole((rows, seen)),
        ],
        [
            whole((rows, D)),
            whole((rows, side)),
            whole((8, D)),
            whole((D, side)),
            whole((D, side)),
            pl.BlockSpec((HEAD, D), lambda i: (i, 0)),
            head,
            pl.BlockSpec((seen, HEAD), lambda i: (0, i // group)),
            pl.BlockSpec((seen, HEAD), lambda i: (0, i // group)),
        ],
        [
            ((rows, D), F32),
            ((rows, side), BF16),
            ((8, D), F32),
            ((D, side), F32),
            ((D, side), F32),
            ((HEADS * HEAD, D), BF16),
            ((rows, HEADS * HEAD), F32),
            ((seen, KV_HEADS * HEAD), F32),
            ((seen, KV_HEADS * HEAD), F32),
        ],
        [pltpu.VMEM((rows, D), BF16)],
    )(
        gains, grad_in, grad_after, mixed, attn_raw, mid, low, full, full, full, context, qkv, keys_all, keys_all,
        visible,
    )


def turn_back(grad, cosine, sine):
    half = HEAD // 2
    first, second = grad[:, :half], grad[:, half:]
    return jnp.concatenate([first * cosine + second * sine, second * cosine - first * sine], 1)


def query_back_kernel(grad_query, raw, cosine, sine, head_gain, low, weight, grad_w, grad_low, grad_head):
    at = pl.program_id(0)
    turned = turn_back(grad_query[...], cosine[...], sine[...])
    back, gain = norm_back(raw[...], head_gain[0:1], turned)
    back_low = back.astype(BF16)
    grad_w[...] = left_dot(low[...], back_low).astype(BF16)
    term = right_dot(back_low, weight[...])

    @pl.when(at == 0)
    def _():
        grad_low[...] = term
        grad_head[...] = gain

    @pl.when(at > 0)
    def _():
        grad_low[...] += term
        grad_head[...] += gain


def query_back(grad_query, raw, cosine, sine, head_gain, low, full):
    rows = low.shape[0]
    head = pl.BlockSpec((rows, HEAD), lambda i: (0, i))
    return piece(
        query_back_kernel,
        "query_back",
        (HEADS,),
        [
            head,
            head,
            whole(cosine.shape),
            whole(sine.shape),
            whole((2, HEAD)),
            whole((rows, D)),
            pl.BlockSpec((D, HEAD), lambda i: (0, HEADS + i)),
        ],
        [pl.BlockSpec((D, HEAD), lambda i: (0, i)), whole((rows, D)), whole((1, HEAD))],
        [((D, HEADS * HEAD), BF16), ((rows, D), F32), ((1, HEAD), F32)],
    )(grad_query, raw, cosine, sine, head_gain, low, full)


def key_back_kernel(
    grad_kv, raw, cosine, sine, head_gain, low, weight, before, grad_mixed, grad_mid, lleft, tokens, gains,
    grad_w, grad_tokens, grad_head, grad_gain, total,
):
    at = pl.program_id(0)
    is_key = at < KV_HEADS
    grad = grad_kv[...]
    turned = jnp.where(is_key, turn_back(grad, cosine[...], sine[...]), grad)
    back, gain = norm_back(raw[...], jnp.where(is_key, head_gain[1:2], 1.0), turned)
    back_low = back.astype(BF16)
    grad_w[...] = left_dot(low[...], back_low).astype(BF16)
    term = right_dot(back_low, weight[...])

    @pl.when(at == 0)
    def _():
        total[...] = before[...] + term
        grad_head[...] = gain

    @pl.when(at > 0)
    def _():
        total[...] += term
        grad_head[...] += jnp.where(is_key, gain, 0.0)

    @pl.when(at == 2 * KV_HEADS - 1)
    def _():
        grad_normed = total[...] + grad_mixed[...] + right_dot(grad_mid[...], lleft[...])
        back, gain_0 = norm_back(tokens[...].astype(F32), gains[0:1], grad_normed)
        grad_tokens[...] = grad_mixed[...] + back
        grad_gain[...] = gain_0


def key_back(grad_kv, raw, cosine, sine, head_gain, low, full, before, grad_mixed, grad_mid, tokens, gains):
    rows = low.shape[0]
    side = 128
    left_at = full.shape[1] // side - 2
    return piece(
        key_back_kernel,
        "key_back",
        (2 * KV_HEADS,),
        [
            pl.BlockSpec((rows, HEAD), lambda i: (0, i)),
            pl.BlockSpec((rows, HEAD), lambda i: (0, HEADS + i)),
            whole(cosine.shape),
            whole(sine.shape),
            whole((2, HEAD)),
            whole((rows, D)),
            pl.BlockSpec((D, HEAD), lambda i: (0, 2 * HEADS + i)),
            whole((rows, D)),
            whole((rows, D)),
            whole((rows, side)),
            pl.BlockSpec((D, side), lambda i: (0, left_at)),
            whole((rows, D)),
            whole(gains.shape),
        ],
        [
            pl.BlockSpec((D, HEAD), lambda i: (0, i)),
            whole((rows, D)),
            whole((1, HEAD)),
            whole((1, D)),
        ],
        [
            ((D, 2 * KV_HEADS * HEAD), BF16),
            ((rows, D), F32),
            ((1, HEAD), F32),
            ((1, D), F32),
        ],
        [pltpu.VMEM((rows, D), F32)],
    )(grad_kv, raw, cosine, sine, head_gain, low, full, before, grad_mixed, grad_mid, full, tokens, gains)


def tie(*values):
    return lax.optimization_barrier(values)


def shares(total, count):
    return [total // count + (1 if i < total % count else 0) for i in range(count)]


def pair_of_rows(own):
    return jnp.concatenate([own, swap(own, "fsdp")], 0)


def both_pairs(pair):
    return jnp.concatenate([pair, swap(pair, "core")], 0)


def rows_of_four(own):
    return both_pairs(pair_of_rows(own))


def sum_of_four(partial):
    count = partial.shape[0] // 4
    low = partial[2 * count :].astype(BF16)
    pair = partial[: 2 * count] + swap(low, "core").astype(F32)
    low = pair[count:].astype(BF16)
    return pair[:count] + swap(low, "fsdp").astype(F32)


def body(
    tokens,
    per_layer,
    teacher,
    cont_lengths,
    w_query,
    w_kv,
    w_out,
    laurel_left,
    laurel_right,
    pl_gate,
    pl_proj,
    norm_gains,
    head_gains,
    ffn_weight,
):
    layer_in = per_layer[0].astype(F32)
    target = teacher[0].astype(F32)
    row_count = tokens.shape[1]
    chips = lax.axis_size("zy")
    seq_count = 2 * chips
    group_count = lax.axis_size("fsdp")
    shards = seq_count * group_count
    chip = lax.axis_index("zy")
    core = lax.axis_index("core")
    seq_index = chip * 2 + core
    group_index = lax.axis_index("fsdp")
    half_point = seq_count // 2
    prompt_len = half_point * row_count
    cont_shards = CONT_LEN // row_count
    cont_count = prompt_len // CONT_LEN
    is_cont = seq_index >= half_point
    rel_index = seq_index - half_point
    local_shard = jnp.where(is_cont, rel_index % cont_shards, 0)
    cont_index = jnp.where(is_cont, rel_index // cont_shards, 0)
    first_place = jnp.where(is_cont, prompt_len + local_shard * row_count, seq_index * row_count)
    row_range = jnp.arange(row_count, dtype=jnp.int32)
    places = first_place + row_range
    group_lengths = jnp.sum(
        jnp.where(
            jnp.arange(group_count, dtype=jnp.int32)[:, None] == group_index, cont_lengths, 0
        ),
        axis=0,
    )
    my_length = jnp.sum(
        jnp.where(jnp.arange(cont_count, dtype=jnp.int32) == cont_index, group_lengths, 0)
    )
    valid = jnp.logical_or(
        jnp.logical_not(is_cont), local_shard * row_count + row_range < my_length
    )
    weight_mask = valid.astype(F32)
    count = F32(group_count * prompt_len) + jnp.sum(cont_lengths).astype(F32)
    total_slots = float(row_count * seq_count * group_count)
    shard_rows = w_query.shape[0]
    key_cols = KV_HEADS * HEAD
    proj_cols = pl_proj.shape[0] * D // shard_rows
    misc_cols = RANK
    head_part = head_gains.reshape(-1, 1)
    misc = jnp.concatenate(
        [
            norm_gains.T,
            jnp.pad(head_part, ((0, shard_rows - head_part.shape[0]), (0, 0))),
            jnp.zeros((shard_rows, misc_cols - 7), BF16),
        ],
        1,
    )
    pack = jnp.concatenate(
        [
            w_out,
            w_query,
            w_kv,
            pl_gate,
            pl_proj.reshape(shard_rows, proj_cols),
            laurel_left,
            misc,
            laurel_right.T,
            jnp.zeros((shard_rows, 128 - RANK), BF16),
        ],
        1,
    )

    units = ffn_weight.shape[0]
    half = units // 2
    by_kind = ffn_weight.transpose(1, 0, 2)
    ups, downs = [by_kind[:, :half]], [by_kind[:, half:]]
    stage_steps = shares(chips - 1, 7)

    def pass_on(stage):
        for _ in range(stage_steps[stage]):
            ups.append(ring(ups[-1], 1))
            downs.append(ring(downs[-1], -1))

    def stage_end(values):
        (ups[-1], downs[-1]), values = tie((ups[-1], downs[-1]), values)
        return values

    pass_on(0)
    full = gather_all(pack, chips)
    at = 2 * D + 2 * key_cols
    plg = full[:, at : at + PLD]
    plp = full[:, at + PLD : at + PLD + proj_cols].reshape(PLD, D)
    at += PLD + proj_cols + RANK
    misc_full = stage_end(full[:, at : at + misc_cols])
    pass_on(1)
    gains = jnp.pad(misc_full[:, :6].T.astype(F32), ((0, 2), (0, 0)))
    head_n = head_gains.shape[1]
    head_gain = (
        misc_full[:, 6]
        .reshape(shards, shard_rows)[:, : 2 * head_n]
        .reshape(shards, 2, head_n)
        .transpose(1, 0, 2)
        .reshape(2, HEAD)
        .astype(F32)
    )
    freqs = jnp.exp(
        jnp.arange(HEAD // 2, dtype=F32) * (-2.0 * math.log(ROPE_BASE) / HEAD)
    )
    angles = places.astype(F32)[:, None] * freqs
    cosine, sine = jnp.cos(angles), jnp.sin(angles)
    normed_low, qkv_raw, qkv = make_qkv(tokens[0], gains, head_gain, cosine, sine, full)
    kv_own = qkv[:, D:]

    mid = chips // 2
    chain = [(i, i + 1) for i in range(mid - 1)] + [(mid - 1, mid + 1)]
    kv_before = jnp.where(
        chip == mid,
        lax.ppermute(kv_own, "zy", [(mid - 1, mid)]),
        lax.ppermute(kv_own, "zy", chain),
    )
    spans = []
    span = 2
    while span < mid:
        spans.append(span)
        span *= 2
    for span in spans:
        moved = lax.ppermute(
            kv_before, "zy", [(mid + i, mid + i + span) for i in range(min(span, mid - span))]
        )
        fresh = jnp.logical_and(chip >= mid + span, chip < mid + 2 * span)
        kv_before = jnp.where(fresh, moved, kv_before)
    kv_other = swap(jnp.where(core == 0, kv_own, kv_before), "core")
    keys_all = jnp.concatenate([kv_before, kv_other, kv_own], 0)
    keys_all = stage_end(keys_all)
    pass_on(2)
    key_len = keys_all.shape[0]
    key_places = first_place - 2 * row_count + jnp.arange(key_len, dtype=jnp.int32)
    visible = (
        (key_places[None, :] <= places[:, None])
        & (places[:, None] - key_places[None, :] < WINDOW)
        & (key_places[None, :] >= 0)
    ).astype(F32)
    context_low, attn_raw, mixed, ffn_in, laurel_mid = attend(
        tokens[0], gains, normed_low, qkv, keys_all, visible, full
    )

    pair = stage_end(pair_of_rows(ffn_in))
    here = len(ups)
    pass_on(3)
    ffn_rows = both_pairs(pair)
    gates, uppers, hiddens, part_weights, parts = [], [], [], [], []

    def forward_part(running, first, last):
        weights = [w for k in range(first, last) for w in (ups[k], downs[k])]
        running, gate, upper, hidden = ffn_forward(ffn_rows, running, weights)
        gates.append(gate)
        uppers.append(upper)
        hiddens.append(hidden)
        part_weights.append(weights)
        parts.append(range(first, last))
        return running

    running = stage_end(forward_part(None, 0, here))
    pass_on(4)
    stage_end(())
    then = len(ups)
    pass_on(5)
    running = stage_end(forward_part(running, here, then))
    here = len(ups)
    pass_on(6)
    running = stage_end(forward_part(running, then, here))
    if here < chips:
        running = forward_part(running, here, chips)
    down_out = sum_of_four(running)
    after_ffn = mixed + rms_norm(down_out, gains[4])
    after_low = after_ffn.astype(BF16)
    pl_raw = full_dot(after_low, plg)
    pl_act = gelu_tanh(pl_raw)
    pl_mid = (pl_act * layer_in).astype(BF16)
    pl_out = full_dot(pl_mid, plp)
    result = after_ffn + rms_norm(pl_out, gains[5])
    errors = result - target
    squares = jnp.sum(weight_mask[:, None] * errors * errors)

    grad_out = weight_mask[:, None] * errors * (total_slots / count)
    unused, pl_norm_back = jax.vjp(rms_norm, pl_out, gains[5])
    grad_pl_out, grad_g5 = pl_norm_back(grad_out)
    grad_pl_low = grad_pl_out.astype(BF16)
    grad_plp = left_dot(pl_mid, grad_pl_low)
    grad_pl_mid = right_dot(grad_pl_low, plp)
    grad_layer_in = grad_pl_mid * pl_act
    unused, gelu_back = jax.vjp(gelu_tanh, pl_raw)
    grad_pl_raw = gelu_back(grad_pl_mid * layer_in)[0].astype(BF16)
    grad_plg = left_dot(after_low, grad_pl_raw)
    grad_after = grad_out + right_dot(grad_pl_raw, plg)
    unused, down_norm_back = jax.vjp(rms_norm, down_out, gains[4])
    grad_down, grad_g4 = down_norm_back(grad_after)
    grad_down_low = grad_down.astype(BF16)

    grad_down_rows = rows_of_four(grad_down_low)
    grad_parts = []

    def backward_part(first, last, running):
        return ffn_backward(
            grad_down_rows,
            running,
            [w for weights in part_weights[first:last] for w in weights],
            gates[first:last],
            uppers[first:last],
        )

    def unit_grads(k):
        for part, (gg, gu), hid in zip(parts, grad_parts, hiddens):
            if k in part:
                return unit_grads_of(k - part[0], units, gg, gu, hid, ffn_rows, grad_down_rows)

    order = list(range(1, chips)) + [0]
    ring_steps = shares(chips - 1, 7)
    done = 0

    def beside(stage, work):
        nonlocal done, up_sum, down_sum
        values = None
        for step in range(ring_steps[stage]):
            up_in = ring(up_sum.astype(BF16), 1)
            down_in = ring(down_sum.astype(BF16), -1)
            if step == 0:
                values = work()
            done += 1
            terms = unit_grads(order[done])
            (up_in, down_in), terms, values = tie((up_in, down_in), terms, values)
            up_sum = up_in.astype(F32) + terms[:, :half]
            down_sum = down_in.astype(F32) + terms[:, half:]
        return work() if values is None else values

    running, grads = backward_part(0, 1, None)
    grad_parts += grads
    terms = unit_grads(order[0])
    up_sum, down_sum = terms[:, :half], terms[:, half:]

    def work():
        total, grads = backward_part(1, len(parts), running)
        grad_parts.extend(grads)
        return total

    running = beside(0, work)
    grad_ffn_in = beside(1, lambda: sum_of_four(running))
    (
        grad_scaled,
        grad_mid_low,
        grad_mid_gains,
        grad_lleft,
        grad_lright_t,
        grad_wo,
        grad_queries,
        grad_keys,
        grad_values,
    ) = beside(
        2,
        lambda: attend_back(
            gains, grad_ffn_in, grad_after, mixed, attn_raw, laurel_mid, normed_low, full, context_low, qkv, keys_all,
            visible,
        ),
    )

    def work():
        grad_kv = jnp.concatenate([grad_keys, grad_values], 1)
        grad_before = grad_kv[:row_count]
        grad_own = grad_kv[2 * row_count :]
        returned = swap(grad_kv[row_count : 2 * row_count].astype(BF16), "core").astype(F32)
        grad_own = grad_own + jnp.where(core == 0, returned, 0.0)
        grad_before = grad_before + jnp.where(core == 0, 0.0, returned)
        for span in reversed(spans):
            back = [(mid + i + span, mid + i) for i in range(min(span, mid - span))]
            grad_before = grad_before + lax.ppermute(grad_before.astype(BF16), "zy", back).astype(F32)
        before_low = grad_before.astype(BF16)
        grad_own = (
            grad_own
            + lax.ppermute(before_low, "zy", [(b, a) for a, b in chain]).astype(F32)
            + lax.ppermute(before_low, "zy", [(mid, mid - 1)]).astype(F32)
        )
        return grad_own, query_back(grad_queries, qkv_raw, cosine, sine, head_gain, normed_low, full)

    grad_own, (grad_wq, grad_normed, grad_hq) = beside(3, work)
    grad_wkv, grad_tokens, grad_hk, grad_g0 = beside(
        4,
        lambda: key_back(
            grad_own, qkv_raw, cosine, sine, head_gain, normed_low, full, grad_normed, grad_scaled, grad_mid_low,
            tokens[0], gains,
        ),
    )
    def work():
        head_back = jnp.concatenate([grad_hq, grad_hk], 0).reshape(2, shards, head_n).transpose(1, 0, 2)
        head_back = head_back.reshape(shards, 2 * head_n)
        head_back = jnp.pad(head_back, ((0, 0), (0, shard_rows - 2 * head_n))).reshape(1, D)
        misc_back = jnp.concatenate(
            [grad_g0, grad_mid_gains[:3], grad_g4[None], grad_g5[None], head_back, jnp.zeros((1, D), F32)], 0
        )
        return jnp.concatenate(
            [
                grad_plg.astype(BF16),
                grad_plp.astype(BF16).reshape(D, proj_cols),
                grad_lleft[:, :RANK].astype(BF16),
                jnp.pad(misc_back.T, ((0, 0), (0, misc_cols - 8))).astype(BF16),
                grad_lright_t.astype(BF16),
            ],
            1,
        )

    rest_back = beside(5, work)
    beside(6, lambda: ())
    grad_ffn = jnp.concatenate([up_sum, down_sum], 1).transpose(1, 0, 2)

    sums_wq, sums_wkv, sums_wo, sums_rest, total = sum_all(
        [grad_wq, grad_wkv, grad_wo, rest_back],
        (False, False, True, True),
        jnp.broadcast_to(squares, (8, 128)),
        chips,
    )
    at = 0
    rest = []
    for width in (PLD, proj_cols, RANK, misc_cols, RANK):
        rest.append(sums_rest[:, at : at + width])
        at += width

    match_loss = total[0, 0] / (2.0 * D * count)

    return (
        result[None],
        match_loss,
        grad_tokens[None],
        grad_layer_in[None],
        sums_wq,
        sums_wkv,
        sums_wo,
        rest[2],
        rest[4].T,
        rest[0],
        rest[1].reshape(pl_proj.shape),
        rest[3][:, :6].T,
        rest[3][: 2 * head_n, 6].reshape(2, head_n),
        grad_ffn,
    )


def solution(mesh):
    seq, fsdp = mesh.shape["seq"], mesh.shape["fsdp"]
    fine = Mesh(mesh.devices.reshape(seq // 2, 2, fsdp), ("zy", "core", "fsdp"))
    rows = P("fsdp", ("zy", "core"), None)
    split = ("zy", "core", "fsdp")
    weights = (
        P(split, None),
        P(split, None),
        P(split, None),
        P(split, None),
        P(None, split),
        P(split, None),
        P(split, None),
        P(None, split),
        P(None, split),
        P(split, None, None),
    )
    return jax.shard_map(
        body,
        mesh=fine,
        in_specs=(rows, rows, rows, P()) + weights,
        out_specs=(rows, P(), rows, rows) + weights,
        check_vma=False,
    )
```

```python
import functools
import math

import jax
import jax.numpy as jnp
from jax import lax
from jax.experimental import pallas as pl
from jax.experimental.pallas import tpu as pltpu
from jax.sharding import Mesh, PartitionSpec as P

D = 2048
HEADS = 8
KV_HEADS = 2
HEAD = 256
WINDOW = 512
CONT_LEN = 512
RANK = 64
PLD = 256

EPSILON = 1e-06
INV_SQRT2 = 0.7071067811865476
ROPE_BASE = 10000.0
BF16 = jnp.bfloat16
F32 = jnp.float32


def rms_norm(values, gain):
    return values * lax.rsqrt(jnp.mean(values * values, axis=-1, keepdims=True) + EPSILON) * gain


def gelu_tanh(values):
    return jax.nn.gelu(values, approximate=True)


def gated_product(gate_in, up_in):
    return gelu_tanh(gate_in) * up_in


def full_dot(left, right):
    return jnp.dot(left, right, preferred_element_type=F32)


def left_dot(left, right):
    return lax.dot_general(left, right, (((0,), (0,)), ((), ())), preferred_element_type=F32)


def right_dot(left, right):
    return lax.dot_general(left, right, (((1,), (1,)), ((), ())), preferred_element_type=F32)


def ring_order(n):
    return list(range(0, n, 2)) + list(range(n - 1, 0, -2))


def ring_pairs(n, by):
    order = ring_order(n)
    return [(order[i], order[(i + by) % n]) for i in range(n)]


def ring(value, by):
    return lax.ppermute(value, "zy", ring_pairs(lax.axis_size("zy"), by))


def swap(value, axis):
    return lax.ppermute(value, axis, [(0, 1), (1, 0)])


MESH = pl.DeviceIdType.MESH


def ring_chip(spot, chips):
    spot = lax.rem(spot, chips)
    return jnp.where(spot < chips // 2, 2 * spot, 2 * (chips - 1 - spot) + 1)


def ring_spot(chip, chips):
    return jnp.where(lax.rem(chip, 2) == 0, chip // 2, chips - 1 - chip // 2)


def gather_kernel(chips, streams, shard, full, ring_send, ring_recv, x_send, x_recv, core_send, core_recv, own_sem):
    chip = lax.axis_index("zy")
    core = lax.axis_index("core")
    side = lax.axis_index("fsdp")
    spot = ring_spot(chip, chips)
    rows = shard.shape[0]

    def neighbour(by):
        return {"zy": ring_chip(spot + chips + by, chips)}

    other_core = {"core": 1 - core}
    other_side = {"fsdp": 1 - side}

    barrier = pltpu.get_barrier_semaphore()
    for peer in (neighbour(1), neighbour(-1), other_core, other_side):
        pl.semaphore_signal(barrier, inc=1, device_id=peer, device_id_type=MESH)
    pl.semaphore_wait(barrier, 4)

    def place(owner, its_core, its_side, stream):
        row = ((owner * 2 + its_core) * 2 + its_side) * rows
        return full.at[pl.ds(pl.multiple_of(row, rows), rows), pl.ds(stream[0], stream[1])]

    def owner_at(step, stream):
        return ring_chip(spot + chips - stream[2] * step, chips)

    def send(src, dst, sems, at, peer):
        return pltpu.make_async_remote_copy(
            src_ref=src,
            dst_ref=dst,
            send_sem=sems[0].at[at],
            recv_sem=sems[1].at[at],
            device_id=peer,
            device_id_type=MESH,
        )

    ring_sems, x_sems, core_sems = (ring_send, ring_recv), (x_send, x_recv), (core_send, core_recv)

    def ring_copy(number, away, step, src=None):
        stream = streams[number]
        its_side = 1 - side if away else side
        spot_ref = place(owner_at(step, stream), core, its_side, stream)
        return send(src if src is not None else spot_ref, spot_ref, ring_sems, (number, away, step), neighbour(stream[2]))

    def ring_arrival(number, away, step):
        stream = streams[number]
        its_side = 1 - side if away else side
        spot_ref = place(owner_at(step, stream), core, its_side, stream)
        return send(spot_ref, spot_ref, ring_sems, (number, away, step - 1), neighbour(stream[2]))

    def x_copy(number, step, its_side, src=None):
        stream = streams[number]
        spot_ref = place(owner_at(step, stream), core, its_side, stream)
        return send(src if src is not None else spot_ref, spot_ref, x_sems, (number, step), other_side)

    def core_copy(number, away, step, its_core, src=None):
        stream = streams[number]
        its_side = 1 - side if away else side
        spot_ref = place(owner_at(step, stream), its_core, its_side, stream)
        return send(src if src is not None else spot_ref, spot_ref, core_sems, (number, away, step), other_core)

    def cut(stream):
        return shard.at[:, pl.ds(stream[0], stream[1])]

    own_row = ((chip * 2 + core) * 2 + side) * rows
    own = pltpu.make_async_copy(
        shard, full.at[pl.ds(pl.multiple_of(own_row, rows), rows), :], own_sem
    )
    own.start()
    numbers = range(len(streams))
    for number in numbers:
        if streams[number][3]:
            x_copy(number, 0, side, cut(streams[number])).start()
    for number in numbers:
        ring_copy(number, 0, 0, cut(streams[number])).start()
    for number in numbers:
        if not streams[number][3]:
            x_copy(number, 0, side, cut(streams[number])).start()
    for number in numbers:
        core_copy(number, 0, 0, core, cut(streams[number])).start()
    for number in numbers:
        if streams[number][3]:
            x_copy(number, 0, 1 - side).wait_recv()
            ring_copy(number, 1, 0).start()
            core_copy(number, 1, 0, core).start()

    def turn(step, carry):
        for number in numbers:
            aways = (0, 1) if streams[number][3] else (0,)
            for away in aways:
                ring_arrival(number, away, step).wait_recv()

                @pl.when(step < chips - 1)
                def _(number=number, away=away):
                    ring_copy(number, away, step).start()

                core_copy(number, away, step, core).start()
            if not streams[number][3]:
                x_copy(number, step, side).start()
        for number in numbers:
            if not streams[number][3]:
                x_copy(number, step - 1, 1 - side).wait_recv()
                core_copy(number, 1, step - 1, core).start()
        return carry

    lax.fori_loop(1, chips, turn, 0)
    for number in numbers:
        if not streams[number][3]:
            x_copy(number, chips - 1, 1 - side).wait_recv()
            core_copy(number, 1, chips - 1, core).start()
    own.wait()

    def drain(step, carry):
        for number in numbers:
            first = streams[number][3]
            for away in (0, 1):
                core_copy(number, away, step, 1 - core).wait_recv()
                core_copy(number, away, step, core).wait_send()
                if first or not away:

                    @pl.when(step < chips - 1)
                    def _(number=number, away=away):
                        ring_copy(number, away, step).wait_send()

            if not first:
                x_copy(number, step, side).wait_send()
        return carry

    lax.fori_loop(0, chips, drain, 0)
    for number in numbers:
        if streams[number][3]:
            x_copy(number, 0, side).wait_send()


def gather_all(shard, chips):
    rows, cols = shard.shape
    tiles = cols // 128
    first = int(round(tiles * 0.43)) // 2 * 2
    rest = tiles - first
    bounds = [0, first // 2, first, first + rest // 2, tiles]
    streams = tuple(
        (128 * bounds[i], 128 * (bounds[i + 1] - bounds[i]), 1 if i % 2 == 0 else -1, i < 2)
        for i in range(4)
    )
    dma = pltpu.SemaphoreType.DMA
    return pl.pallas_call(
        functools.partial(gather_kernel, chips, streams),
        out_shape=jax.ShapeDtypeStruct((rows * 4 * chips, cols), shard.dtype),
        in_specs=[pl.BlockSpec(memory_space=pl.ANY)],
        out_specs=pl.BlockSpec(memory_space=pl.ANY),
        scratch_shapes=[
            dma((4, 2, chips)),
            dma((4, 2, chips)),
            dma((4, chips)),
            dma((4, chips)),
            dma((4, 2, chips)),
            dma((4, 2, chips)),
            dma,
        ],
        compiler_params=pltpu.CompilerParams(collective_id=0, has_side_effects=True),
        cost_estimate=pl.CostEstimate(
            flops=0, bytes_accessed=2 * rows * 4 * chips * cols * 2, transcendentals=0
        ),
        name="gather_all",
    )(shard)


def sum_kernel(chips, streams, counts, *refs):
    arrays, (tile, up_sum, down_sum, terms), outs, (tile_out, units_out), held, core_in, ring_in, x_in, tiles, sems = refs_of(counts, refs)
    load_sem, core_send, core_recv, ring_send, ring_recv, x_send, x_recv, tile_send, tile_recv, hop_send, hop_recv = sems
    tile_pairs, tile_ring, up_in, down_in = tiles
    chip = lax.axis_index("zy")
    core = lax.axis_index("core")
    side = lax.axis_index("fsdp")
    spot = ring_spot(chip, chips)
    far = 1 - side

    def neighbour(by):
        return {"zy": ring_chip(spot + chips + by, chips)}

    other_core = {"core": 1 - core}
    other_side = {"fsdp": 1 - side}
    barrier = pltpu.get_barrier_semaphore()
    for peer in (neighbour(1), neighbour(-1), other_core, other_side):
        pl.semaphore_signal(barrier, inc=1, device_id=peer, device_id_type=MESH)
    pl.semaphore_wait(barrier, 4)

    numbers = range(len(streams))

    def owner_at(number, turn):
        return ring_chip(spot + 2 * chips - streams[number][3] * turn, chips)

    def cols(number):
        return pl.ds(streams[number][1], streams[number][2])

    def remote(src, dst, send, recv, peer):
        return pltpu.make_async_remote_copy(
            src_ref=src, dst_ref=dst, send_sem=send, recv_sem=recv, device_id=peer, device_id_type=MESH
        )

    def core_copy(number, turn):
        owner = owner_at(number, turn)
        array = streams[number][0]
        return remote(
            arrays[array].at[owner, 1 - core, :, :, cols(number)],
            core_in[array].at[owner, :, :, cols(number)],
            core_send.at[number, turn - 1],
            core_recv.at[number, turn - 1],
            other_core,
        )

    def x_copy(number, turn):
        array = streams[number][0]
        first = streams[number][4]
        slot = turn - 1 if first else 0
        return remote(
            held[array].at[owner_at(number, turn), far, :, cols(number)],
            x_in[number].at[slot],
            x_send.at[number, slot],
            x_recv.at[number, slot],
            other_side,
        )

    def ring_copy(number, turn):
        array = streams[number][0]
        owner = owner_at(number, turn)
        if streams[number][4]:
            src = held[array].at[owner, pl.ds(side, 1), :, cols(number)]
        else:
            src = held[array].at[owner, :, :, cols(number)]
        return remote(
            src,
            ring_in[number].at[turn - 1],
            ring_send.at[number, turn - 1],
            ring_recv.at[number, turn - 1],
            neighbour(streams[number][3]),
        )

    loads = [
        pltpu.make_async_copy(arrays[i].at[:, core], held[i], load_sem.at[i])
        for i in range(len(arrays))
    ]

    def send_cores(turn, carry):
        for number in numbers:
            core_copy(number, turn).start()
        return carry

    half = up_in.shape[1]

    def hop_copy(way, kind):
        src, dst = ((up_sum, up_in), (down_sum, down_in))[way]
        return remote(src.at[kind], dst.at[kind], hop_send.at[way, kind], hop_recv.at[way, kind], neighbour(1 - 2 * way))

    def hop_done(kind):
        for way, arrived in enumerate((up_in, down_in)):
            rows_here = pl.ds(way * half, half)
            hop_copy(way, kind).wait()
            units_out[kind, rows_here] = terms[kind, rows_here].astype(F32) + arrived[kind].astype(F32)

    def tile_copy(src, dst, number, peer):
        return remote(src, dst, tile_send.at[number], tile_recv.at[number], peer)

    def tile_turn(turn):
        spot_ref = tile_ring.at[ring_chip(spot + 2 * chips - turn + 1, chips)]
        return tile_copy(spot_ref, spot_ref, turn + 1, neighbour(1))

    def tile_arrival(turn):
        spot_ref = tile_ring.at[ring_chip(spot + 2 * chips - turn, chips)]
        return tile_copy(spot_ref, spot_ref, turn + 1, neighbour(1))

    tile_copy(tile, tile_pairs.at[0], 0, other_core).start()
    lax.fori_loop(1, 2, send_cores, 0)
    for load in loads:
        load.start()
    tile_copy(tile, tile_pairs.at[0], 0, other_core).wait()
    tile_pairs[1] = tile[...] + tile_pairs[0]
    tile_copy(tile_pairs.at[1], tile_pairs.at[2], 1, other_side).start()
    lax.fori_loop(2, chips + 1, send_cores, 0)
    for load in loads:
        load.wait()

    def add_cores(number, turn):
        array = streams[number][0]
        owner = owner_at(number, turn)
        core_copy(number, turn).wait_recv()
        for its_side in range(2):
            held[array][owner, its_side, :, cols(number)] = (
                held[array][owner, its_side, :, cols(number)].astype(F32)
                + core_in[array][owner, its_side, :, cols(number)].astype(F32)
            ).astype(BF16)

    def begin(turn):
        for number in numbers:
            if streams[number][4]:
                add_cores(number, turn)
                x_copy(number, turn).start()

    begin(1)
    tile_copy(tile_pairs.at[1], tile_pairs.at[2], 1, other_side).wait()
    tile_ring[chip] = tile_pairs[1] + tile_pairs[2]

    def round_trip(turn, carry):
        @pl.when(turn > 1)
        def _():
            tile_arrival(turn - 1).wait_recv()

        @pl.when(turn < chips)
        def _():
            tile_turn(turn).start()

        for kind in range(3):

            @pl.when(turn == 1 + kind)
            def _(kind=kind):
                for way in range(2):
                    hop_copy(way, kind).start()

            @pl.when(turn == 5 + kind)
            def _(kind=kind):
                hop_done(kind)

        @pl.when(turn < chips)
        def _():
            begin(turn + 1)

        for number in numbers:
            array = streams[number][0]
            owner = owner_at(number, turn)
            if not streams[number][4]:
                add_cores(number, turn)

                @pl.when(turn > 1)
                def _(number=number, array=array, owner=owner):
                    ring_copy(number, turn - 1).wait_recv()
                    for its_side in range(2):
                        held[array][owner, its_side, :, cols(number)] = (
                            held[array][owner, its_side, :, cols(number)].astype(F32)
                            + ring_in[number][turn - 2, its_side].astype(F32)
                        ).astype(BF16)

                @pl.when(turn < chips)
                def _(number=number):
                    ring_copy(number, turn).start()

        for number in numbers:
            array = streams[number][0]
            owner = owner_at(number, turn)
            if streams[number][4]:
                x_copy(number, turn).wait_recv()

                @pl.when(turn == 1)
                def _(number=number, array=array, owner=owner):
                    held[array][owner, side, :, cols(number)] = (
                        held[array][owner, side, :, cols(number)].astype(F32)
                        + x_in[number][turn - 1].astype(F32)
                    ).astype(BF16)

                @pl.when(turn > 1)
                def _(number=number, array=array, owner=owner):
                    ring_copy(number, turn - 1).wait_recv()
                    total = (
                        held[array][owner, side, :, cols(number)].astype(F32)
                        + x_in[number][turn - 1].astype(F32)
                        + ring_in[number][turn - 2, 0].astype(F32)
                    )
                    held[array][owner, side, :, cols(number)] = total.astype(BF16)

                    @pl.when(turn == chips)
                    def _():
                        outs[array][:, cols(number)] = total

                @pl.when(turn < chips)
                def _(number=number):
                    ring_copy(number, turn).start()

        return carry

    lax.fori_loop(1, chips + 1, round_trip, 0)
    for number in numbers:
        if not streams[number][4]:
            x_copy(number, chips).start()
    tile_out[...] = lax.fori_loop(1, chips, lambda i, total: total + tile_ring[i], tile_ring[0])
    for number in numbers:
        array = streams[number][0]
        if not streams[number][4]:
            x_copy(number, chips).wait_recv()
            outs[array][:, cols(number)] = held[array][chip, side, :, cols(number)].astype(
                F32
            ) + x_in[number][0].astype(F32)

    def drain(turn, carry):
        for number in numbers:
            core_copy(number, turn).wait_send()
            if streams[number][4]:
                x_copy(number, turn).wait_send()

            @pl.when(turn < chips)
            def _(number=number):
                ring_copy(number, turn).wait_send()

        @pl.when(turn < chips)
        def _():
            tile_turn(turn).wait_send()

        return carry

    lax.fori_loop(1, chips + 1, drain, 0)
    for number in numbers:
        if not streams[number][4]:
            x_copy(number, chips).wait_send()


def refs_of(counts, refs):
    groups, at = [], 0
    for count in counts:
        groups.append(refs[at : at + count])
        at += count
    return groups


def sum_all(arrays, firsts, tile, up_sum, down_sum, terms, chips):
    rows = arrays[0].shape[0] // (4 * chips)
    streams = []
    for i, (array, first) in enumerate(zip(arrays, firsts)):
        width = array.shape[1]
        left = width // 256 * 128
        streams.append((i, 0, left, 1, first))
        streams.append((i, left, width - left, -1, first))
    streams = tuple(sorted(streams, key=lambda stream: stream[4]))
    count, number = len(arrays), len(streams)
    dma = pltpu.SemaphoreType.DMA
    vmem = pltpu.VMEM
    scratch = (
        [vmem((chips, 2, rows, a.shape[1]), BF16) for a in arrays]
        + [vmem((chips, 2, rows, a.shape[1]), BF16) for a in arrays]
        + [vmem((chips - 1, 1 if first else 2, rows, width), BF16) for _, _, width, _, first in streams]
        + [vmem((chips if first else 1, rows, width), BF16) for _, _, width, _, first in streams]
        + [vmem((3, 8, 128), F32), vmem((chips, 8, 128), F32)]
        + [vmem(up_sum.shape, BF16), vmem(down_sum.shape, BF16)]
        + [dma((count,))]
        + [dma((number, chips)) for _ in range(6)]
        + [dma((chips + 1,)) for _ in range(2)]
        + [dma((2, 3)) for _ in range(2)]
    )
    return pl.pallas_call(
        functools.partial(
            sum_kernel, chips, streams, (count, 4, count, 2, count, count, number, number, 4, 11)
        ),
        out_shape=[jax.ShapeDtypeStruct((rows, a.shape[1]), F32) for a in arrays]
        + [jax.ShapeDtypeStruct((8, 128), F32), jax.ShapeDtypeStruct(terms.shape, F32)],
        in_specs=[pl.BlockSpec(memory_space=pl.ANY)] * count
        + [pl.BlockSpec(memory_space=pltpu.VMEM)]
        + [pl.BlockSpec(memory_space=pl.ANY)] * 2
        + [pl.BlockSpec(memory_space=pltpu.VMEM)],
        out_specs=[pl.BlockSpec(memory_space=pltpu.VMEM)] * (count + 2),
        scratch_shapes=scratch,
        compiler_params=pltpu.CompilerParams(
            collective_id=1, has_side_effects=True, vmem_limit_bytes=58 << 20
        ),
        cost_estimate=pl.CostEstimate(
            flops=0, bytes_accessed=sum(2 * a.size for a in arrays), transcendentals=0
        ),
        name="sum_all",
    )(*[a.reshape(chips, 2, 2, rows, a.shape[1]) for a in arrays], tile, up_sum, down_sum, terms)


LITTLE = pl.CostEstimate(flops=0, bytes_accessed=1024, transcendentals=0)
VMEM_LIMIT = 56 << 20


def whole(shape):
    return pl.BlockSpec(shape, lambda *_: (0,) * len(shape))


def piece(kernel, name, grid, in_specs, out_specs, out_shapes, scratch=()):
    return pl.pallas_call(
        kernel,
        grid=grid,
        in_specs=in_specs,
        out_specs=out_specs,
        out_shape=[jax.ShapeDtypeStruct(shape, dtype) for shape, dtype in out_shapes],
        scratch_shapes=list(scratch),
        compiler_params=pltpu.CompilerParams(vmem_limit_bytes=VMEM_LIMIT),
        cost_estimate=LITTLE,
        name=name,
    )


def inverse_rms(values):
    return lax.rsqrt(jnp.mean(values * values, axis=-1, keepdims=True) + EPSILON)


def norm_back(values, gain, grad):
    scale = inverse_rms(values)
    scaled = grad * gain
    mean = jnp.mean(values * scaled, axis=-1, keepdims=True)
    back = scale * scaled - values * (scale * scale * scale * mean)
    return back, jnp.sum(grad * (values * scale), axis=0, keepdims=True)


def qkv_kernel(tokens, gains, head_gain, cosine, sine, weight, low, raw, new):
    at = pl.program_id(0)

    @pl.when(at == 0)
    def _():
        states = tokens[...].astype(F32)
        low[...] = (states * inverse_rms(states) * gains[0:1]).astype(BF16)

    out = full_dot(low[...], weight[...])
    raw[...] = out
    plain = out * inverse_rms(out)
    values = plain * jnp.where(at < HEADS, head_gain[0:1], head_gain[1:2])
    half = HEAD // 2
    first, second = values[:, :half], values[:, half:]
    turned = jnp.concatenate(
        [first * cosine[...] - second * sine[...], second * cosine[...] + first * sine[...]], 1
    )
    new[...] = jnp.where(at < HEADS + KV_HEADS, turned, plain).astype(BF16)


def make_qkv(tokens, gains, head_gain, cosine, sine, full):
    rows = tokens.shape[0]
    heads = HEADS + 2 * KV_HEADS
    return piece(
        qkv_kernel,
        "make_qkv",
        (heads,),
        [
            whole((rows, D)),
            whole(gains.shape),
            whole((2, HEAD)),
            whole(cosine.shape),
            whole(sine.shape),
            pl.BlockSpec((D, HEAD), lambda i: (0, HEADS + i)),
        ],
        [
            whole((rows, D)),
            pl.BlockSpec((rows, HEAD), lambda i: (0, i)),
            pl.BlockSpec((rows, HEAD), lambda i: (0, i)),
        ],
        [((rows, D), BF16), ((rows, heads * HEAD), F32), ((rows, heads * HEAD), BF16)],
    )(tokens, gains, head_gain, cosine, sine, full)


def softmax_of(query, key, visible):
    scores = jnp.where(visible > 0.0, right_dot(query, key), -1e30)
    expo = jnp.exp(scores - jnp.max(scores, axis=-1, keepdims=True))
    return expo / jnp.sum(expo, axis=-1, keepdims=True)


def attend_kernel(
    tokens, gains, low, query, key, value, visible, w_out, lleft, lright,
    context, attn_raw, mixed, ffn_in, mid,
):
    at = pl.program_id(0)
    probs = softmax_of(query[...], key[...], visible[...]).astype(BF16)
    here = full_dot(probs, value[...]).astype(BF16)
    context[...] = here
    term = full_dot(here, w_out[...])

    @pl.when(at == 0)
    def _():
        attn_raw[...] = term

    @pl.when(at > 0)
    def _():
        attn_raw[...] += term

    @pl.when(at == HEADS - 1)
    def _():
        states = tokens[...].astype(F32)
        raw = attn_raw[...]
        total = states + raw * inverse_rms(raw) * gains[1:2]
        total = total + states * inverse_rms(states) * gains[0:1]
        mid[...] = full_dot(low[...], lleft[...]).astype(BF16)
        laurel = right_dot(mid[...], lright[...])
        total = (total + laurel * inverse_rms(laurel) * gains[2:3]) * INV_SQRT2
        mixed[...] = total
        ffn_in[...] = (total * inverse_rms(total) * gains[3:4]).astype(BF16)


def attend(tokens, gains, low, qkv, keys_all, visible, full):
    rows = tokens.shape[0]
    seen = keys_all.shape[0]
    group = HEADS // KV_HEADS
    side = 128
    left_at, right_at = full.shape[1] // side - 2, full.shape[1] // side - 1
    return piece(
        attend_kernel,
        "attend",
        (HEADS,),
        [
            whole((rows, D)),
            whole(gains.shape),
            whole((rows, D)),
            pl.BlockSpec((rows, HEAD), lambda i: (0, i)),
            pl.BlockSpec((seen, HEAD), lambda i: (0, i // group)),
            pl.BlockSpec((seen, HEAD), lambda i: (0, KV_HEADS + i // group)),
            whole((rows, seen)),
            pl.BlockSpec((HEAD, D), lambda i: (i, 0)),
            pl.BlockSpec((D, side), lambda i: (0, left_at)),
            pl.BlockSpec((D, side), lambda i: (0, right_at)),
        ],
        [
            pl.BlockSpec((rows, HEAD), lambda i: (0, i)),
            whole((rows, D)),
            whole((rows, D)),
            whole((rows, D)),
            whole((rows, side)),
        ],
        [
            ((rows, HEADS * HEAD), BF16),
            ((rows, D), F32),
            ((rows, D), F32),
            ((rows, D), BF16),
            ((rows, side), BF16),
        ],
    )(tokens, gains, low, qkv, keys_all, keys_all, visible, full, full, full)


def load_weights(weights, held, sems):
    copies, at = [], 0
    for number, ref in enumerate(weights):
        count = ref.shape[1]
        copies.append(pltpu.make_async_copy(ref, held.at[:, pl.ds(at, count)], sems.at[number]))
        at += count

    @pl.when(pl.program_id(0) == 0)
    def _():
        for copy in copies:
            copy.start()
        for copy in copies:
            copy.wait()


ROW_BLOCK = 256
UNIT_BLOCK = 512


def unit_blocks(steps, units):
    many = max(1, UNIT_BLOCK // units)
    return [range(first, min(first + many, steps)) for first in range(0, steps, many)]


def ffn_forward_kernel(steps, add, last, *refs):
    weights, refs = refs[: 2 * steps], refs[2 * steps :]
    if add:
        before, refs = refs[0], refs[1:]
    rows, total, refs = refs[0], refs[1], refs[2:]
    if last:
        low_total, refs = refs[0], refs[1:]
    gates, uppers, hiddens, (held, sems) = refs_of((steps, steps, steps, 2), refs)
    load_weights(weights, held, sems)
    units = held.shape[1] // steps
    here = rows[...]
    running = before[...] if add else None
    for block in unit_blocks(steps, units):
        cut = slice(block[0] * units, (block[-1] + 1) * units)
        gate_in = right_dot(here, held[0, cut])
        upper_in = right_dot(here, held[1, cut])
        low = gated_product(gate_in, upper_in).astype(BF16)
        for i, step in enumerate(block):
            own = slice(i * units, (i + 1) * units)
            gates[step][...] = gate_in[:, own]
            uppers[step][...] = upper_in[:, own]
            hiddens[step][...] = low[:, own]
        term = full_dot(low, held[2, cut])
        running = term if running is None else running + term
    write_sum(running, total, low_total if last else None)


def write_sum(running, total, low_total):
    if low_total is None:
        total[...] = running
        return
    half = pl.num_programs(0) // 2

    @pl.when(pl.program_id(0) < half)
    def _():
        low_total[...] = running.astype(BF16)

    @pl.when(pl.program_id(0) >= half)
    def _():
        total[...] = running


def sum_specs(many, last):
    blocks = many // ROW_BLOCK
    half = blocks // 2
    if not last:
        return (lambda i: i), [pl.BlockSpec((ROW_BLOCK, D), lambda i: (i, 0))], [((many, D), F32)]
    specs = [
        pl.BlockSpec((ROW_BLOCK, D), lambda i: (jnp.maximum(i - half, 0), 0)),
        pl.BlockSpec((ROW_BLOCK, D), lambda i: (jnp.minimum(i, half - 1), 0)),
    ]
    return (lambda i: lax.rem(i + half, blocks)), specs, [((many // 2, D), F32), ((many // 2, D), BF16)]


def ffn_forward(rows, before, weights, last):
    many = rows.shape[0]
    steps, units = len(weights) // 2, 2 * weights[0].shape[1]
    at, sums, sum_shapes = sum_specs(many, last)
    by_row = lambda width: pl.BlockSpec((ROW_BLOCK, width), lambda i: (at(i), 0))
    add = before is not None
    outs = piece(
        functools.partial(ffn_forward_kernel, steps, add, last),
        "ffn_forward",
        (many // ROW_BLOCK,),
        [pl.BlockSpec(memory_space=pl.ANY)] * len(weights) + [by_row(D)] * (1 + add),
        sums + [by_row(units)] * (3 * steps),
        sum_shapes + [((many, units), F32)] * (2 * steps) + [((many, units), BF16)] * steps,
        [pltpu.VMEM((3, steps * units, D), BF16), pltpu.SemaphoreType.DMA((len(weights),))],
    )(*weights, *([before] if add else []), rows)
    return refs_of((len(sums), steps, steps, steps), outs)


def ffn_backward_kernel(steps, add, last, *refs):
    weights, refs = refs[: 2 * steps], refs[2 * steps :]
    if add:
        before, refs = refs[0], refs[1:]
    (rows,), gates, uppers, totals, grad_gates, grad_uppers, (held, sems) = refs_of(
        (1, steps, steps, 1 + last, steps, steps, 2), refs
    )
    load_weights(weights, held, sems)
    units = held.shape[1] // steps
    here = rows[...]
    running = before[...] if add else None
    for block in unit_blocks(steps, units):
        cut = slice(block[0] * units, (block[-1] + 1) * units)
        grad_hidden = right_dot(here, held[2, cut])
        low_gates, low_uppers = [], []
        for i, step in enumerate(block):
            unused, act_back = jax.vjp(gated_product, gates[step][...], uppers[step][...])
            back_gate, back_upper = act_back(grad_hidden[:, i * units : (i + 1) * units])
            low_gates.append(back_gate.astype(BF16))
            low_uppers.append(back_upper.astype(BF16))
            grad_gates[step][...] = low_gates[-1]
            grad_uppers[step][...] = low_uppers[-1]
        term = full_dot(jnp.concatenate(low_gates, 1), held[0, cut])
        term = term + full_dot(jnp.concatenate(low_uppers, 1), held[1, cut])
        running = term if running is None else running + term
    write_sum(running, totals[0], totals[1] if last else None)


def ffn_backward(rows, before, weights, gates, uppers, last):
    many = rows.shape[0]
    steps, units = len(gates), gates[0].shape[1]
    at, sums, sum_shapes = sum_specs(many, last)
    by_row = lambda width: pl.BlockSpec((ROW_BLOCK, width), lambda i: (at(i), 0))
    add = before is not None
    outs = piece(
        functools.partial(ffn_backward_kernel, steps, add, last),
        "ffn_backward",
        (many // ROW_BLOCK,),
        [pl.BlockSpec(memory_space=pl.ANY)] * len(weights)
        + [by_row(D)] * (1 + add)
        + [by_row(units)] * (2 * steps),
        sums + [by_row(units)] * (2 * steps),
        sum_shapes + [((many, units), BF16)] * (2 * steps),
        [pltpu.VMEM((3, steps * units, D), BF16), pltpu.SemaphoreType.DMA((len(weights),))],
    )(*weights, *([before] if add else []), rows, *gates, *uppers)
    return refs_of((len(sums), steps, steps), outs)


def unit_grads_kernel(grad_gate, grad_upper, hidden, rows, down_rows, out):
    out[0] = left_dot(grad_gate[...], rows[...]).astype(BF16)
    out[1] = left_dot(grad_upper[...], rows[...]).astype(BF16)
    out[2] = left_dot(hidden[...], down_rows[...]).astype(BF16)


def unit_grads_of(grad_gate, grad_upper, hidden, rows, down_rows):
    many, units = hidden.shape
    width = 1024
    narrow = whole((many, units))
    wide = pl.BlockSpec((many, width), lambda i: (0, i))
    return piece(
        unit_grads_kernel,
        "unit_grads",
        (D // width,),
        [narrow, narrow, narrow, wide, wide],
        [pl.BlockSpec((3, units, width), lambda i: (0, 0, i))],
        [((3, units, D), BF16)],
    )(grad_gate, grad_upper, hidden, rows, down_rows)[0]


def attend_back_kernel(
    gains, grad_in, grad_after, mixed, attn_raw, mid, low, lleft, lright, w_out, context, query, key, value, visible,
    grad_mixed, grad_mid, grad_gains, grad_left, grad_right, grad_w_out, grad_query, grad_key, grad_value,
    grad_attn,
):
    at = pl.program_id(0)

    @pl.when(at == 0)
    def _():
        back, gain_3 = norm_back(mixed[...], gains[3:4], grad_in[...])
        total = (grad_after[...] + back) * INV_SQRT2
        grad_mixed[...] = total
        back, gain_2 = norm_back(right_dot(mid[...], lright[...]), gains[2:3], total)
        back_low = back.astype(BF16)
        grad_right[...] = left_dot(back_low, mid[...])
        mid_low = full_dot(back_low, lright[...]).astype(BF16)
        grad_mid[...] = mid_low
        grad_left[...] = left_dot(low[...], mid_low)
        back, gain_1 = norm_back(attn_raw[...], gains[1:2], total)
        grad_attn[...] = back.astype(BF16)
        grad_gains[...] = jnp.concatenate(
            [gain_1, gain_2, gain_3, jnp.zeros((5, D), F32)], 0
        )

    grad_context = right_dot(grad_attn[...], w_out[...]).astype(BF16)
    grad_w_out[...] = left_dot(context[...], grad_attn[...]).astype(BF16)
    probs = softmax_of(query[...], key[...], visible[...])
    grad_probs = right_dot(grad_context, value[...])
    inner = jnp.sum(probs * grad_probs, axis=-1, keepdims=True)
    grad_scores = (probs * (grad_probs - inner)).astype(BF16)
    grad_query[...] = full_dot(grad_scores, key[...])
    key_term = left_dot(grad_scores, query[...])
    value_term = left_dot(probs.astype(BF16), grad_context)
    group = HEADS // KV_HEADS

    @pl.when(lax.rem(at, group) == 0)
    def _():
        grad_key[...] = key_term
        grad_value[...] = value_term

    @pl.when(lax.rem(at, group) > 0)
    def _():
        grad_key[...] += key_term
        grad_value[...] += value_term


def attend_back(gains, grad_in, grad_after, mixed, attn_raw, mid, low, full, context, qkv, keys_all, visible):
    rows = low.shape[0]
    seen = keys_all.shape[0]
    group = HEADS // KV_HEADS
    side = 128
    left_at, right_at = full.shape[1] // side - 2, full.shape[1] // side - 1
    head = pl.BlockSpec((rows, HEAD), lambda i: (0, i))
    once = lambda shape: pl.BlockSpec(shape, lambda i: (0, 0), pipeline_mode=pl.Buffered(1))
    return piece(
        attend_back_kernel,
        "attend_back",
        (HEADS,),
        [
            whole(gains.shape),
            once((rows, D)),
            once((rows, D)),
            once((rows, D)),
            once((rows, D)),
            whole((rows, side)),
            whole((rows, D)),
            pl.BlockSpec((D, side), lambda i: (0, left_at)),
            pl.BlockSpec((D, side), lambda i: (0, right_at)),
            pl.BlockSpec((HEAD, D), lambda i: (i, 0)),
            head,
            head,
            pl.BlockSpec((seen, HEAD), lambda i: (0, i // group)),
            pl.BlockSpec((seen, HEAD), lambda i: (0, KV_HEADS + i // group)),
            whole((rows, seen)),
        ],
        [
            whole((rows, D)),
            whole((rows, side)),
            whole((8, D)),
            whole((D, side)),
            whole((D, side)),
            pl.BlockSpec((HEAD, D), lambda i: (i, 0)),
            head,
            pl.BlockSpec((seen, HEAD), lambda i: (0, i // group)),
            pl.BlockSpec((seen, HEAD), lambda i: (0, i // group)),
        ],
        [
            ((rows, D), F32),
            ((rows, side), BF16),
            ((8, D), F32),
            ((D, side), F32),
            ((D, side), F32),
            ((HEADS * HEAD, D), BF16),
            ((rows, HEADS * HEAD), F32),
            ((seen, KV_HEADS * HEAD), F32),
            ((seen, KV_HEADS * HEAD), F32),
        ],
        [pltpu.VMEM((rows, D), BF16)],
    )(
        gains, grad_in, grad_after, mixed, attn_raw, mid, low, full, full, full, context, qkv, keys_all, keys_all,
        visible,
    )


def turn_back(grad, cosine, sine):
    half = HEAD // 2
    first, second = grad[:, :half], grad[:, half:]
    return jnp.concatenate([first * cosine + second * sine, second * cosine - first * sine], 1)


def query_back_kernel(grad_query, raw, cosine, sine, head_gain, low, weight, grad_w, grad_low, grad_head):
    at = pl.program_id(0)
    turned = turn_back(grad_query[...], cosine[...], sine[...])
    back, gain = norm_back(raw[...], head_gain[0:1], turned)
    back_low = back.astype(BF16)
    grad_w[...] = left_dot(low[...], back_low).astype(BF16)
    term = right_dot(back_low, weight[...])

    @pl.when(at == 0)
    def _():
        grad_low[...] = term
        grad_head[...] = gain

    @pl.when(at > 0)
    def _():
        grad_low[...] += term
        grad_head[...] += gain


def query_back(grad_query, raw, cosine, sine, head_gain, low, full):
    rows = low.shape[0]
    head = pl.BlockSpec((rows, HEAD), lambda i: (0, i))
    return piece(
        query_back_kernel,
        "query_back",
        (HEADS,),
        [
            head,
            head,
            whole(cosine.shape),
            whole(sine.shape),
            whole((2, HEAD)),
            whole((rows, D)),
            pl.BlockSpec((D, HEAD), lambda i: (0, HEADS + i)),
        ],
        [pl.BlockSpec((D, HEAD), lambda i: (0, i)), whole((rows, D)), whole((1, HEAD))],
        [((D, HEADS * HEAD), BF16), ((rows, D), F32), ((1, HEAD), F32)],
    )(grad_query, raw, cosine, sine, head_gain, low, full)


def key_back_kernel(
    grad_kv, raw, cosine, sine, head_gain, low, weight, before, grad_mixed, grad_mid, lleft, tokens, gains,
    grad_w, grad_tokens, grad_head, grad_gain, total,
):
    at = pl.program_id(0)
    is_key = at < KV_HEADS
    grad = grad_kv[...]
    turned = jnp.where(is_key, turn_back(grad, cosine[...], sine[...]), grad)
    back, gain = norm_back(raw[...], jnp.where(is_key, head_gain[1:2], 1.0), turned)
    back_low = back.astype(BF16)
    grad_w[...] = left_dot(low[...], back_low).astype(BF16)
    term = right_dot(back_low, weight[...])

    @pl.when(at == 0)
    def _():
        total[...] = before[...] + term
        grad_head[...] = gain

    @pl.when(at > 0)
    def _():
        total[...] += term
        grad_head[...] += jnp.where(is_key, gain, 0.0)

    @pl.when(at == 2 * KV_HEADS - 1)
    def _():
        grad_normed = total[...] + grad_mixed[...] + right_dot(grad_mid[...], lleft[...])
        back, gain_0 = norm_back(tokens[...].astype(F32), gains[0:1], grad_normed)
        grad_tokens[...] = grad_mixed[...] + back
        grad_gain[...] = gain_0


def key_back(grad_kv, raw, cosine, sine, head_gain, low, full, before, grad_mixed, grad_mid, tokens, gains):
    rows = low.shape[0]
    side = 128
    left_at = full.shape[1] // side - 2
    return piece(
        key_back_kernel,
        "key_back",
        (2 * KV_HEADS,),
        [
            pl.BlockSpec((rows, HEAD), lambda i: (0, i)),
            pl.BlockSpec((rows, HEAD), lambda i: (0, HEADS + i)),
            whole(cosine.shape),
            whole(sine.shape),
            whole((2, HEAD)),
            whole((rows, D)),
            pl.BlockSpec((D, HEAD), lambda i: (0, 2 * HEADS + i)),
            whole((rows, D)),
            whole((rows, D)),
            whole((rows, side)),
            pl.BlockSpec((D, side), lambda i: (0, left_at)),
            whole((rows, D)),
            whole(gains.shape),
        ],
        [
            pl.BlockSpec((D, HEAD), lambda i: (0, i)),
            whole((rows, D)),
            whole((1, HEAD)),
            whole((1, D)),
        ],
        [
            ((D, 2 * KV_HEADS * HEAD), BF16),
            ((rows, D), F32),
            ((1, HEAD), F32),
            ((1, D), F32),
        ],
        [pltpu.VMEM((rows, D), F32)],
    )(grad_kv, raw, cosine, sine, head_gain, low, full, before, grad_mixed, grad_mid, full, tokens, gains)


def tie(*values):
    return lax.optimization_barrier(values)


def shares(total, count):
    return [total // count + (1 if i < total % count else 0) for i in range(count)]


def greet(peers):
    barrier = pltpu.get_barrier_semaphore()
    for peer in peers:
        pl.semaphore_signal(barrier, inc=1, device_id=peer, device_id_type=MESH)
    pl.semaphore_wait(barrier, len(peers))


def partners():
    return {"core": 1 - lax.axis_index("core")}, {"fsdp": 1 - lax.axis_index("fsdp")}


CUTS = 4


def spread_kernel(own, rows, x_send, x_recv, near_send, near_recv, far_send, far_recv, own_sem):
    count = own.shape[0]
    cut = count // CUTS
    other_core, other_side = partners()
    greet((other_core, other_side))

    def copy(src, block, at, send, recv, peer):
        return pltpu.make_async_remote_copy(
            src_ref=src,
            dst_ref=rows.at[pl.ds(block * count + at * cut, cut)],
            send_sem=send.at[at],
            recv_sem=recv.at[at],
            device_id=peer,
            device_id_type=MESH,
        )

    mine = [own.at[pl.ds(at * cut, cut)] for at in range(CUTS)]
    came = [rows.at[pl.ds(count + at * cut, cut)] for at in range(CUTS)]
    across = [copy(mine[at], 1, at, x_send, x_recv, other_side) for at in range(CUTS)]
    near = [copy(mine[at], 2, at, near_send, near_recv, other_core) for at in range(CUTS)]
    far = [copy(came[at], 3, at, far_send, far_recv, other_core) for at in range(CUTS)]
    for one in across + near:
        one.start()
    keep = pltpu.make_async_copy(own, rows.at[pl.ds(0, count)], own_sem)
    keep.start()
    for at in range(CUTS):
        across[at].wait_recv()
        far[at].start()
    for one in near + far:
        one.wait()
    for one in across:
        one.wait_send()
    keep.wait()


def rows_of_four(own, number):
    count = own.shape[0]
    dma = pltpu.SemaphoreType.DMA
    return pl.pallas_call(
        spread_kernel,
        out_shape=jax.ShapeDtypeStruct((4 * count, D), BF16),
        in_specs=[pl.BlockSpec(memory_space=pl.ANY)],
        out_specs=pl.BlockSpec(memory_space=pl.ANY),
        scratch_shapes=[dma((CUTS,)) for _ in range(6)] + [dma],
        compiler_params=pltpu.CompilerParams(collective_id=number, has_side_effects=True),
        cost_estimate=LITTLE,
        name="spread_rows",
    )(own)


def gather_sum_kernel(own, low, out, core_in, pair_low, x_in, core_send, core_recv, x_send, x_recv):
    count = out.shape[0]
    cut = count // CUTS
    other_core, other_side = partners()
    greet((other_core, other_side))

    def core_copy(block, at):
        here = pl.ds(block * count + at * cut, cut)
        number = block * CUTS + at
        return pltpu.make_async_remote_copy(
            src_ref=low.at[here],
            dst_ref=core_in.at[here],
            send_sem=core_send.at[number],
            recv_sem=core_recv.at[number],
            device_id=other_core,
            device_id_type=MESH,
        )

    def x_copy(at):
        here = pl.ds(at * cut, cut)
        return pltpu.make_async_remote_copy(
            src_ref=pair_low.at[here],
            dst_ref=x_in.at[here],
            send_sem=x_send.at[at],
            recv_sem=x_recv.at[at],
            device_id=other_side,
            device_id_type=MESH,
        )

    for block in (1, 0):
        for at in range(CUTS):
            core_copy(block, at).start()
    for at in range(CUTS):
        there = pl.ds(count + at * cut, cut)
        core_copy(1, at).wait_recv()
        pair_low[pl.ds(at * cut, cut)] = (own[there] + core_in[there].astype(F32)).astype(BF16)
        x_copy(at).start()
    for at in range(CUTS):
        here = pl.ds(at * cut, cut)
        core_copy(0, at).wait_recv()
        out[here] = own[here] + core_in[here].astype(F32)
    for at in range(CUTS):
        here = pl.ds(at * cut, cut)
        x_copy(at).wait_recv()
        out[here] += x_in[here].astype(F32)
    for at in range(CUTS):
        x_copy(at).wait_send()
        for block in (0, 1):
            core_copy(block, at).wait_send()


def sum_of_four(own, low, number):
    count = own.shape[0] // 2
    dma = pltpu.SemaphoreType.DMA
    return pl.pallas_call(
        gather_sum_kernel,
        out_shape=jax.ShapeDtypeStruct((count, D), F32),
        in_specs=[pl.BlockSpec(memory_space=pltpu.VMEM), pl.BlockSpec(memory_space=pl.ANY)],
        out_specs=pl.BlockSpec(memory_space=pltpu.VMEM),
        scratch_shapes=[
            pltpu.VMEM((2 * count, D), BF16),
            pltpu.VMEM((count, D), BF16),
            pltpu.VMEM((count, D), BF16),
            dma((2 * CUTS,)),
            dma((2 * CUTS,)),
            dma((CUTS,)),
            dma((CUTS,)),
        ],
        compiler_params=pltpu.CompilerParams(
            collective_id=number, has_side_effects=True, vmem_limit_bytes=VMEM_LIMIT
        ),
        cost_estimate=LITTLE,
        name="gather_sum",
    )(own, low)


def body(
    tokens,
    per_layer,
    teacher,
    cont_lengths,
    w_query,
    w_kv,
    w_out,
    laurel_left,
    laurel_right,
    pl_gate,
    pl_proj,
    norm_gains,
    head_gains,
    ffn_weight,
):
    layer_in = per_layer[0].astype(F32)
    target = teacher[0].astype(F32)
    row_count = tokens.shape[1]
    chips = lax.axis_size("zy")
    seq_count = 2 * chips
    group_count = lax.axis_size("fsdp")
    shards = seq_count * group_count
    chip = lax.axis_index("zy")
    core = lax.axis_index("core")
    seq_index = chip * 2 + core
    group_index = lax.axis_index("fsdp")
    half_point = seq_count // 2
    prompt_len = half_point * row_count
    cont_shards = CONT_LEN // row_count
    cont_count = prompt_len // CONT_LEN
    is_cont = seq_index >= half_point
    rel_index = seq_index - half_point
    local_shard = jnp.where(is_cont, rel_index % cont_shards, 0)
    cont_index = jnp.where(is_cont, rel_index // cont_shards, 0)
    first_place = jnp.where(is_cont, prompt_len + local_shard * row_count, seq_index * row_count)
    row_range = jnp.arange(row_count, dtype=jnp.int32)
    places = first_place + row_range
    group_lengths = jnp.sum(
        jnp.where(
            jnp.arange(group_count, dtype=jnp.int32)[:, None] == group_index, cont_lengths, 0
        ),
        axis=0,
    )
    my_length = jnp.sum(
        jnp.where(jnp.arange(cont_count, dtype=jnp.int32) == cont_index, group_lengths, 0)
    )
    valid = jnp.logical_or(
        jnp.logical_not(is_cont), local_shard * row_count + row_range < my_length
    )
    weight_mask = valid.astype(F32)
    count = F32(group_count * prompt_len) + jnp.sum(cont_lengths).astype(F32)
    total_slots = float(row_count * seq_count * group_count)
    shard_rows = w_query.shape[0]
    key_cols = KV_HEADS * HEAD
    proj_cols = pl_proj.shape[0] * D // shard_rows
    misc_cols = RANK
    head_part = head_gains.reshape(-1, 1)
    misc = jnp.concatenate(
        [
            norm_gains.T,
            jnp.pad(head_part, ((0, shard_rows - head_part.shape[0]), (0, 0))),
            jnp.zeros((shard_rows, misc_cols - 7), BF16),
        ],
        1,
    )
    pack = jnp.concatenate(
        [
            w_out,
            w_query,
            w_kv,
            pl_gate,
            pl_proj.reshape(shard_rows, proj_cols),
            laurel_left,
            misc,
            laurel_right.T,
            jnp.zeros((shard_rows, 128 - RANK), BF16),
        ],
        1,
    )

    units = ffn_weight.shape[0]
    half = units // 2
    by_kind = ffn_weight.transpose(1, 0, 2)
    ups, downs = [by_kind[:, :half]], [by_kind[:, half:]]
    stage_steps = shares(chips - 1, 7)

    def pass_on(stage):
        for _ in range(stage_steps[stage]):
            ups.append(ring(ups[-1], 1))
            downs.append(ring(downs[-1], -1))

    def stage_end(values):
        (ups[-1], downs[-1]), values = tie((ups[-1], downs[-1]), values)
        return values

    pass_on(0)
    full = gather_all(pack, chips)
    at = 2 * D + 2 * key_cols
    plg = full[:, at : at + PLD]
    plp = full[:, at + PLD : at + PLD + proj_cols].reshape(PLD, D)
    at += PLD + proj_cols + RANK
    misc_full = stage_end(full[:, at : at + misc_cols])
    pass_on(1)
    gains = jnp.pad(misc_full[:, :6].T.astype(F32), ((0, 2), (0, 0)))
    head_n = head_gains.shape[1]
    head_gain = (
        misc_full[:, 6]
        .reshape(shards, shard_rows)[:, : 2 * head_n]
        .reshape(shards, 2, head_n)
        .transpose(1, 0, 2)
        .reshape(2, HEAD)
        .astype(F32)
    )
    freqs = jnp.exp(
        jnp.arange(HEAD // 2, dtype=F32) * (-2.0 * math.log(ROPE_BASE) / HEAD)
    )
    angles = places.astype(F32)[:, None] * freqs
    cosine, sine = jnp.cos(angles), jnp.sin(angles)
    normed_low, qkv_raw, qkv = make_qkv(tokens[0], gains, head_gain, cosine, sine, full)
    qkv = stage_end(qkv)
    kv_own = qkv[:, D:]
    pass_on(2)

    mid = chips // 2
    chain = [(i, i + 1) for i in range(mid - 1)] + [(mid - 1, mid + 1)]
    kv_before = jnp.where(
        chip == mid,
        lax.ppermute(kv_own, "zy", [(mid - 1, mid)]),
        lax.ppermute(kv_own, "zy", chain),
    )
    spans = []
    span = 2
    while span < mid:
        spans.append(span)
        span *= 2
    for span in spans:
        moved = lax.ppermute(
            kv_before, "zy", [(mid + i, mid + i + span) for i in range(min(span, mid - span))]
        )
        fresh = jnp.logical_and(chip >= mid + span, chip < mid + 2 * span)
        kv_before = jnp.where(fresh, moved, kv_before)
    kv_other = swap(jnp.where(core == 0, kv_own, kv_before), "core")
    keys_all = jnp.concatenate([kv_before, kv_other, kv_own], 0)
    keys_all = stage_end(keys_all)
    pass_on(3)
    key_len = keys_all.shape[0]
    key_places = first_place - 2 * row_count + jnp.arange(key_len, dtype=jnp.int32)
    visible = (
        (key_places[None, :] <= places[:, None])
        & (places[:, None] - key_places[None, :] < WINDOW)
        & (key_places[None, :] >= 0)
    ).astype(F32)
    context_low, attn_raw, mixed, ffn_in, laurel_mid = attend(
        tokens[0], gains, normed_low, qkv, keys_all, visible, full
    )

    ffn_in = stage_end(ffn_in)
    pass_on(4)
    ffn_rows = stage_end(rows_of_four(ffn_in, 2))
    here = len(ups)
    pass_on(5)
    gates, uppers, hiddens = [], [], []

    def weights_of(steps):
        return [w for k in steps for w in (ups[k], downs[k])]

    def forward_part(running, first, end, last=False):
        sums, gate, upper, hidden = ffn_forward(ffn_rows, running, weights_of(range(first, end)), last)
        gates.extend(gate)
        uppers.extend(upper)
        hiddens.extend(hidden)
        return sums if last else sums[0]

    running = stage_end(forward_part(None, 0, here))
    then = len(ups)
    pass_on(6)
    running = stage_end(forward_part(running, here, then))
    own_sum, low_sum = forward_part(running, then, chips, True)
    down_out = sum_of_four(own_sum, low_sum, 3)
    after_ffn = mixed + rms_norm(down_out, gains[4])
    after_low = after_ffn.astype(BF16)
    pl_raw = full_dot(after_low, plg)
    pl_act = gelu_tanh(pl_raw)
    pl_mid = (pl_act * layer_in).astype(BF16)
    pl_out = full_dot(pl_mid, plp)
    result = after_ffn + rms_norm(pl_out, gains[5])
    errors = result - target
    squares = jnp.sum(weight_mask[:, None] * errors * errors)

    grad_out = weight_mask[:, None] * errors * (total_slots / count)
    unused, pl_norm_back = jax.vjp(rms_norm, pl_out, gains[5])
    grad_pl_out, grad_g5 = pl_norm_back(grad_out)
    grad_pl_low = grad_pl_out.astype(BF16)
    grad_plp = left_dot(pl_mid, grad_pl_low)
    grad_pl_mid = right_dot(grad_pl_low, plp)
    grad_layer_in = grad_pl_mid * pl_act
    unused, gelu_back = jax.vjp(gelu_tanh, pl_raw)
    grad_pl_raw = gelu_back(grad_pl_mid * layer_in)[0].astype(BF16)
    grad_plg = left_dot(after_low, grad_pl_raw)
    grad_after = grad_out + right_dot(grad_pl_raw, plg)
    unused, down_norm_back = jax.vjp(rms_norm, down_out, gains[4])
    grad_down, grad_g4 = down_norm_back(grad_after)
    grad_down_low = grad_down.astype(BF16)

    grad_down_rows = rows_of_four(grad_down_low, 4)
    grad_gates, grad_uppers = [None] * chips, [None] * chips

    def backward_part(steps, running, last=False):
        sums, grad_gate, grad_upper = ffn_backward(
            grad_down_rows, running, weights_of(steps), [gates[k] for k in steps], [uppers[k] for k in steps], last
        )
        for k, gg, gu in zip(steps, grad_gate, grad_upper):
            grad_gates[k], grad_uppers[k] = gg, gu
        return sums if last else sums[0]

    def unit_grads(k):
        return unit_grads_of(grad_gates[k], grad_uppers[k], hiddens[k], ffn_rows, grad_down_rows)

    order = list(range(1, chips)) + [0]
    ring_steps = shares(chips - 2, 6)
    done = 0

    def beside(stage, work):
        nonlocal done, up_sum, down_sum
        values = None
        for step in range(ring_steps[stage]):
            up_in = ring(up_sum, 1)
            down_in = ring(down_sum, -1)
            if step == 0:
                values = work()
            done += 1
            terms = unit_grads(order[done])
            (up_in, down_in), terms, values = tie((up_in, down_in), terms, values)
            up_sum = (up_in.astype(F32) + terms[:, :half].astype(F32)).astype(BF16)
            down_sum = (down_in.astype(F32) + terms[:, half:].astype(F32)).astype(BF16)
        return work() if values is None else values

    first = ring_steps[0]
    then = first + 1 + ring_steps[0] + ring_steps[1]
    running = backward_part(order[:first], None)
    terms = unit_grads(order[0])
    up_sum, down_sum = terms[:, :half], terms[:, half:]
    running = beside(0, lambda: backward_part(order[first:then], running))
    own_sum, low_sum = beside(1, lambda: backward_part(order[then:], running, True))
    grad_ffn_in = beside(
        2, lambda: sum_of_four(own_sum, low_sum, 5)
    )
    (
        grad_scaled,
        grad_mid_low,
        grad_mid_gains,
        grad_lleft,
        grad_lright_t,
        grad_wo,
        grad_queries,
        grad_keys,
        grad_values,
    ) = beside(
        3,
        lambda: attend_back(
            gains, grad_ffn_in, grad_after, mixed, attn_raw, laurel_mid, normed_low, full, context_low, qkv, keys_all,
            visible,
        ),
    )

    def work():
        grad_kv = jnp.concatenate([grad_keys, grad_values], 1)
        grad_before = grad_kv[:row_count]
        grad_own = grad_kv[2 * row_count :]
        returned = swap(grad_kv[row_count : 2 * row_count].astype(BF16), "core").astype(F32)
        grad_own = grad_own + jnp.where(core == 0, returned, 0.0)
        grad_before = grad_before + jnp.where(core == 0, 0.0, returned)
        for span in reversed(spans):
            back = [(mid + i + span, mid + i) for i in range(min(span, mid - span))]
            grad_before = grad_before + lax.ppermute(grad_before.astype(BF16), "zy", back).astype(F32)
        before_low = grad_before.astype(BF16)
        grad_own = (
            grad_own
            + lax.ppermute(before_low, "zy", [(b, a) for a, b in chain]).astype(F32)
            + lax.ppermute(before_low, "zy", [(mid, mid - 1)]).astype(F32)
        )
        return grad_own, query_back(grad_queries, qkv_raw, cosine, sine, head_gain, normed_low, full)

    grad_own, (grad_wq, grad_normed, grad_hq) = beside(4, work)
    def work():
        grad_wkv, grad_tokens, grad_hk, grad_g0 = key_back(
            grad_own, qkv_raw, cosine, sine, head_gain, normed_low, full, grad_normed, grad_scaled, grad_mid_low,
            tokens[0], gains,
        )
        head_back = jnp.concatenate([grad_hq, grad_hk], 0).reshape(2, shards, head_n).transpose(1, 0, 2)
        head_back = head_back.reshape(shards, 2 * head_n)
        head_back = jnp.pad(head_back, ((0, 0), (0, shard_rows - 2 * head_n))).reshape(1, D)
        misc_back = jnp.concatenate(
            [grad_g0, grad_mid_gains[:3], grad_g4[None], grad_g5[None], head_back, jnp.zeros((1, D), F32)], 0
        )
        return grad_wkv, grad_tokens, jnp.concatenate(
            [
                grad_plg.astype(BF16),
                grad_plp.astype(BF16).reshape(D, proj_cols),
                grad_lleft[:, :RANK].astype(BF16),
                jnp.pad(misc_back.T, ((0, 0), (0, misc_cols - 8))).astype(BF16),
                grad_lright_t.astype(BF16),
            ],
            1,
        )

    grad_wkv, grad_tokens, rest_back = beside(5, work)
    sums_wq, sums_wkv, sums_wo, sums_rest, total, grad_units = sum_all(
        [grad_wq, grad_wkv, grad_wo, rest_back],
        (True, True, True, False),
        jnp.broadcast_to(squares, (8, 128)),
        up_sum,
        down_sum,
        unit_grads(0),
        chips,
    )
    grad_ffn = grad_units.transpose(1, 0, 2)
    at = 0
    rest = []
    for width in (PLD, proj_cols, RANK, misc_cols, RANK):
        rest.append(sums_rest[:, at : at + width])
        at += width

    match_loss = total[0, 0] / (2.0 * D * count)

    return (
        result[None],
        match_loss,
        grad_tokens[None],
        grad_layer_in[None],
        sums_wq,
        sums_wkv,
        sums_wo,
        rest[2],
        rest[4].T,
        rest[0],
        rest[1].reshape(pl_proj.shape),
        rest[3][:, :6].T,
        rest[3][: 2 * head_n, 6].reshape(2, head_n),
        grad_ffn,
    )


def solution(mesh):
    seq, fsdp = mesh.shape["seq"], mesh.shape["fsdp"]
    fine = Mesh(mesh.devices.reshape(seq // 2, 2, fsdp), ("zy", "core", "fsdp"))
    rows = P("fsdp", ("zy", "core"), None)
    split = ("zy", "core", "fsdp")
    weights = (
        P(split, None),
        P(split, None),
        P(split, None),
        P(split, None),
        P(None, split),
        P(split, None),
        P(split, None),
        P(None, split),
        P(None, split),
        P(split, None, None),
    )
    return jax.shard_map(
        body,
        mesh=fine,
        in_specs=(rows, rows, rows, P()) + weights,
        out_specs=(rows, P(), rows, rows) + weights,
        check_vma=False,
    )
```

```python
import functools
import math

import jax
import jax.numpy as jnp
from jax import lax
from jax.experimental import pallas as pl
from jax.experimental.pallas import tpu as pltpu
from jax.sharding import Mesh, PartitionSpec as P

D = 2048
HEADS = 8
KV_HEADS = 2
HEAD = 256
WINDOW = 512
CONT_LEN = 512
RANK = 64
PLD = 256

EPSILON = 1e-06
INV_SQRT2 = 0.7071067811865476
ROPE_BASE = 10000.0
BF16 = jnp.bfloat16
F32 = jnp.float32


def rms_norm(values, gain):
    return values * lax.rsqrt(jnp.mean(values * values, axis=-1, keepdims=True) + EPSILON) * gain


def gelu_tanh(values):
    return jax.nn.gelu(values, approximate=True)


def gated_product(gate_in, up_in):
    return gelu_tanh(gate_in) * up_in


def full_dot(left, right):
    return jnp.dot(left, right, preferred_element_type=F32)


def left_dot(left, right):
    return lax.dot_general(left, right, (((0,), (0,)), ((), ())), preferred_element_type=F32)


def right_dot(left, right):
    return lax.dot_general(left, right, (((1,), (1,)), ((), ())), preferred_element_type=F32)


def ring_order(n):
    return list(range(0, n, 2)) + list(range(n - 1, 0, -2))


def ring_pairs(n, by):
    order = ring_order(n)
    return [(order[i], order[(i + by) % n]) for i in range(n)]


def ring(value, by):
    return lax.ppermute(value, "zy", ring_pairs(lax.axis_size("zy"), by))


def swap(value, axis):
    return lax.ppermute(value, axis, [(0, 1), (1, 0)])


MESH = pl.DeviceIdType.MESH


def ring_chip(spot, chips):
    spot = lax.rem(spot, chips)
    return jnp.where(spot < chips // 2, 2 * spot, 2 * (chips - 1 - spot) + 1)


def ring_spot(chip, chips):
    return jnp.where(lax.rem(chip, 2) == 0, chip // 2, chips - 1 - chip // 2)


def gather_kernel(chips, streams, shard, full, ring_send, ring_recv, x_send, x_recv, core_send, core_recv, own_sem):
    chip = lax.axis_index("zy")
    core = lax.axis_index("core")
    side = lax.axis_index("fsdp")
    spot = ring_spot(chip, chips)
    rows = shard.shape[0]

    def neighbour(by):
        return {"zy": ring_chip(spot + chips + by, chips)}

    other_core = {"core": 1 - core}
    other_side = {"fsdp": 1 - side}

    barrier = pltpu.get_barrier_semaphore()
    for peer in (neighbour(1), neighbour(-1), other_core, other_side):
        pl.semaphore_signal(barrier, inc=1, device_id=peer, device_id_type=MESH)
    pl.semaphore_wait(barrier, 4)

    def place(owner, its_core, its_side, stream):
        row = ((owner * 2 + its_core) * 2 + its_side) * rows
        return full.at[pl.ds(pl.multiple_of(row, rows), rows), pl.ds(stream[0], stream[1])]

    def owner_at(step, stream):
        return ring_chip(spot + chips - stream[2] * step, chips)

    def send(src, dst, sems, at, peer):
        return pltpu.make_async_remote_copy(
            src_ref=src,
            dst_ref=dst,
            send_sem=sems[0].at[at],
            recv_sem=sems[1].at[at],
            device_id=peer,
            device_id_type=MESH,
        )

    ring_sems, x_sems, core_sems = (ring_send, ring_recv), (x_send, x_recv), (core_send, core_recv)

    def ring_copy(number, away, step, src=None):
        stream = streams[number]
        its_side = 1 - side if away else side
        spot_ref = place(owner_at(step, stream), core, its_side, stream)
        return send(src if src is not None else spot_ref, spot_ref, ring_sems, (number, away, step), neighbour(stream[2]))

    def ring_arrival(number, away, step):
        stream = streams[number]
        its_side = 1 - side if away else side
        spot_ref = place(owner_at(step, stream), core, its_side, stream)
        return send(spot_ref, spot_ref, ring_sems, (number, away, step - 1), neighbour(stream[2]))

    def x_copy(number, step, its_side, src=None):
        stream = streams[number]
        spot_ref = place(owner_at(step, stream), core, its_side, stream)
        return send(src if src is not None else spot_ref, spot_ref, x_sems, (number, step), other_side)

    def core_copy(number, away, step, its_core, src=None):
        stream = streams[number]
        its_side = 1 - side if away else side
        spot_ref = place(owner_at(step, stream), its_core, its_side, stream)
        return send(src if src is not None else spot_ref, spot_ref, core_sems, (number, away, step), other_core)

    def cut(stream):
        return shard.at[:, pl.ds(stream[0], stream[1])]

    own_row = ((chip * 2 + core) * 2 + side) * rows
    own = pltpu.make_async_copy(
        shard, full.at[pl.ds(pl.multiple_of(own_row, rows), rows), :], own_sem
    )
    own.start()
    numbers = range(len(streams))
    for number in numbers:
        if streams[number][3]:
            x_copy(number, 0, side, cut(streams[number])).start()
    for number in numbers:
        ring_copy(number, 0, 0, cut(streams[number])).start()
    for number in numbers:
        if not streams[number][3]:
            x_copy(number, 0, side, cut(streams[number])).start()
    for number in numbers:
        core_copy(number, 0, 0, core, cut(streams[number])).start()
    for number in numbers:
        if streams[number][3]:
            x_copy(number, 0, 1 - side).wait_recv()
            ring_copy(number, 1, 0).start()
            core_copy(number, 1, 0, core).start()

    def turn(step, carry):
        for number in numbers:
            aways = (0, 1) if streams[number][3] else (0,)
            for away in aways:
                ring_arrival(number, away, step).wait_recv()

                @pl.when(step < chips - 1)
                def _(number=number, away=away):
                    ring_copy(number, away, step).start()

                core_copy(number, away, step, core).start()
            if not streams[number][3]:
                x_copy(number, step, side).start()
        for number in numbers:
            if not streams[number][3]:
                x_copy(number, step - 1, 1 - side).wait_recv()
                core_copy(number, 1, step - 1, core).start()
        return carry

    lax.fori_loop(1, chips, turn, 0)
    for number in numbers:
        if not streams[number][3]:
            x_copy(number, chips - 1, 1 - side).wait_recv()
            core_copy(number, 1, chips - 1, core).start()
    own.wait()

    def drain(step, carry):
        for number in numbers:
            first = streams[number][3]
            for away in (0, 1):
                core_copy(number, away, step, 1 - core).wait_recv()
                core_copy(number, away, step, core).wait_send()
                if first or not away:

                    @pl.when(step < chips - 1)
                    def _(number=number, away=away):
                        ring_copy(number, away, step).wait_send()

            if not first:
                x_copy(number, step, side).wait_send()
        return carry

    lax.fori_loop(0, chips, drain, 0)
    for number in numbers:
        if streams[number][3]:
            x_copy(number, 0, side).wait_send()


def gather_all(shard, chips):
    rows, cols = shard.shape
    tiles = cols // 128
    first = int(round(tiles * 0.43)) // 2 * 2
    rest = tiles - first
    bounds = [0, first // 2, first, first + rest // 2, tiles]
    streams = tuple(
        (128 * bounds[i], 128 * (bounds[i + 1] - bounds[i]), 1 if i % 2 == 0 else -1, i < 2)
        for i in range(4)
    )
    dma = pltpu.SemaphoreType.DMA
    return pl.pallas_call(
        functools.partial(gather_kernel, chips, streams),
        out_shape=jax.ShapeDtypeStruct((rows * 4 * chips, cols), shard.dtype),
        in_specs=[pl.BlockSpec(memory_space=pl.ANY)],
        out_specs=pl.BlockSpec(memory_space=pl.ANY),
        scratch_shapes=[
            dma((4, 2, chips)),
            dma((4, 2, chips)),
            dma((4, chips)),
            dma((4, chips)),
            dma((4, 2, chips)),
            dma((4, 2, chips)),
            dma,
        ],
        compiler_params=pltpu.CompilerParams(collective_id=0, has_side_effects=True),
        cost_estimate=pl.CostEstimate(
            flops=0, bytes_accessed=2 * rows * 4 * chips * cols * 2, transcendentals=0
        ),
        name="gather_all",
    )(shard)


def sum_kernel(chips, streams, counts, *refs):
    arrays, (tile, up_sum, down_sum), outs, (tile_out, up_in, down_in), held, core_in, ring_in, x_in, tiles, sems = refs_of(counts, refs)
    load_sem, core_send, core_recv, ring_send, ring_recv, x_send, x_recv, tile_send, tile_recv, hop_send, hop_recv = sems
    tile_pairs, tile_ring = tiles
    chip = lax.axis_index("zy")
    core = lax.axis_index("core")
    side = lax.axis_index("fsdp")
    spot = ring_spot(chip, chips)
    far = 1 - side

    def neighbour(by):
        return {"zy": ring_chip(spot + chips + by, chips)}

    other_core = {"core": 1 - core}
    other_side = {"fsdp": 1 - side}
    barrier = pltpu.get_barrier_semaphore()
    for peer in (neighbour(1), neighbour(-1), other_core, other_side):
        pl.semaphore_signal(barrier, inc=1, device_id=peer, device_id_type=MESH)
    pl.semaphore_wait(barrier, 4)

    numbers = range(len(streams))

    def owner_at(number, turn):
        return ring_chip(spot + 2 * chips - streams[number][3] * turn, chips)

    def cols(number):
        return pl.ds(streams[number][1], streams[number][2])

    def remote(src, dst, send, recv, peer):
        return pltpu.make_async_remote_copy(
            src_ref=src, dst_ref=dst, send_sem=send, recv_sem=recv, device_id=peer, device_id_type=MESH
        )

    def core_copy(number, turn):
        owner = owner_at(number, turn)
        array = streams[number][0]
        return remote(
            arrays[array].at[owner, 1 - core, :, :, cols(number)],
            core_in[array].at[owner, :, :, cols(number)],
            core_send.at[number, turn - 1],
            core_recv.at[number, turn - 1],
            other_core,
        )

    def x_copy(number, turn):
        array = streams[number][0]
        first = streams[number][4]
        slot = turn - 1 if first else 0
        return remote(
            held[array].at[owner_at(number, turn), far, :, cols(number)],
            x_in[number].at[slot],
            x_send.at[number, slot],
            x_recv.at[number, slot],
            other_side,
        )

    def ring_copy(number, turn):
        array = streams[number][0]
        owner = owner_at(number, turn)
        if streams[number][4]:
            src = held[array].at[owner, pl.ds(side, 1), :, cols(number)]
        else:
            src = held[array].at[owner, :, :, cols(number)]
        return remote(
            src,
            ring_in[number].at[turn - 1],
            ring_send.at[number, turn - 1],
            ring_recv.at[number, turn - 1],
            neighbour(streams[number][3]),
        )

    loads = [
        pltpu.make_async_copy(arrays[i].at[:, core], held[i], load_sem.at[i])
        for i in range(len(arrays))
    ]

    def send_cores(turn, carry):
        for number in numbers:
            core_copy(number, turn).start()
        return carry

    def hop_copy(way, kind):
        src, dst = ((up_sum, up_in), (down_sum, down_in))[way]
        return remote(src.at[kind], dst.at[kind], hop_send.at[way, kind], hop_recv.at[way, kind], neighbour(1 - 2 * way))

    def tile_copy(src, dst, number, peer):
        return remote(src, dst, tile_send.at[number], tile_recv.at[number], peer)

    def tile_turn(turn):
        spot_ref = tile_ring.at[ring_chip(spot + 2 * chips - turn + 1, chips)]
        return tile_copy(spot_ref, spot_ref, turn + 1, neighbour(1))

    def tile_arrival(turn):
        spot_ref = tile_ring.at[ring_chip(spot + 2 * chips - turn, chips)]
        return tile_copy(spot_ref, spot_ref, turn + 1, neighbour(1))

    tile_copy(tile, tile_pairs.at[0], 0, other_core).start()
    lax.fori_loop(1, 2, send_cores, 0)
    for load in loads:
        load.start()
    tile_copy(tile, tile_pairs.at[0], 0, other_core).wait()
    tile_pairs[1] = tile[...] + tile_pairs[0]
    tile_copy(tile_pairs.at[1], tile_pairs.at[2], 1, other_side).start()
    lax.fori_loop(2, chips + 1, send_cores, 0)
    for load in loads:
        load.wait()

    def add_cores(number, turn):
        array = streams[number][0]
        owner = owner_at(number, turn)
        core_copy(number, turn).wait_recv()
        for its_side in range(2):
            held[array][owner, its_side, :, cols(number)] = (
                held[array][owner, its_side, :, cols(number)].astype(F32)
                + core_in[array][owner, its_side, :, cols(number)].astype(F32)
            ).astype(BF16)

    def begin(turn):
        for number in numbers:
            if streams[number][4]:
                add_cores(number, turn)
                x_copy(number, turn).start()

    begin(1)
    tile_copy(tile_pairs.at[1], tile_pairs.at[2], 1, other_side).wait()
    tile_ring[chip] = tile_pairs[1] + tile_pairs[2]

    def round_trip(turn, carry):
        @pl.when(turn > 1)
        def _():
            tile_arrival(turn - 1).wait_recv()

        @pl.when(turn < chips)
        def _():
            tile_turn(turn).start()

        for kind in range(3):

            @pl.when(turn == 1 + kind)
            def _(kind=kind):
                for way in range(2):
                    hop_copy(way, kind).start()

        @pl.when(turn < chips)
        def _():
            begin(turn + 1)

        for number in numbers:
            array = streams[number][0]
            owner = owner_at(number, turn)
            if not streams[number][4]:
                add_cores(number, turn)

                @pl.when(turn > 1)
                def _(number=number, array=array, owner=owner):
                    ring_copy(number, turn - 1).wait_recv()
                    for its_side in range(2):
                        held[array][owner, its_side, :, cols(number)] = (
                            held[array][owner, its_side, :, cols(number)].astype(F32)
                            + ring_in[number][turn - 2, its_side].astype(F32)
                        ).astype(BF16)

                @pl.when(turn < chips)
                def _(number=number):
                    ring_copy(number, turn).start()

        for number in numbers:
            array = streams[number][0]
            owner = owner_at(number, turn)
            if streams[number][4]:
                x_copy(number, turn).wait_recv()

                @pl.when(turn == 1)
                def _(number=number, array=array, owner=owner):
                    held[array][owner, side, :, cols(number)] = (
                        held[array][owner, side, :, cols(number)].astype(F32)
                        + x_in[number][turn - 1].astype(F32)
                    ).astype(BF16)

                @pl.when(turn > 1)
                def _(number=number, array=array, owner=owner):
                    ring_copy(number, turn - 1).wait_recv()
                    total = (
                        held[array][owner, side, :, cols(number)].astype(F32)
                        + x_in[number][turn - 1].astype(F32)
                        + ring_in[number][turn - 2, 0].astype(F32)
                    )
                    held[array][owner, side, :, cols(number)] = total.astype(BF16)

                    @pl.when(turn == chips)
                    def _():
                        outs[array][:, cols(number)] = total

                @pl.when(turn < chips)
                def _(number=number):
                    ring_copy(number, turn).start()

        return carry

    lax.fori_loop(1, chips + 1, round_trip, 0)
    for number in numbers:
        if not streams[number][4]:
            x_copy(number, chips).start()
    tile_out[...] = lax.fori_loop(1, chips, lambda i, total: total + tile_ring[i], tile_ring[0])
    for number in numbers:
        array = streams[number][0]
        if not streams[number][4]:
            x_copy(number, chips).wait_recv()
            outs[array][:, cols(number)] = held[array][chip, side, :, cols(number)].astype(
                F32
            ) + x_in[number][0].astype(F32)

    for kind in range(3):
        for way in range(2):
            hop_copy(way, kind).wait()

    def drain(turn, carry):
        for number in numbers:
            core_copy(number, turn).wait_send()
            if streams[number][4]:
                x_copy(number, turn).wait_send()

            @pl.when(turn < chips)
            def _(number=number):
                ring_copy(number, turn).wait_send()

        @pl.when(turn < chips)
        def _():
            tile_turn(turn).wait_send()

        return carry

    lax.fori_loop(1, chips + 1, drain, 0)
    for number in numbers:
        if not streams[number][4]:
            x_copy(number, chips).wait_send()


def refs_of(counts, refs):
    groups, at = [], 0
    for count in counts:
        groups.append(refs[at : at + count])
        at += count
    return groups


def sum_all(arrays, firsts, tile, up_sum, down_sum, chips):
    rows = arrays[0].shape[0] // (4 * chips)
    streams = []
    for i, (array, first) in enumerate(zip(arrays, firsts)):
        width = array.shape[1]
        left = width // 256 * 128
        streams.append((i, 0, left, 1, first))
        streams.append((i, left, width - left, -1, first))
    streams = tuple(sorted(streams, key=lambda stream: stream[4]))
    count, number = len(arrays), len(streams)
    dma = pltpu.SemaphoreType.DMA
    vmem = pltpu.VMEM
    scratch = (
        [vmem((chips, 2, rows, a.shape[1]), BF16) for a in arrays]
        + [vmem((chips, 2, rows, a.shape[1]), BF16) for a in arrays]
        + [vmem((chips - 1, 1 if first else 2, rows, width), BF16) for _, _, width, _, first in streams]
        + [vmem((chips if first else 1, rows, width), BF16) for _, _, width, _, first in streams]
        + [vmem((3, 8, 128), F32), vmem((chips, 8, 128), F32)]
        + [dma((count,))]
        + [dma((number, chips)) for _ in range(6)]
        + [dma((chips + 1,)) for _ in range(2)]
        + [dma((2, 3)) for _ in range(2)]
    )
    return pl.pallas_call(
        functools.partial(
            sum_kernel, chips, streams, (count, 3, count, 3, count, count, number, number, 2, 11)
        ),
        out_shape=[jax.ShapeDtypeStruct((rows, a.shape[1]), F32) for a in arrays]
        + [jax.ShapeDtypeStruct((8, 128), F32)]
        + [jax.ShapeDtypeStruct(up_sum.shape, BF16)] * 2,
        in_specs=[pl.BlockSpec(memory_space=pl.ANY)] * count
        + [pl.BlockSpec(memory_space=pltpu.VMEM)]
        + [pl.BlockSpec(memory_space=pl.ANY)] * 2,
        out_specs=[pl.BlockSpec(memory_space=pltpu.VMEM)] * (count + 1) + [pl.BlockSpec(memory_space=pl.ANY)] * 2,
        scratch_shapes=scratch,
        compiler_params=pltpu.CompilerParams(
            collective_id=1, has_side_effects=True, vmem_limit_bytes=58 << 20
        ),
        cost_estimate=pl.CostEstimate(
            flops=0, bytes_accessed=sum(2 * a.size for a in arrays), transcendentals=0
        ),
        name="sum_all",
    )(*[a.reshape(chips, 2, 2, rows, a.shape[1]) for a in arrays], tile, up_sum, down_sum)


LITTLE = pl.CostEstimate(flops=0, bytes_accessed=1024, transcendentals=0)
VMEM_LIMIT = 56 << 20


def whole(shape):
    return pl.BlockSpec(shape, lambda *_: (0,) * len(shape))


def piece(kernel, name, grid, in_specs, out_specs, out_shapes, scratch=()):
    return pl.pallas_call(
        kernel,
        grid=grid,
        in_specs=in_specs,
        out_specs=out_specs,
        out_shape=[jax.ShapeDtypeStruct(shape, dtype) for shape, dtype in out_shapes],
        scratch_shapes=list(scratch),
        compiler_params=pltpu.CompilerParams(vmem_limit_bytes=VMEM_LIMIT),
        cost_estimate=LITTLE,
        name=name,
    )


def inverse_rms(values):
    return lax.rsqrt(jnp.mean(values * values, axis=-1, keepdims=True) + EPSILON)


def norm_back(values, gain, grad):
    scale = inverse_rms(values)
    scaled = grad * gain
    mean = jnp.mean(values * scaled, axis=-1, keepdims=True)
    back = scale * scaled - values * (scale * scale * scale * mean)
    return back, jnp.sum(grad * (values * scale), axis=0, keepdims=True)


def qkv_kernel(tokens, gains, head_gain, cosine, sine, weight, low, raw, new):
    at = pl.program_id(0)

    @pl.when(at == 0)
    def _():
        states = tokens[...].astype(F32)
        low[...] = (states * inverse_rms(states) * gains[0:1]).astype(BF16)

    out = full_dot(low[...], weight[...])
    raw[...] = out
    plain = out * inverse_rms(out)
    values = plain * jnp.where(at < HEADS, head_gain[0:1], head_gain[1:2])
    half = HEAD // 2
    first, second = values[:, :half], values[:, half:]
    turned = jnp.concatenate(
        [first * cosine[...] - second * sine[...], second * cosine[...] + first * sine[...]], 1
    )
    new[...] = jnp.where(at < HEADS + KV_HEADS, turned, plain).astype(BF16)


def make_qkv(tokens, gains, head_gain, cosine, sine, full):
    rows = tokens.shape[0]
    heads = HEADS + 2 * KV_HEADS
    return piece(
        qkv_kernel,
        "make_qkv",
        (heads,),
        [
            whole((rows, D)),
            whole(gains.shape),
            whole((2, HEAD)),
            whole(cosine.shape),
            whole(sine.shape),
            pl.BlockSpec((D, HEAD), lambda i: (0, HEADS + i)),
        ],
        [
            whole((rows, D)),
            pl.BlockSpec((rows, HEAD), lambda i: (0, i)),
            pl.BlockSpec((rows, HEAD), lambda i: (0, i)),
        ],
        [((rows, D), BF16), ((rows, heads * HEAD), F32), ((rows, heads * HEAD), BF16)],
    )(tokens, gains, head_gain, cosine, sine, full)


def softmax_of(query, key, visible):
    scores = jnp.where(visible > 0.0, right_dot(query, key), -1e30)
    expo = jnp.exp(scores - jnp.max(scores, axis=-1, keepdims=True))
    return expo / jnp.sum(expo, axis=-1, keepdims=True)


def attend_kernel(
    tokens, gains, low, query, key, value, visible, w_out, lleft, lright,
    context, attn_raw, mixed, ffn_in, mid,
):
    at = pl.program_id(0)
    probs = softmax_of(query[...], key[...], visible[...]).astype(BF16)
    here = full_dot(probs, value[...]).astype(BF16)
    context[...] = here
    term = full_dot(here, w_out[...])

    @pl.when(at == 0)
    def _():
        attn_raw[...] = term

    @pl.when(at > 0)
    def _():
        attn_raw[...] += term

    @pl.when(at == HEADS - 1)
    def _():
        states = tokens[...].astype(F32)
        raw = attn_raw[...]
        total = states + raw * inverse_rms(raw) * gains[1:2]
        total = total + states * inverse_rms(states) * gains[0:1]
        mid[...] = full_dot(low[...], lleft[...]).astype(BF16)
        laurel = right_dot(mid[...], lright[...])
        total = (total + laurel * inverse_rms(laurel) * gains[2:3]) * INV_SQRT2
        mixed[...] = total
        ffn_in[...] = (total * inverse_rms(total) * gains[3:4]).astype(BF16)


def attend(tokens, gains, low, qkv, keys_all, visible, full):
    rows = tokens.shape[0]
    seen = keys_all.shape[0]
    group = HEADS // KV_HEADS
    side = 128
    left_at, right_at = full.shape[1] // side - 2, full.shape[1] // side - 1
    return piece(
        attend_kernel,
        "attend",
        (HEADS,),
        [
            whole((rows, D)),
            whole(gains.shape),
            whole((rows, D)),
            pl.BlockSpec((rows, HEAD), lambda i: (0, i)),
            pl.BlockSpec((seen, HEAD), lambda i: (0, i // group)),
            pl.BlockSpec((seen, HEAD), lambda i: (0, KV_HEADS + i // group)),
            whole((rows, seen)),
            pl.BlockSpec((HEAD, D), lambda i: (i, 0)),
            pl.BlockSpec((D, side), lambda i: (0, left_at)),
            pl.BlockSpec((D, side), lambda i: (0, right_at)),
        ],
        [
            pl.BlockSpec((rows, HEAD), lambda i: (0, i)),
            whole((rows, D)),
            whole((rows, D)),
            whole((rows, D)),
            whole((rows, side)),
        ],
        [
            ((rows, HEADS * HEAD), BF16),
            ((rows, D), F32),
            ((rows, D), F32),
            ((rows, D), BF16),
            ((rows, side), BF16),
        ],
    )(tokens, gains, low, qkv, keys_all, keys_all, visible, full, full, full)


def load_weights(weights, held, sems):
    copies, at = [], 0
    for number, ref in enumerate(weights):
        count = ref.shape[1]
        copies.append(pltpu.make_async_copy(ref, held.at[:, pl.ds(at, count)], sems.at[number]))
        at += count

    @pl.when(pl.program_id(0) == 0)
    def _():
        for copy in copies:
            copy.start()
        for copy in copies:
            copy.wait()


ROW_BLOCK = 256
UNIT_BLOCK = 512


def unit_blocks(steps, units):
    many = max(1, UNIT_BLOCK // units)
    return [range(first, min(first + many, steps)) for first in range(0, steps, many)]


def ffn_forward_kernel(steps, add, last, *refs):
    weights, refs = refs[: 2 * steps], refs[2 * steps :]
    if add:
        before, refs = refs[0], refs[1:]
    rows, total, refs = refs[0], refs[1], refs[2:]
    if last:
        low_total, refs = refs[0], refs[1:]
    gates, uppers, hiddens, (held, sems) = refs_of((steps, steps, steps, 2), refs)
    load_weights(weights, held, sems)
    units = held.shape[1] // steps
    here = rows[...]
    running = before[...] if add else None
    for block in unit_blocks(steps, units):
        cut = slice(block[0] * units, (block[-1] + 1) * units)
        gate_in = right_dot(here, held[0, cut])
        upper_in = right_dot(here, held[1, cut])
        low = gated_product(gate_in, upper_in).astype(BF16)
        for i, step in enumerate(block):
            own = slice(i * units, (i + 1) * units)
            gates[step][...] = gate_in[:, own]
            uppers[step][...] = upper_in[:, own]
            hiddens[step][...] = low[:, own]
        term = full_dot(low, held[2, cut])
        running = term if running is None else running + term
    write_sum(running, total, low_total if last else None)


def write_sum(running, total, low_total):
    if low_total is None:
        total[...] = running
        return
    half = pl.num_programs(0) // 2

    @pl.when(pl.program_id(0) < half)
    def _():
        low_total[...] = running.astype(BF16)

    @pl.when(pl.program_id(0) >= half)
    def _():
        total[...] = running


def sum_specs(many, last):
    blocks = many // ROW_BLOCK
    half = blocks // 2
    if not last:
        return (lambda i: i), [pl.BlockSpec((ROW_BLOCK, D), lambda i: (i, 0))], [((many, D), F32)]
    specs = [
        pl.BlockSpec((ROW_BLOCK, D), lambda i: (jnp.maximum(i - half, 0), 0)),
        pl.BlockSpec((ROW_BLOCK, D), lambda i: (jnp.minimum(i, half - 1), 0)),
    ]
    return (lambda i: lax.rem(i + half, blocks)), specs, [((many // 2, D), F32), ((many // 2, D), BF16)]


def ffn_forward(rows, before, weights, last):
    many = rows.shape[0]
    steps, units = len(weights) // 2, 2 * weights[0].shape[1]
    at, sums, sum_shapes = sum_specs(many, last)
    by_row = lambda width: pl.BlockSpec((ROW_BLOCK, width), lambda i: (at(i), 0))
    add = before is not None
    outs = piece(
        functools.partial(ffn_forward_kernel, steps, add, last),
        "ffn_forward",
        (many // ROW_BLOCK,),
        [pl.BlockSpec(memory_space=pl.ANY)] * len(weights) + [by_row(D)] * (1 + add),
        sums + [by_row(units)] * (3 * steps),
        sum_shapes + [((many, units), F32)] * (2 * steps) + [((many, units), BF16)] * steps,
        [pltpu.VMEM((3, steps * units, D), BF16), pltpu.SemaphoreType.DMA((len(weights),))],
    )(*weights, *([before] if add else []), rows)
    return refs_of((len(sums), steps, steps, steps), outs)


def ffn_backward_kernel(steps, add, last, *refs):
    weights, refs = refs[: 2 * steps], refs[2 * steps :]
    if add:
        before, refs = refs[0], refs[1:]
    (rows,), gates, uppers, totals, grad_gates, grad_uppers, (held, sems) = refs_of(
        (1, steps, steps, 1 + last, steps, steps, 2), refs
    )
    load_weights(weights, held, sems)
    units = held.shape[1] // steps
    here = rows[...]
    running = before[...] if add else None
    for block in unit_blocks(steps, units):
        cut = slice(block[0] * units, (block[-1] + 1) * units)
        grad_hidden = right_dot(here, held[2, cut])
        low_gates, low_uppers = [], []
        for i, step in enumerate(block):
            unused, act_back = jax.vjp(gated_product, gates[step][...], uppers[step][...])
            back_gate, back_upper = act_back(grad_hidden[:, i * units : (i + 1) * units])
            low_gates.append(back_gate.astype(BF16))
            low_uppers.append(back_upper.astype(BF16))
            grad_gates[step][...] = low_gates[-1]
            grad_uppers[step][...] = low_uppers[-1]
        term = full_dot(jnp.concatenate(low_gates, 1), held[0, cut])
        term = term + full_dot(jnp.concatenate(low_uppers, 1), held[1, cut])
        running = term if running is None else running + term
    write_sum(running, totals[0], totals[1] if last else None)


def ffn_backward(rows, before, weights, gates, uppers, last):
    many = rows.shape[0]
    steps, units = len(gates), gates[0].shape[1]
    at, sums, sum_shapes = sum_specs(many, last)
    by_row = lambda width: pl.BlockSpec((ROW_BLOCK, width), lambda i: (at(i), 0))
    add = before is not None
    outs = piece(
        functools.partial(ffn_backward_kernel, steps, add, last),
        "ffn_backward",
        (many // ROW_BLOCK,),
        [pl.BlockSpec(memory_space=pl.ANY)] * len(weights)
        + [by_row(D)] * (1 + add)
        + [by_row(units)] * (2 * steps),
        sums + [by_row(units)] * (2 * steps),
        sum_shapes + [((many, units), BF16)] * (2 * steps),
        [pltpu.VMEM((3, steps * units, D), BF16), pltpu.SemaphoreType.DMA((len(weights),))],
    )(*weights, *([before] if add else []), rows, *gates, *uppers)
    return refs_of((len(sums), steps, steps), outs)


def unit_grads_kernel(grad_gate, grad_upper, hidden, rows, down_rows, up_out, down_out):
    half = up_out.shape[1]
    pairs = ((grad_gate, rows), (grad_upper, rows), (hidden, down_rows))
    for kind, (left, right) in enumerate(pairs):
        out = left_dot(left[...], right[...]).astype(BF16)
        up_out[kind] = out[:half]
        down_out[kind] = out[half:]


def unit_grads_of(grad_gate, grad_upper, hidden, rows, down_rows):
    many, units = hidden.shape
    width = 1024
    narrow = whole((many, units))
    wide = pl.BlockSpec((many, width), lambda i: (0, i))
    part = pl.BlockSpec((3, units // 2, width), lambda i: (0, 0, i))
    return piece(
        unit_grads_kernel,
        "unit_grads",
        (D // width,),
        [narrow, narrow, narrow, wide, wide],
        [part, part],
        [((3, units // 2, D), BF16)] * 2,
    )(grad_gate, grad_upper, hidden, rows, down_rows)


def attend_back_kernel(
    gains, grad_in, grad_after, mixed, attn_raw, mid, low, lleft, lright, w_out, context, query, key, value, visible,
    grad_mixed, grad_mid, grad_gains, grad_left, grad_right, grad_w_out, grad_query, grad_key, grad_value,
    grad_attn,
):
    at = pl.program_id(0)

    @pl.when(at == 0)
    def _():
        back, gain_3 = norm_back(mixed[...], gains[3:4], grad_in[...])
        total = (grad_after[...] + back) * INV_SQRT2
        grad_mixed[...] = total
        back, gain_2 = norm_back(right_dot(mid[...], lright[...]), gains[2:3], total)
        back_low = back.astype(BF16)
        grad_right[...] = left_dot(back_low, mid[...])
        mid_low = full_dot(back_low, lright[...]).astype(BF16)
        grad_mid[...] = mid_low
        grad_left[...] = left_dot(low[...], mid_low)
        back, gain_1 = norm_back(attn_raw[...], gains[1:2], total)
        grad_attn[...] = back.astype(BF16)
        grad_gains[...] = jnp.concatenate(
            [gain_1, gain_2, gain_3, jnp.zeros((5, D), F32)], 0
        )

    grad_context = right_dot(grad_attn[...], w_out[...]).astype(BF16)
    grad_w_out[...] = left_dot(context[...], grad_attn[...]).astype(BF16)
    probs = softmax_of(query[...], key[...], visible[...])
    grad_probs = right_dot(grad_context, value[...])
    inner = jnp.sum(probs * grad_probs, axis=-1, keepdims=True)
    grad_scores = (probs * (grad_probs - inner)).astype(BF16)
    grad_query[...] = full_dot(grad_scores, key[...])
    key_term = left_dot(grad_scores, query[...])
    value_term = left_dot(probs.astype(BF16), grad_context)
    group = HEADS // KV_HEADS

    @pl.when(lax.rem(at, group) == 0)
    def _():
        grad_key[...] = key_term
        grad_value[...] = value_term

    @pl.when(lax.rem(at, group) > 0)
    def _():
        grad_key[...] += key_term
        grad_value[...] += value_term


def attend_back(gains, grad_in, grad_after, mixed, attn_raw, mid, low, full, context, qkv, keys_all, visible):
    rows = low.shape[0]
    seen = keys_all.shape[0]
    group = HEADS // KV_HEADS
    side = 128
    left_at, right_at = full.shape[1] // side - 2, full.shape[1] // side - 1
    head = pl.BlockSpec((rows, HEAD), lambda i: (0, i))
    once = lambda shape: pl.BlockSpec(shape, lambda i: (0, 0), pipeline_mode=pl.Buffered(1))
    return piece(
        attend_back_kernel,
        "attend_back",
        (HEADS,),
        [
            whole(gains.shape),
            once((rows, D)),
            once((rows, D)),
            once((rows, D)),
            once((rows, D)),
            whole((rows, side)),
            whole((rows, D)),
            pl.BlockSpec((D, side), lambda i: (0, left_at)),
            pl.BlockSpec((D, side), lambda i: (0, right_at)),
            pl.BlockSpec((HEAD, D), lambda i: (i, 0)),
            head,
            head,
            pl.BlockSpec((seen, HEAD), lambda i: (0, i // group)),
            pl.BlockSpec((seen, HEAD), lambda i: (0, KV_HEADS + i // group)),
            whole((rows, seen)),
        ],
        [
            whole((rows, D)),
            whole((rows, side)),
            whole((8, D)),
            whole((D, side)),
            whole((D, side)),
            pl.BlockSpec((HEAD, D), lambda i: (i, 0)),
            head,
            pl.BlockSpec((seen, HEAD), lambda i: (0, i // group)),
            pl.BlockSpec((seen, HEAD), lambda i: (0, i // group)),
        ],
        [
            ((rows, D), F32),
            ((rows, side), BF16),
            ((8, D), F32),
            ((D, side), F32),
            ((D, side), F32),
            ((HEADS * HEAD, D), BF16),
            ((rows, HEADS * HEAD), F32),
            ((seen, KV_HEADS * HEAD), F32),
            ((seen, KV_HEADS * HEAD), F32),
        ],
        [pltpu.VMEM((rows, D), BF16)],
    )(
        gains, grad_in, grad_after, mixed, attn_raw, mid, low, full, full, full, context, qkv, keys_all, keys_all,
        visible,
    )


def turn_back(grad, cosine, sine):
    half = HEAD // 2
    first, second = grad[:, :half], grad[:, half:]
    return jnp.concatenate([first * cosine + second * sine, second * cosine - first * sine], 1)


def query_back_kernel(grad_query, raw, cosine, sine, head_gain, low, weight, grad_w, grad_low, grad_head):
    at = pl.program_id(0)
    turned = turn_back(grad_query[...], cosine[...], sine[...])
    back, gain = norm_back(raw[...], head_gain[0:1], turned)
    back_low = back.astype(BF16)
    grad_w[...] = left_dot(low[...], back_low).astype(BF16)
    term = right_dot(back_low, weight[...])

    @pl.when(at == 0)
    def _():
        grad_low[...] = term
        grad_head[...] = gain

    @pl.when(at > 0)
    def _():
        grad_low[...] += term
        grad_head[...] += gain


def query_back(grad_query, raw, cosine, sine, head_gain, low, full):
    rows = low.shape[0]
    head = pl.BlockSpec((rows, HEAD), lambda i: (0, i))
    return piece(
        query_back_kernel,
        "query_back",
        (HEADS,),
        [
            head,
            head,
            whole(cosine.shape),
            whole(sine.shape),
            whole((2, HEAD)),
            whole((rows, D)),
            pl.BlockSpec((D, HEAD), lambda i: (0, HEADS + i)),
        ],
        [pl.BlockSpec((D, HEAD), lambda i: (0, i)), whole((rows, D)), whole((1, HEAD))],
        [((D, HEADS * HEAD), BF16), ((rows, D), F32), ((1, HEAD), F32)],
    )(grad_query, raw, cosine, sine, head_gain, low, full)


def key_back_kernel(
    grad_kv, raw, cosine, sine, head_gain, low, weight, before, grad_mixed, grad_mid, lleft, tokens, gains,
    grad_w, grad_tokens, grad_head, grad_gain, total,
):
    at = pl.program_id(0)
    is_key = at < KV_HEADS
    grad = grad_kv[...]
    turned = jnp.where(is_key, turn_back(grad, cosine[...], sine[...]), grad)
    back, gain = norm_back(raw[...], jnp.where(is_key, head_gain[1:2], 1.0), turned)
    back_low = back.astype(BF16)
    grad_w[...] = left_dot(low[...], back_low).astype(BF16)
    term = right_dot(back_low, weight[...])

    @pl.when(at == 0)
    def _():
        total[...] = before[...] + term
        grad_head[...] = gain

    @pl.when(at > 0)
    def _():
        total[...] += term
        grad_head[...] += jnp.where(is_key, gain, 0.0)

    @pl.when(at == 2 * KV_HEADS - 1)
    def _():
        grad_normed = total[...] + grad_mixed[...] + right_dot(grad_mid[...], lleft[...])
        back, gain_0 = norm_back(tokens[...].astype(F32), gains[0:1], grad_normed)
        grad_tokens[...] = grad_mixed[...] + back
        grad_gain[...] = gain_0


def key_back(grad_kv, raw, cosine, sine, head_gain, low, full, before, grad_mixed, grad_mid, tokens, gains):
    rows = low.shape[0]
    side = 128
    left_at = full.shape[1] // side - 2
    return piece(
        key_back_kernel,
        "key_back",
        (2 * KV_HEADS,),
        [
            pl.BlockSpec((rows, HEAD), lambda i: (0, i)),
            pl.BlockSpec((rows, HEAD), lambda i: (0, HEADS + i)),
            whole(cosine.shape),
            whole(sine.shape),
            whole((2, HEAD)),
            whole((rows, D)),
            pl.BlockSpec((D, HEAD), lambda i: (0, 2 * HEADS + i)),
            whole((rows, D)),
            whole((rows, D)),
            whole((rows, side)),
            pl.BlockSpec((D, side), lambda i: (0, left_at)),
            whole((rows, D)),
            whole(gains.shape),
        ],
        [
            pl.BlockSpec((D, HEAD), lambda i: (0, i)),
            whole((rows, D)),
            whole((1, HEAD)),
            whole((1, D)),
        ],
        [
            ((D, 2 * KV_HEADS * HEAD), BF16),
            ((rows, D), F32),
            ((1, HEAD), F32),
            ((1, D), F32),
        ],
        [pltpu.VMEM((rows, D), F32)],
    )(grad_kv, raw, cosine, sine, head_gain, low, full, before, grad_mixed, grad_mid, full, tokens, gains)


def tie(*values):
    return lax.optimization_barrier(values)


def shares(total, count):
    return [total // count + (1 if i < total % count else 0) for i in range(count)]


def greet(peers):
    barrier = pltpu.get_barrier_semaphore()
    for peer in peers:
        pl.semaphore_signal(barrier, inc=1, device_id=peer, device_id_type=MESH)
    pl.semaphore_wait(barrier, len(peers))


def partners():
    return {"core": 1 - lax.axis_index("core")}, {"fsdp": 1 - lax.axis_index("fsdp")}


CUTS = 8
FLYING = 2


def spread_kernel(own, rows, x_send, x_recv, near_send, near_recv, far_send, far_recv, own_sem):
    count = own.shape[0]
    cut = count // CUTS
    other_core, other_side = partners()
    greet((other_core, other_side))

    def copy(src, block, at, send, recv, peer):
        return pltpu.make_async_remote_copy(
            src_ref=src,
            dst_ref=rows.at[pl.ds(block * count + at * cut, cut)],
            send_sem=send.at[at],
            recv_sem=recv.at[at],
            device_id=peer,
            device_id_type=MESH,
        )

    mine = [own.at[pl.ds(at * cut, cut)] for at in range(CUTS)]
    came = [rows.at[pl.ds(count + at * cut, cut)] for at in range(CUTS)]
    across = [copy(mine[at], 1, at, x_send, x_recv, other_side) for at in range(CUTS)]
    near = [copy(mine[at], 2, at, near_send, near_recv, other_core) for at in range(CUTS)]
    far = [copy(came[at], 3, at, far_send, far_recv, other_core) for at in range(CUTS)]
    for one in across[:FLYING] + near:
        one.start()
    keep = pltpu.make_async_copy(own, rows.at[pl.ds(0, count)], own_sem)
    keep.start()
    for at in range(CUTS):
        across[at].wait_send()
        if at + FLYING < CUTS:
            across[at + FLYING].start()
        across[at].wait_recv()
        far[at].start()
    for one in near + far:
        one.wait()
    keep.wait()


def rows_of_four(own, number):
    count = own.shape[0]
    dma = pltpu.SemaphoreType.DMA
    return pl.pallas_call(
        spread_kernel,
        out_shape=jax.ShapeDtypeStruct((4 * count, D), BF16),
        in_specs=[pl.BlockSpec(memory_space=pltpu.VMEM)],
        out_specs=pl.BlockSpec(memory_space=pl.ANY),
        scratch_shapes=[dma((CUTS,)) for _ in range(6)] + [dma],
        compiler_params=pltpu.CompilerParams(collective_id=number, has_side_effects=True),
        cost_estimate=LITTLE,
        name="spread_rows",
    )(own)


def gather_sum_kernel(steps, *refs):
    if steps:
        (own, low, rows, down_rows), sides, (out,), grads, more, held, sems = refs_of(
            (4, 3 * steps, 1, 2 * steps, 4 + 4, 3, 3), refs
        )
        core_in, pair_low, x_in, parts, *copy_sems = more
        core_send, core_recv, x_send, x_recv = copy_sems
        rows_in, down_in, more_out = held
        loads_sem, parts_sem, grads_sem = sems
        parts_out = more_out

        def store(step, way):
            return pltpu.make_async_copy(parts_out.at[step, way], grads[2 * step + way], grads_sem.at[step, way])

        loads = [
            pltpu.make_async_copy(rows, rows_in, loads_sem.at[0]),
            pltpu.make_async_copy(down_rows, down_in, loads_sem.at[1]),
        ]
        part_loads = [
            pltpu.make_async_copy(side, parts.at[number], parts_sem.at[number]) for number, side in enumerate(sides)
        ]
        for load in loads + part_loads:
            load.start()
    else:
        own, low, out, core_in, pair_low, x_in, core_send, core_recv, x_send, x_recv = refs
    count = out.shape[0]
    cut = count // CUTS
    other_core, other_side = partners()
    greet((other_core, other_side))

    def core_copy(block, at):
        here = pl.ds(block * count + at * cut, cut)
        number = block * CUTS + at
        return pltpu.make_async_remote_copy(
            src_ref=low.at[here],
            dst_ref=core_in.at[here],
            send_sem=core_send.at[number],
            recv_sem=core_recv.at[number],
            device_id=other_core,
            device_id_type=MESH,
        )

    def x_copy(at):
        here = pl.ds(at * cut, cut)
        return pltpu.make_async_remote_copy(
            src_ref=pair_low.at[here],
            dst_ref=x_in.at[here],
            send_sem=x_send.at[at],
            recv_sem=x_recv.at[at],
            device_id=other_side,
            device_id_type=MESH,
        )

    pieces = [(block, at) for block in (1, 0) for at in range(CUTS)]

    def next_piece(number):
        core_copy(*pieces[number]).wait_send()
        if number + FLYING < len(pieces):
            core_copy(*pieces[number + FLYING]).start()

    for one in pieces[:FLYING]:
        core_copy(*one).start()
    for at in range(CUTS):
        there = pl.ds(count + at * cut, cut)
        next_piece(at)
        core_copy(1, at).wait_recv()
        pair_low[pl.ds(at * cut, cut)] = (own[there] + core_in[there].astype(F32)).astype(BF16)
        x_copy(at).start()
    for at in range(CUTS):
        here = pl.ds(at * cut, cut)
        next_piece(CUTS + at)
        core_copy(0, at).wait_recv()
        out[here] = own[here] + core_in[here].astype(F32)
    if steps:
        for load in loads:
            load.wait()
        half = grads[0].shape[1]
        width = D // 2
        for step in range(steps):
            for kind in range(3):
                number = 3 * step + kind
                part_loads[number].wait()
                left, right = parts[number], down_in if kind == 2 else rows_in
                for first in range(0, D, width):
                    cols = slice(first, first + width)
                    term = left_dot(left, right[:, cols]).astype(BF16)
                    parts_out[step, 0, kind, :, cols] = term[:half]
                    parts_out[step, 1, kind, :, cols] = term[half:]
            for way in range(2):
                store(step, way).start()
    for at in range(CUTS):
        here = pl.ds(at * cut, cut)
        x_copy(at).wait_recv()
        out[here] += x_in[here].astype(F32)
    for at in range(CUTS):
        x_copy(at).wait_send()
    for step in range(steps):
        for way in range(2):
            store(step, way).wait()


def sum_of_four(own, low, number, units=(), rows=None, down_rows=None):
    count = own.shape[0] // 2
    steps = len(units)
    dma = pltpu.SemaphoreType.DMA
    vmem, anywhere = pltpu.VMEM, pl.BlockSpec(memory_space=pl.ANY)
    scratch = [vmem((2 * count, D), BF16), vmem((count, D), BF16), vmem((count, D), BF16)]
    copy_sems = [dma((2 * CUTS,)), dma((2 * CUTS,)), dma((CUTS,)), dma((CUTS,))]
    operands, shapes = [], []
    if steps:
        many, width = units[0][0].shape
        operands = [rows, down_rows] + [side for sides in units for side in sides]
        shapes = [jax.ShapeDtypeStruct((3, width // 2, D), BF16)] * (2 * steps)
        scratch += [vmem((3 * steps, many, width), BF16)]
        copy_sems += [vmem((many, D), BF16), vmem((many, D), BF16), vmem((steps, 2, 3, width // 2, D), BF16)]
        copy_sems += [dma((2,)), dma((3 * steps,)), dma((steps, 2))]
    total, *grads = pl.pallas_call(
        functools.partial(gather_sum_kernel, steps),
        out_shape=[jax.ShapeDtypeStruct((count, D), F32)] + shapes,
        in_specs=[pl.BlockSpec(memory_space=pltpu.VMEM), anywhere] + [anywhere] * len(operands),
        out_specs=[pl.BlockSpec(memory_space=pltpu.VMEM)] + [anywhere] * len(shapes),
        scratch_shapes=scratch + copy_sems,
        compiler_params=pltpu.CompilerParams(
            collective_id=number, has_side_effects=True, vmem_limit_bytes=VMEM_LIMIT
        ),
        cost_estimate=LITTLE,
        name="gather_sum",
    )(own, low, *operands)
    return total, [(grads[2 * i], grads[2 * i + 1]) for i in range(steps)]


def body(
    tokens,
    per_layer,
    teacher,
    cont_lengths,
    w_query,
    w_kv,
    w_out,
    laurel_left,
    laurel_right,
    pl_gate,
    pl_proj,
    norm_gains,
    head_gains,
    ffn_weight,
):
    layer_in = per_layer[0].astype(F32)
    target = teacher[0].astype(F32)
    row_count = tokens.shape[1]
    chips = lax.axis_size("zy")
    seq_count = 2 * chips
    group_count = lax.axis_size("fsdp")
    shards = seq_count * group_count
    chip = lax.axis_index("zy")
    core = lax.axis_index("core")
    seq_index = chip * 2 + core
    group_index = lax.axis_index("fsdp")
    half_point = seq_count // 2
    prompt_len = half_point * row_count
    cont_shards = CONT_LEN // row_count
    cont_count = prompt_len // CONT_LEN
    is_cont = seq_index >= half_point
    rel_index = seq_index - half_point
    local_shard = jnp.where(is_cont, rel_index % cont_shards, 0)
    cont_index = jnp.where(is_cont, rel_index // cont_shards, 0)
    first_place = jnp.where(is_cont, prompt_len + local_shard * row_count, seq_index * row_count)
    row_range = jnp.arange(row_count, dtype=jnp.int32)
    places = first_place + row_range
    group_lengths = jnp.sum(
        jnp.where(
            jnp.arange(group_count, dtype=jnp.int32)[:, None] == group_index, cont_lengths, 0
        ),
        axis=0,
    )
    my_length = jnp.sum(
        jnp.where(jnp.arange(cont_count, dtype=jnp.int32) == cont_index, group_lengths, 0)
    )
    valid = jnp.logical_or(
        jnp.logical_not(is_cont), local_shard * row_count + row_range < my_length
    )
    weight_mask = valid.astype(F32)
    count = F32(group_count * prompt_len) + jnp.sum(cont_lengths).astype(F32)
    total_slots = float(row_count * seq_count * group_count)
    shard_rows = w_query.shape[0]
    key_cols = KV_HEADS * HEAD
    proj_cols = pl_proj.shape[0] * D // shard_rows
    misc_cols = RANK
    head_part = head_gains.reshape(-1, 1)
    misc = jnp.concatenate(
        [
            norm_gains.T,
            jnp.pad(head_part, ((0, shard_rows - head_part.shape[0]), (0, 0))),
            jnp.zeros((shard_rows, misc_cols - 7), BF16),
        ],
        1,
    )
    pack = jnp.concatenate(
        [
            w_out,
            w_query,
            w_kv,
            pl_gate,
            pl_proj.reshape(shard_rows, proj_cols),
            laurel_left,
            misc,
            laurel_right.T,
            jnp.zeros((shard_rows, 128 - RANK), BF16),
        ],
        1,
    )

    units = ffn_weight.shape[0]
    half = units // 2
    by_kind = ffn_weight.transpose(1, 0, 2)
    ups, downs = [by_kind[:, :half]], [by_kind[:, half:]]
    stage_steps = shares(chips - 1, 7)

    def pass_on(stage):
        for _ in range(stage_steps[stage]):
            ups.append(ring(ups[-1], 1))
            downs.append(ring(downs[-1], -1))

    def stage_end(values):
        (ups[-1], downs[-1]), values = tie((ups[-1], downs[-1]), values)
        return values

    pass_on(0)
    full = gather_all(pack, chips)
    at = 2 * D + 2 * key_cols
    plg = full[:, at : at + PLD]
    plp = full[:, at + PLD : at + PLD + proj_cols].reshape(PLD, D)
    at += PLD + proj_cols + RANK
    misc_full = stage_end(full[:, at : at + misc_cols])
    pass_on(1)
    gains = jnp.pad(misc_full[:, :6].T.astype(F32), ((0, 2), (0, 0)))
    head_n = head_gains.shape[1]
    head_gain = (
        misc_full[:, 6]
        .reshape(shards, shard_rows)[:, : 2 * head_n]
        .reshape(shards, 2, head_n)
        .transpose(1, 0, 2)
        .reshape(2, HEAD)
        .astype(F32)
    )
    freqs = jnp.exp(
        jnp.arange(HEAD // 2, dtype=F32) * (-2.0 * math.log(ROPE_BASE) / HEAD)
    )
    angles = places.astype(F32)[:, None] * freqs
    cosine, sine = jnp.cos(angles), jnp.sin(angles)
    normed_low, qkv_raw, qkv = make_qkv(tokens[0], gains, head_gain, cosine, sine, full)
    qkv = stage_end(qkv)
    kv_own = qkv[:, D:]
    pass_on(2)

    mid = chips // 2
    chain = [(i, i + 1) for i in range(mid - 1)] + [(mid - 1, mid + 1)]
    kv_before = jnp.where(
        chip == mid,
        lax.ppermute(kv_own, "zy", [(mid - 1, mid)]),
        lax.ppermute(kv_own, "zy", chain),
    )
    spans = []
    span = 2
    while span < mid:
        spans.append(span)
        span *= 2
    for span in spans:
        moved = lax.ppermute(
            kv_before, "zy", [(mid + i, mid + i + span) for i in range(min(span, mid - span))]
        )
        fresh = jnp.logical_and(chip >= mid + span, chip < mid + 2 * span)
        kv_before = jnp.where(fresh, moved, kv_before)
    kv_other = swap(jnp.where(core == 0, kv_own, kv_before), "core")
    keys_all = jnp.concatenate([kv_before, kv_other, kv_own], 0)
    keys_all = stage_end(keys_all)
    pass_on(3)
    key_len = keys_all.shape[0]
    key_places = first_place - 2 * row_count + jnp.arange(key_len, dtype=jnp.int32)
    visible = (
        (key_places[None, :] <= places[:, None])
        & (places[:, None] - key_places[None, :] < WINDOW)
        & (key_places[None, :] >= 0)
    ).astype(F32)
    context_low, attn_raw, mixed, ffn_in, laurel_mid = attend(
        tokens[0], gains, normed_low, qkv, keys_all, visible, full
    )

    ffn_in = stage_end(ffn_in)
    pass_on(4)
    ffn_rows = stage_end(rows_of_four(ffn_in, 2))
    here = len(ups)
    pass_on(5)
    gates, uppers, hiddens = [], [], []

    def weights_of(steps):
        return [w for k in steps for w in (ups[k], downs[k])]

    def forward_part(running, first, end, last=False):
        sums, gate, upper, hidden = ffn_forward(ffn_rows, running, weights_of(range(first, end)), last)
        gates.extend(gate)
        uppers.extend(upper)
        hiddens.extend(hidden)
        return sums if last else sums[0]

    running = stage_end(forward_part(None, 0, here))
    then = len(ups)
    pass_on(6)
    running = stage_end(forward_part(running, here, then))
    own_sum, low_sum = forward_part(running, then, chips, True)
    down_out, unused = sum_of_four(own_sum, low_sum, 3)
    after_ffn = mixed + rms_norm(down_out, gains[4])
    after_low = after_ffn.astype(BF16)
    pl_raw = full_dot(after_low, plg)
    pl_act = gelu_tanh(pl_raw)
    pl_mid = (pl_act * layer_in).astype(BF16)
    pl_out = full_dot(pl_mid, plp)
    result = after_ffn + rms_norm(pl_out, gains[5])
    errors = result - target
    squares = jnp.sum(weight_mask[:, None] * errors * errors)

    grad_out = weight_mask[:, None] * errors * (total_slots / count)
    unused, pl_norm_back = jax.vjp(rms_norm, pl_out, gains[5])
    grad_pl_out, grad_g5 = pl_norm_back(grad_out)
    grad_pl_low = grad_pl_out.astype(BF16)
    grad_plp = left_dot(pl_mid, grad_pl_low)
    grad_pl_mid = right_dot(grad_pl_low, plp)
    grad_layer_in = grad_pl_mid * pl_act
    unused, gelu_back = jax.vjp(gelu_tanh, pl_raw)
    grad_pl_raw = gelu_back(grad_pl_mid * layer_in)[0].astype(BF16)
    grad_plg = left_dot(after_low, grad_pl_raw)
    grad_after = grad_out + right_dot(grad_pl_raw, plg)
    unused, down_norm_back = jax.vjp(rms_norm, down_out, gains[4])
    grad_down, grad_g4 = down_norm_back(grad_after)
    grad_down_low = grad_down.astype(BF16)

    grad_down_rows = rows_of_four(grad_down_low, 4)
    grad_gates, grad_uppers = [None] * chips, [None] * chips

    def backward_part(steps, running, last=False):
        sums, grad_gate, grad_upper = ffn_backward(
            grad_down_rows, running, weights_of(steps), [gates[k] for k in steps], [uppers[k] for k in steps], last
        )
        for k, gg, gu in zip(steps, grad_gate, grad_upper):
            grad_gates[k], grad_uppers[k] = gg, gu
        return sums if last else sums[0]

    ready = {}

    def unit_grads(k):
        if k in ready:
            return ready[k]
        return unit_grads_of(grad_gates[k], grad_uppers[k], hiddens[k], ffn_rows, grad_down_rows)

    order = list(range(1, chips)) + [0]
    ring_steps = shares(chips - 2, 6)
    done = 0

    def beside(stage, work):
        nonlocal done, up_sum, down_sum
        values = None
        for step in range(ring_steps[stage]):
            up_in = ring(up_sum, 1)
            down_in = ring(down_sum, -1)
            if step == 0:
                values = work()
            done += 1
            terms = unit_grads(order[done])
            (up_in, down_in), terms, values = tie((up_in, down_in), terms, values)
            up_sum = (up_in.astype(F32) + terms[0].astype(F32)).astype(BF16)
            down_sum = (down_in.astype(F32) + terms[1].astype(F32)).astype(BF16)
        return work() if values is None else values

    first = ring_steps[0]
    then = first + 1 + ring_steps[0] + ring_steps[1]
    running = backward_part(order[:first], None)
    up_sum, down_sum = unit_grads(order[0])
    running = beside(0, lambda: backward_part(order[first:then], running))
    own_sum, low_sum = beside(1, lambda: backward_part(order[then:], running, True))

    def work():
        steps = order[done + ring_steps[2] :] if units % 128 == 0 else []
        total, grads = sum_of_four(
            own_sum,
            low_sum,
            5,
            [(grad_gates[k], grad_uppers[k], hiddens[k]) for k in steps],
            ffn_rows,
            grad_down_rows,
        )
        ready.update(zip(steps, grads))
        return total

    grad_ffn_in = beside(2, work)
    (
        grad_scaled,
        grad_mid_low,
        grad_mid_gains,
        grad_lleft,
        grad_lright_t,
        grad_wo,
        grad_queries,
        grad_keys,
        grad_values,
    ) = beside(
        3,
        lambda: attend_back(
            gains, grad_ffn_in, grad_after, mixed, attn_raw, laurel_mid, normed_low, full, context_low, qkv, keys_all,
            visible,
        ),
    )

    def work():
        grad_kv = jnp.concatenate([grad_keys, grad_values], 1)
        grad_before = grad_kv[:row_count]
        grad_own = grad_kv[2 * row_count :]
        returned = swap(grad_kv[row_count : 2 * row_count].astype(BF16), "core").astype(F32)
        grad_own = grad_own + jnp.where(core == 0, returned, 0.0)
        grad_before = grad_before + jnp.where(core == 0, 0.0, returned)
        for span in reversed(spans):
            back = [(mid + i + span, mid + i) for i in range(min(span, mid - span))]
            grad_before = grad_before + lax.ppermute(grad_before.astype(BF16), "zy", back).astype(F32)
        before_low = grad_before.astype(BF16)
        grad_own = (
            grad_own
            + lax.ppermute(before_low, "zy", [(b, a) for a, b in chain]).astype(F32)
            + lax.ppermute(before_low, "zy", [(mid, mid - 1)]).astype(F32)
        )
        return grad_own, query_back(grad_queries, qkv_raw, cosine, sine, head_gain, normed_low, full)

    grad_own, (grad_wq, grad_normed, grad_hq) = beside(4, work)
    def work():
        grad_wkv, grad_tokens, grad_hk, grad_g0 = key_back(
            grad_own, qkv_raw, cosine, sine, head_gain, normed_low, full, grad_normed, grad_scaled, grad_mid_low,
            tokens[0], gains,
        )
        head_back = jnp.concatenate([grad_hq, grad_hk], 0).reshape(2, shards, head_n).transpose(1, 0, 2)
        head_back = head_back.reshape(shards, 2 * head_n)
        head_back = jnp.pad(head_back, ((0, 0), (0, shard_rows - 2 * head_n))).reshape(1, D)
        misc_back = jnp.concatenate(
            [grad_g0, grad_mid_gains[:3], grad_g4[None], grad_g5[None], head_back, jnp.zeros((1, D), F32)], 0
        )
        return grad_wkv, grad_tokens, jnp.concatenate(
            [
                grad_plg.astype(BF16),
                grad_plp.astype(BF16).reshape(D, proj_cols),
                grad_lleft[:, :RANK].astype(BF16),
                jnp.pad(misc_back.T, ((0, 0), (0, misc_cols - 8))).astype(BF16),
                grad_lright_t.astype(BF16),
            ],
            1,
        )

    last_terms, (grad_wkv, grad_tokens, rest_back) = beside(5, lambda: (unit_grads(0), work()))
    sums_wq, sums_wkv, sums_wo, sums_rest, total, up_in, down_in = sum_all(
        [grad_wq, grad_wkv, grad_wo, rest_back],
        (True, True, True, False),
        jnp.broadcast_to(squares, (8, 128)),
        up_sum,
        down_sum,
        chips,
    )
    grad_ffn = jnp.concatenate(
        [
            (arrived.astype(F32) + term.astype(F32)).transpose(1, 0, 2)
            for arrived, term in zip((up_in, down_in), last_terms)
        ],
        0,
    )
    at = 0
    rest = []
    for width in (PLD, proj_cols, RANK, misc_cols, RANK):
        rest.append(sums_rest[:, at : at + width])
        at += width

    match_loss = total[0, 0] / (2.0 * D * count)

    return (
        result[None],
        match_loss,
        grad_tokens[None],
        grad_layer_in[None],
        sums_wq,
        sums_wkv,
        sums_wo,
        rest[2],
        rest[4].T,
        rest[0],
        rest[1].reshape(pl_proj.shape),
        rest[3][:, :6].T,
        rest[3][: 2 * head_n, 6].reshape(2, head_n),
        grad_ffn,
    )


def solution(mesh):
    seq, fsdp = mesh.shape["seq"], mesh.shape["fsdp"]
    fine = Mesh(mesh.devices.reshape(seq // 2, 2, fsdp), ("zy", "core", "fsdp"))
    rows = P("fsdp", ("zy", "core"), None)
    split = ("zy", "core", "fsdp")
    weights = (
        P(split, None),
        P(split, None),
        P(split, None),
        P(split, None),
        P(None, split),
        P(split, None),
        P(split, None),
        P(None, split),
        P(None, split),
        P(split, None, None),
    )
    return jax.shard_map(
        body,
        mesh=fine,
        in_specs=(rows, rows, rows, P()) + weights,
        out_specs=(rows, P(), rows, rows) + weights,
        check_vma=False,
    )
```

```python
import functools
import math

import jax
import jax.numpy as jnp
from jax import lax
from jax.experimental import pallas as pl
from jax.experimental.pallas import tpu as pltpu
from jax.sharding import Mesh, PartitionSpec as P

D = 2048
HEADS = 8
KV_HEADS = 2
HEAD = 256
WINDOW = 512
CONT_LEN = 512
RANK = 64
PLD = 256

EPSILON = 1e-06
INV_SQRT2 = 0.7071067811865476
ROPE_BASE = 10000.0
BF16 = jnp.bfloat16
F32 = jnp.float32


def gelu_tanh(values):
    return jax.nn.gelu(values, approximate=True)


def gated_product(gate_in, up_in):
    return gelu_tanh(gate_in) * up_in


def full_dot(left, right):
    return jnp.dot(left, right, preferred_element_type=F32)


def left_dot(left, right):
    return lax.dot_general(left, right, (((0,), (0,)), ((), ())), preferred_element_type=F32)


def right_dot(left, right):
    return lax.dot_general(left, right, (((1,), (1,)), ((), ())), preferred_element_type=F32)


def ring_order(n):
    return list(range(0, n, 2)) + list(range(n - 1, 0, -2))


def ring_pairs(n, by):
    order = ring_order(n)
    return [(order[i], order[(i + by) % n]) for i in range(n)]


def ring(value, by):
    return lax.ppermute(value, "zy", ring_pairs(lax.axis_size("zy"), by))


def swap(value, axis):
    return lax.ppermute(value, axis, [(0, 1), (1, 0)])


MESH = pl.DeviceIdType.MESH


def ring_chip(spot, chips):
    spot = lax.rem(spot, chips)
    return jnp.where(spot < chips // 2, 2 * spot, 2 * (chips - 1 - spot) + 1)


def ring_spot(chip, chips):
    return jnp.where(lax.rem(chip, 2) == 0, chip // 2, chips - 1 - chip // 2)


def gather_kernel(chips, streams, shard, full, ring_send, ring_recv, x_send, x_recv, core_send, core_recv, own_sem):
    chip = lax.axis_index("zy")
    core = lax.axis_index("core")
    side = lax.axis_index("fsdp")
    spot = ring_spot(chip, chips)
    rows = shard.shape[0]

    def neighbour(by):
        return {"zy": ring_chip(spot + chips + by, chips)}

    other_core = {"core": 1 - core}
    other_side = {"fsdp": 1 - side}

    barrier = pltpu.get_barrier_semaphore()
    for peer in (neighbour(1), neighbour(-1), other_core, other_side):
        pl.semaphore_signal(barrier, inc=1, device_id=peer, device_id_type=MESH)
    pl.semaphore_wait(barrier, 4)

    def place(owner, its_core, its_side, stream):
        row = ((owner * 2 + its_core) * 2 + its_side) * rows
        return full.at[pl.ds(pl.multiple_of(row, rows), rows), pl.ds(stream[0], stream[1])]

    def owner_at(step, stream):
        return ring_chip(spot + chips - stream[2] * step, chips)

    def send(src, dst, sems, at, peer):
        return pltpu.make_async_remote_copy(
            src_ref=src,
            dst_ref=dst,
            send_sem=sems[0].at[at],
            recv_sem=sems[1].at[at],
            device_id=peer,
            device_id_type=MESH,
        )

    ring_sems, x_sems, core_sems = (ring_send, ring_recv), (x_send, x_recv), (core_send, core_recv)

    def ring_copy(number, away, step, src=None):
        stream = streams[number]
        its_side = 1 - side if away else side
        spot_ref = place(owner_at(step, stream), core, its_side, stream)
        return send(src if src is not None else spot_ref, spot_ref, ring_sems, (number, away, step), neighbour(stream[2]))

    def ring_arrival(number, away, step):
        stream = streams[number]
        its_side = 1 - side if away else side
        spot_ref = place(owner_at(step, stream), core, its_side, stream)
        return send(spot_ref, spot_ref, ring_sems, (number, away, step - 1), neighbour(stream[2]))

    def x_copy(number, step, its_side, src=None):
        stream = streams[number]
        spot_ref = place(owner_at(step, stream), core, its_side, stream)
        return send(src if src is not None else spot_ref, spot_ref, x_sems, (number, step), other_side)

    def core_copy(number, away, step, its_core, src=None):
        stream = streams[number]
        its_side = 1 - side if away else side
        spot_ref = place(owner_at(step, stream), its_core, its_side, stream)
        return send(src if src is not None else spot_ref, spot_ref, core_sems, (number, away, step), other_core)

    def cut(stream):
        return shard.at[:, pl.ds(stream[0], stream[1])]

    own_row = ((chip * 2 + core) * 2 + side) * rows
    own = pltpu.make_async_copy(
        shard, full.at[pl.ds(pl.multiple_of(own_row, rows), rows), :], own_sem
    )
    own.start()
    numbers = range(len(streams))
    for number in numbers:
        if streams[number][3]:
            x_copy(number, 0, side, cut(streams[number])).start()
    for number in numbers:
        ring_copy(number, 0, 0, cut(streams[number])).start()
    for number in numbers:
        if not streams[number][3]:
            x_copy(number, 0, side, cut(streams[number])).start()
    for number in numbers:
        core_copy(number, 0, 0, core, cut(streams[number])).start()
    for number in numbers:
        if streams[number][3]:
            x_copy(number, 0, 1 - side).wait_recv()
            ring_copy(number, 1, 0).start()
            core_copy(number, 1, 0, core).start()

    def turn(step, carry):
        for number in numbers:
            aways = (0, 1) if streams[number][3] else (0,)
            for away in aways:
                ring_arrival(number, away, step).wait_recv()

                @pl.when(step < chips - 1)
                def _(number=number, away=away):
                    ring_copy(number, away, step).start()

                core_copy(number, away, step, core).start()
            if not streams[number][3]:
                x_copy(number, step, side).start()
        for number in numbers:
            if not streams[number][3]:
                x_copy(number, step - 1, 1 - side).wait_recv()
                core_copy(number, 1, step - 1, core).start()
        return carry

    lax.fori_loop(1, chips, turn, 0)
    for number in numbers:
        if not streams[number][3]:
            x_copy(number, chips - 1, 1 - side).wait_recv()
            core_copy(number, 1, chips - 1, core).start()
    own.wait()

    def drain(step, carry):
        for number in numbers:
            first = streams[number][3]
            for away in (0, 1):
                core_copy(number, away, step, 1 - core).wait_recv()
                core_copy(number, away, step, core).wait_send()
                if first or not away:

                    @pl.when(step < chips - 1)
                    def _(number=number, away=away):
                        ring_copy(number, away, step).wait_send()

            if not first:
                x_copy(number, step, side).wait_send()
        return carry

    lax.fori_loop(0, chips, drain, 0)
    for number in numbers:
        if streams[number][3]:
            x_copy(number, 0, side).wait_send()


def gather_all(shard, chips):
    rows, cols = shard.shape
    tiles = cols // 128
    first = int(round(tiles * 0.43)) // 2 * 2
    rest = tiles - first
    bounds = [0, first // 2, first, first + rest // 2, tiles]
    streams = tuple(
        (128 * bounds[i], 128 * (bounds[i + 1] - bounds[i]), 1 if i % 2 == 0 else -1, i < 2)
        for i in range(4)
    )
    dma = pltpu.SemaphoreType.DMA
    return pl.pallas_call(
        functools.partial(gather_kernel, chips, streams),
        out_shape=jax.ShapeDtypeStruct((rows * 4 * chips, cols), shard.dtype),
        in_specs=[pl.BlockSpec(memory_space=pl.ANY)],
        out_specs=pl.BlockSpec(memory_space=pl.ANY),
        scratch_shapes=[
            dma((4, 2, chips)),
            dma((4, 2, chips)),
            dma((4, chips)),
            dma((4, chips)),
            dma((4, 2, chips)),
            dma((4, 2, chips)),
            dma,
        ],
        compiler_params=pltpu.CompilerParams(collective_id=0, has_side_effects=True),
        cost_estimate=pl.CostEstimate(
            flops=0, bytes_accessed=2 * rows * 4 * chips * cols * 2, transcendentals=0
        ),
        name="gather_all",
    )(shard)


def sum_kernel(chips, streams, counts, *refs):
    arrays, (tile, up_sum, down_sum), outs, (tile_out, up_in, down_in), held, core_in, ring_in, x_in, tiles, sems = refs_of(counts, refs)
    load_sem, core_send, core_recv, ring_send, ring_recv, x_send, x_recv, tile_send, tile_recv, hop_send, hop_recv = sems
    tile_pairs, tile_ring = tiles
    chip = lax.axis_index("zy")
    core = lax.axis_index("core")
    side = lax.axis_index("fsdp")
    spot = ring_spot(chip, chips)
    far = 1 - side

    def neighbour(by):
        return {"zy": ring_chip(spot + chips + by, chips)}

    other_core = {"core": 1 - core}
    other_side = {"fsdp": 1 - side}
    barrier = pltpu.get_barrier_semaphore()
    for peer in (neighbour(1), neighbour(-1), other_core, other_side):
        pl.semaphore_signal(barrier, inc=1, device_id=peer, device_id_type=MESH)
    pl.semaphore_wait(barrier, 4)

    numbers = range(len(streams))

    def owner_at(number, turn):
        return ring_chip(spot + 2 * chips - streams[number][3] * turn, chips)

    def cols(number):
        return pl.ds(streams[number][1], streams[number][2])

    def remote(src, dst, send, recv, peer):
        return pltpu.make_async_remote_copy(
            src_ref=src, dst_ref=dst, send_sem=send, recv_sem=recv, device_id=peer, device_id_type=MESH
        )

    def core_copy(number, turn):
        owner = owner_at(number, turn)
        array = streams[number][0]
        return remote(
            arrays[array].at[owner, 1 - core, :, :, cols(number)],
            core_in[array].at[owner, :, :, cols(number)],
            core_send.at[number, turn - 1],
            core_recv.at[number, turn - 1],
            other_core,
        )

    def x_copy(number, turn):
        array = streams[number][0]
        first = streams[number][4]
        slot = turn - 1 if first else 0
        return remote(
            held[array].at[owner_at(number, turn), far, :, cols(number)],
            x_in[number].at[slot],
            x_send.at[number, slot],
            x_recv.at[number, slot],
            other_side,
        )

    def ring_copy(number, turn):
        array = streams[number][0]
        owner = owner_at(number, turn)
        if streams[number][4]:
            src = held[array].at[owner, pl.ds(side, 1), :, cols(number)]
        else:
            src = held[array].at[owner, :, :, cols(number)]
        return remote(
            src,
            ring_in[number].at[turn - 1],
            ring_send.at[number, turn - 1],
            ring_recv.at[number, turn - 1],
            neighbour(streams[number][3]),
        )

    loads = [
        pltpu.make_async_copy(arrays[i].at[:, core], held[i], load_sem.at[i])
        for i in range(len(arrays))
    ]

    def send_cores(turn, carry):
        for number in numbers:
            core_copy(number, turn).start()
        return carry

    def hop_copy(way, kind):
        src, dst = ((up_sum, up_in), (down_sum, down_in))[way]
        return remote(src.at[kind], dst.at[kind], hop_send.at[way, kind], hop_recv.at[way, kind], neighbour(1 - 2 * way))

    def tile_copy(src, dst, number, peer):
        return remote(src, dst, tile_send.at[number], tile_recv.at[number], peer)

    def tile_turn(turn):
        spot_ref = tile_ring.at[ring_chip(spot + 2 * chips - turn + 1, chips)]
        return tile_copy(spot_ref, spot_ref, turn + 1, neighbour(1))

    def tile_arrival(turn):
        spot_ref = tile_ring.at[ring_chip(spot + 2 * chips - turn, chips)]
        return tile_copy(spot_ref, spot_ref, turn + 1, neighbour(1))

    tile_copy(tile, tile_pairs.at[0], 0, other_core).start()
    lax.fori_loop(1, 2, send_cores, 0)
    for load in loads:
        load.start()
    tile_copy(tile, tile_pairs.at[0], 0, other_core).wait()
    tile_pairs[1] = tile[...] + tile_pairs[0]
    tile_copy(tile_pairs.at[1], tile_pairs.at[2], 1, other_side).start()
    lax.fori_loop(2, chips + 1, send_cores, 0)
    for load in loads:
        load.wait()

    def add_cores(number, turn):
        array = streams[number][0]
        owner = owner_at(number, turn)
        core_copy(number, turn).wait_recv()
        for its_side in range(2):
            held[array][owner, its_side, :, cols(number)] = (
                held[array][owner, its_side, :, cols(number)].astype(F32)
                + core_in[array][owner, its_side, :, cols(number)].astype(F32)
            ).astype(BF16)

    def begin(turn):
        for number in numbers:
            if streams[number][4]:
                add_cores(number, turn)
                x_copy(number, turn).start()

    begin(1)
    tile_copy(tile_pairs.at[1], tile_pairs.at[2], 1, other_side).wait()
    tile_ring[chip] = tile_pairs[1] + tile_pairs[2]

    def round_trip(turn, carry):
        @pl.when(turn > 1)
        def _():
            tile_arrival(turn - 1).wait_recv()

        @pl.when(turn < chips)
        def _():
            tile_turn(turn).start()

        for kind in range(3):

            @pl.when(turn == 1 + kind)
            def _(kind=kind):
                for way in range(2):
                    hop_copy(way, kind).start()

        @pl.when(turn < chips)
        def _():
            begin(turn + 1)

        for number in numbers:
            array = streams[number][0]
            owner = owner_at(number, turn)
            if not streams[number][4]:
                add_cores(number, turn)

                @pl.when(turn > 1)
                def _(number=number, array=array, owner=owner):
                    ring_copy(number, turn - 1).wait_recv()
                    for its_side in range(2):
                        held[array][owner, its_side, :, cols(number)] = (
                            held[array][owner, its_side, :, cols(number)].astype(F32)
                            + ring_in[number][turn - 2, its_side].astype(F32)
                        ).astype(BF16)

                @pl.when(turn < chips)
                def _(number=number):
                    ring_copy(number, turn).start()

        for number in numbers:
            array = streams[number][0]
            owner = owner_at(number, turn)
            if streams[number][4]:
                x_copy(number, turn).wait_recv()

                @pl.when(turn == 1)
                def _(number=number, array=array, owner=owner):
                    held[array][owner, side, :, cols(number)] = (
                        held[array][owner, side, :, cols(number)].astype(F32)
                        + x_in[number][turn - 1].astype(F32)
                    ).astype(BF16)

                @pl.when(turn > 1)
                def _(number=number, array=array, owner=owner):
                    ring_copy(number, turn - 1).wait_recv()
                    total = (
                        held[array][owner, side, :, cols(number)].astype(F32)
                        + x_in[number][turn - 1].astype(F32)
                        + ring_in[number][turn - 2, 0].astype(F32)
                    )
                    held[array][owner, side, :, cols(number)] = total.astype(BF16)

                    @pl.when(turn == chips)
                    def _():
                        outs[array][:, cols(number)] = total

                @pl.when(turn < chips)
                def _(number=number):
                    ring_copy(number, turn).start()

        return carry

    lax.fori_loop(1, chips + 1, round_trip, 0)
    for number in numbers:
        if not streams[number][4]:
            x_copy(number, chips).start()
    tile_out[...] = lax.fori_loop(1, chips, lambda i, total: total + tile_ring[i], tile_ring[0])
    for number in numbers:
        array = streams[number][0]
        if not streams[number][4]:
            x_copy(number, chips).wait_recv()
            outs[array][:, cols(number)] = held[array][chip, side, :, cols(number)].astype(
                F32
            ) + x_in[number][0].astype(F32)

    for kind in range(3):
        for way in range(2):
            hop_copy(way, kind).wait()

    def drain(turn, carry):
        for number in numbers:
            core_copy(number, turn).wait_send()
            if streams[number][4]:
                x_copy(number, turn).wait_send()

            @pl.when(turn < chips)
            def _(number=number):
                ring_copy(number, turn).wait_send()

        @pl.when(turn < chips)
        def _():
            tile_turn(turn).wait_send()

        return carry

    lax.fori_loop(1, chips + 1, drain, 0)
    for number in numbers:
        if not streams[number][4]:
            x_copy(number, chips).wait_send()


def refs_of(counts, refs):
    groups, at = [], 0
    for count in counts:
        groups.append(refs[at : at + count])
        at += count
    return groups


def sum_all(arrays, firsts, tile, up_sum, down_sum, chips):
    rows = arrays[0].shape[0] // (4 * chips)
    streams = []
    for i, (array, first) in enumerate(zip(arrays, firsts)):
        width = array.shape[1]
        left = width // 256 * 128
        streams.append((i, 0, left, 1, first))
        streams.append((i, left, width - left, -1, first))
    streams = tuple(sorted(streams, key=lambda stream: stream[4]))
    count, number = len(arrays), len(streams)
    dma = pltpu.SemaphoreType.DMA
    vmem = pltpu.VMEM
    scratch = (
        [vmem((chips, 2, rows, a.shape[1]), BF16) for a in arrays]
        + [vmem((chips, 2, rows, a.shape[1]), BF16) for a in arrays]
        + [vmem((chips - 1, 1 if first else 2, rows, width), BF16) for _, _, width, _, first in streams]
        + [vmem((chips if first else 1, rows, width), BF16) for _, _, width, _, first in streams]
        + [vmem((3, 8, 128), F32), vmem((chips, 8, 128), F32)]
        + [dma((count,))]
        + [dma((number, chips)) for _ in range(6)]
        + [dma((chips + 1,)) for _ in range(2)]
        + [dma((2, 3)) for _ in range(2)]
    )
    return pl.pallas_call(
        functools.partial(
            sum_kernel, chips, streams, (count, 3, count, 3, count, count, number, number, 2, 11)
        ),
        out_shape=[jax.ShapeDtypeStruct((rows, a.shape[1]), F32) for a in arrays]
        + [jax.ShapeDtypeStruct((8, 128), F32)]
        + [jax.ShapeDtypeStruct(up_sum.shape, BF16)] * 2,
        in_specs=[pl.BlockSpec(memory_space=pl.ANY)] * count
        + [pl.BlockSpec(memory_space=pltpu.VMEM)]
        + [pl.BlockSpec(memory_space=pl.ANY)] * 2,
        out_specs=[pl.BlockSpec(memory_space=pltpu.VMEM)] * (count + 1) + [pl.BlockSpec(memory_space=pl.ANY)] * 2,
        scratch_shapes=scratch,
        compiler_params=pltpu.CompilerParams(
            collective_id=1, has_side_effects=True, vmem_limit_bytes=58 << 20
        ),
        cost_estimate=pl.CostEstimate(
            flops=0, bytes_accessed=sum(2 * a.size for a in arrays), transcendentals=0
        ),
        name="sum_all",
    )(*[a.reshape(chips, 2, 2, rows, a.shape[1]) for a in arrays], tile, up_sum, down_sum)


LITTLE = pl.CostEstimate(flops=0, bytes_accessed=1024, transcendentals=0)
VMEM_LIMIT = 56 << 20


def whole(shape):
    return pl.BlockSpec(shape, lambda *_: (0,) * len(shape))


def piece(kernel, name, grid, in_specs, out_specs, out_shapes, scratch=()):
    return pl.pallas_call(
        kernel,
        grid=grid,
        in_specs=in_specs,
        out_specs=out_specs,
        out_shape=[jax.ShapeDtypeStruct(shape, dtype) for shape, dtype in out_shapes],
        scratch_shapes=list(scratch),
        compiler_params=pltpu.CompilerParams(vmem_limit_bytes=VMEM_LIMIT),
        cost_estimate=LITTLE,
        name=name,
    )


def inverse_rms(values):
    return lax.rsqrt(jnp.mean(values * values, axis=-1, keepdims=True) + EPSILON)


def norm_back(values, gain, grad):
    scale = inverse_rms(values)
    scaled = grad * gain
    mean = jnp.mean(values * scaled, axis=-1, keepdims=True)
    back = scale * scaled - values * (scale * scale * scale * mean)
    return back, jnp.sum(grad * (values * scale), axis=0, keepdims=True)


def qkv_kernel(tokens, gains, head_gain, cosine, sine, weight, low, raw, new):
    at = pl.program_id(0)

    @pl.when(at == 0)
    def _():
        states = tokens[...].astype(F32)
        low[...] = (states * inverse_rms(states) * gains[0:1]).astype(BF16)

    out = full_dot(low[...], weight[...])
    raw[...] = out
    plain = out * inverse_rms(out)
    values = plain * jnp.where(at < HEADS, head_gain[0:1], head_gain[1:2])
    half = HEAD // 2
    first, second = values[:, :half], values[:, half:]
    turned = jnp.concatenate(
        [first * cosine[...] - second * sine[...], second * cosine[...] + first * sine[...]], 1
    )
    new[...] = jnp.where(at < HEADS + KV_HEADS, turned, plain).astype(BF16)


def make_qkv(tokens, gains, head_gain, cosine, sine, full):
    rows = tokens.shape[0]
    heads = HEADS + 2 * KV_HEADS
    return piece(
        qkv_kernel,
        "make_qkv",
        (heads,),
        [
            whole((rows, D)),
            whole(gains.shape),
            whole((2, HEAD)),
            whole(cosine.shape),
            whole(sine.shape),
            pl.BlockSpec((D, HEAD), lambda i: (0, HEADS + i)),
        ],
        [
            whole((rows, D)),
            pl.BlockSpec((rows, HEAD), lambda i: (0, i)),
            pl.BlockSpec((rows, HEAD), lambda i: (0, i)),
        ],
        [((rows, D), BF16), ((rows, heads * HEAD), F32), ((rows, heads * HEAD), BF16)],
    )(tokens, gains, head_gain, cosine, sine, full)


def softmax_of(query, key, visible):
    scores = jnp.where(visible > 0.0, right_dot(query, key), -1e30)
    expo = jnp.exp(scores - jnp.max(scores, axis=-1, keepdims=True))
    return expo / jnp.sum(expo, axis=-1, keepdims=True)


def attend_kernel(
    tokens, gains, low, query, key, value, visible, w_out, lleft, lright,
    context, attn_raw, mixed, ffn_in, mid,
):
    at = pl.program_id(0)
    probs = softmax_of(query[...], key[...], visible[...]).astype(BF16)
    here = full_dot(probs, value[...]).astype(BF16)
    context[...] = here
    term = full_dot(here, w_out[...])

    @pl.when(at == 0)
    def _():
        attn_raw[...] = term

    @pl.when(at > 0)
    def _():
        attn_raw[...] += term

    @pl.when(at == HEADS - 1)
    def _():
        states = tokens[...].astype(F32)
        raw = attn_raw[...]
        total = states + raw * inverse_rms(raw) * gains[1:2]
        total = total + states * inverse_rms(states) * gains[0:1]
        mid[...] = full_dot(low[...], lleft[...]).astype(BF16)
        laurel = right_dot(mid[...], lright[...])
        total = (total + laurel * inverse_rms(laurel) * gains[2:3]) * INV_SQRT2
        mixed[...] = total
        ffn_in[...] = (total * inverse_rms(total) * gains[3:4]).astype(BF16)


def attend(tokens, gains, low, qkv, keys_all, visible, full):
    rows = tokens.shape[0]
    seen = keys_all.shape[0]
    group = HEADS // KV_HEADS
    side = 128
    left_at, right_at = full.shape[1] // side - 2, full.shape[1] // side - 1
    return piece(
        attend_kernel,
        "attend",
        (HEADS,),
        [
            whole((rows, D)),
            whole(gains.shape),
            whole((rows, D)),
            pl.BlockSpec((rows, HEAD), lambda i: (0, i)),
            pl.BlockSpec((seen, HEAD), lambda i: (0, i // group)),
            pl.BlockSpec((seen, HEAD), lambda i: (0, KV_HEADS + i // group)),
            whole((rows, seen)),
            pl.BlockSpec((HEAD, D), lambda i: (i, 0)),
            pl.BlockSpec((D, side), lambda i: (0, left_at)),
            pl.BlockSpec((D, side), lambda i: (0, right_at)),
        ],
        [
            pl.BlockSpec((rows, HEAD), lambda i: (0, i)),
            whole((rows, D)),
            whole((rows, D)),
            whole((rows, D)),
            whole((rows, side)),
        ],
        [
            ((rows, HEADS * HEAD), BF16),
            ((rows, D), F32),
            ((rows, D), F32),
            ((rows, D), BF16),
            ((rows, side), BF16),
        ],
    )(tokens, gains, low, qkv, keys_all, keys_all, visible, full, full, full)


def load_weights(weights, held, sems):
    copies, at = [], 0
    for number, ref in enumerate(weights):
        count = ref.shape[1]
        copies.append(pltpu.make_async_copy(ref, held.at[:, pl.ds(at, count)], sems.at[number]))
        at += count

    @pl.when(pl.program_id(0) == 0)
    def _():
        for copy in copies:
            copy.start()
        for copy in copies:
            copy.wait()


ROW_BLOCK = 256
UNIT_BLOCK = 512


def unit_blocks(steps, units):
    many = max(1, UNIT_BLOCK // units)
    return [range(first, min(first + many, steps)) for first in range(0, steps, many)]


def ffn_forward_kernel(steps, add, last, *refs):
    weights, refs = refs[: 2 * steps], refs[2 * steps :]
    if add:
        before, refs = refs[0], refs[1:]
    rows, total, refs = refs[0], refs[1], refs[2:]
    if last:
        low_total, refs = refs[0], refs[1:]
    gates, uppers, hiddens, (held, sems) = refs_of((steps, steps, steps, 2), refs)
    load_weights(weights, held, sems)
    units = held.shape[1] // steps
    here = rows[...]
    running = before[...] if add else None
    for block in unit_blocks(steps, units):
        cut = slice(block[0] * units, (block[-1] + 1) * units)
        gate_in = right_dot(here, held[0, cut])
        upper_in = right_dot(here, held[1, cut])
        low = gated_product(gate_in, upper_in).astype(BF16)
        for i, step in enumerate(block):
            own = slice(i * units, (i + 1) * units)
            gates[step][...] = gate_in[:, own]
            uppers[step][...] = upper_in[:, own]
            hiddens[step][...] = low[:, own]
        term = full_dot(low, held[2, cut])
        running = term if running is None else running + term
    write_sum(running, total, low_total if last else None)


def write_sum(running, total, low_total):
    if low_total is None:
        total[...] = running
        return
    half = pl.num_programs(0) // 2

    @pl.when(pl.program_id(0) < half)
    def _():
        low_total[...] = running.astype(BF16)

    @pl.when(pl.program_id(0) >= half)
    def _():
        total[...] = running


def sum_specs(many, last):
    blocks = many // ROW_BLOCK
    half = blocks // 2
    if not last:
        return (lambda i: i), [pl.BlockSpec((ROW_BLOCK, D), lambda i: (i, 0))], [((many, D), F32)]
    specs = [
        pl.BlockSpec((ROW_BLOCK, D), lambda i: (jnp.maximum(i - half, 0), 0)),
        pl.BlockSpec((ROW_BLOCK, D), lambda i: (jnp.minimum(i, half - 1), 0)),
    ]
    return (lambda i: lax.rem(i + half, blocks)), specs, [((many // 2, D), F32), ((many // 2, D), BF16)]


def ffn_forward(rows, before, weights, last):
    many = rows.shape[0]
    steps, units = len(weights) // 2, 2 * weights[0].shape[1]
    at, sums, sum_shapes = sum_specs(many, last)
    by_row = lambda width: pl.BlockSpec((ROW_BLOCK, width), lambda i: (at(i), 0))
    add = before is not None
    outs = piece(
        functools.partial(ffn_forward_kernel, steps, add, last),
        "ffn_forward",
        (many // ROW_BLOCK,),
        [pl.BlockSpec(memory_space=pl.ANY)] * len(weights) + [by_row(D)] * (1 + add),
        sums + [by_row(units)] * (3 * steps),
        sum_shapes + [((many, units), F32)] * (2 * steps) + [((many, units), BF16)] * steps,
        [pltpu.VMEM((3, steps * units, D), BF16), pltpu.SemaphoreType.DMA((len(weights),))],
    )(*weights, *([before] if add else []), rows)
    return refs_of((len(sums), steps, steps, steps), outs)


def ffn_backward_kernel(steps, add, last, *refs):
    weights, refs = refs[: 2 * steps], refs[2 * steps :]
    if add:
        before, refs = refs[0], refs[1:]
    (rows,), gates, uppers, totals, grad_gates, grad_uppers, (held, sems) = refs_of(
        (1, steps, steps, 1 + last, steps, steps, 2), refs
    )
    load_weights(weights, held, sems)
    units = held.shape[1] // steps
    here = rows[...]
    running = before[...] if add else None
    for block in unit_blocks(steps, units):
        cut = slice(block[0] * units, (block[-1] + 1) * units)
        grad_hidden = right_dot(here, held[2, cut])
        low_gates, low_uppers = [], []
        for i, step in enumerate(block):
            unused, act_back = jax.vjp(gated_product, gates[step][...], uppers[step][...])
            back_gate, back_upper = act_back(grad_hidden[:, i * units : (i + 1) * units])
            low_gates.append(back_gate.astype(BF16))
            low_uppers.append(back_upper.astype(BF16))
            grad_gates[step][...] = low_gates[-1]
            grad_uppers[step][...] = low_uppers[-1]
        term = full_dot(jnp.concatenate(low_gates, 1), held[0, cut])
        term = term + full_dot(jnp.concatenate(low_uppers, 1), held[1, cut])
        running = term if running is None else running + term
    write_sum(running, totals[0], totals[1] if last else None)


def ffn_backward(rows, before, weights, gates, uppers, last):
    many = rows.shape[0]
    steps, units = len(gates), gates[0].shape[1]
    at, sums, sum_shapes = sum_specs(many, last)
    by_row = lambda width: pl.BlockSpec((ROW_BLOCK, width), lambda i: (at(i), 0))
    add = before is not None
    outs = piece(
        functools.partial(ffn_backward_kernel, steps, add, last),
        "ffn_backward",
        (many // ROW_BLOCK,),
        [pl.BlockSpec(memory_space=pl.ANY)] * len(weights)
        + [by_row(D)] * (1 + add)
        + [by_row(units)] * (2 * steps),
        sums + [by_row(units)] * (2 * steps),
        sum_shapes + [((many, units), BF16)] * (2 * steps),
        [pltpu.VMEM((3, steps * units, D), BF16), pltpu.SemaphoreType.DMA((len(weights),))],
    )(*weights, *([before] if add else []), rows, *gates, *uppers)
    return refs_of((len(sums), steps, steps), outs)


def unit_grads_kernel(grad_gate, grad_upper, hidden, rows, down_rows, up_out, down_out):
    half = up_out.shape[1]
    pairs = ((grad_gate, rows), (grad_upper, rows), (hidden, down_rows))
    for kind, (left, right) in enumerate(pairs):
        out = left_dot(left[...], right[...]).astype(BF16)
        up_out[kind] = out[:half]
        down_out[kind] = out[half:]


def unit_grads_of(grad_gate, grad_upper, hidden, rows, down_rows):
    many, units = hidden.shape
    width = 1024
    narrow = whole((many, units))
    wide = pl.BlockSpec((many, width), lambda i: (0, i))
    part = pl.BlockSpec((3, units // 2, width), lambda i: (0, 0, i))
    return piece(
        unit_grads_kernel,
        "unit_grads",
        (D // width,),
        [narrow, narrow, narrow, wide, wide],
        [part, part],
        [((3, units // 2, D), BF16)] * 2,
    )(grad_gate, grad_upper, hidden, rows, down_rows)


def attend_back_kernel(
    gains, grad_in, grad_after, mixed, attn_raw, mid, low, lleft, lright, w_out, context, query, key, value, visible,
    grad_mixed, grad_mid, grad_gains, grad_left, grad_right, grad_w_out, grad_query, grad_key, grad_value,
    grad_attn,
):
    at = pl.program_id(0)

    @pl.when(at == 0)
    def _():
        back, gain_3 = norm_back(mixed[...], gains[3:4], grad_in[...])
        total = (grad_after[...] + back) * INV_SQRT2
        grad_mixed[...] = total
        back, gain_2 = norm_back(right_dot(mid[...], lright[...]), gains[2:3], total)
        back_low = back.astype(BF16)
        grad_right[...] = left_dot(back_low, mid[...])
        mid_low = full_dot(back_low, lright[...]).astype(BF16)
        grad_mid[...] = mid_low
        grad_left[...] = left_dot(low[...], mid_low)
        back, gain_1 = norm_back(attn_raw[...], gains[1:2], total)
        grad_attn[...] = back.astype(BF16)
        grad_gains[...] = jnp.concatenate(
            [gain_1, gain_2, gain_3, jnp.zeros((5, D), F32)], 0
        )

    grad_context = right_dot(grad_attn[...], w_out[...]).astype(BF16)
    grad_w_out[...] = left_dot(context[...], grad_attn[...]).astype(BF16)
    probs = softmax_of(query[...], key[...], visible[...])
    grad_probs = right_dot(grad_context, value[...])
    inner = jnp.sum(probs * grad_probs, axis=-1, keepdims=True)
    grad_scores = (probs * (grad_probs - inner)).astype(BF16)
    grad_query[...] = full_dot(grad_scores, key[...])
    key_term = left_dot(grad_scores, query[...])
    value_term = left_dot(probs.astype(BF16), grad_context)
    group = HEADS // KV_HEADS

    @pl.when(lax.rem(at, group) == 0)
    def _():
        grad_key[...] = key_term
        grad_value[...] = value_term

    @pl.when(lax.rem(at, group) > 0)
    def _():
        grad_key[...] += key_term
        grad_value[...] += value_term


def attend_back(gains, grad_in, grad_after, mixed, attn_raw, mid, low, full, context, qkv, keys_all, visible):
    rows = low.shape[0]
    seen = keys_all.shape[0]
    group = HEADS // KV_HEADS
    side = 128
    left_at, right_at = full.shape[1] // side - 2, full.shape[1] // side - 1
    head = pl.BlockSpec((rows, HEAD), lambda i: (0, i))
    once = lambda shape: pl.BlockSpec(shape, lambda i: (0, 0), pipeline_mode=pl.Buffered(1))
    return piece(
        attend_back_kernel,
        "attend_back",
        (HEADS,),
        [
            whole(gains.shape),
            once((rows, D)),
            once((rows, D)),
            once((rows, D)),
            once((rows, D)),
            whole((rows, side)),
            whole((rows, D)),
            pl.BlockSpec((D, side), lambda i: (0, left_at)),
            pl.BlockSpec((D, side), lambda i: (0, right_at)),
            pl.BlockSpec((HEAD, D), lambda i: (i, 0)),
            head,
            head,
            pl.BlockSpec((seen, HEAD), lambda i: (0, i // group)),
            pl.BlockSpec((seen, HEAD), lambda i: (0, KV_HEADS + i // group)),
            whole((rows, seen)),
        ],
        [
            whole((rows, D)),
            whole((rows, side)),
            whole((8, D)),
            whole((D, side)),
            whole((D, side)),
            pl.BlockSpec((HEAD, D), lambda i: (i, 0)),
            head,
            pl.BlockSpec((seen, HEAD), lambda i: (0, i // group)),
            pl.BlockSpec((seen, HEAD), lambda i: (0, i // group)),
        ],
        [
            ((rows, D), F32),
            ((rows, side), BF16),
            ((8, D), F32),
            ((D, side), F32),
            ((D, side), F32),
            ((HEADS * HEAD, D), BF16),
            ((rows, HEADS * HEAD), F32),
            ((seen, KV_HEADS * HEAD), F32),
            ((seen, KV_HEADS * HEAD), F32),
        ],
        [pltpu.VMEM((rows, D), BF16)],
    )(
        gains, grad_in, grad_after, mixed, attn_raw, mid, low, full, full, full, context, qkv, keys_all, keys_all,
        visible,
    )


def turn_back(grad, cosine, sine):
    half = HEAD // 2
    first, second = grad[:, :half], grad[:, half:]
    return jnp.concatenate([first * cosine + second * sine, second * cosine - first * sine], 1)


def query_back_kernel(grad_query, raw, cosine, sine, head_gain, low, weight, grad_w, grad_low, grad_head):
    at = pl.program_id(0)
    turned = turn_back(grad_query[...], cosine[...], sine[...])
    back, gain = norm_back(raw[...], head_gain[0:1], turned)
    back_low = back.astype(BF16)
    grad_w[...] = left_dot(low[...], back_low).astype(BF16)
    term = right_dot(back_low, weight[...])

    @pl.when(at == 0)
    def _():
        grad_low[...] = term
        grad_head[...] = gain

    @pl.when(at > 0)
    def _():
        grad_low[...] += term
        grad_head[...] += gain


def query_back(grad_query, raw, cosine, sine, head_gain, low, full):
    rows = low.shape[0]
    head = pl.BlockSpec((rows, HEAD), lambda i: (0, i))
    return piece(
        query_back_kernel,
        "query_back",
        (HEADS,),
        [
            head,
            head,
            whole(cosine.shape),
            whole(sine.shape),
            whole((2, HEAD)),
            whole((rows, D)),
            pl.BlockSpec((D, HEAD), lambda i: (0, HEADS + i)),
        ],
        [pl.BlockSpec((D, HEAD), lambda i: (0, i)), whole((rows, D)), whole((1, HEAD))],
        [((D, HEADS * HEAD), BF16), ((rows, D), F32), ((1, HEAD), F32)],
    )(grad_query, raw, cosine, sine, head_gain, low, full)


def key_back_kernel(
    grad_kv, raw, cosine, sine, head_gain, low, weight, before, grad_mixed, grad_mid, lleft, tokens, gains,
    grad_w, grad_tokens, grad_head, grad_gain, total,
):
    at = pl.program_id(0)
    is_key = at < KV_HEADS
    grad = grad_kv[...]
    turned = jnp.where(is_key, turn_back(grad, cosine[...], sine[...]), grad)
    back, gain = norm_back(raw[...], jnp.where(is_key, head_gain[1:2], 1.0), turned)
    back_low = back.astype(BF16)
    grad_w[...] = left_dot(low[...], back_low).astype(BF16)
    term = right_dot(back_low, weight[...])

    @pl.when(at == 0)
    def _():
        total[...] = before[...] + term
        grad_head[...] = gain

    @pl.when(at > 0)
    def _():
        total[...] += term
        grad_head[...] += jnp.where(is_key, gain, 0.0)

    @pl.when(at == 2 * KV_HEADS - 1)
    def _():
        grad_normed = total[...] + grad_mixed[...] + right_dot(grad_mid[...], lleft[...])
        back, gain_0 = norm_back(tokens[...].astype(F32), gains[0:1], grad_normed)
        grad_tokens[...] = grad_mixed[...] + back
        grad_gain[...] = gain_0


def key_back(grad_kv, raw, cosine, sine, head_gain, low, full, before, grad_mixed, grad_mid, tokens, gains):
    rows = low.shape[0]
    side = 128
    left_at = full.shape[1] // side - 2
    return piece(
        key_back_kernel,
        "key_back",
        (2 * KV_HEADS,),
        [
            pl.BlockSpec((rows, HEAD), lambda i: (0, i)),
            pl.BlockSpec((rows, HEAD), lambda i: (0, HEADS + i)),
            whole(cosine.shape),
            whole(sine.shape),
            whole((2, HEAD)),
            whole((rows, D)),
            pl.BlockSpec((D, HEAD), lambda i: (0, 2 * HEADS + i)),
            whole((rows, D)),
            whole((rows, D)),
            whole((rows, side)),
            pl.BlockSpec((D, side), lambda i: (0, left_at)),
            whole((rows, D)),
            whole(gains.shape),
        ],
        [
            pl.BlockSpec((D, HEAD), lambda i: (0, i)),
            whole((rows, D)),
            whole((1, HEAD)),
            whole((1, D)),
        ],
        [
            ((D, 2 * KV_HEADS * HEAD), BF16),
            ((rows, D), F32),
            ((1, HEAD), F32),
            ((1, D), F32),
        ],
        [pltpu.VMEM((rows, D), F32)],
    )(grad_kv, raw, cosine, sine, head_gain, low, full, before, grad_mixed, grad_mid, full, tokens, gains)


def tie(*values):
    return lax.optimization_barrier(values)


def shares(total, count):
    return [total // count + (1 if i < total % count else 0) for i in range(count)]


def greet(peers):
    barrier = pltpu.get_barrier_semaphore()
    for peer in peers:
        pl.semaphore_signal(barrier, inc=1, device_id=peer, device_id_type=MESH)
    pl.semaphore_wait(barrier, len(peers))


def partners():
    return {"core": 1 - lax.axis_index("core")}, {"fsdp": 1 - lax.axis_index("fsdp")}


CUTS = 8
FLYING = 2


def spread_kernel(own, rows, x_send, x_recv, near_send, near_recv, far_send, far_recv, own_sem):
    count = own.shape[0]
    cut = count // CUTS
    other_core, other_side = partners()
    greet((other_core, other_side))

    def copy(src, block, at, send, recv, peer):
        return pltpu.make_async_remote_copy(
            src_ref=src,
            dst_ref=rows.at[pl.ds(block * count + at * cut, cut)],
            send_sem=send.at[at],
            recv_sem=recv.at[at],
            device_id=peer,
            device_id_type=MESH,
        )

    mine = [own.at[pl.ds(at * cut, cut)] for at in range(CUTS)]
    came = [rows.at[pl.ds(count + at * cut, cut)] for at in range(CUTS)]
    across = [copy(mine[at], 1, at, x_send, x_recv, other_side) for at in range(CUTS)]
    near = [copy(mine[at], 2, at, near_send, near_recv, other_core) for at in range(CUTS)]
    far = [copy(came[at], 3, at, far_send, far_recv, other_core) for at in range(CUTS)]
    for one in across[:FLYING] + near:
        one.start()
    keep = pltpu.make_async_copy(own, rows.at[pl.ds(0, count)], own_sem)
    keep.start()
    for at in range(CUTS):
        across[at].wait_send()
        if at + FLYING < CUTS:
            across[at + FLYING].start()
        across[at].wait_recv()
        far[at].start()
    for one in near + far:
        one.wait()
    keep.wait()


def rows_of_four(own, number):
    count = own.shape[0]
    dma = pltpu.SemaphoreType.DMA
    return pl.pallas_call(
        spread_kernel,
        out_shape=jax.ShapeDtypeStruct((4 * count, D), BF16),
        in_specs=[pl.BlockSpec(memory_space=pltpu.VMEM)],
        out_specs=pl.BlockSpec(memory_space=pl.ANY),
        scratch_shapes=[dma((CUTS,)) for _ in range(6)] + [dma],
        compiler_params=pltpu.CompilerParams(collective_id=number, has_side_effects=True),
        cost_estimate=LITTLE,
        name="spread_rows",
    )(own)


def gather_sum_kernel(steps, *refs):
    if steps:
        (own, low, rows, down_rows), sides, (out,), grads, more, held, sems = refs_of(
            (4, 3 * steps, 1, 2 * steps, 4 + 4, 3, 3), refs
        )
        core_in, pair_low, x_in, parts, *copy_sems = more
        core_send, core_recv, x_send, x_recv = copy_sems
        rows_in, down_in, more_out = held
        loads_sem, parts_sem, grads_sem = sems
        parts_out = more_out

        def store(step, way):
            return pltpu.make_async_copy(parts_out.at[step, way], grads[2 * step + way], grads_sem.at[step, way])

        loads = [
            pltpu.make_async_copy(rows, rows_in, loads_sem.at[0]),
            pltpu.make_async_copy(down_rows, down_in, loads_sem.at[1]),
        ]
        part_loads = [
            pltpu.make_async_copy(side, parts.at[number], parts_sem.at[number]) for number, side in enumerate(sides)
        ]
        for load in loads + part_loads:
            load.start()
    else:
        own, low, out, core_in, pair_low, x_in, core_send, core_recv, x_send, x_recv = refs
    count = out.shape[0]
    cut = count // CUTS
    other_core, other_side = partners()
    greet((other_core, other_side))

    def core_copy(block, at):
        here = pl.ds(block * count + at * cut, cut)
        number = block * CUTS + at
        return pltpu.make_async_remote_copy(
            src_ref=low.at[here],
            dst_ref=core_in.at[here],
            send_sem=core_send.at[number],
            recv_sem=core_recv.at[number],
            device_id=other_core,
            device_id_type=MESH,
        )

    def x_copy(at):
        here = pl.ds(at * cut, cut)
        return pltpu.make_async_remote_copy(
            src_ref=pair_low.at[here],
            dst_ref=x_in.at[here],
            send_sem=x_send.at[at],
            recv_sem=x_recv.at[at],
            device_id=other_side,
            device_id_type=MESH,
        )

    pieces = [(block, at) for block in (1, 0) for at in range(CUTS)]

    def next_piece(number):
        core_copy(*pieces[number]).wait_send()
        if number + FLYING < len(pieces):
            core_copy(*pieces[number + FLYING]).start()

    for one in pieces[:FLYING]:
        core_copy(*one).start()
    for at in range(CUTS):
        there = pl.ds(count + at * cut, cut)
        next_piece(at)
        core_copy(1, at).wait_recv()
        pair_low[pl.ds(at * cut, cut)] = (own[there] + core_in[there].astype(F32)).astype(BF16)
        x_copy(at).start()
    for at in range(CUTS):
        here = pl.ds(at * cut, cut)
        next_piece(CUTS + at)
        core_copy(0, at).wait_recv()
        out[here] = own[here] + core_in[here].astype(F32)
    if steps:
        for load in loads:
            load.wait()
        half = grads[0].shape[1]
        width = D // 2
        for step in range(steps):
            for kind in range(3):
                number = 3 * step + kind
                part_loads[number].wait()
                left, right = parts[number], down_in if kind == 2 else rows_in
                for first in range(0, D, width):
                    cols = slice(first, first + width)
                    term = left_dot(left, right[:, cols]).astype(BF16)
                    parts_out[step, 0, kind, :, cols] = term[:half]
                    parts_out[step, 1, kind, :, cols] = term[half:]
            for way in range(2):
                store(step, way).start()
    for at in range(CUTS):
        here = pl.ds(at * cut, cut)
        x_copy(at).wait_recv()
        out[here] += x_in[here].astype(F32)
    for at in range(CUTS):
        x_copy(at).wait_send()
    for step in range(steps):
        for way in range(2):
            store(step, way).wait()


def sum_of_four(own, low, number, units=(), rows=None, down_rows=None):
    count = own.shape[0] // 2
    steps = len(units)
    dma = pltpu.SemaphoreType.DMA
    vmem, anywhere = pltpu.VMEM, pl.BlockSpec(memory_space=pl.ANY)
    scratch = [vmem((2 * count, D), BF16), vmem((count, D), BF16), vmem((count, D), BF16)]
    copy_sems = [dma((2 * CUTS,)), dma((2 * CUTS,)), dma((CUTS,)), dma((CUTS,))]
    operands, shapes = [], []
    if steps:
        many, width = units[0][0].shape
        operands = [rows, down_rows] + [side for sides in units for side in sides]
        shapes = [jax.ShapeDtypeStruct((3, width // 2, D), BF16)] * (2 * steps)
        scratch += [vmem((3 * steps, many, width), BF16)]
        copy_sems += [vmem((many, D), BF16), vmem((many, D), BF16), vmem((steps, 2, 3, width // 2, D), BF16)]
        copy_sems += [dma((2,)), dma((3 * steps,)), dma((steps, 2))]
    total, *grads = pl.pallas_call(
        functools.partial(gather_sum_kernel, steps),
        out_shape=[jax.ShapeDtypeStruct((count, D), F32)] + shapes,
        in_specs=[pl.BlockSpec(memory_space=pltpu.VMEM), anywhere] + [anywhere] * len(operands),
        out_specs=[pl.BlockSpec(memory_space=pltpu.VMEM)] + [anywhere] * len(shapes),
        scratch_shapes=scratch + copy_sems,
        compiler_params=pltpu.CompilerParams(
            collective_id=number, has_side_effects=True, vmem_limit_bytes=VMEM_LIMIT
        ),
        cost_estimate=LITTLE,
        name="gather_sum",
    )(own, low, *operands)
    return total, [(grads[2 * i], grads[2 * i + 1]) for i in range(steps)]


PARTS = 4


def middle_kernel(
    own, low, mixed, layer_in, teacher, mask, scale, gains, gate_w, proj_w,
    result, grad_after, grad_layer, rows, grad_gate_w, grad_proj_w, grad_gains, squares,
    own_in, mixed_in, teacher_in, gate_in, proj_in, core_in, pair_low, x_in,
    result_out, after_out, after_low, mid_low, grad_pl, grad_raw, grad_low,
    loads, stores, core_send, core_recv, x_send, x_recv, y_send, y_recv, near_send, near_recv, far_send, far_recv,
):
    count = mixed.shape[0]
    cut = count // PARTS
    other_core, other_side = partners()

    def load(number, src, dst):
        return pltpu.make_async_copy(src, dst, loads.at[number])

    incoming = [
        load(0, own.at[pl.ds(count, count)], own_in.at[pl.ds(count, count)]),
        load(1, own.at[pl.ds(0, count)], own_in.at[pl.ds(0, count)]),
        load(2, mixed, mixed_in),
        load(3, gate_w, gate_in),
        load(4, proj_w, proj_in),
        load(5, teacher, teacher_in),
    ]
    for one in incoming:
        one.start()
    greet((other_core, other_side))

    def remote(src, dst, send, recv, peer):
        return pltpu.make_async_remote_copy(
            src_ref=src, dst_ref=dst, send_sem=send, recv_sem=recv, device_id=peer, device_id_type=MESH
        )

    def piece_of(at):
        return pl.ds(at * cut, cut)

    def core_copy(block, at):
        here = pl.ds(block * count + at * cut, cut)
        number = block * PARTS + at
        return remote(low.at[here], core_in.at[here], core_send.at[number], core_recv.at[number], other_core)

    def x_copy(at):
        here = piece_of(at)
        return remote(pair_low.at[here], x_in.at[here], x_send.at[at], x_recv.at[at], other_side)

    def out_copy(src, block, at, send, recv, peer):
        return remote(src, rows.at[pl.ds(block * count + at * cut, cut)], send.at[at], recv.at[at], peer)

    def across(at):
        return out_copy(grad_low.at[piece_of(at)], 1, at, y_send, y_recv, other_side)

    def near(at):
        return out_copy(grad_low.at[piece_of(at)], 2, at, near_send, near_recv, other_core)

    def far(at):
        return out_copy(rows.at[pl.ds(count + at * cut, cut)], 3, at, far_send, far_recv, other_core)

    def kept(number, at):
        here = piece_of(at)
        src, dst = ((result_out, result), (after_out, grad_after), (grad_low, rows))[number]
        return pltpu.make_async_copy(src.at[here], dst.at[here], stores.at[number, at])

    for block in (1, 0):
        for at in range(PARTS):
            core_copy(block, at).start()
    incoming[0].wait()
    for at in range(PARTS):
        there = pl.ds(count + at * cut, cut)
        core_copy(1, at).wait_recv()
        pair_low[piece_of(at)] = (own_in[there] + core_in[there].astype(F32)).astype(BF16)
        x_copy(at).start()
    for one in incoming[1:]:
        one.wait()
    gain_4, gain_5 = gains[4:5], gains[5:6]
    total = jnp.zeros((), F32)
    sum_4 = sum_5 = jnp.zeros((1, D), F32)
    for at in range(PARTS):
        here = piece_of(at)
        core_copy(0, at).wait_recv()
        x_copy(at).wait_recv()
        down = own_in[here] + core_in[here].astype(F32) + x_in[here].astype(F32)
        after = mixed_in[here] + down * inverse_rms(down) * gain_4
        low_here = after.astype(BF16)
        after_low[here] = low_here
        raw = full_dot(low_here, gate_in[...])
        act, act_back = jax.vjp(gelu_tanh, raw)
        layer = layer_in[here].astype(F32)
        mid = (act * layer).astype(BF16)
        mid_low[here] = mid
        out = full_dot(mid, proj_in[...])
        done = after + out * inverse_rms(out) * gain_5
        result_out[here] = done
        kept(0, at).start()
        errors = done - teacher_in[here].astype(F32)
        masked = mask[here][:, 0:1] * errors
        total += jnp.sum(masked * errors)
        grad_out = masked * scale[0:1, 0:1]
        back, term = norm_back(out, gain_5, grad_out)
        sum_5 += term
        back_low = back.astype(BF16)
        grad_pl[here] = back_low
        grad_mid = right_dot(back_low, proj_in[...])
        grad_layer[here] = grad_mid * act
        raw_low = act_back(grad_mid * layer)[0].astype(BF16)
        grad_raw[here] = raw_low
        grad_here = grad_out + right_dot(raw_low, gate_in[...])
        after_out[here] = grad_here
        kept(1, at).start()
        back, term = norm_back(down, gain_4, grad_here)
        sum_4 += term
        grad_low[here] = back.astype(BF16)
        across(at).start()
        near(at).start()
        kept(2, at).start()
    grad_gains[...] = jnp.concatenate([sum_4, sum_5, jnp.zeros((6, D), F32)], 0)
    squares[...] = jnp.broadcast_to(total, squares.shape)
    for at in range(PARTS // 2):
        across(at).wait_recv()
        far(at).start()
    grad_proj_w[...] = left_dot(mid_low[...], grad_pl[...]).astype(BF16)
    grad_gate_w[...] = left_dot(after_low[...], grad_raw[...]).astype(BF16)
    for at in range(PARTS // 2, PARTS):
        across(at).wait_recv()
        far(at).start()
    for at in range(PARTS):
        far(at).wait()
        near(at).wait()
        across(at).wait_send()
        x_copy(at).wait_send()
        for block in (0, 1):
            core_copy(block, at).wait_send()
        for number in range(3):
            kept(number, at).wait()


def middle(own, low, mixed, layer_in, teacher, mask, scale, gains, gate_w, proj_w):
    count = mixed.shape[0]
    dma, vmem = pltpu.SemaphoreType.DMA, pltpu.VMEM
    anywhere, inside = pl.BlockSpec(memory_space=pl.ANY), pl.BlockSpec(memory_space=pltpu.VMEM)
    shape = jax.ShapeDtypeStruct
    return pl.pallas_call(
        middle_kernel,
        out_shape=[
            shape((count, D), F32),
            shape((count, D), F32),
            shape((count, PLD), F32),
            shape((4 * count, D), BF16),
            shape((D, PLD), BF16),
            shape((PLD, D), BF16),
            shape((8, D), F32),
            shape((8, 128), F32),
        ],
        in_specs=[anywhere, anywhere, anywhere, inside, anywhere, inside, inside, inside, anywhere, anywhere],
        out_specs=[anywhere, anywhere, inside, anywhere, inside, inside, inside, inside],
        scratch_shapes=[
            vmem((2 * count, D), F32),
            vmem((count, D), F32),
            vmem((count, D), BF16),
            vmem((D, PLD), BF16),
            vmem((PLD, D), BF16),
            vmem((2 * count, D), BF16),
            vmem((count, D), BF16),
            vmem((count, D), BF16),
            vmem((count, D), F32),
            vmem((count, D), F32),
            vmem((count, D), BF16),
            vmem((count, PLD), BF16),
            vmem((count, D), BF16),
            vmem((count, PLD), BF16),
            vmem((count, D), BF16),
            dma((6,)),
            dma((3, PARTS)),
            dma((2 * PARTS,)),
            dma((2 * PARTS,)),
        ]
        + [dma((PARTS,)) for _ in range(8)],
        compiler_params=pltpu.CompilerParams(
            collective_id=3, has_side_effects=True, vmem_limit_bytes=VMEM_LIMIT
        ),
        cost_estimate=LITTLE,
        name="middle",
    )(own, low, mixed, layer_in, teacher, mask, scale, gains, gate_w, proj_w)


def body(
    tokens,
    per_layer,
    teacher,
    cont_lengths,
    w_query,
    w_kv,
    w_out,
    laurel_left,
    laurel_right,
    pl_gate,
    pl_proj,
    norm_gains,
    head_gains,
    ffn_weight,
):
    row_count = tokens.shape[1]
    chips = lax.axis_size("zy")
    seq_count = 2 * chips
    group_count = lax.axis_size("fsdp")
    shards = seq_count * group_count
    chip = lax.axis_index("zy")
    core = lax.axis_index("core")
    seq_index = chip * 2 + core
    group_index = lax.axis_index("fsdp")
    half_point = seq_count // 2
    prompt_len = half_point * row_count
    cont_shards = CONT_LEN // row_count
    cont_count = prompt_len // CONT_LEN
    is_cont = seq_index >= half_point
    rel_index = seq_index - half_point
    local_shard = jnp.where(is_cont, rel_index % cont_shards, 0)
    cont_index = jnp.where(is_cont, rel_index // cont_shards, 0)
    first_place = jnp.where(is_cont, prompt_len + local_shard * row_count, seq_index * row_count)
    row_range = jnp.arange(row_count, dtype=jnp.int32)
    places = first_place + row_range
    group_lengths = jnp.sum(
        jnp.where(
            jnp.arange(group_count, dtype=jnp.int32)[:, None] == group_index, cont_lengths, 0
        ),
        axis=0,
    )
    my_length = jnp.sum(
        jnp.where(jnp.arange(cont_count, dtype=jnp.int32) == cont_index, group_lengths, 0)
    )
    valid = jnp.logical_or(
        jnp.logical_not(is_cont), local_shard * row_count + row_range < my_length
    )
    weight_mask = valid.astype(F32)
    count = F32(group_count * prompt_len) + jnp.sum(cont_lengths).astype(F32)
    total_slots = float(row_count * seq_count * group_count)
    shard_rows = w_query.shape[0]
    key_cols = KV_HEADS * HEAD
    proj_cols = pl_proj.shape[0] * D // shard_rows
    misc_cols = RANK
    head_part = head_gains.reshape(-1, 1)
    misc = jnp.concatenate(
        [
            norm_gains.T,
            jnp.pad(head_part, ((0, shard_rows - head_part.shape[0]), (0, 0))),
            jnp.zeros((shard_rows, misc_cols - 7), BF16),
        ],
        1,
    )
    pack = jnp.concatenate(
        [
            w_out,
            w_query,
            w_kv,
            pl_gate,
            pl_proj.reshape(shard_rows, proj_cols),
            laurel_left,
            misc,
            laurel_right.T,
            jnp.zeros((shard_rows, 128 - RANK), BF16),
        ],
        1,
    )

    units = ffn_weight.shape[0]
    half = units // 2
    by_kind = ffn_weight.transpose(1, 0, 2)
    ups, downs = [by_kind[:, :half]], [by_kind[:, half:]]
    stage_steps = shares(chips - 1, 7)

    def pass_on(stage):
        for _ in range(stage_steps[stage]):
            ups.append(ring(ups[-1], 1))
            downs.append(ring(downs[-1], -1))

    def stage_end(values):
        (ups[-1], downs[-1]), values = tie((ups[-1], downs[-1]), values)
        return values

    pass_on(0)
    full = gather_all(pack, chips)
    at = 2 * D + 2 * key_cols
    plg = full[:, at : at + PLD]
    plp = full[:, at + PLD : at + PLD + proj_cols].reshape(PLD, D)
    at += PLD + proj_cols + RANK
    misc_full = stage_end(full[:, at : at + misc_cols])
    pass_on(1)
    gains = jnp.pad(misc_full[:, :6].T.astype(F32), ((0, 2), (0, 0)))
    head_n = head_gains.shape[1]
    head_gain = (
        misc_full[:, 6]
        .reshape(shards, shard_rows)[:, : 2 * head_n]
        .reshape(shards, 2, head_n)
        .transpose(1, 0, 2)
        .reshape(2, HEAD)
        .astype(F32)
    )
    freqs = jnp.exp(
        jnp.arange(HEAD // 2, dtype=F32) * (-2.0 * math.log(ROPE_BASE) / HEAD)
    )
    angles = places.astype(F32)[:, None] * freqs
    cosine, sine = jnp.cos(angles), jnp.sin(angles)
    normed_low, qkv_raw, qkv = make_qkv(tokens[0], gains, head_gain, cosine, sine, full)
    qkv = stage_end(qkv)
    kv_own = qkv[:, D:]
    pass_on(2)

    mid = chips // 2
    chain = [(i, i + 1) for i in range(mid - 1)] + [(mid - 1, mid + 1)]
    kv_before = jnp.where(
        chip == mid,
        lax.ppermute(kv_own, "zy", [(mid - 1, mid)]),
        lax.ppermute(kv_own, "zy", chain),
    )
    spans = []
    span = 2
    while span < mid:
        spans.append(span)
        span *= 2
    for span in spans:
        moved = lax.ppermute(
            kv_before, "zy", [(mid + i, mid + i + span) for i in range(min(span, mid - span))]
        )
        fresh = jnp.logical_and(chip >= mid + span, chip < mid + 2 * span)
        kv_before = jnp.where(fresh, moved, kv_before)
    kv_other = swap(jnp.where(core == 0, kv_own, kv_before), "core")
    keys_all = jnp.concatenate([kv_before, kv_other, kv_own], 0)
    keys_all = stage_end(keys_all)
    pass_on(3)
    key_len = keys_all.shape[0]
    key_places = first_place - 2 * row_count + jnp.arange(key_len, dtype=jnp.int32)
    visible = (
        (key_places[None, :] <= places[:, None])
        & (places[:, None] - key_places[None, :] < WINDOW)
        & (key_places[None, :] >= 0)
    ).astype(F32)
    context_low, attn_raw, mixed, ffn_in, laurel_mid = attend(
        tokens[0], gains, normed_low, qkv, keys_all, visible, full
    )

    ffn_in = stage_end(ffn_in)
    pass_on(4)
    ffn_rows = stage_end(rows_of_four(ffn_in, 2))
    here = len(ups)
    pass_on(5)
    gates, uppers, hiddens = [], [], []

    def weights_of(steps):
        return [w for k in steps for w in (ups[k], downs[k])]

    def forward_part(running, first, end, last=False):
        sums, gate, upper, hidden = ffn_forward(ffn_rows, running, weights_of(range(first, end)), last)
        gates.extend(gate)
        uppers.extend(upper)
        hiddens.extend(hidden)
        return sums if last else sums[0]

    running = stage_end(forward_part(None, 0, here))
    then = len(ups)
    pass_on(6)
    running = stage_end(forward_part(running, here, then))
    own_sum, low_sum = forward_part(running, then, chips, True)
    result, grad_after, grad_layer_in, grad_down_rows, grad_plg, grad_plp, late_gains, squares = middle(
        own_sum,
        low_sum,
        mixed,
        per_layer[0],
        teacher[0],
        jnp.broadcast_to(weight_mask[:, None], (row_count, 128)),
        jnp.broadcast_to(total_slots / count, (8, 128)),
        gains,
        plg,
        plp,
    )
    grad_gates, grad_uppers = [None] * chips, [None] * chips

    def backward_part(steps, running, last=False):
        sums, grad_gate, grad_upper = ffn_backward(
            grad_down_rows, running, weights_of(steps), [gates[k] for k in steps], [uppers[k] for k in steps], last
        )
        for k, gg, gu in zip(steps, grad_gate, grad_upper):
            grad_gates[k], grad_uppers[k] = gg, gu
        return sums if last else sums[0]

    ready = {}

    def unit_grads(k):
        if k in ready:
            return ready[k]
        return unit_grads_of(grad_gates[k], grad_uppers[k], hiddens[k], ffn_rows, grad_down_rows)

    order = list(range(1, chips)) + [0]
    ring_steps = shares(chips - 2, 6)
    done = 0

    def beside(stage, work):
        nonlocal done, up_sum, down_sum
        values = None
        for step in range(ring_steps[stage]):
            up_in = ring(up_sum, 1)
            down_in = ring(down_sum, -1)
            if step == 0:
                values = work()
            done += 1
            terms = unit_grads(order[done])
            (up_in, down_in), terms, values = tie((up_in, down_in), terms, values)
            up_sum = (up_in.astype(F32) + terms[0].astype(F32)).astype(BF16)
            down_sum = (down_in.astype(F32) + terms[1].astype(F32)).astype(BF16)
        return work() if values is None else values

    first = ring_steps[0]
    then = first + 1 + ring_steps[0] + ring_steps[1]
    running = backward_part(order[:first], None)
    up_sum, down_sum = unit_grads(order[0])
    running = beside(0, lambda: backward_part(order[first:then], running))
    own_sum, low_sum = beside(1, lambda: backward_part(order[then:], running, True))

    def work():
        steps = order[done + ring_steps[2] :] if units % 128 == 0 else []
        total, grads = sum_of_four(
            own_sum,
            low_sum,
            5,
            [(grad_gates[k], grad_uppers[k], hiddens[k]) for k in steps],
            ffn_rows,
            grad_down_rows,
        )
        ready.update(zip(steps, grads))
        return total

    grad_ffn_in = beside(2, work)
    (
        grad_scaled,
        grad_mid_low,
        grad_mid_gains,
        grad_lleft,
        grad_lright_t,
        grad_wo,
        grad_queries,
        grad_keys,
        grad_values,
    ) = beside(
        3,
        lambda: attend_back(
            gains, grad_ffn_in, grad_after, mixed, attn_raw, laurel_mid, normed_low, full, context_low, qkv, keys_all,
            visible,
        ),
    )

    def work():
        grad_kv = jnp.concatenate([grad_keys, grad_values], 1)
        grad_before = grad_kv[:row_count]
        grad_own = grad_kv[2 * row_count :]
        returned = swap(grad_kv[row_count : 2 * row_count].astype(BF16), "core").astype(F32)
        grad_own = grad_own + jnp.where(core == 0, returned, 0.0)
        grad_before = grad_before + jnp.where(core == 0, 0.0, returned)
        for span in reversed(spans):
            back = [(mid + i + span, mid + i) for i in range(min(span, mid - span))]
            grad_before = grad_before + lax.ppermute(grad_before.astype(BF16), "zy", back).astype(F32)
        before_low = grad_before.astype(BF16)
        grad_own = (
            grad_own
            + lax.ppermute(before_low, "zy", [(b, a) for a, b in chain]).astype(F32)
            + lax.ppermute(before_low, "zy", [(mid, mid - 1)]).astype(F32)
        )
        return grad_own, query_back(grad_queries, qkv_raw, cosine, sine, head_gain, normed_low, full)

    grad_own, (grad_wq, grad_normed, grad_hq) = beside(4, work)
    def work():
        grad_wkv, grad_tokens, grad_hk, grad_g0 = key_back(
            grad_own, qkv_raw, cosine, sine, head_gain, normed_low, full, grad_normed, grad_scaled, grad_mid_low,
            tokens[0], gains,
        )
        head_back = jnp.concatenate([grad_hq, grad_hk], 0).reshape(2, shards, head_n).transpose(1, 0, 2)
        head_back = head_back.reshape(shards, 2 * head_n)
        head_back = jnp.pad(head_back, ((0, 0), (0, shard_rows - 2 * head_n))).reshape(1, D)
        misc_back = jnp.concatenate(
            [grad_g0, grad_mid_gains[:3], late_gains[:2], head_back, jnp.zeros((1, D), F32)], 0
        )
        return grad_wkv, grad_tokens, jnp.concatenate(
            [
                grad_plg,
                grad_plp.reshape(D, proj_cols),
                grad_lleft[:, :RANK].astype(BF16),
                jnp.pad(misc_back.T, ((0, 0), (0, misc_cols - 8))).astype(BF16),
                grad_lright_t.astype(BF16),
            ],
            1,
        )

    last_terms, (grad_wkv, grad_tokens, rest_back) = beside(5, lambda: (unit_grads(0), work()))
    sums_wq, sums_wkv, sums_wo, sums_rest, total, up_in, down_in = sum_all(
        [grad_wq, grad_wkv, grad_wo, rest_back],
        (True, True, True, False),
        squares,
        up_sum,
        down_sum,
        chips,
    )
    grad_ffn = jnp.concatenate(
        [
            (arrived.astype(F32) + term.astype(F32)).transpose(1, 0, 2)
            for arrived, term in zip((up_in, down_in), last_terms)
        ],
        0,
    )
    at = 0
    rest = []
    for width in (PLD, proj_cols, RANK, misc_cols, RANK):
        rest.append(sums_rest[:, at : at + width])
        at += width

    match_loss = total[0, 0] / (2.0 * D * count)

    return (
        result[None],
        match_loss,
        grad_tokens[None],
        grad_layer_in[None],
        sums_wq,
        sums_wkv,
        sums_wo,
        rest[2],
        rest[4].T,
        rest[0],
        rest[1].reshape(pl_proj.shape),
        rest[3][:, :6].T,
        rest[3][: 2 * head_n, 6].reshape(2, head_n),
        grad_ffn,
    )


def solution(mesh):
    seq, fsdp = mesh.shape["seq"], mesh.shape["fsdp"]
    fine = Mesh(mesh.devices.reshape(seq // 2, 2, fsdp), ("zy", "core", "fsdp"))
    rows = P("fsdp", ("zy", "core"), None)
    split = ("zy", "core", "fsdp")
    weights = (
        P(split, None),
        P(split, None),
        P(split, None),
        P(split, None),
        P(None, split),
        P(split, None),
        P(split, None),
        P(None, split),
        P(None, split),
        P(split, None, None),
    )
    return jax.shard_map(
        body,
        mesh=fine,
        in_specs=(rows, rows, rows, P()) + weights,
        out_specs=(rows, P(), rows, rows) + weights,
        check_vma=False,
    )
```

```python
import functools
import math

import jax
import jax.numpy as jnp
from jax import lax
from jax.experimental import pallas as pl
from jax.experimental.pallas import tpu as pltpu
from jax.sharding import Mesh, PartitionSpec as P

D = 2048
HEADS = 8
KV_HEADS = 2
HEAD = 256
WINDOW = 512
CONT_LEN = 512
RANK = 64
PLD = 256

EPSILON = 1e-06
INV_SQRT2 = 0.7071067811865476
ROPE_BASE = 10000.0
BF16 = jnp.bfloat16
F32 = jnp.float32


def gelu_tanh(values):
    return jax.nn.gelu(values, approximate=True)


def gated_product(gate_in, up_in):
    return gelu_tanh(gate_in) * up_in


def full_dot(left, right):
    return jnp.dot(left, right, preferred_element_type=F32)


def left_dot(left, right):
    return lax.dot_general(left, right, (((0,), (0,)), ((), ())), preferred_element_type=F32)


def right_dot(left, right):
    return lax.dot_general(left, right, (((1,), (1,)), ((), ())), preferred_element_type=F32)


def ring_order(n):
    return list(range(0, n, 2)) + list(range(n - 1, 0, -2))


def ring_pairs(n, by):
    order = ring_order(n)
    return [(order[i], order[(i + by) % n]) for i in range(n)]


def ring(value, by):
    return lax.ppermute(value, "zy", ring_pairs(lax.axis_size("zy"), by))


def swap(value, axis):
    return lax.ppermute(value, axis, [(0, 1), (1, 0)])


MESH = pl.DeviceIdType.MESH


def ring_chip(spot, chips):
    spot = lax.rem(spot, chips)
    return jnp.where(spot < chips // 2, 2 * spot, 2 * (chips - 1 - spot) + 1)


def ring_spot(chip, chips):
    return jnp.where(lax.rem(chip, 2) == 0, chip // 2, chips - 1 - chip // 2)


def gather_kernel(chips, streams, shard, full, ring_send, ring_recv, x_send, x_recv, core_send, core_recv, own_sem):
    chip = lax.axis_index("zy")
    core = lax.axis_index("core")
    side = lax.axis_index("fsdp")
    spot = ring_spot(chip, chips)
    rows = shard.shape[0]

    def neighbour(by):
        return {"zy": ring_chip(spot + chips + by, chips)}

    other_core = {"core": 1 - core}
    other_side = {"fsdp": 1 - side}

    barrier = pltpu.get_barrier_semaphore()
    for peer in (neighbour(1), neighbour(-1), other_core, other_side):
        pl.semaphore_signal(barrier, inc=1, device_id=peer, device_id_type=MESH)
    pl.semaphore_wait(barrier, 4)

    def place(owner, its_core, its_side, stream):
        row = ((owner * 2 + its_core) * 2 + its_side) * rows
        return full.at[pl.ds(pl.multiple_of(row, rows), rows), pl.ds(stream[0], stream[1])]

    def owner_at(step, stream):
        return ring_chip(spot + chips - stream[2] * step, chips)

    def send(src, dst, sems, at, peer):
        return pltpu.make_async_remote_copy(
            src_ref=src,
            dst_ref=dst,
            send_sem=sems[0].at[at],
            recv_sem=sems[1].at[at],
            device_id=peer,
            device_id_type=MESH,
        )

    ring_sems, x_sems, core_sems = (ring_send, ring_recv), (x_send, x_recv), (core_send, core_recv)

    def ring_copy(number, away, step, src=None):
        stream = streams[number]
        its_side = 1 - side if away else side
        spot_ref = place(owner_at(step, stream), core, its_side, stream)
        return send(src if src is not None else spot_ref, spot_ref, ring_sems, (number, away, step), neighbour(stream[2]))

    def ring_arrival(number, away, step):
        stream = streams[number]
        its_side = 1 - side if away else side
        spot_ref = place(owner_at(step, stream), core, its_side, stream)
        return send(spot_ref, spot_ref, ring_sems, (number, away, step - 1), neighbour(stream[2]))

    def x_copy(number, step, its_side, src=None):
        stream = streams[number]
        spot_ref = place(owner_at(step, stream), core, its_side, stream)
        return send(src if src is not None else spot_ref, spot_ref, x_sems, (number, step), other_side)

    def core_copy(number, away, step, its_core, src=None):
        stream = streams[number]
        its_side = 1 - side if away else side
        spot_ref = place(owner_at(step, stream), its_core, its_side, stream)
        return send(src if src is not None else spot_ref, spot_ref, core_sems, (number, away, step), other_core)

    def cut(stream):
        return shard.at[:, pl.ds(stream[0], stream[1])]

    own_row = ((chip * 2 + core) * 2 + side) * rows
    own = pltpu.make_async_copy(
        shard, full.at[pl.ds(pl.multiple_of(own_row, rows), rows), :], own_sem
    )
    own.start()
    numbers = range(len(streams))
    for number in numbers:
        if streams[number][3]:
            x_copy(number, 0, side, cut(streams[number])).start()
    for number in numbers:
        ring_copy(number, 0, 0, cut(streams[number])).start()
    for number in numbers:
        if not streams[number][3]:
            x_copy(number, 0, side, cut(streams[number])).start()
    for number in numbers:
        core_copy(number, 0, 0, core, cut(streams[number])).start()
    for number in numbers:
        if streams[number][3]:
            x_copy(number, 0, 1 - side).wait_recv()
            ring_copy(number, 1, 0).start()
            core_copy(number, 1, 0, core).start()

    def turn(step, carry):
        for number in numbers:
            aways = (0, 1) if streams[number][3] else (0,)
            for away in aways:
                ring_arrival(number, away, step).wait_recv()

                @pl.when(step < chips - 1)
                def _(number=number, away=away):
                    ring_copy(number, away, step).start()

                core_copy(number, away, step, core).start()
            if not streams[number][3]:
                x_copy(number, step, side).start()
        for number in numbers:
            if not streams[number][3]:
                x_copy(number, step - 1, 1 - side).wait_recv()
                core_copy(number, 1, step - 1, core).start()
        return carry

    lax.fori_loop(1, chips, turn, 0)
    for number in numbers:
        if not streams[number][3]:
            x_copy(number, chips - 1, 1 - side).wait_recv()
            core_copy(number, 1, chips - 1, core).start()
    own.wait()

    def drain(step, carry):
        for number in numbers:
            first = streams[number][3]
            for away in (0, 1):
                core_copy(number, away, step, 1 - core).wait_recv()
                core_copy(number, away, step, core).wait_send()
                if first or not away:

                    @pl.when(step < chips - 1)
                    def _(number=number, away=away):
                        ring_copy(number, away, step).wait_send()

            if not first:
                x_copy(number, step, side).wait_send()
        return carry

    lax.fori_loop(0, chips, drain, 0)
    for number in numbers:
        if streams[number][3]:
            x_copy(number, 0, side).wait_send()


def gather_all(shard, chips):
    rows, cols = shard.shape
    tiles = cols // 128
    first = int(round(tiles * 0.43)) // 2 * 2
    rest = tiles - first
    bounds = [0, first // 2, first, first + rest // 2, tiles]
    streams = tuple(
        (128 * bounds[i], 128 * (bounds[i + 1] - bounds[i]), 1 if i % 2 == 0 else -1, i < 2)
        for i in range(4)
    )
    dma = pltpu.SemaphoreType.DMA
    return pl.pallas_call(
        functools.partial(gather_kernel, chips, streams),
        out_shape=jax.ShapeDtypeStruct((rows * 4 * chips, cols), shard.dtype),
        in_specs=[pl.BlockSpec(memory_space=pl.ANY)],
        out_specs=pl.BlockSpec(memory_space=pl.ANY),
        scratch_shapes=[
            dma((4, 2, chips)),
            dma((4, 2, chips)),
            dma((4, chips)),
            dma((4, chips)),
            dma((4, 2, chips)),
            dma((4, 2, chips)),
            dma,
        ],
        compiler_params=pltpu.CompilerParams(collective_id=0, has_side_effects=True),
        cost_estimate=pl.CostEstimate(
            flops=0, bytes_accessed=2 * rows * 4 * chips * cols * 2, transcendentals=0
        ),
        name="gather_all",
    )(shard)


def sum_kernel(chips, streams, counts, *refs):
    arrays, (tile, up_sum, down_sum), outs, (tile_out, up_in, down_in), held, core_in, ring_in, x_in, tiles, sems = refs_of(counts, refs)
    load_sem, core_send, core_recv, ring_send, ring_recv, x_send, x_recv, tile_send, tile_recv, hop_send, hop_recv = sems
    tile_pairs, tile_ring = tiles
    chip = lax.axis_index("zy")
    core = lax.axis_index("core")
    side = lax.axis_index("fsdp")
    spot = ring_spot(chip, chips)
    far = 1 - side

    def neighbour(by):
        return {"zy": ring_chip(spot + chips + by, chips)}

    other_core = {"core": 1 - core}
    other_side = {"fsdp": 1 - side}
    barrier = pltpu.get_barrier_semaphore()
    for peer in (neighbour(1), neighbour(-1), other_core, other_side):
        pl.semaphore_signal(barrier, inc=1, device_id=peer, device_id_type=MESH)
    pl.semaphore_wait(barrier, 4)

    numbers = range(len(streams))

    def owner_at(number, turn):
        return ring_chip(spot + 2 * chips - streams[number][3] * turn, chips)

    def cols(number):
        return pl.ds(streams[number][1], streams[number][2])

    def remote(src, dst, send, recv, peer):
        return pltpu.make_async_remote_copy(
            src_ref=src, dst_ref=dst, send_sem=send, recv_sem=recv, device_id=peer, device_id_type=MESH
        )

    def core_copy(number, turn):
        owner = owner_at(number, turn)
        array = streams[number][0]
        return remote(
            arrays[array].at[owner, 1 - core, :, :, cols(number)],
            core_in[array].at[owner, :, :, cols(number)],
            core_send.at[number, turn - 1],
            core_recv.at[number, turn - 1],
            other_core,
        )

    def x_copy(number, turn):
        array = streams[number][0]
        first = streams[number][4]
        slot = turn - 1 if first else 0
        return remote(
            held[array].at[owner_at(number, turn), far, :, cols(number)],
            x_in[number].at[slot],
            x_send.at[number, slot],
            x_recv.at[number, slot],
            other_side,
        )

    def ring_copy(number, turn):
        array = streams[number][0]
        owner = owner_at(number, turn)
        if streams[number][4]:
            src = held[array].at[owner, pl.ds(side, 1), :, cols(number)]
        else:
            src = held[array].at[owner, :, :, cols(number)]
        return remote(
            src,
            ring_in[number].at[turn - 1],
            ring_send.at[number, turn - 1],
            ring_recv.at[number, turn - 1],
            neighbour(streams[number][3]),
        )

    loads = [
        pltpu.make_async_copy(arrays[i].at[:, core], held[i], load_sem.at[i])
        for i in range(len(arrays))
    ]

    def send_cores(turn, carry):
        for number in numbers:
            core_copy(number, turn).start()
        return carry

    def hop_copy(way, kind):
        src, dst = ((up_sum, up_in), (down_sum, down_in))[way]
        return remote(src.at[kind], dst.at[kind], hop_send.at[way, kind], hop_recv.at[way, kind], neighbour(1 - 2 * way))

    def tile_copy(src, dst, number, peer):
        return remote(src, dst, tile_send.at[number], tile_recv.at[number], peer)

    def tile_turn(turn):
        spot_ref = tile_ring.at[ring_chip(spot + 2 * chips - turn + 1, chips)]
        return tile_copy(spot_ref, spot_ref, turn + 1, neighbour(1))

    def tile_arrival(turn):
        spot_ref = tile_ring.at[ring_chip(spot + 2 * chips - turn, chips)]
        return tile_copy(spot_ref, spot_ref, turn + 1, neighbour(1))

    tile_copy(tile, tile_pairs.at[0], 0, other_core).start()
    lax.fori_loop(1, 2, send_cores, 0)
    for load in loads:
        load.start()
    tile_copy(tile, tile_pairs.at[0], 0, other_core).wait()
    tile_pairs[1] = tile[...] + tile_pairs[0]
    tile_copy(tile_pairs.at[1], tile_pairs.at[2], 1, other_side).start()
    lax.fori_loop(2, chips + 1, send_cores, 0)
    for load in loads:
        load.wait()

    def add_cores(number, turn):
        array = streams[number][0]
        owner = owner_at(number, turn)
        core_copy(number, turn).wait_recv()
        for its_side in range(2):
            held[array][owner, its_side, :, cols(number)] = (
                held[array][owner, its_side, :, cols(number)].astype(F32)
                + core_in[array][owner, its_side, :, cols(number)].astype(F32)
            ).astype(BF16)

    def begin(turn):
        for number in numbers:
            if streams[number][4]:
                add_cores(number, turn)
                x_copy(number, turn).start()

    begin(1)
    tile_copy(tile_pairs.at[1], tile_pairs.at[2], 1, other_side).wait()
    tile_ring[chip] = tile_pairs[1] + tile_pairs[2]

    def round_trip(turn, carry):
        @pl.when(turn > 1)
        def _():
            tile_arrival(turn - 1).wait_recv()

        @pl.when(turn < chips)
        def _():
            tile_turn(turn).start()

        for kind in range(3):

            @pl.when(turn == 1 + kind)
            def _(kind=kind):
                for way in range(2):
                    hop_copy(way, kind).start()

        @pl.when(turn < chips)
        def _():
            begin(turn + 1)

        for number in numbers:
            array = streams[number][0]
            owner = owner_at(number, turn)
            if not streams[number][4]:
                add_cores(number, turn)

                @pl.when(turn > 1)
                def _(number=number, array=array, owner=owner):
                    ring_copy(number, turn - 1).wait_recv()
                    for its_side in range(2):
                        held[array][owner, its_side, :, cols(number)] = (
                            held[array][owner, its_side, :, cols(number)].astype(F32)
                            + ring_in[number][turn - 2, its_side].astype(F32)
                        ).astype(BF16)

                @pl.when(turn < chips)
                def _(number=number):
                    ring_copy(number, turn).start()

        for number in numbers:
            array = streams[number][0]
            owner = owner_at(number, turn)
            if streams[number][4]:
                x_copy(number, turn).wait_recv()

                @pl.when(turn == 1)
                def _(number=number, array=array, owner=owner):
                    held[array][owner, side, :, cols(number)] = (
                        held[array][owner, side, :, cols(number)].astype(F32)
                        + x_in[number][turn - 1].astype(F32)
                    ).astype(BF16)

                @pl.when(turn > 1)
                def _(number=number, array=array, owner=owner):
                    ring_copy(number, turn - 1).wait_recv()
                    total = (
                        held[array][owner, side, :, cols(number)].astype(F32)
                        + x_in[number][turn - 1].astype(F32)
                        + ring_in[number][turn - 2, 0].astype(F32)
                    )
                    held[array][owner, side, :, cols(number)] = total.astype(BF16)

                    @pl.when(turn == chips)
                    def _():
                        outs[array][:, cols(number)] = total

                @pl.when(turn < chips)
                def _(number=number):
                    ring_copy(number, turn).start()

        return carry

    lax.fori_loop(1, chips + 1, round_trip, 0)
    for number in numbers:
        if not streams[number][4]:
            x_copy(number, chips).start()
    tile_out[...] = lax.fori_loop(1, chips, lambda i, total: total + tile_ring[i], tile_ring[0])
    for number in numbers:
        array = streams[number][0]
        if not streams[number][4]:
            x_copy(number, chips).wait_recv()
            outs[array][:, cols(number)] = held[array][chip, side, :, cols(number)].astype(
                F32
            ) + x_in[number][0].astype(F32)

    for kind in range(3):
        for way in range(2):
            hop_copy(way, kind).wait()

    def drain(turn, carry):
        for number in numbers:
            core_copy(number, turn).wait_send()
            if streams[number][4]:
                x_copy(number, turn).wait_send()

            @pl.when(turn < chips)
            def _(number=number):
                ring_copy(number, turn).wait_send()

        @pl.when(turn < chips)
        def _():
            tile_turn(turn).wait_send()

        return carry

    lax.fori_loop(1, chips + 1, drain, 0)
    for number in numbers:
        if not streams[number][4]:
            x_copy(number, chips).wait_send()


def refs_of(counts, refs):
    groups, at = [], 0
    for count in counts:
        groups.append(refs[at : at + count])
        at += count
    return groups


def sum_all(arrays, firsts, tile, up_sum, down_sum, chips):
    rows = arrays[0].shape[0] // (4 * chips)
    streams = []
    for i, (array, first) in enumerate(zip(arrays, firsts)):
        for low, high, is_first in ((0, first, True), (first, array.shape[1], False)):
            left = (high - low) // 256 * 128
            if high > low:
                streams.append((i, low, left, 1, is_first))
                streams.append((i, low + left, high - low - left, -1, is_first))
    streams = tuple(sorted(streams, key=lambda stream: stream[4]))
    count, number = len(arrays), len(streams)
    dma = pltpu.SemaphoreType.DMA
    vmem = pltpu.VMEM
    scratch = (
        [vmem((chips, 2, rows, a.shape[1]), BF16) for a in arrays]
        + [vmem((chips, 2, rows, a.shape[1]), BF16) for a in arrays]
        + [vmem((chips - 1, 1 if first else 2, rows, width), BF16) for _, _, width, _, first in streams]
        + [vmem((chips if first else 1, rows, width), BF16) for _, _, width, _, first in streams]
        + [vmem((3, 8, 128), F32), vmem((chips, 8, 128), F32)]
        + [dma((count,))]
        + [dma((number, chips)) for _ in range(6)]
        + [dma((chips + 1,)) for _ in range(2)]
        + [dma((2, 3)) for _ in range(2)]
    )
    return pl.pallas_call(
        functools.partial(
            sum_kernel, chips, streams, (count, 3, count, 3, count, count, number, number, 2, 11)
        ),
        out_shape=[jax.ShapeDtypeStruct((rows, a.shape[1]), F32) for a in arrays]
        + [jax.ShapeDtypeStruct((8, 128), F32)]
        + [jax.ShapeDtypeStruct(up_sum.shape, BF16)] * 2,
        in_specs=[pl.BlockSpec(memory_space=pl.ANY)] * count
        + [pl.BlockSpec(memory_space=pltpu.VMEM)]
        + [pl.BlockSpec(memory_space=pl.ANY)] * 2,
        out_specs=[pl.BlockSpec(memory_space=pltpu.VMEM)] * (count + 1) + [pl.BlockSpec(memory_space=pl.ANY)] * 2,
        scratch_shapes=scratch,
        compiler_params=pltpu.CompilerParams(
            collective_id=1, has_side_effects=True, vmem_limit_bytes=58 << 20
        ),
        cost_estimate=pl.CostEstimate(
            flops=0, bytes_accessed=sum(2 * a.size for a in arrays), transcendentals=0
        ),
        name="sum_all",
    )(*[a.reshape(chips, 2, 2, rows, a.shape[1]) for a in arrays], tile, up_sum, down_sum)


LITTLE = pl.CostEstimate(flops=0, bytes_accessed=1024, transcendentals=0)
VMEM_LIMIT = 56 << 20


def whole(shape):
    return pl.BlockSpec(shape, lambda *_: (0,) * len(shape))


def piece(kernel, name, grid, in_specs, out_specs, out_shapes, scratch=()):
    return pl.pallas_call(
        kernel,
        grid=grid,
        in_specs=in_specs,
        out_specs=out_specs,
        out_shape=[jax.ShapeDtypeStruct(shape, dtype) for shape, dtype in out_shapes],
        scratch_shapes=list(scratch),
        compiler_params=pltpu.CompilerParams(vmem_limit_bytes=VMEM_LIMIT),
        cost_estimate=LITTLE,
        name=name,
    )


def inverse_rms(values):
    return lax.rsqrt(jnp.mean(values * values, axis=-1, keepdims=True) + EPSILON)


def norm_back(values, gain, grad):
    scale = inverse_rms(values)
    scaled = grad * gain
    mean = jnp.mean(values * scaled, axis=-1, keepdims=True)
    back = scale * scaled - values * (scale * scale * scale * mean)
    return back, jnp.sum(grad * (values * scale), axis=0, keepdims=True)


def qkv_kernel(tokens, gains, head_gain, cosine, sine, weight, low, raw, new):
    at = pl.program_id(0)

    @pl.when(at == 0)
    def _():
        states = tokens[...].astype(F32)
        low[...] = (states * inverse_rms(states) * gains[0:1]).astype(BF16)

    out = full_dot(low[...], weight[...])
    raw[...] = out
    plain = out * inverse_rms(out)
    values = plain * jnp.where(at < HEADS, head_gain[0:1], head_gain[1:2])
    half = HEAD // 2
    first, second = values[:, :half], values[:, half:]
    turned = jnp.concatenate(
        [first * cosine[...] - second * sine[...], second * cosine[...] + first * sine[...]], 1
    )
    new[...] = jnp.where(at < HEADS + KV_HEADS, turned, plain).astype(BF16)


def make_qkv(tokens, gains, head_gain, cosine, sine, full):
    rows = tokens.shape[0]
    heads = HEADS + 2 * KV_HEADS
    return piece(
        qkv_kernel,
        "make_qkv",
        (heads,),
        [
            whole((rows, D)),
            whole(gains.shape),
            whole((2, HEAD)),
            whole(cosine.shape),
            whole(sine.shape),
            pl.BlockSpec((D, HEAD), lambda i: (0, HEADS + i)),
        ],
        [
            whole((rows, D)),
            pl.BlockSpec((rows, HEAD), lambda i: (0, i)),
            pl.BlockSpec((rows, HEAD), lambda i: (0, i)),
        ],
        [((rows, D), BF16), ((rows, heads * HEAD), F32), ((rows, heads * HEAD), BF16)],
    )(tokens, gains, head_gain, cosine, sine, full)


def softmax_of(query, key, visible):
    scores = jnp.where(visible > 0.0, right_dot(query, key), -1e30)
    expo = jnp.exp(scores - jnp.max(scores, axis=-1, keepdims=True))
    return expo / jnp.sum(expo, axis=-1, keepdims=True)


def attend_kernel(
    tokens, gains, low, query, key, value, visible, w_out, lleft, lright,
    context, attn_raw, mixed, ffn_in, mid,
):
    at = pl.program_id(0)
    probs = softmax_of(query[...], key[...], visible[...]).astype(BF16)
    here = full_dot(probs, value[...]).astype(BF16)
    context[...] = here
    term = full_dot(here, w_out[...])

    @pl.when(at == 0)
    def _():
        attn_raw[...] = term

    @pl.when(at > 0)
    def _():
        attn_raw[...] += term

    @pl.when(at == HEADS - 1)
    def _():
        states = tokens[...].astype(F32)
        raw = attn_raw[...]
        total = states + raw * inverse_rms(raw) * gains[1:2]
        total = total + states * inverse_rms(states) * gains[0:1]
        mid[...] = full_dot(low[...], lleft[...]).astype(BF16)
        laurel = right_dot(mid[...], lright[...])
        total = (total + laurel * inverse_rms(laurel) * gains[2:3]) * INV_SQRT2
        mixed[...] = total
        ffn_in[...] = (total * inverse_rms(total) * gains[3:4]).astype(BF16)


def attend(tokens, gains, low, qkv, keys_all, visible, full):
    rows = tokens.shape[0]
    seen = keys_all.shape[0]
    group = HEADS // KV_HEADS
    side = 128
    left_at, right_at = full.shape[1] // side - 2, full.shape[1] // side - 1
    return piece(
        attend_kernel,
        "attend",
        (HEADS,),
        [
            whole((rows, D)),
            whole(gains.shape),
            whole((rows, D)),
            pl.BlockSpec((rows, HEAD), lambda i: (0, i)),
            pl.BlockSpec((seen, HEAD), lambda i: (0, i // group)),
            pl.BlockSpec((seen, HEAD), lambda i: (0, KV_HEADS + i // group)),
            whole((rows, seen)),
            pl.BlockSpec((HEAD, D), lambda i: (i, 0)),
            pl.BlockSpec((D, side), lambda i: (0, left_at)),
            pl.BlockSpec((D, side), lambda i: (0, right_at)),
        ],
        [
            pl.BlockSpec((rows, HEAD), lambda i: (0, i)),
            whole((rows, D)),
            whole((rows, D)),
            whole((rows, D)),
            whole((rows, side)),
        ],
        [
            ((rows, HEADS * HEAD), BF16),
            ((rows, D), F32),
            ((rows, D), F32),
            ((rows, D), BF16),
            ((rows, side), BF16),
        ],
    )(tokens, gains, low, qkv, keys_all, keys_all, visible, full, full, full)


def load_weights(weights, held, sems):
    copies, at = [], 0
    for number, ref in enumerate(weights):
        count = ref.shape[1]
        copies.append(pltpu.make_async_copy(ref, held.at[:, pl.ds(at, count)], sems.at[number]))
        at += count

    @pl.when(pl.program_id(0) == 0)
    def _():
        for copy in copies:
            copy.start()
        for copy in copies:
            copy.wait()


ROW_BLOCK = 256
UNIT_BLOCK = 512


def unit_blocks(steps, units):
    many = max(1, UNIT_BLOCK // units)
    return [range(first, min(first + many, steps)) for first in range(0, steps, many)]


def ffn_forward_kernel(steps, add, last, *refs):
    weights, refs = refs[: 2 * steps], refs[2 * steps :]
    if add:
        before, refs = refs[0], refs[1:]
    rows, total, refs = refs[0], refs[1], refs[2:]
    if last:
        low_total, refs = refs[0], refs[1:]
    gates, uppers, hiddens, (held, sems) = refs_of((steps, steps, steps, 2), refs)
    load_weights(weights, held, sems)
    units = held.shape[1] // steps
    here = rows[...]
    running = before[...] if add else None
    for block in unit_blocks(steps, units):
        cut = slice(block[0] * units, (block[-1] + 1) * units)
        gate_in = right_dot(here, held[0, cut])
        upper_in = right_dot(here, held[1, cut])
        low = gated_product(gate_in, upper_in).astype(BF16)
        for i, step in enumerate(block):
            own = slice(i * units, (i + 1) * units)
            gates[step][...] = gate_in[:, own]
            uppers[step][...] = upper_in[:, own]
            hiddens[step][...] = low[:, own]
        term = full_dot(low, held[2, cut])
        running = term if running is None else running + term
    write_sum(running, total, low_total if last else None)


def write_sum(running, total, low_total):
    if low_total is None:
        total[...] = running
        return
    half = pl.num_programs(0) // 2

    @pl.when(pl.program_id(0) < half)
    def _():
        low_total[...] = running.astype(BF16)

    @pl.when(pl.program_id(0) >= half)
    def _():
        total[...] = running


def sum_specs(many, last):
    blocks = many // ROW_BLOCK
    half = blocks // 2
    if not last:
        return (lambda i: i), [pl.BlockSpec((ROW_BLOCK, D), lambda i: (i, 0))], [((many, D), F32)]
    specs = [
        pl.BlockSpec((ROW_BLOCK, D), lambda i: (jnp.maximum(i - half, 0), 0)),
        pl.BlockSpec((ROW_BLOCK, D), lambda i: (jnp.minimum(i, half - 1), 0)),
    ]
    return (lambda i: lax.rem(i + half, blocks)), specs, [((many // 2, D), F32), ((many // 2, D), BF16)]


def ffn_forward(rows, before, weights, last):
    many = rows.shape[0]
    steps, units = len(weights) // 2, 2 * weights[0].shape[1]
    at, sums, sum_shapes = sum_specs(many, last)
    by_row = lambda width: pl.BlockSpec((ROW_BLOCK, width), lambda i: (at(i), 0))
    add = before is not None
    outs = piece(
        functools.partial(ffn_forward_kernel, steps, add, last),
        "ffn_forward",
        (many // ROW_BLOCK,),
        [pl.BlockSpec(memory_space=pl.ANY)] * len(weights) + [by_row(D)] * (1 + add),
        sums + [by_row(units)] * (3 * steps),
        sum_shapes + [((many, units), F32)] * (2 * steps) + [((many, units), BF16)] * steps,
        [pltpu.VMEM((3, steps * units, D), BF16), pltpu.SemaphoreType.DMA((len(weights),))],
    )(*weights, *([before] if add else []), rows)
    return refs_of((len(sums), steps, steps, steps), outs)


def ffn_backward_kernel(steps, add, last, *refs):
    weights, refs = refs[: 2 * steps], refs[2 * steps :]
    if add:
        before, refs = refs[0], refs[1:]
    (rows,), gates, uppers, totals, grad_gates, grad_uppers, (held, sems) = refs_of(
        (1, steps, steps, 1 + last, steps, steps, 2), refs
    )
    load_weights(weights, held, sems)
    units = held.shape[1] // steps
    here = rows[...]
    running = before[...] if add else None
    for block in unit_blocks(steps, units):
        cut = slice(block[0] * units, (block[-1] + 1) * units)
        grad_hidden = right_dot(here, held[2, cut])
        low_gates, low_uppers = [], []
        for i, step in enumerate(block):
            unused, act_back = jax.vjp(gated_product, gates[step][...], uppers[step][...])
            back_gate, back_upper = act_back(grad_hidden[:, i * units : (i + 1) * units])
            low_gates.append(back_gate.astype(BF16))
            low_uppers.append(back_upper.astype(BF16))
            grad_gates[step][...] = low_gates[-1]
            grad_uppers[step][...] = low_uppers[-1]
        term = full_dot(jnp.concatenate(low_gates, 1), held[0, cut])
        term = term + full_dot(jnp.concatenate(low_uppers, 1), held[1, cut])
        running = term if running is None else running + term
    write_sum(running, totals[0], totals[1] if last else None)


def ffn_backward(rows, before, weights, gates, uppers, last):
    many = rows.shape[0]
    steps, units = len(gates), gates[0].shape[1]
    at, sums, sum_shapes = sum_specs(many, last)
    by_row = lambda width: pl.BlockSpec((ROW_BLOCK, width), lambda i: (at(i), 0))
    add = before is not None
    outs = piece(
        functools.partial(ffn_backward_kernel, steps, add, last),
        "ffn_backward",
        (many // ROW_BLOCK,),
        [pl.BlockSpec(memory_space=pl.ANY)] * len(weights)
        + [by_row(D)] * (1 + add)
        + [by_row(units)] * (2 * steps),
        sums + [by_row(units)] * (2 * steps),
        sum_shapes + [((many, units), BF16)] * (2 * steps),
        [pltpu.VMEM((3, steps * units, D), BF16), pltpu.SemaphoreType.DMA((len(weights),))],
    )(*weights, *([before] if add else []), rows, *gates, *uppers)
    return refs_of((len(sums), steps, steps), outs)


def unit_grads_kernel(grad_gate, grad_upper, hidden, rows, down_rows, up_out, down_out):
    half = up_out.shape[1]
    pairs = ((grad_gate, rows), (grad_upper, rows), (hidden, down_rows))
    for kind, (left, right) in enumerate(pairs):
        out = left_dot(left[...], right[...]).astype(BF16)
        up_out[kind] = out[:half]
        down_out[kind] = out[half:]


def unit_grads_of(grad_gate, grad_upper, hidden, rows, down_rows):
    many, units = hidden.shape
    width = 1024
    narrow = whole((many, units))
    wide = pl.BlockSpec((many, width), lambda i: (0, i))
    part = pl.BlockSpec((3, units // 2, width), lambda i: (0, 0, i))
    return piece(
        unit_grads_kernel,
        "unit_grads",
        (D // width,),
        [narrow, narrow, narrow, wide, wide],
        [part, part],
        [((3, units // 2, D), BF16)] * 2,
    )(grad_gate, grad_upper, hidden, rows, down_rows)


def attend_back_kernel(
    gains, grad_in, grad_after, mixed, attn_raw, mid, low, lleft, lright, w_out, context, query, key, value, visible,
    grad_mixed, grad_mid, grad_gains, grad_left, grad_right, grad_w_out, grad_query, grad_key, grad_value,
    grad_attn,
):
    at = pl.program_id(0)

    @pl.when(at == 0)
    def _():
        back, gain_3 = norm_back(mixed[...], gains[3:4], grad_in[...])
        total = (grad_after[...] + back) * INV_SQRT2
        grad_mixed[...] = total
        back, gain_2 = norm_back(right_dot(mid[...], lright[...]), gains[2:3], total)
        back_low = back.astype(BF16)
        grad_right[...] = left_dot(back_low, mid[...])
        mid_low = full_dot(back_low, lright[...]).astype(BF16)
        grad_mid[...] = mid_low
        grad_left[...] = left_dot(low[...], mid_low)
        back, gain_1 = norm_back(attn_raw[...], gains[1:2], total)
        grad_attn[...] = back.astype(BF16)
        grad_gains[...] = jnp.concatenate(
            [gain_1, gain_2, gain_3, jnp.zeros((5, D), F32)], 0
        )

    grad_context = right_dot(grad_attn[...], w_out[...]).astype(BF16)
    grad_w_out[...] = left_dot(context[...], grad_attn[...]).astype(BF16)
    probs = softmax_of(query[...], key[...], visible[...])
    grad_probs = right_dot(grad_context, value[...])
    inner = jnp.sum(probs * grad_probs, axis=-1, keepdims=True)
    grad_scores = (probs * (grad_probs - inner)).astype(BF16)
    grad_query[...] = full_dot(grad_scores, key[...])
    key_term = left_dot(grad_scores, query[...])
    value_term = left_dot(probs.astype(BF16), grad_context)
    group = HEADS // KV_HEADS

    @pl.when(lax.rem(at, group) == 0)
    def _():
        grad_key[...] = key_term
        grad_value[...] = value_term

    @pl.when(lax.rem(at, group) > 0)
    def _():
        grad_key[...] += key_term
        grad_value[...] += value_term


def attend_back(gains, grad_in, grad_after, mixed, attn_raw, mid, low, full, context, qkv, keys_all, visible):
    rows = low.shape[0]
    seen = keys_all.shape[0]
    group = HEADS // KV_HEADS
    side = 128
    left_at, right_at = full.shape[1] // side - 2, full.shape[1] // side - 1
    head = pl.BlockSpec((rows, HEAD), lambda i: (0, i))
    once = lambda shape: pl.BlockSpec(shape, lambda i: (0, 0), pipeline_mode=pl.Buffered(1))
    return piece(
        attend_back_kernel,
        "attend_back",
        (HEADS,),
        [
            whole(gains.shape),
            once((rows, D)),
            once((rows, D)),
            once((rows, D)),
            once((rows, D)),
            whole((rows, side)),
            whole((rows, D)),
            pl.BlockSpec((D, side), lambda i: (0, left_at)),
            pl.BlockSpec((D, side), lambda i: (0, right_at)),
            pl.BlockSpec((HEAD, D), lambda i: (i, 0)),
            head,
            head,
            pl.BlockSpec((seen, HEAD), lambda i: (0, i // group)),
            pl.BlockSpec((seen, HEAD), lambda i: (0, KV_HEADS + i // group)),
            whole((rows, seen)),
        ],
        [
            whole((rows, D)),
            whole((rows, side)),
            whole((8, D)),
            whole((D, side)),
            whole((D, side)),
            pl.BlockSpec((HEAD, D), lambda i: (i, 0)),
            head,
            pl.BlockSpec((seen, HEAD), lambda i: (0, i // group)),
            pl.BlockSpec((seen, HEAD), lambda i: (0, i // group)),
        ],
        [
            ((rows, D), F32),
            ((rows, side), BF16),
            ((8, D), F32),
            ((D, side), F32),
            ((D, side), F32),
            ((HEADS * HEAD, D), BF16),
            ((rows, HEADS * HEAD), F32),
            ((seen, KV_HEADS * HEAD), F32),
            ((seen, KV_HEADS * HEAD), F32),
        ],
        [pltpu.VMEM((rows, D), BF16)],
    )(
        gains, grad_in, grad_after, mixed, attn_raw, mid, low, full, full, full, context, qkv, keys_all, keys_all,
        visible,
    )


def turn_back(grad, cosine, sine):
    half = HEAD // 2
    first, second = grad[:, :half], grad[:, half:]
    return jnp.concatenate([first * cosine + second * sine, second * cosine - first * sine], 1)


def query_back_kernel(grad_query, raw, cosine, sine, head_gain, low, weight, grad_w, grad_low, grad_head):
    at = pl.program_id(0)
    turned = turn_back(grad_query[...], cosine[...], sine[...])
    back, gain = norm_back(raw[...], head_gain[0:1], turned)
    back_low = back.astype(BF16)
    grad_w[...] = left_dot(low[...], back_low).astype(BF16)
    term = right_dot(back_low, weight[...])

    @pl.when(at == 0)
    def _():
        grad_low[...] = term
        grad_head[...] = gain

    @pl.when(at > 0)
    def _():
        grad_low[...] += term
        grad_head[...] += gain


def query_back(grad_query, raw, cosine, sine, head_gain, low, full):
    rows = low.shape[0]
    head = pl.BlockSpec((rows, HEAD), lambda i: (0, i))
    return piece(
        query_back_kernel,
        "query_back",
        (HEADS,),
        [
            head,
            head,
            whole(cosine.shape),
            whole(sine.shape),
            whole((2, HEAD)),
            whole((rows, D)),
            pl.BlockSpec((D, HEAD), lambda i: (0, HEADS + i)),
        ],
        [pl.BlockSpec((D, HEAD), lambda i: (0, i)), whole((rows, D)), whole((1, HEAD))],
        [((D, HEADS * HEAD), BF16), ((rows, D), F32), ((1, HEAD), F32)],
    )(grad_query, raw, cosine, sine, head_gain, low, full)


def key_back_kernel(
    grad_kv, raw, cosine, sine, head_gain, low, weight, before, grad_mixed, grad_mid, lleft, tokens, gains,
    grad_w, grad_tokens, grad_head, grad_gain, total,
):
    at = pl.program_id(0)
    is_key = at < KV_HEADS
    grad = grad_kv[...]
    turned = jnp.where(is_key, turn_back(grad, cosine[...], sine[...]), grad)
    back, gain = norm_back(raw[...], jnp.where(is_key, head_gain[1:2], 1.0), turned)
    back_low = back.astype(BF16)
    grad_w[...] = left_dot(low[...], back_low).astype(BF16)
    term = right_dot(back_low, weight[...])

    @pl.when(at == 0)
    def _():
        total[...] = before[...] + term
        grad_head[...] = gain

    @pl.when(at > 0)
    def _():
        total[...] += term
        grad_head[...] += jnp.where(is_key, gain, 0.0)

    @pl.when(at == 2 * KV_HEADS - 1)
    def _():
        grad_normed = total[...] + grad_mixed[...] + right_dot(grad_mid[...], lleft[...])
        back, gain_0 = norm_back(tokens[...].astype(F32), gains[0:1], grad_normed)
        grad_tokens[...] = grad_mixed[...] + back
        grad_gain[...] = gain_0


def key_back(grad_kv, raw, cosine, sine, head_gain, low, full, before, grad_mixed, grad_mid, tokens, gains):
    rows = low.shape[0]
    side = 128
    left_at = full.shape[1] // side - 2
    return piece(
        key_back_kernel,
        "key_back",
        (2 * KV_HEADS,),
        [
            pl.BlockSpec((rows, HEAD), lambda i: (0, i)),
            pl.BlockSpec((rows, HEAD), lambda i: (0, HEADS + i)),
            whole(cosine.shape),
            whole(sine.shape),
            whole((2, HEAD)),
            whole((rows, D)),
            pl.BlockSpec((D, HEAD), lambda i: (0, 2 * HEADS + i)),
            whole((rows, D)),
            whole((rows, D)),
            whole((rows, side)),
            pl.BlockSpec((D, side), lambda i: (0, left_at)),
            whole((rows, D)),
            whole(gains.shape),
        ],
        [
            pl.BlockSpec((D, HEAD), lambda i: (0, i)),
            whole((rows, D)),
            whole((1, HEAD)),
            whole((1, D)),
        ],
        [
            ((D, 2 * KV_HEADS * HEAD), BF16),
            ((rows, D), F32),
            ((1, HEAD), F32),
            ((1, D), F32),
        ],
        [pltpu.VMEM((rows, D), F32)],
    )(grad_kv, raw, cosine, sine, head_gain, low, full, before, grad_mixed, grad_mid, full, tokens, gains)


def tie(*values):
    return lax.optimization_barrier(values)


def shares(total, count):
    return [total // count + (1 if i < total % count else 0) for i in range(count)]


def greet(peers):
    barrier = pltpu.get_barrier_semaphore()
    for peer in peers:
        pl.semaphore_signal(barrier, inc=1, device_id=peer, device_id_type=MESH)
    pl.semaphore_wait(barrier, len(peers))


def partners():
    return {"core": 1 - lax.axis_index("core")}, {"fsdp": 1 - lax.axis_index("fsdp")}


CUTS = 8
FLYING = 2


def spread_kernel(own, rows, x_send, x_recv, near_send, near_recv, far_send, far_recv, own_sem):
    count = own.shape[0]
    cut = count // CUTS
    other_core, other_side = partners()
    greet((other_core, other_side))

    def copy(src, block, at, send, recv, peer):
        return pltpu.make_async_remote_copy(
            src_ref=src,
            dst_ref=rows.at[pl.ds(block * count + at * cut, cut)],
            send_sem=send.at[at],
            recv_sem=recv.at[at],
            device_id=peer,
            device_id_type=MESH,
        )

    mine = [own.at[pl.ds(at * cut, cut)] for at in range(CUTS)]
    came = [rows.at[pl.ds(count + at * cut, cut)] for at in range(CUTS)]
    across = [copy(mine[at], 1, at, x_send, x_recv, other_side) for at in range(CUTS)]
    near = [copy(mine[at], 2, at, near_send, near_recv, other_core) for at in range(CUTS)]
    far = [copy(came[at], 3, at, far_send, far_recv, other_core) for at in range(CUTS)]
    for one in across[:FLYING] + near:
        one.start()
    keep = pltpu.make_async_copy(own, rows.at[pl.ds(0, count)], own_sem)
    keep.start()
    for at in range(CUTS):
        across[at].wait_send()
        if at + FLYING < CUTS:
            across[at + FLYING].start()
        across[at].wait_recv()
        far[at].start()
    for one in near + far:
        one.wait()
    keep.wait()


def rows_of_four(own, number):
    count = own.shape[0]
    dma = pltpu.SemaphoreType.DMA
    return pl.pallas_call(
        spread_kernel,
        out_shape=jax.ShapeDtypeStruct((4 * count, D), BF16),
        in_specs=[pl.BlockSpec(memory_space=pltpu.VMEM)],
        out_specs=pl.BlockSpec(memory_space=pl.ANY),
        scratch_shapes=[dma((CUTS,)) for _ in range(6)] + [dma],
        compiler_params=pltpu.CompilerParams(collective_id=number, has_side_effects=True),
        cost_estimate=LITTLE,
        name="spread_rows",
    )(own)


def gather_sum_kernel(steps, *refs):
    if steps:
        (own, low, rows, down_rows), sides, (out,), grads, more, held, sems = refs_of(
            (4, 3 * steps, 1, 2 * steps, 4 + 4, 3, 3), refs
        )
        core_in, pair_low, x_in, parts, *copy_sems = more
        core_send, core_recv, x_send, x_recv = copy_sems
        rows_in, down_in, more_out = held
        loads_sem, parts_sem, grads_sem = sems
        parts_out = more_out

        def store(step, way):
            return pltpu.make_async_copy(parts_out.at[step, way], grads[2 * step + way], grads_sem.at[step, way])

        loads = [
            pltpu.make_async_copy(rows, rows_in, loads_sem.at[0]),
            pltpu.make_async_copy(down_rows, down_in, loads_sem.at[1]),
        ]
        part_loads = [
            pltpu.make_async_copy(side, parts.at[number], parts_sem.at[number]) for number, side in enumerate(sides)
        ]
        for load in loads + part_loads:
            load.start()
    else:
        own, low, out, core_in, pair_low, x_in, core_send, core_recv, x_send, x_recv = refs
    count = out.shape[0]
    cut = count // CUTS
    other_core, other_side = partners()
    greet((other_core, other_side))

    def core_copy(block, at):
        here = pl.ds(block * count + at * cut, cut)
        number = block * CUTS + at
        return pltpu.make_async_remote_copy(
            src_ref=low.at[here],
            dst_ref=core_in.at[here],
            send_sem=core_send.at[number],
            recv_sem=core_recv.at[number],
            device_id=other_core,
            device_id_type=MESH,
        )

    def x_copy(at):
        here = pl.ds(at * cut, cut)
        return pltpu.make_async_remote_copy(
            src_ref=pair_low.at[here],
            dst_ref=x_in.at[here],
            send_sem=x_send.at[at],
            recv_sem=x_recv.at[at],
            device_id=other_side,
            device_id_type=MESH,
        )

    pieces = [(block, at) for block in (1, 0) for at in range(CUTS)]

    def next_piece(number):
        core_copy(*pieces[number]).wait_send()
        if number + FLYING < len(pieces):
            core_copy(*pieces[number + FLYING]).start()

    for one in pieces[:FLYING]:
        core_copy(*one).start()
    for at in range(CUTS):
        there = pl.ds(count + at * cut, cut)
        next_piece(at)
        core_copy(1, at).wait_recv()
        pair_low[pl.ds(at * cut, cut)] = (own[there] + core_in[there].astype(F32)).astype(BF16)
        x_copy(at).start()
    for at in range(CUTS):
        here = pl.ds(at * cut, cut)
        next_piece(CUTS + at)
        core_copy(0, at).wait_recv()
        out[here] = own[here] + core_in[here].astype(F32)
    if steps:
        for load in loads:
            load.wait()
        half = grads[0].shape[1]
        width = D // 2
        for step in range(steps):
            for kind in range(3):
                number = 3 * step + kind
                part_loads[number].wait()
                left, right = parts[number], down_in if kind == 2 else rows_in
                for first in range(0, D, width):
                    cols = slice(first, first + width)
                    term = left_dot(left, right[:, cols]).astype(BF16)
                    parts_out[step, 0, kind, :, cols] = term[:half]
                    parts_out[step, 1, kind, :, cols] = term[half:]
            for way in range(2):
                store(step, way).start()
    for at in range(CUTS):
        here = pl.ds(at * cut, cut)
        x_copy(at).wait_recv()
        out[here] += x_in[here].astype(F32)
    for at in range(CUTS):
        x_copy(at).wait_send()
    for step in range(steps):
        for way in range(2):
            store(step, way).wait()


def sum_of_four(own, low, number, units=(), rows=None, down_rows=None):
    count = own.shape[0] // 2
    steps = len(units)
    dma = pltpu.SemaphoreType.DMA
    vmem, anywhere = pltpu.VMEM, pl.BlockSpec(memory_space=pl.ANY)
    scratch = [vmem((2 * count, D), BF16), vmem((count, D), BF16), vmem((count, D), BF16)]
    copy_sems = [dma((2 * CUTS,)), dma((2 * CUTS,)), dma((CUTS,)), dma((CUTS,))]
    operands, shapes = [], []
    if steps:
        many, width = units[0][0].shape
        operands = [rows, down_rows] + [side for sides in units for side in sides]
        shapes = [jax.ShapeDtypeStruct((3, width // 2, D), BF16)] * (2 * steps)
        scratch += [vmem((3 * steps, many, width), BF16)]
        copy_sems += [vmem((many, D), BF16), vmem((many, D), BF16), vmem((steps, 2, 3, width // 2, D), BF16)]
        copy_sems += [dma((2,)), dma((3 * steps,)), dma((steps, 2))]
    total, *grads = pl.pallas_call(
        functools.partial(gather_sum_kernel, steps),
        out_shape=[jax.ShapeDtypeStruct((count, D), F32)] + shapes,
        in_specs=[pl.BlockSpec(memory_space=pltpu.VMEM), anywhere] + [anywhere] * len(operands),
        out_specs=[pl.BlockSpec(memory_space=pltpu.VMEM)] + [anywhere] * len(shapes),
        scratch_shapes=scratch + copy_sems,
        compiler_params=pltpu.CompilerParams(
            collective_id=number, has_side_effects=True, vmem_limit_bytes=VMEM_LIMIT
        ),
        cost_estimate=LITTLE,
        name="gather_sum",
    )(own, low, *operands)
    return total, [(grads[2 * i], grads[2 * i + 1]) for i in range(steps)]


PARTS = 4


def middle_kernel(
    own, low, mixed, layer_in, teacher, mask, scale, gains, gate_w, proj_w,
    result, grad_after, grad_layer, rows, grad_gate_w, grad_proj_w, grad_gains, squares,
    own_in, mixed_in, teacher_in, gate_in, proj_in, core_in, pair_low, x_in,
    result_out, after_out, after_low, mid_low, grad_pl, grad_raw, grad_low,
    loads, stores, core_send, core_recv, x_send, x_recv, y_send, y_recv, near_send, near_recv, far_send, far_recv,
):
    count = mixed.shape[0]
    cut = count // PARTS
    other_core, other_side = partners()

    def load(number, src, dst):
        return pltpu.make_async_copy(src, dst, loads.at[number])

    incoming = [
        load(0, own.at[pl.ds(count, count)], own_in.at[pl.ds(count, count)]),
        load(1, own.at[pl.ds(0, count)], own_in.at[pl.ds(0, count)]),
        load(2, mixed, mixed_in),
        load(3, gate_w, gate_in),
        load(4, proj_w, proj_in),
        load(5, teacher, teacher_in),
    ]
    for one in incoming:
        one.start()
    greet((other_core, other_side))

    def remote(src, dst, send, recv, peer):
        return pltpu.make_async_remote_copy(
            src_ref=src, dst_ref=dst, send_sem=send, recv_sem=recv, device_id=peer, device_id_type=MESH
        )

    def piece_of(at):
        return pl.ds(at * cut, cut)

    def core_copy(block, at):
        here = pl.ds(block * count + at * cut, cut)
        number = block * PARTS + at
        return remote(low.at[here], core_in.at[here], core_send.at[number], core_recv.at[number], other_core)

    def x_copy(at):
        here = piece_of(at)
        return remote(pair_low.at[here], x_in.at[here], x_send.at[at], x_recv.at[at], other_side)

    def out_copy(src, block, at, send, recv, peer):
        return remote(src, rows.at[pl.ds(block * count + at * cut, cut)], send.at[at], recv.at[at], peer)

    def across(at):
        return out_copy(grad_low.at[piece_of(at)], 1, at, y_send, y_recv, other_side)

    def near(at):
        return out_copy(grad_low.at[piece_of(at)], 2, at, near_send, near_recv, other_core)

    def far(at):
        return out_copy(rows.at[pl.ds(count + at * cut, cut)], 3, at, far_send, far_recv, other_core)

    def kept(number, at):
        here = piece_of(at)
        src, dst = ((result_out, result), (after_out, grad_after), (grad_low, rows))[number]
        return pltpu.make_async_copy(src.at[here], dst.at[here], stores.at[number, at])

    for block in (1, 0):
        for at in range(PARTS):
            core_copy(block, at).start()
    incoming[0].wait()
    for at in range(PARTS):
        there = pl.ds(count + at * cut, cut)
        core_copy(1, at).wait_recv()
        pair_low[piece_of(at)] = (own_in[there] + core_in[there].astype(F32)).astype(BF16)
        x_copy(at).start()
    for one in incoming[1:]:
        one.wait()
    gain_4, gain_5 = gains[4:5], gains[5:6]
    total = jnp.zeros((), F32)
    sum_4 = sum_5 = jnp.zeros((1, D), F32)
    for at in range(PARTS):
        here = piece_of(at)
        core_copy(0, at).wait_recv()
        x_copy(at).wait_recv()
        down = own_in[here] + core_in[here].astype(F32) + x_in[here].astype(F32)
        after = mixed_in[here] + down * inverse_rms(down) * gain_4
        low_here = after.astype(BF16)
        after_low[here] = low_here
        raw = full_dot(low_here, gate_in[...])
        act, act_back = jax.vjp(gelu_tanh, raw)
        layer = layer_in[here].astype(F32)
        mid = (act * layer).astype(BF16)
        mid_low[here] = mid
        out = full_dot(mid, proj_in[...])
        done = after + out * inverse_rms(out) * gain_5
        result_out[here] = done
        kept(0, at).start()
        errors = done - teacher_in[here].astype(F32)
        masked = mask[here][:, 0:1] * errors
        total += jnp.sum(masked * errors)
        grad_out = masked * scale[0:1, 0:1]
        back, term = norm_back(out, gain_5, grad_out)
        sum_5 += term
        back_low = back.astype(BF16)
        grad_pl[here] = back_low
        grad_mid = right_dot(back_low, proj_in[...])
        grad_layer[here] = grad_mid * act
        raw_low = act_back(grad_mid * layer)[0].astype(BF16)
        grad_raw[here] = raw_low
        grad_here = grad_out + right_dot(raw_low, gate_in[...])
        after_out[here] = grad_here
        kept(1, at).start()
        back, term = norm_back(down, gain_4, grad_here)
        sum_4 += term
        grad_low[here] = back.astype(BF16)
        across(at).start()
        near(at).start()
        kept(2, at).start()
    grad_gains[...] = jnp.concatenate([sum_4, sum_5, jnp.zeros((6, D), F32)], 0)
    squares[...] = jnp.broadcast_to(total, squares.shape)
    for at in range(PARTS // 2):
        across(at).wait_recv()
        far(at).start()
    grad_proj_w[...] = left_dot(mid_low[...], grad_pl[...]).astype(BF16)
    grad_gate_w[...] = left_dot(after_low[...], grad_raw[...]).astype(BF16)
    for at in range(PARTS // 2, PARTS):
        across(at).wait_recv()
        far(at).start()
    for at in range(PARTS):
        far(at).wait()
        near(at).wait()
        across(at).wait_send()
        x_copy(at).wait_send()
        for block in (0, 1):
            core_copy(block, at).wait_send()
        for number in range(3):
            kept(number, at).wait()


def middle(own, low, mixed, layer_in, teacher, mask, scale, gains, gate_w, proj_w):
    count = mixed.shape[0]
    dma, vmem = pltpu.SemaphoreType.DMA, pltpu.VMEM
    anywhere, inside = pl.BlockSpec(memory_space=pl.ANY), pl.BlockSpec(memory_space=pltpu.VMEM)
    shape = jax.ShapeDtypeStruct
    return pl.pallas_call(
        middle_kernel,
        out_shape=[
            shape((count, D), F32),
            shape((count, D), F32),
            shape((count, PLD), F32),
            shape((4 * count, D), BF16),
            shape((D, PLD), BF16),
            shape((PLD, D), BF16),
            shape((8, D), F32),
            shape((8, 128), F32),
        ],
        in_specs=[anywhere, anywhere, anywhere, inside, anywhere, inside, inside, inside, anywhere, anywhere],
        out_specs=[anywhere, anywhere, inside, anywhere, inside, inside, inside, inside],
        scratch_shapes=[
            vmem((2 * count, D), F32),
            vmem((count, D), F32),
            vmem((count, D), BF16),
            vmem((D, PLD), BF16),
            vmem((PLD, D), BF16),
            vmem((2 * count, D), BF16),
            vmem((count, D), BF16),
            vmem((count, D), BF16),
            vmem((count, D), F32),
            vmem((count, D), F32),
            vmem((count, D), BF16),
            vmem((count, PLD), BF16),
            vmem((count, D), BF16),
            vmem((count, PLD), BF16),
            vmem((count, D), BF16),
            dma((6,)),
            dma((3, PARTS)),
            dma((2 * PARTS,)),
            dma((2 * PARTS,)),
        ]
        + [dma((PARTS,)) for _ in range(8)],
        compiler_params=pltpu.CompilerParams(
            collective_id=3, has_side_effects=True, vmem_limit_bytes=VMEM_LIMIT
        ),
        cost_estimate=LITTLE,
        name="middle",
    )(own, low, mixed, layer_in, teacher, mask, scale, gains, gate_w, proj_w)


def body(
    tokens,
    per_layer,
    teacher,
    cont_lengths,
    w_query,
    w_kv,
    w_out,
    laurel_left,
    laurel_right,
    pl_gate,
    pl_proj,
    norm_gains,
    head_gains,
    ffn_weight,
):
    row_count = tokens.shape[1]
    chips = lax.axis_size("zy")
    seq_count = 2 * chips
    group_count = lax.axis_size("fsdp")
    shards = seq_count * group_count
    chip = lax.axis_index("zy")
    core = lax.axis_index("core")
    seq_index = chip * 2 + core
    group_index = lax.axis_index("fsdp")
    half_point = seq_count // 2
    prompt_len = half_point * row_count
    cont_shards = CONT_LEN // row_count
    cont_count = prompt_len // CONT_LEN
    is_cont = seq_index >= half_point
    rel_index = seq_index - half_point
    local_shard = jnp.where(is_cont, rel_index % cont_shards, 0)
    cont_index = jnp.where(is_cont, rel_index // cont_shards, 0)
    first_place = jnp.where(is_cont, prompt_len + local_shard * row_count, seq_index * row_count)
    row_range = jnp.arange(row_count, dtype=jnp.int32)
    places = first_place + row_range
    group_lengths = jnp.sum(
        jnp.where(
            jnp.arange(group_count, dtype=jnp.int32)[:, None] == group_index, cont_lengths, 0
        ),
        axis=0,
    )
    my_length = jnp.sum(
        jnp.where(jnp.arange(cont_count, dtype=jnp.int32) == cont_index, group_lengths, 0)
    )
    valid = jnp.logical_or(
        jnp.logical_not(is_cont), local_shard * row_count + row_range < my_length
    )
    weight_mask = valid.astype(F32)
    count = F32(group_count * prompt_len) + jnp.sum(cont_lengths).astype(F32)
    total_slots = float(row_count * seq_count * group_count)
    shard_rows = w_query.shape[0]
    key_cols = KV_HEADS * HEAD
    proj_cols = pl_proj.shape[0] * D // shard_rows
    misc_cols = RANK
    head_part = head_gains.reshape(-1, 1)
    misc = jnp.concatenate(
        [
            norm_gains.T,
            jnp.pad(head_part, ((0, shard_rows - head_part.shape[0]), (0, 0))),
            jnp.zeros((shard_rows, misc_cols - 7), BF16),
        ],
        1,
    )
    pack = jnp.concatenate(
        [
            w_out,
            w_query,
            w_kv,
            pl_gate,
            pl_proj.reshape(shard_rows, proj_cols),
            laurel_left,
            misc,
            laurel_right.T,
            jnp.zeros((shard_rows, 128 - RANK), BF16),
        ],
        1,
    )

    units = ffn_weight.shape[0]
    half = units // 2
    by_kind = ffn_weight.transpose(1, 0, 2)
    ups, downs = [by_kind[:, :half]], [by_kind[:, half:]]
    stage_steps = shares(chips - 1, 7)

    def pass_on(stage):
        for _ in range(stage_steps[stage]):
            ups.append(ring(ups[-1], 1))
            downs.append(ring(downs[-1], -1))

    def stage_end(values):
        (ups[-1], downs[-1]), values = tie((ups[-1], downs[-1]), values)
        return values

    pass_on(0)
    full = gather_all(pack, chips)
    at = 2 * D + 2 * key_cols
    plg = full[:, at : at + PLD]
    plp = full[:, at + PLD : at + PLD + proj_cols].reshape(PLD, D)
    at += PLD + proj_cols + RANK
    misc_full = stage_end(full[:, at : at + misc_cols])
    pass_on(1)
    gains = jnp.pad(misc_full[:, :6].T.astype(F32), ((0, 2), (0, 0)))
    head_n = head_gains.shape[1]
    head_gain = (
        misc_full[:, 6]
        .reshape(shards, shard_rows)[:, : 2 * head_n]
        .reshape(shards, 2, head_n)
        .transpose(1, 0, 2)
        .reshape(2, HEAD)
        .astype(F32)
    )
    freqs = jnp.exp(
        jnp.arange(HEAD // 2, dtype=F32) * (-2.0 * math.log(ROPE_BASE) / HEAD)
    )
    angles = places.astype(F32)[:, None] * freqs
    cosine, sine = jnp.cos(angles), jnp.sin(angles)
    normed_low, qkv_raw, qkv = make_qkv(tokens[0], gains, head_gain, cosine, sine, full)
    qkv = stage_end(qkv)
    kv_own = qkv[:, D:]
    pass_on(2)

    mid = chips // 2
    chain = [(i, i + 1) for i in range(mid - 1)] + [(mid - 1, mid + 1)]
    kv_before = jnp.where(
        chip == mid,
        lax.ppermute(kv_own, "zy", [(mid - 1, mid)]),
        lax.ppermute(kv_own, "zy", chain),
    )
    spans = []
    span = 2
    while span < mid:
        spans.append(span)
        span *= 2
    for span in spans:
        moved = lax.ppermute(
            kv_before, "zy", [(mid + i, mid + i + span) for i in range(min(span, mid - span))]
        )
        fresh = jnp.logical_and(chip >= mid + span, chip < mid + 2 * span)
        kv_before = jnp.where(fresh, moved, kv_before)
    kv_other = swap(jnp.where(core == 0, kv_own, kv_before), "core")
    keys_all = jnp.concatenate([kv_before, kv_other, kv_own], 0)
    keys_all = stage_end(keys_all)
    pass_on(3)
    key_len = keys_all.shape[0]
    key_places = first_place - 2 * row_count + jnp.arange(key_len, dtype=jnp.int32)
    visible = (
        (key_places[None, :] <= places[:, None])
        & (places[:, None] - key_places[None, :] < WINDOW)
        & (key_places[None, :] >= 0)
    ).astype(F32)
    context_low, attn_raw, mixed, ffn_in, laurel_mid = attend(
        tokens[0], gains, normed_low, qkv, keys_all, visible, full
    )

    ffn_in = stage_end(ffn_in)
    pass_on(4)
    ffn_rows = stage_end(rows_of_four(ffn_in, 2))
    here = len(ups)
    pass_on(5)
    gates, uppers, hiddens = [], [], []

    def weights_of(steps):
        return [w for k in steps for w in (ups[k], downs[k])]

    def forward_part(running, first, end, last=False):
        sums, gate, upper, hidden = ffn_forward(ffn_rows, running, weights_of(range(first, end)), last)
        gates.extend(gate)
        uppers.extend(upper)
        hiddens.extend(hidden)
        return sums if last else sums[0]

    running = stage_end(forward_part(None, 0, here))
    then = len(ups)
    pass_on(6)
    running = stage_end(forward_part(running, here, then))
    own_sum, low_sum = forward_part(running, then, chips, True)
    result, grad_after, grad_layer_in, grad_down_rows, grad_plg, grad_plp, late_gains, squares = middle(
        own_sum,
        low_sum,
        mixed,
        per_layer[0],
        teacher[0],
        jnp.broadcast_to(weight_mask[:, None], (row_count, 128)),
        jnp.broadcast_to(total_slots / count, (8, 128)),
        gains,
        plg,
        plp,
    )
    grad_gates, grad_uppers = [None] * chips, [None] * chips

    def backward_part(steps, running, last=False):
        sums, grad_gate, grad_upper = ffn_backward(
            grad_down_rows, running, weights_of(steps), [gates[k] for k in steps], [uppers[k] for k in steps], last
        )
        for k, gg, gu in zip(steps, grad_gate, grad_upper):
            grad_gates[k], grad_uppers[k] = gg, gu
        return sums if last else sums[0]

    ready = {}

    def unit_grads(k):
        if k in ready:
            return ready[k]
        return unit_grads_of(grad_gates[k], grad_uppers[k], hiddens[k], ffn_rows, grad_down_rows)

    order = list(range(1, chips)) + [0]
    ring_steps = shares(chips - 2, 6)
    done = 0

    def beside(stage, work):
        nonlocal done, up_sum, down_sum
        values = None
        for step in range(ring_steps[stage]):
            up_in = ring(up_sum, 1)
            down_in = ring(down_sum, -1)
            if step == 0:
                values = work()
            done += 1
            terms = unit_grads(order[done])
            (up_in, down_in), terms, values = tie((up_in, down_in), terms, values)
            up_sum = (up_in.astype(F32) + terms[0].astype(F32)).astype(BF16)
            down_sum = (down_in.astype(F32) + terms[1].astype(F32)).astype(BF16)
        return work() if values is None else values

    first = ring_steps[0]
    then = first + 1 + ring_steps[0] + ring_steps[1]
    running = backward_part(order[:first], None)
    up_sum, down_sum = unit_grads(order[0])
    running = beside(0, lambda: backward_part(order[first:then], running))
    own_sum, low_sum = beside(1, lambda: backward_part(order[then:], running, True))

    def work():
        steps = order[done + ring_steps[2] :] if units % 128 == 0 else []
        total, grads = sum_of_four(
            own_sum,
            low_sum,
            5,
            [(grad_gates[k], grad_uppers[k], hiddens[k]) for k in steps],
            ffn_rows,
            grad_down_rows,
        )
        ready.update(zip(steps, grads))
        return total

    grad_ffn_in = beside(2, work)
    def work():
        *out, grad_keys, grad_values = attend_back(
            gains, grad_ffn_in, grad_after, mixed, attn_raw, laurel_mid, normed_low, full, context_low, qkv, keys_all,
            visible,
        )
        grad_kv = jnp.concatenate([grad_keys, grad_values], 1)
        grad_before = grad_kv[:row_count]
        grad_own = grad_kv[2 * row_count :]
        returned = swap(grad_kv[row_count : 2 * row_count].astype(BF16), "core").astype(F32)
        grad_own = grad_own + jnp.where(core == 0, returned, 0.0)
        grad_before = grad_before + jnp.where(core == 0, 0.0, returned)
        return out, grad_own, grad_before

    out, grad_own, grad_before = beside(3, work)
    (
        grad_scaled,
        grad_mid_low,
        grad_mid_gains,
        grad_lleft,
        grad_lright_t,
        grad_wo,
        grad_queries,
    ) = out

    def work():
        total = grad_before
        for span in reversed(spans):
            back = [(mid + i + span, mid + i) for i in range(min(span, mid - span))]
            total = total + lax.ppermute(total.astype(BF16), "zy", back).astype(F32)
        before_low = total.astype(BF16)
        return (
            grad_own
            + lax.ppermute(before_low, "zy", [(b, a) for a, b in chain]).astype(F32)
            + lax.ppermute(before_low, "zy", [(mid, mid - 1)]).astype(F32)
        ), query_back(grad_queries, qkv_raw, cosine, sine, head_gain, normed_low, full)

    grad_own, (grad_wq, grad_normed, grad_hq) = beside(4, work)

    def work():
        grad_wkv, grad_tokens, grad_hk, grad_g0 = key_back(
            grad_own, qkv_raw, cosine, sine, head_gain, normed_low, full, grad_normed, grad_scaled, grad_mid_low,
            tokens[0], gains,
        )
        head_back = jnp.concatenate([grad_hq, grad_hk], 0).reshape(2, shards, head_n).transpose(1, 0, 2)
        head_back = head_back.reshape(shards, 2 * head_n)
        head_back = jnp.pad(head_back, ((0, 0), (0, shard_rows - 2 * head_n))).reshape(1, D)
        misc_back = jnp.concatenate(
            [grad_g0, grad_mid_gains[:3], late_gains[:2], head_back, jnp.zeros((1, D), F32)], 0
        )
        return grad_wkv, grad_tokens, jnp.concatenate(
            [
                grad_plg,
                grad_plp.reshape(D, proj_cols),
                grad_lleft[:, :RANK].astype(BF16),
                jnp.pad(misc_back.T, ((0, 0), (0, misc_cols - 8))).astype(BF16),
                grad_lright_t.astype(BF16),
            ],
            1,
        )

    last_terms, (grad_wkv, grad_tokens, rest_back) = beside(5, lambda: (unit_grads(0), work()))
    sums_wq, sums_wkv, sums_wo, sums_rest, total, up_in, down_in = sum_all(
        [grad_wq, grad_wkv, grad_wo, rest_back],
        (D, 2 * key_cols, D - 512, 0),
        squares,
        up_sum,
        down_sum,
        chips,
    )
    grad_ffn = jnp.concatenate(
        [
            (arrived.astype(F32) + term.astype(F32)).transpose(1, 0, 2)
            for arrived, term in zip((up_in, down_in), last_terms)
        ],
        0,
    )
    at = 0
    rest = []
    for width in (PLD, proj_cols, RANK, misc_cols, RANK):
        rest.append(sums_rest[:, at : at + width])
        at += width

    match_loss = total[0, 0] / (2.0 * D * count)

    return (
        result[None],
        match_loss,
        grad_tokens[None],
        grad_layer_in[None],
        sums_wq,
        sums_wkv,
        sums_wo,
        rest[2],
        rest[4].T,
        rest[0],
        rest[1].reshape(pl_proj.shape),
        rest[3][:, :6].T,
        rest[3][: 2 * head_n, 6].reshape(2, head_n),
        grad_ffn,
    )


def solution(mesh):
    seq, fsdp = mesh.shape["seq"], mesh.shape["fsdp"]
    fine = Mesh(mesh.devices.reshape(seq // 2, 2, fsdp), ("zy", "core", "fsdp"))
    rows = P("fsdp", ("zy", "core"), None)
    split = ("zy", "core", "fsdp")
    weights = (
        P(split, None),
        P(split, None),
        P(split, None),
        P(split, None),
        P(None, split),
        P(split, None),
        P(split, None),
        P(None, split),
        P(None, split),
        P(split, None, None),
    )
    return jax.shard_map(
        body,
        mesh=fine,
        in_specs=(rows, rows, rows, P()) + weights,
        out_specs=(rows, P(), rows, rows) + weights,
        check_vma=False,
    )
```

```python
import functools
import math

import jax
import jax.numpy as jnp
from jax import lax
from jax.experimental import pallas as pl
from jax.experimental.pallas import tpu as pltpu
from jax.sharding import Mesh, PartitionSpec as P

D = 2048
HEADS = 8
KV_HEADS = 2
HEAD = 256
WINDOW = 512
CONT_LEN = 512
RANK = 64
PLD = 256

EPSILON = 1e-06
INV_SQRT2 = 0.7071067811865476
ROPE_BASE = 10000.0
BF16 = jnp.bfloat16
F32 = jnp.float32


def gelu_tanh(values):
    return jax.nn.gelu(values, approximate=True)


def gated_product(gate_in, up_in):
    return gelu_tanh(gate_in) * up_in


def full_dot(left, right):
    return jnp.dot(left, right, preferred_element_type=F32)


def left_dot(left, right):
    return lax.dot_general(left, right, (((0,), (0,)), ((), ())), preferred_element_type=F32)


def right_dot(left, right):
    return lax.dot_general(left, right, (((1,), (1,)), ((), ())), preferred_element_type=F32)


def ring_order(n):
    return list(range(0, n, 2)) + list(range(n - 1, 0, -2))


def ring_pairs(n, by):
    order = ring_order(n)
    return [(order[i], order[(i + by) % n]) for i in range(n)]


def ring(value, by):
    return lax.ppermute(value, "zy", ring_pairs(lax.axis_size("zy"), by))


def swap(value, axis):
    return lax.ppermute(value, axis, [(0, 1), (1, 0)])


MESH = pl.DeviceIdType.MESH


def ring_chip(spot, chips):
    spot = lax.rem(spot, chips)
    return jnp.where(spot < chips // 2, 2 * spot, 2 * (chips - 1 - spot) + 1)


def ring_spot(chip, chips):
    return jnp.where(lax.rem(chip, 2) == 0, chip // 2, chips - 1 - chip // 2)


def gather_kernel(chips, streams, shard, full, ring_send, ring_recv, x_send, x_recv, core_send, core_recv, own_sem):
    chip = lax.axis_index("zy")
    core = lax.axis_index("core")
    side = lax.axis_index("fsdp")
    spot = ring_spot(chip, chips)
    rows = shard.shape[0]

    def neighbour(by):
        return {"zy": ring_chip(spot + chips + by, chips)}

    other_core = {"core": 1 - core}
    other_side = {"fsdp": 1 - side}

    barrier = pltpu.get_barrier_semaphore()
    for peer in (neighbour(1), neighbour(-1), other_core, other_side):
        pl.semaphore_signal(barrier, inc=1, device_id=peer, device_id_type=MESH)
    pl.semaphore_wait(barrier, 4)

    def place(owner, its_core, its_side, stream):
        row = ((owner * 2 + its_core) * 2 + its_side) * rows
        return full.at[pl.ds(pl.multiple_of(row, rows), rows), pl.ds(stream[0], stream[1])]

    def owner_at(step, stream):
        return ring_chip(spot + chips - stream[2] * step, chips)

    def send(src, dst, sems, at, peer):
        return pltpu.make_async_remote_copy(
            src_ref=src,
            dst_ref=dst,
            send_sem=sems[0].at[at],
            recv_sem=sems[1].at[at],
            device_id=peer,
            device_id_type=MESH,
        )

    ring_sems, x_sems, core_sems = (ring_send, ring_recv), (x_send, x_recv), (core_send, core_recv)

    def ring_copy(number, away, step, src=None):
        stream = streams[number]
        its_side = 1 - side if away else side
        spot_ref = place(owner_at(step, stream), core, its_side, stream)
        return send(src if src is not None else spot_ref, spot_ref, ring_sems, (number, away, step), neighbour(stream[2]))

    def ring_arrival(number, away, step):
        stream = streams[number]
        its_side = 1 - side if away else side
        spot_ref = place(owner_at(step, stream), core, its_side, stream)
        return send(spot_ref, spot_ref, ring_sems, (number, away, step - 1), neighbour(stream[2]))

    def x_copy(number, step, its_side, src=None):
        stream = streams[number]
        spot_ref = place(owner_at(step, stream), core, its_side, stream)
        return send(src if src is not None else spot_ref, spot_ref, x_sems, (number, step), other_side)

    def core_copy(number, away, step, its_core, src=None):
        stream = streams[number]
        its_side = 1 - side if away else side
        spot_ref = place(owner_at(step, stream), its_core, its_side, stream)
        return send(src if src is not None else spot_ref, spot_ref, core_sems, (number, away, step), other_core)

    def cut(stream):
        return shard.at[:, pl.ds(stream[0], stream[1])]

    own_row = ((chip * 2 + core) * 2 + side) * rows
    own = pltpu.make_async_copy(
        shard, full.at[pl.ds(pl.multiple_of(own_row, rows), rows), :], own_sem
    )
    own.start()
    numbers = range(len(streams))
    for number in numbers:
        if streams[number][3]:
            x_copy(number, 0, side, cut(streams[number])).start()
    for number in numbers:
        ring_copy(number, 0, 0, cut(streams[number])).start()
    for number in numbers:
        if not streams[number][3]:
            x_copy(number, 0, side, cut(streams[number])).start()
    for number in numbers:
        core_copy(number, 0, 0, core, cut(streams[number])).start()
    for number in numbers:
        if streams[number][3]:
            x_copy(number, 0, 1 - side).wait_recv()
            ring_copy(number, 1, 0).start()
            core_copy(number, 1, 0, core).start()

    def turn(step, carry):
        for number in numbers:
            aways = (0, 1) if streams[number][3] else (0,)
            for away in aways:
                ring_arrival(number, away, step).wait_recv()

                @pl.when(step < chips - 1)
                def _(number=number, away=away):
                    ring_copy(number, away, step).start()

                core_copy(number, away, step, core).start()
            if not streams[number][3]:
                x_copy(number, step, side).start()
        for number in numbers:
            if not streams[number][3]:
                x_copy(number, step - 1, 1 - side).wait_recv()
                core_copy(number, 1, step - 1, core).start()
        return carry

    lax.fori_loop(1, chips, turn, 0)
    for number in numbers:
        if not streams[number][3]:
            x_copy(number, chips - 1, 1 - side).wait_recv()
            core_copy(number, 1, chips - 1, core).start()
    own.wait()

    def drain(step, carry):
        for number in numbers:
            first = streams[number][3]
            for away in (0, 1):
                core_copy(number, away, step, 1 - core).wait_recv()
                core_copy(number, away, step, core).wait_send()
                if first or not away:

                    @pl.when(step < chips - 1)
                    def _(number=number, away=away):
                        ring_copy(number, away, step).wait_send()

            if not first:
                x_copy(number, step, side).wait_send()
        return carry

    lax.fori_loop(0, chips, drain, 0)
    for number in numbers:
        if streams[number][3]:
            x_copy(number, 0, side).wait_send()


def gather_all(shard, chips):
    rows, cols = shard.shape
    tiles = cols // 128
    first = int(round(tiles * 0.43)) // 2 * 2
    rest = tiles - first
    bounds = [0, first // 2, first, first + rest // 2, tiles]
    streams = tuple(
        (128 * bounds[i], 128 * (bounds[i + 1] - bounds[i]), 1 if i % 2 == 0 else -1, i < 2)
        for i in range(4)
    )
    dma = pltpu.SemaphoreType.DMA
    return pl.pallas_call(
        functools.partial(gather_kernel, chips, streams),
        out_shape=jax.ShapeDtypeStruct((rows * 4 * chips, cols), shard.dtype),
        in_specs=[pl.BlockSpec(memory_space=pl.ANY)],
        out_specs=pl.BlockSpec(memory_space=pl.ANY),
        scratch_shapes=[
            dma((4, 2, chips)),
            dma((4, 2, chips)),
            dma((4, chips)),
            dma((4, chips)),
            dma((4, 2, chips)),
            dma((4, 2, chips)),
            dma,
        ],
        compiler_params=pltpu.CompilerParams(collective_id=0, has_side_effects=True),
        cost_estimate=pl.CostEstimate(
            flops=0, bytes_accessed=2 * rows * 4 * chips * cols * 2, transcendentals=0
        ),
        name="gather_all",
    )(shard)


def sum_kernel(chips, streams, counts, *refs):
    arrays, (tile, up_sum, down_sum), outs, (tile_out, up_in, down_in), held, core_in, ring_in, x_in, tiles, sems = refs_of(counts, refs)
    load_sem, core_send, core_recv, ring_send, ring_recv, x_send, x_recv, tile_send, tile_recv, hop_send, hop_recv = sems
    tile_pairs, tile_ring = tiles
    chip = lax.axis_index("zy")
    core = lax.axis_index("core")
    side = lax.axis_index("fsdp")
    spot = ring_spot(chip, chips)
    far = 1 - side

    def neighbour(by):
        return {"zy": ring_chip(spot + chips + by, chips)}

    other_core = {"core": 1 - core}
    other_side = {"fsdp": 1 - side}
    barrier = pltpu.get_barrier_semaphore()
    for peer in (neighbour(1), neighbour(-1), other_core, other_side):
        pl.semaphore_signal(barrier, inc=1, device_id=peer, device_id_type=MESH)
    pl.semaphore_wait(barrier, 4)

    numbers = range(len(streams))

    def owner_at(number, turn):
        return ring_chip(spot + 2 * chips - streams[number][3] * turn, chips)

    def cols(number):
        return pl.ds(streams[number][1], streams[number][2])

    def remote(src, dst, send, recv, peer):
        return pltpu.make_async_remote_copy(
            src_ref=src, dst_ref=dst, send_sem=send, recv_sem=recv, device_id=peer, device_id_type=MESH
        )

    def core_copy(number, turn):
        owner = owner_at(number, turn)
        array = streams[number][0]
        return remote(
            arrays[array].at[owner, 1 - core, :, :, cols(number)],
            core_in[array].at[owner, :, :, cols(number)],
            core_send.at[number, turn - 1],
            core_recv.at[number, turn - 1],
            other_core,
        )

    def x_copy(number, turn):
        array = streams[number][0]
        first = streams[number][4]
        slot = turn - 1 if first else 0
        return remote(
            held[array].at[owner_at(number, turn), far, :, cols(number)],
            x_in[number].at[slot],
            x_send.at[number, slot],
            x_recv.at[number, slot],
            other_side,
        )

    def ring_copy(number, turn):
        array = streams[number][0]
        owner = owner_at(number, turn)
        if streams[number][4]:
            src = held[array].at[owner, pl.ds(side, 1), :, cols(number)]
        else:
            src = held[array].at[owner, :, :, cols(number)]
        return remote(
            src,
            ring_in[number].at[turn - 1],
            ring_send.at[number, turn - 1],
            ring_recv.at[number, turn - 1],
            neighbour(streams[number][3]),
        )

    loads = [
        pltpu.make_async_copy(arrays[i].at[:, core], held[i], load_sem.at[i])
        for i in range(len(arrays))
    ]

    def send_cores(turn, carry):
        for number in numbers:
            core_copy(number, turn).start()
        return carry

    def hop_copy(way, kind):
        src, dst = ((up_sum, up_in), (down_sum, down_in))[way]
        return remote(src.at[kind], dst.at[kind], hop_send.at[way, kind], hop_recv.at[way, kind], neighbour(1 - 2 * way))

    def tile_copy(src, dst, number, peer):
        return remote(src, dst, tile_send.at[number], tile_recv.at[number], peer)

    def tile_turn(turn):
        spot_ref = tile_ring.at[ring_chip(spot + 2 * chips - turn + 1, chips)]
        return tile_copy(spot_ref, spot_ref, turn + 1, neighbour(1))

    def tile_arrival(turn):
        spot_ref = tile_ring.at[ring_chip(spot + 2 * chips - turn, chips)]
        return tile_copy(spot_ref, spot_ref, turn + 1, neighbour(1))

    tile_copy(tile, tile_pairs.at[0], 0, other_core).start()
    lax.fori_loop(1, 2, send_cores, 0)
    for load in loads:
        load.start()
    tile_copy(tile, tile_pairs.at[0], 0, other_core).wait()
    tile_pairs[1] = tile[...] + tile_pairs[0]
    tile_copy(tile_pairs.at[1], tile_pairs.at[2], 1, other_side).start()
    lax.fori_loop(2, chips + 1, send_cores, 0)
    for load in loads:
        load.wait()

    def add_cores(number, turn):
        array = streams[number][0]
        owner = owner_at(number, turn)
        core_copy(number, turn).wait_recv()
        for its_side in range(2):
            held[array][owner, its_side, :, cols(number)] = (
                held[array][owner, its_side, :, cols(number)].astype(F32)
                + core_in[array][owner, its_side, :, cols(number)].astype(F32)
            ).astype(BF16)

    def begin(turn):
        for number in numbers:
            if streams[number][4]:
                add_cores(number, turn)
                x_copy(number, turn).start()

    begin(1)
    tile_copy(tile_pairs.at[1], tile_pairs.at[2], 1, other_side).wait()
    tile_ring[chip] = tile_pairs[1] + tile_pairs[2]

    def round_trip(turn, carry):
        @pl.when(turn > 1)
        def _():
            tile_arrival(turn - 1).wait_recv()

        @pl.when(turn < chips)
        def _():
            tile_turn(turn).start()

        for kind in range(3):

            @pl.when(turn == 1 + kind)
            def _(kind=kind):
                for way in range(2):
                    hop_copy(way, kind).start()

        @pl.when(turn < chips)
        def _():
            begin(turn + 1)

        for number in numbers:
            array = streams[number][0]
            owner = owner_at(number, turn)
            if not streams[number][4]:
                add_cores(number, turn)

                @pl.when(turn > 1)
                def _(number=number, array=array, owner=owner):
                    ring_copy(number, turn - 1).wait_recv()
                    for its_side in range(2):
                        held[array][owner, its_side, :, cols(number)] = (
                            held[array][owner, its_side, :, cols(number)].astype(F32)
                            + ring_in[number][turn - 2, its_side].astype(F32)
                        ).astype(BF16)

                @pl.when(turn < chips)
                def _(number=number):
                    ring_copy(number, turn).start()

        for number in numbers:
            array = streams[number][0]
            owner = owner_at(number, turn)
            if streams[number][4]:
                x_copy(number, turn).wait_recv()

                @pl.when(turn == 1)
                def _(number=number, array=array, owner=owner):
                    held[array][owner, side, :, cols(number)] = (
                        held[array][owner, side, :, cols(number)].astype(F32)
                        + x_in[number][turn - 1].astype(F32)
                    ).astype(BF16)

                @pl.when(turn > 1)
                def _(number=number, array=array, owner=owner):
                    ring_copy(number, turn - 1).wait_recv()
                    total = (
                        held[array][owner, side, :, cols(number)].astype(F32)
                        + x_in[number][turn - 1].astype(F32)
                        + ring_in[number][turn - 2, 0].astype(F32)
                    )
                    held[array][owner, side, :, cols(number)] = total.astype(BF16)

                    @pl.when(turn == chips)
                    def _():
                        outs[array][:, cols(number)] = total

                @pl.when(turn < chips)
                def _(number=number):
                    ring_copy(number, turn).start()

        return carry

    lax.fori_loop(1, chips + 1, round_trip, 0)
    for number in numbers:
        if not streams[number][4]:
            x_copy(number, chips).start()
    tile_out[...] = lax.fori_loop(1, chips, lambda i, total: total + tile_ring[i], tile_ring[0])
    for number in numbers:
        array = streams[number][0]
        if not streams[number][4]:
            x_copy(number, chips).wait_recv()
            outs[array][:, cols(number)] = held[array][chip, side, :, cols(number)].astype(
                F32
            ) + x_in[number][0].astype(F32)

    for kind in range(3):
        for way in range(2):
            hop_copy(way, kind).wait()

    def drain(turn, carry):
        for number in numbers:
            core_copy(number, turn).wait_send()
            if streams[number][4]:
                x_copy(number, turn).wait_send()

            @pl.when(turn < chips)
            def _(number=number):
                ring_copy(number, turn).wait_send()

        @pl.when(turn < chips)
        def _():
            tile_turn(turn).wait_send()

        return carry

    lax.fori_loop(1, chips + 1, drain, 0)
    for number in numbers:
        if not streams[number][4]:
            x_copy(number, chips).wait_send()


def refs_of(counts, refs):
    groups, at = [], 0
    for count in counts:
        groups.append(refs[at : at + count])
        at += count
    return groups


def sum_all(arrays, firsts, tile, up_sum, down_sum, chips):
    rows = arrays[0].shape[0] // (4 * chips)
    streams = []
    for i, (array, first) in enumerate(zip(arrays, firsts)):
        for low, high, is_first in ((0, first, True), (first, array.shape[1], False)):
            left = (high - low) // 256 * 128
            if high > low:
                streams.append((i, low, left, 1, is_first))
                streams.append((i, low + left, high - low - left, -1, is_first))
    streams = tuple(sorted(streams, key=lambda stream: stream[4]))
    count, number = len(arrays), len(streams)
    dma = pltpu.SemaphoreType.DMA
    vmem = pltpu.VMEM
    scratch = (
        [vmem((chips, 2, rows, a.shape[1]), BF16) for a in arrays]
        + [vmem((chips, 2, rows, a.shape[1]), BF16) for a in arrays]
        + [vmem((chips - 1, 1 if first else 2, rows, width), BF16) for _, _, width, _, first in streams]
        + [vmem((chips if first else 1, rows, width), BF16) for _, _, width, _, first in streams]
        + [vmem((3, 8, 128), F32), vmem((chips, 8, 128), F32)]
        + [dma((count,))]
        + [dma((number, chips)) for _ in range(6)]
        + [dma((chips + 1,)) for _ in range(2)]
        + [dma((2, 3)) for _ in range(2)]
    )
    return pl.pallas_call(
        functools.partial(
            sum_kernel, chips, streams, (count, 3, count, 3, count, count, number, number, 2, 11)
        ),
        out_shape=[jax.ShapeDtypeStruct((rows, a.shape[1]), F32) for a in arrays]
        + [jax.ShapeDtypeStruct((8, 128), F32)]
        + [jax.ShapeDtypeStruct(up_sum.shape, BF16)] * 2,
        in_specs=[pl.BlockSpec(memory_space=pl.ANY)] * count
        + [pl.BlockSpec(memory_space=pltpu.VMEM)]
        + [pl.BlockSpec(memory_space=pl.ANY)] * 2,
        out_specs=[pl.BlockSpec(memory_space=pltpu.VMEM)] * (count + 1) + [pl.BlockSpec(memory_space=pl.ANY)] * 2,
        scratch_shapes=scratch,
        compiler_params=pltpu.CompilerParams(
            collective_id=1, has_side_effects=True, vmem_limit_bytes=58 << 20
        ),
        cost_estimate=pl.CostEstimate(
            flops=0, bytes_accessed=sum(2 * a.size for a in arrays), transcendentals=0
        ),
        name="sum_all",
    )(*[a.reshape(chips, 2, 2, rows, a.shape[1]) for a in arrays], tile, up_sum, down_sum)


LITTLE = pl.CostEstimate(flops=0, bytes_accessed=1024, transcendentals=0)
VMEM_LIMIT = 56 << 20


def whole(shape):
    return pl.BlockSpec(shape, lambda *_: (0,) * len(shape))


def piece(kernel, name, grid, in_specs, out_specs, out_shapes, scratch=()):
    return pl.pallas_call(
        kernel,
        grid=grid,
        in_specs=in_specs,
        out_specs=out_specs,
        out_shape=[jax.ShapeDtypeStruct(shape, dtype) for shape, dtype in out_shapes],
        scratch_shapes=list(scratch),
        compiler_params=pltpu.CompilerParams(vmem_limit_bytes=VMEM_LIMIT),
        cost_estimate=LITTLE,
        name=name,
    )


def inverse_rms(values):
    return lax.rsqrt(jnp.mean(values * values, axis=-1, keepdims=True) + EPSILON)


def norm_back(values, gain, grad):
    scale = inverse_rms(values)
    scaled = grad * gain
    mean = jnp.mean(values * scaled, axis=-1, keepdims=True)
    back = scale * scaled - values * (scale * scale * scale * mean)
    return back, jnp.sum(grad * (values * scale), axis=0, keepdims=True)


def qkv_kernel(tokens, gains, head_gain, cosine, sine, weight, low, raw, new):
    at = pl.program_id(0)

    @pl.when(at == 0)
    def _():
        states = tokens[...].astype(F32)
        low[...] = (states * inverse_rms(states) * gains[0:1]).astype(BF16)

    out = full_dot(low[...], weight[...])
    raw[...] = out
    plain = out * inverse_rms(out)
    values = plain * jnp.where(at < HEADS, head_gain[0:1], head_gain[1:2])
    half = HEAD // 2
    first, second = values[:, :half], values[:, half:]
    turned = jnp.concatenate(
        [first * cosine[...] - second * sine[...], second * cosine[...] + first * sine[...]], 1
    )
    new[...] = jnp.where(at < HEADS + KV_HEADS, turned, plain).astype(BF16)


def make_qkv(tokens, gains, head_gain, cosine, sine, full):
    rows = tokens.shape[0]
    heads = HEADS + 2 * KV_HEADS
    return piece(
        qkv_kernel,
        "make_qkv",
        (heads,),
        [
            whole((rows, D)),
            whole(gains.shape),
            whole((2, HEAD)),
            whole(cosine.shape),
            whole(sine.shape),
            pl.BlockSpec((D, HEAD), lambda i: (0, HEADS + i)),
        ],
        [
            whole((rows, D)),
            pl.BlockSpec((rows, HEAD), lambda i: (0, i)),
            pl.BlockSpec((rows, HEAD), lambda i: (0, i)),
        ],
        [((rows, D), BF16), ((rows, heads * HEAD), F32), ((rows, heads * HEAD), BF16)],
    )(tokens, gains, head_gain, cosine, sine, full)


def softmax_of(query, key, visible):
    scores = jnp.where(visible > 0.0, right_dot(query, key), -1e30)
    expo = jnp.exp(scores - jnp.max(scores, axis=-1, keepdims=True))
    return expo / jnp.sum(expo, axis=-1, keepdims=True)


def attend_kernel(
    tokens, gains, low, query, key, value, visible, w_out, lleft, lright,
    context, attn_raw, mixed, ffn_in, mid,
):
    at = pl.program_id(0)
    probs = softmax_of(query[...], key[...], visible[...]).astype(BF16)
    here = full_dot(probs, value[...]).astype(BF16)
    context[...] = here
    term = full_dot(here, w_out[...])

    @pl.when(at == 0)
    def _():
        attn_raw[...] = term

    @pl.when(at > 0)
    def _():
        attn_raw[...] += term

    @pl.when(at == HEADS - 1)
    def _():
        states = tokens[...].astype(F32)
        raw = attn_raw[...]
        total = states + raw * inverse_rms(raw) * gains[1:2]
        total = total + states * inverse_rms(states) * gains[0:1]
        mid[...] = full_dot(low[...], lleft[...]).astype(BF16)
        laurel = right_dot(mid[...], lright[...])
        total = (total + laurel * inverse_rms(laurel) * gains[2:3]) * INV_SQRT2
        mixed[...] = total
        ffn_in[...] = (total * inverse_rms(total) * gains[3:4]).astype(BF16)


def attend(tokens, gains, low, qkv, keys_all, visible, full):
    rows = tokens.shape[0]
    seen = keys_all.shape[0]
    group = HEADS // KV_HEADS
    side = 128
    left_at, right_at = full.shape[1] // side - 2, full.shape[1] // side - 1
    return piece(
        attend_kernel,
        "attend",
        (HEADS,),
        [
            whole((rows, D)),
            whole(gains.shape),
            whole((rows, D)),
            pl.BlockSpec((rows, HEAD), lambda i: (0, i)),
            pl.BlockSpec((seen, HEAD), lambda i: (0, i // group)),
            pl.BlockSpec((seen, HEAD), lambda i: (0, KV_HEADS + i // group)),
            whole((rows, seen)),
            pl.BlockSpec((HEAD, D), lambda i: (i, 0)),
            pl.BlockSpec((D, side), lambda i: (0, left_at)),
            pl.BlockSpec((D, side), lambda i: (0, right_at)),
        ],
        [
            pl.BlockSpec((rows, HEAD), lambda i: (0, i)),
            whole((rows, D)),
            whole((rows, D)),
            whole((rows, D)),
            whole((rows, side)),
        ],
        [
            ((rows, HEADS * HEAD), BF16),
            ((rows, D), F32),
            ((rows, D), F32),
            ((rows, D), BF16),
            ((rows, side), BF16),
        ],
    )(tokens, gains, low, qkv, keys_all, keys_all, visible, full, full, full)


def load_weights(weights, held, sems):
    copies, at = [], 0
    for number, ref in enumerate(weights):
        count = ref.shape[1]
        copies.append(pltpu.make_async_copy(ref, held.at[:, pl.ds(at, count)], sems.at[number]))
        at += count

    @pl.when(pl.program_id(0) == 0)
    def _():
        for copy in copies:
            copy.start()
        for copy in copies:
            copy.wait()


ROW_BLOCK = 256
UNIT_BLOCK = 512


def unit_blocks(steps, units):
    many = max(1, UNIT_BLOCK // units)
    return [range(first, min(first + many, steps)) for first in range(0, steps, many)]


def ffn_forward_kernel(steps, add, *refs):
    weights, refs = refs[: 2 * steps], refs[2 * steps :]
    if add:
        before, refs = refs[0], refs[1:]
    rows, total, refs = refs[0], refs[1], refs[2:]
    gates, uppers, hiddens, (held, sems) = refs_of((steps, steps, steps, 2), refs)
    load_weights(weights, held, sems)
    units = held.shape[1] // steps
    here = rows[...]
    running = before[...] if add else None
    for block in unit_blocks(steps, units):
        cut = slice(block[0] * units, (block[-1] + 1) * units)
        gate_in = right_dot(here, held[0, cut])
        upper_in = right_dot(here, held[1, cut])
        low = gated_product(gate_in, upper_in).astype(BF16)
        for i, step in enumerate(block):
            own = slice(i * units, (i + 1) * units)
            gates[step][...] = gate_in[:, own]
            uppers[step][...] = upper_in[:, own]
            hiddens[step][...] = low[:, own]
        term = full_dot(low, held[2, cut])
        running = term if running is None else running + term
    total[...] = running


def write_sum(running, total, low_total):
    if low_total is None:
        total[...] = running
        return
    half = pl.num_programs(0) // 2

    @pl.when(pl.program_id(0) < half)
    def _():
        low_total[...] = running.astype(BF16)

    @pl.when(pl.program_id(0) >= half)
    def _():
        total[...] = running


def sum_specs(many, last):
    blocks = many // ROW_BLOCK
    half = blocks // 2
    if not last:
        return (lambda i: i), [pl.BlockSpec((ROW_BLOCK, D), lambda i: (i, 0))], [((many, D), F32)]
    specs = [
        pl.BlockSpec((ROW_BLOCK, D), lambda i: (jnp.maximum(i - half, 0), 0)),
        pl.BlockSpec((ROW_BLOCK, D), lambda i: (jnp.minimum(i, half - 1), 0)),
    ]
    return (lambda i: lax.rem(i + half, blocks)), specs, [((many // 2, D), F32), ((many // 2, D), BF16)]


def ffn_forward(rows, before, weights):
    many = rows.shape[0]
    steps, units = len(weights) // 2, 2 * weights[0].shape[1]
    by_row = lambda width: pl.BlockSpec((ROW_BLOCK, width), lambda i: (i, 0))
    add = before is not None
    outs = piece(
        functools.partial(ffn_forward_kernel, steps, add),
        "ffn_forward",
        (many // ROW_BLOCK,),
        [pl.BlockSpec(memory_space=pl.ANY)] * len(weights) + [by_row(D)] * (1 + add),
        [by_row(D)] + [by_row(units)] * (3 * steps),
        [((many, D), F32)] + [((many, units), F32)] * (2 * steps) + [((many, units), BF16)] * steps,
        [pltpu.VMEM((3, steps * units, D), BF16), pltpu.SemaphoreType.DMA((len(weights),))],
    )(*weights, *([before] if add else []), rows)
    (total,), gate, upper, hidden = refs_of((1, steps, steps, steps), outs)
    return total, gate, upper, hidden


def ffn_backward_kernel(steps, add, last, *refs):
    weights, refs = refs[: 2 * steps], refs[2 * steps :]
    if add:
        before, refs = refs[0], refs[1:]
    (rows,), gates, uppers, totals, grad_gates, grad_uppers, (held, sems) = refs_of(
        (1, steps, steps, 1 + last, steps, steps, 2), refs
    )
    load_weights(weights, held, sems)
    units = held.shape[1] // steps
    here = rows[...]
    running = before[...] if add else None
    for block in unit_blocks(steps, units):
        cut = slice(block[0] * units, (block[-1] + 1) * units)
        grad_hidden = right_dot(here, held[2, cut])
        low_gates, low_uppers = [], []
        for i, step in enumerate(block):
            unused, act_back = jax.vjp(gated_product, gates[step][...], uppers[step][...])
            back_gate, back_upper = act_back(grad_hidden[:, i * units : (i + 1) * units])
            low_gates.append(back_gate.astype(BF16))
            low_uppers.append(back_upper.astype(BF16))
            grad_gates[step][...] = low_gates[-1]
            grad_uppers[step][...] = low_uppers[-1]
        term = full_dot(jnp.concatenate(low_gates, 1), held[0, cut])
        term = term + full_dot(jnp.concatenate(low_uppers, 1), held[1, cut])
        running = term if running is None else running + term
    write_sum(running, totals[0], totals[1] if last else None)


def ffn_backward(rows, before, weights, gates, uppers, last):
    many = rows.shape[0]
    steps, units = len(gates), gates[0].shape[1]
    at, sums, sum_shapes = sum_specs(many, last)
    by_row = lambda width: pl.BlockSpec((ROW_BLOCK, width), lambda i: (at(i), 0))
    add = before is not None
    outs = piece(
        functools.partial(ffn_backward_kernel, steps, add, last),
        "ffn_backward",
        (many // ROW_BLOCK,),
        [pl.BlockSpec(memory_space=pl.ANY)] * len(weights)
        + [by_row(D)] * (1 + add)
        + [by_row(units)] * (2 * steps),
        sums + [by_row(units)] * (2 * steps),
        sum_shapes + [((many, units), BF16)] * (2 * steps),
        [pltpu.VMEM((3, steps * units, D), BF16), pltpu.SemaphoreType.DMA((len(weights),))],
    )(*weights, *([before] if add else []), rows, *gates, *uppers)
    return refs_of((len(sums), steps, steps), outs)


def first_backward_kernel(
    up_w, down_w, down_rows, rows, gate, upper, hidden, total, grad_gate, grad_upper, up_out, down_out, held, sums, sems
):
    load_weights((up_w, down_w), held, sems)
    at = pl.program_id(0)
    unused, act_back = jax.vjp(gated_product, gate[...], upper[...])
    back_gate, back_upper = act_back(right_dot(down_rows[...], held[2]))
    low_gate, low_upper = back_gate.astype(BF16), back_upper.astype(BF16)
    grad_gate[...] = low_gate
    grad_upper[...] = low_upper
    total[...] = full_dot(low_gate, held[0]) + full_dot(low_upper, held[1])
    pairs = ((low_gate, rows), (low_upper, rows), (hidden[...], down_rows))

    @pl.when(at == 0)
    def _():
        for kind, (left, right) in enumerate(pairs):
            sums[kind] = left_dot(left, right[...])

    @pl.when(at > 0)
    def _():
        for kind, (left, right) in enumerate(pairs):
            sums[kind] += left_dot(left, right[...])

    @pl.when(at == pl.num_programs(0) - 1)
    def _():
        half = up_out.shape[1]
        up_out[...] = sums[:, :half].astype(BF16)
        down_out[...] = sums[:, half:].astype(BF16)


def first_backward(down_rows, rows, weights, gate, upper, hidden):
    many, units = gate.shape
    by_row = lambda width: pl.BlockSpec((ROW_BLOCK, width), lambda i: (i, 0))
    part = (3, units // 2, D)
    return piece(
        first_backward_kernel,
        "first_backward",
        (many // ROW_BLOCK,),
        [pl.BlockSpec(memory_space=pl.ANY)] * 2 + [by_row(D)] * 2 + [by_row(units)] * 3,
        [by_row(D)] + [by_row(units)] * 2 + [whole(part)] * 2,
        [((many, D), F32)] + [((many, units), BF16)] * 2 + [(part, BF16)] * 2,
        [pltpu.VMEM((3, units, D), BF16), pltpu.VMEM((3, units, D), F32), pltpu.SemaphoreType.DMA((2,))],
    )(*weights, down_rows, rows, gate, upper, hidden)


def unit_grads_kernel(grad_gate, grad_upper, hidden, rows, down_rows, up_out, down_out):
    half = up_out.shape[1]
    pairs = ((grad_gate, rows), (grad_upper, rows), (hidden, down_rows))
    for kind, (left, right) in enumerate(pairs):
        out = left_dot(left[...], right[...]).astype(BF16)
        up_out[kind] = out[:half]
        down_out[kind] = out[half:]


def unit_grads_of(grad_gate, grad_upper, hidden, rows, down_rows):
    many, units = hidden.shape
    width = 1024
    narrow = whole((many, units))
    wide = pl.BlockSpec((many, width), lambda i: (0, i))
    part = pl.BlockSpec((3, units // 2, width), lambda i: (0, 0, i))
    return piece(
        unit_grads_kernel,
        "unit_grads",
        (D // width,),
        [narrow, narrow, narrow, wide, wide],
        [part, part],
        [((3, units // 2, D), BF16)] * 2,
    )(grad_gate, grad_upper, hidden, rows, down_rows)


def attend_back_kernel(
    gains, grad_in, grad_after, mixed, attn_raw, mid, low, lleft, lright, w_out, context, query, key, value, visible,
    grad_mixed, grad_mid, grad_gains, grad_left, grad_right, grad_w_out, grad_query, grad_key, grad_value,
    grad_attn,
):
    at = pl.program_id(0)

    @pl.when(at == 0)
    def _():
        back, gain_3 = norm_back(mixed[...], gains[3:4], grad_in[...])
        total = (grad_after[...] + back) * INV_SQRT2
        grad_mixed[...] = total
        back, gain_2 = norm_back(right_dot(mid[...], lright[...]), gains[2:3], total)
        back_low = back.astype(BF16)
        grad_right[...] = left_dot(back_low, mid[...])
        mid_low = full_dot(back_low, lright[...]).astype(BF16)
        grad_mid[...] = mid_low
        grad_left[...] = left_dot(low[...], mid_low)
        back, gain_1 = norm_back(attn_raw[...], gains[1:2], total)
        grad_attn[...] = back.astype(BF16)
        grad_gains[...] = jnp.concatenate(
            [gain_1, gain_2, gain_3, jnp.zeros((5, D), F32)], 0
        )

    grad_context = right_dot(grad_attn[...], w_out[...]).astype(BF16)
    grad_w_out[...] = left_dot(context[...], grad_attn[...]).astype(BF16)
    probs = softmax_of(query[...], key[...], visible[...])
    grad_probs = right_dot(grad_context, value[...])
    inner = jnp.sum(probs * grad_probs, axis=-1, keepdims=True)
    grad_scores = (probs * (grad_probs - inner)).astype(BF16)
    grad_query[...] = full_dot(grad_scores, key[...])
    key_term = left_dot(grad_scores, query[...])
    value_term = left_dot(probs.astype(BF16), grad_context)
    group = HEADS // KV_HEADS

    @pl.when(lax.rem(at, group) == 0)
    def _():
        grad_key[...] = key_term
        grad_value[...] = value_term

    @pl.when(lax.rem(at, group) > 0)
    def _():
        grad_key[...] += key_term
        grad_value[...] += value_term


def attend_back(gains, grad_in, grad_after, mixed, attn_raw, mid, low, full, context, qkv, keys_all, visible):
    rows = low.shape[0]
    seen = keys_all.shape[0]
    group = HEADS // KV_HEADS
    side = 128
    left_at, right_at = full.shape[1] // side - 2, full.shape[1] // side - 1
    head = pl.BlockSpec((rows, HEAD), lambda i: (0, i))
    once = lambda shape: pl.BlockSpec(shape, lambda i: (0, 0), pipeline_mode=pl.Buffered(1))
    return piece(
        attend_back_kernel,
        "attend_back",
        (HEADS,),
        [
            whole(gains.shape),
            once((rows, D)),
            once((rows, D)),
            once((rows, D)),
            once((rows, D)),
            whole((rows, side)),
            whole((rows, D)),
            pl.BlockSpec((D, side), lambda i: (0, left_at)),
            pl.BlockSpec((D, side), lambda i: (0, right_at)),
            pl.BlockSpec((HEAD, D), lambda i: (i, 0)),
            head,
            head,
            pl.BlockSpec((seen, HEAD), lambda i: (0, i // group)),
            pl.BlockSpec((seen, HEAD), lambda i: (0, KV_HEADS + i // group)),
            whole((rows, seen)),
        ],
        [
            whole((rows, D)),
            whole((rows, side)),
            whole((8, D)),
            whole((D, side)),
            whole((D, side)),
            pl.BlockSpec((HEAD, D), lambda i: (i, 0)),
            head,
            pl.BlockSpec((seen, HEAD), lambda i: (0, i // group)),
            pl.BlockSpec((seen, HEAD), lambda i: (0, i // group)),
        ],
        [
            ((rows, D), F32),
            ((rows, side), BF16),
            ((8, D), F32),
            ((D, side), F32),
            ((D, side), F32),
            ((HEADS * HEAD, D), BF16),
            ((rows, HEADS * HEAD), F32),
            ((seen, KV_HEADS * HEAD), F32),
            ((seen, KV_HEADS * HEAD), F32),
        ],
        [pltpu.VMEM((rows, D), BF16)],
    )(
        gains, grad_in, grad_after, mixed, attn_raw, mid, low, full, full, full, context, qkv, keys_all, keys_all,
        visible,
    )


def turn_back(grad, cosine, sine):
    half = HEAD // 2
    first, second = grad[:, :half], grad[:, half:]
    return jnp.concatenate([first * cosine + second * sine, second * cosine - first * sine], 1)


def query_back_kernel(grad_query, raw, cosine, sine, head_gain, low, weight, grad_w, grad_low, grad_head):
    at = pl.program_id(0)
    turned = turn_back(grad_query[...], cosine[...], sine[...])
    back, gain = norm_back(raw[...], head_gain[0:1], turned)
    back_low = back.astype(BF16)
    grad_w[...] = left_dot(low[...], back_low).astype(BF16)
    term = right_dot(back_low, weight[...])

    @pl.when(at == 0)
    def _():
        grad_low[...] = term
        grad_head[...] = gain

    @pl.when(at > 0)
    def _():
        grad_low[...] += term
        grad_head[...] += gain


def query_back(grad_query, raw, cosine, sine, head_gain, low, full):
    rows = low.shape[0]
    head = pl.BlockSpec((rows, HEAD), lambda i: (0, i))
    return piece(
        query_back_kernel,
        "query_back",
        (HEADS,),
        [
            head,
            head,
            whole(cosine.shape),
            whole(sine.shape),
            whole((2, HEAD)),
            whole((rows, D)),
            pl.BlockSpec((D, HEAD), lambda i: (0, HEADS + i)),
        ],
        [pl.BlockSpec((D, HEAD), lambda i: (0, i)), whole((rows, D)), whole((1, HEAD))],
        [((D, HEADS * HEAD), BF16), ((rows, D), F32), ((1, HEAD), F32)],
    )(grad_query, raw, cosine, sine, head_gain, low, full)


def key_back_kernel(
    grad_kv, raw, cosine, sine, head_gain, low, weight, before, grad_mixed, grad_mid, lleft, tokens, gains,
    grad_w, grad_tokens, grad_head, grad_gain, total,
):
    at = pl.program_id(0)
    is_key = at < KV_HEADS
    grad = grad_kv[...]
    turned = jnp.where(is_key, turn_back(grad, cosine[...], sine[...]), grad)
    back, gain = norm_back(raw[...], jnp.where(is_key, head_gain[1:2], 1.0), turned)
    back_low = back.astype(BF16)
    grad_w[...] = left_dot(low[...], back_low).astype(BF16)
    term = right_dot(back_low, weight[...])

    @pl.when(at == 0)
    def _():
        total[...] = before[...] + term
        grad_head[...] = gain

    @pl.when(at > 0)
    def _():
        total[...] += term
        grad_head[...] += jnp.where(is_key, gain, 0.0)

    @pl.when(at == 2 * KV_HEADS - 1)
    def _():
        grad_normed = total[...] + grad_mixed[...] + right_dot(grad_mid[...], lleft[...])
        back, gain_0 = norm_back(tokens[...].astype(F32), gains[0:1], grad_normed)
        grad_tokens[...] = grad_mixed[...] + back
        grad_gain[...] = gain_0


def key_back(grad_kv, raw, cosine, sine, head_gain, low, full, before, grad_mixed, grad_mid, tokens, gains):
    rows = low.shape[0]
    side = 128
    left_at = full.shape[1] // side - 2
    return piece(
        key_back_kernel,
        "key_back",
        (2 * KV_HEADS,),
        [
            pl.BlockSpec((rows, HEAD), lambda i: (0, i)),
            pl.BlockSpec((rows, HEAD), lambda i: (0, HEADS + i)),
            whole(cosine.shape),
            whole(sine.shape),
            whole((2, HEAD)),
            whole((rows, D)),
            pl.BlockSpec((D, HEAD), lambda i: (0, 2 * HEADS + i)),
            whole((rows, D)),
            whole((rows, D)),
            whole((rows, side)),
            pl.BlockSpec((D, side), lambda i: (0, left_at)),
            whole((rows, D)),
            whole(gains.shape),
        ],
        [
            pl.BlockSpec((D, HEAD), lambda i: (0, i)),
            whole((rows, D)),
            whole((1, HEAD)),
            whole((1, D)),
        ],
        [
            ((D, 2 * KV_HEADS * HEAD), BF16),
            ((rows, D), F32),
            ((1, HEAD), F32),
            ((1, D), F32),
        ],
        [pltpu.VMEM((rows, D), F32)],
    )(grad_kv, raw, cosine, sine, head_gain, low, full, before, grad_mixed, grad_mid, full, tokens, gains)


def tie(*values):
    return lax.optimization_barrier(values)


def shares(total, count):
    return [total // count + (1 if i < total % count else 0) for i in range(count)]


def greet(peers):
    barrier = pltpu.get_barrier_semaphore()
    for peer in peers:
        pl.semaphore_signal(barrier, inc=1, device_id=peer, device_id_type=MESH)
    pl.semaphore_wait(barrier, len(peers))


def partners():
    return {"core": 1 - lax.axis_index("core")}, {"fsdp": 1 - lax.axis_index("fsdp")}


CUTS = 8
FLYING = 2


def spread_kernel(own, rows, x_send, x_recv, near_send, near_recv, far_send, far_recv, own_sem):
    count = own.shape[0]
    cut = count // CUTS
    other_core, other_side = partners()
    greet((other_core, other_side))

    def copy(src, block, at, send, recv, peer):
        return pltpu.make_async_remote_copy(
            src_ref=src,
            dst_ref=rows.at[pl.ds(block * count + at * cut, cut)],
            send_sem=send.at[at],
            recv_sem=recv.at[at],
            device_id=peer,
            device_id_type=MESH,
        )

    mine = [own.at[pl.ds(at * cut, cut)] for at in range(CUTS)]
    came = [rows.at[pl.ds(count + at * cut, cut)] for at in range(CUTS)]
    across = [copy(mine[at], 1, at, x_send, x_recv, other_side) for at in range(CUTS)]
    near = [copy(mine[at], 2, at, near_send, near_recv, other_core) for at in range(CUTS)]
    far = [copy(came[at], 3, at, far_send, far_recv, other_core) for at in range(CUTS)]
    for one in across[:FLYING] + near:
        one.start()
    keep = pltpu.make_async_copy(own, rows.at[pl.ds(0, count)], own_sem)
    keep.start()
    for at in range(CUTS):
        across[at].wait_send()
        if at + FLYING < CUTS:
            across[at + FLYING].start()
        across[at].wait_recv()
        far[at].start()
    for one in near + far:
        one.wait()
    keep.wait()


def rows_of_four(own, number):
    count = own.shape[0]
    dma = pltpu.SemaphoreType.DMA
    return pl.pallas_call(
        spread_kernel,
        out_shape=jax.ShapeDtypeStruct((4 * count, D), BF16),
        in_specs=[pl.BlockSpec(memory_space=pltpu.VMEM)],
        out_specs=pl.BlockSpec(memory_space=pl.ANY),
        scratch_shapes=[dma((CUTS,)) for _ in range(6)] + [dma],
        compiler_params=pltpu.CompilerParams(collective_id=number, has_side_effects=True),
        cost_estimate=LITTLE,
        name="spread_rows",
    )(own)


def gather_sum_kernel(steps, *refs):
    if steps:
        (own, low, rows, down_rows), sides, (out,), grads, more, held, sems = refs_of(
            (4, 3 * steps, 1, 2 * steps, 4 + 4, 3, 3), refs
        )
        core_in, pair_low, x_in, parts, *copy_sems = more
        core_send, core_recv, x_send, x_recv = copy_sems
        rows_in, down_in, more_out = held
        loads_sem, parts_sem, grads_sem = sems
        parts_out = more_out

        def store(step, way):
            return pltpu.make_async_copy(parts_out.at[step, way], grads[2 * step + way], grads_sem.at[step, way])

        loads = [
            pltpu.make_async_copy(rows, rows_in, loads_sem.at[0]),
            pltpu.make_async_copy(down_rows, down_in, loads_sem.at[1]),
        ]
        part_loads = [
            pltpu.make_async_copy(side, parts.at[number], parts_sem.at[number]) for number, side in enumerate(sides)
        ]
        for load in loads + part_loads:
            load.start()
    else:
        own, low, out, core_in, pair_low, x_in, core_send, core_recv, x_send, x_recv = refs
    count = out.shape[0]
    cut = count // CUTS
    other_core, other_side = partners()
    greet((other_core, other_side))

    def core_copy(block, at):
        here = pl.ds(block * count + at * cut, cut)
        number = block * CUTS + at
        return pltpu.make_async_remote_copy(
            src_ref=low.at[here],
            dst_ref=core_in.at[here],
            send_sem=core_send.at[number],
            recv_sem=core_recv.at[number],
            device_id=other_core,
            device_id_type=MESH,
        )

    def x_copy(at):
        here = pl.ds(at * cut, cut)
        return pltpu.make_async_remote_copy(
            src_ref=pair_low.at[here],
            dst_ref=x_in.at[here],
            send_sem=x_send.at[at],
            recv_sem=x_recv.at[at],
            device_id=other_side,
            device_id_type=MESH,
        )

    pieces = [(block, at) for block in (1, 0) for at in range(CUTS)]

    def next_piece(number):
        core_copy(*pieces[number]).wait_send()
        if number + FLYING < len(pieces):
            core_copy(*pieces[number + FLYING]).start()

    for one in pieces[:FLYING]:
        core_copy(*one).start()
    for at in range(CUTS):
        there = pl.ds(count + at * cut, cut)
        next_piece(at)
        core_copy(1, at).wait_recv()
        pair_low[pl.ds(at * cut, cut)] = (own[there] + core_in[there].astype(F32)).astype(BF16)
        x_copy(at).start()
    for at in range(CUTS):
        here = pl.ds(at * cut, cut)
        next_piece(CUTS + at)
        core_copy(0, at).wait_recv()
        out[here] = own[here] + core_in[here].astype(F32)
    if steps:
        for load in loads:
            load.wait()
        half = grads[0].shape[1]
        width = D // 2
        for step in range(steps):
            for kind in range(3):
                number = 3 * step + kind
                part_loads[number].wait()
                left, right = parts[number], down_in if kind == 2 else rows_in
                for first in range(0, D, width):
                    cols = slice(first, first + width)
                    term = left_dot(left, right[:, cols]).astype(BF16)
                    parts_out[step, 0, kind, :, cols] = term[:half]
                    parts_out[step, 1, kind, :, cols] = term[half:]
            for way in range(2):
                store(step, way).start()
    for at in range(CUTS):
        here = pl.ds(at * cut, cut)
        x_copy(at).wait_recv()
        out[here] += x_in[here].astype(F32)
    for at in range(CUTS):
        x_copy(at).wait_send()
    for step in range(steps):
        for way in range(2):
            store(step, way).wait()


def sum_of_four(own, low, number, units=(), rows=None, down_rows=None):
    count = own.shape[0] // 2
    steps = len(units)
    dma = pltpu.SemaphoreType.DMA
    vmem, anywhere = pltpu.VMEM, pl.BlockSpec(memory_space=pl.ANY)
    scratch = [vmem((2 * count, D), BF16), vmem((count, D), BF16), vmem((count, D), BF16)]
    copy_sems = [dma((2 * CUTS,)), dma((2 * CUTS,)), dma((CUTS,)), dma((CUTS,))]
    operands, shapes = [], []
    if steps:
        many, width = units[0][0].shape
        operands = [rows, down_rows] + [side for sides in units for side in sides]
        shapes = [jax.ShapeDtypeStruct((3, width // 2, D), BF16)] * (2 * steps)
        scratch += [vmem((3 * steps, many, width), BF16)]
        copy_sems += [vmem((many, D), BF16), vmem((many, D), BF16), vmem((steps, 2, 3, width // 2, D), BF16)]
        copy_sems += [dma((2,)), dma((3 * steps,)), dma((steps, 2))]
    total, *grads = pl.pallas_call(
        functools.partial(gather_sum_kernel, steps),
        out_shape=[jax.ShapeDtypeStruct((count, D), F32)] + shapes,
        in_specs=[pl.BlockSpec(memory_space=pltpu.VMEM), anywhere] + [anywhere] * len(operands),
        out_specs=[pl.BlockSpec(memory_space=pltpu.VMEM)] + [anywhere] * len(shapes),
        scratch_shapes=scratch + copy_sems,
        compiler_params=pltpu.CompilerParams(
            collective_id=number, has_side_effects=True, vmem_limit_bytes=VMEM_LIMIT
        ),
        cost_estimate=LITTLE,
        name="gather_sum",
    )(own, low, *operands)
    return total, [(grads[2 * i], grads[2 * i + 1]) for i in range(steps)]


PARTS = 4


def middle_kernel(steps, *refs):
    weights, inputs, outs, unit_outs, scratch, unit_scratch, sems = refs_of((2 * steps, 10, 8, 3 * steps, 15, 6, 14), refs)
    before, ffn_rows, mixed, layer_in, teacher, mask, scale, gains, gate_w, proj_w = inputs
    result, grad_after, grad_layer, rows, grad_gate_w, grad_proj_w, grad_gains, squares = outs
    (
        own_in, mixed_in, teacher_in, gate_in, proj_in, core_in, pair_low, x_in,
        result_out, after_out, after_low, mid_low, grad_pl, grad_raw, grad_low,
    ) = scratch
    rows_in, held, low, *unit_sides = unit_scratch
    (
        loads, stores, core_send, core_recv, x_send, x_recv, y_send, y_recv, near_send, near_recv, far_send, far_recv,
        unit_loads, unit_stores,
    ) = sems
    count = mixed.shape[0]
    cut = count // PARTS
    other_core, other_side = partners()

    def load(number, src, dst):
        return pltpu.make_async_copy(src, dst, loads.at[number])

    units = held.shape[1] // steps
    weight_loads = [
        pltpu.make_async_copy(ref, held.at[:, pl.ds(at * units // 2, units // 2)], unit_loads.at[at])
        for at, ref in enumerate(weights)
    ]
    block_loads = [
        [
            load(2 * block, ffn_rows.at[pl.ds(block * count, count)], rows_in.at[pl.ds(block * count, count)]),
            load(2 * block + 1, before.at[pl.ds(block * count, count)], own_in.at[pl.ds(block * count, count)]),
        ]
        for block in range(4)
    ]
    incoming = [
        load(8, mixed, mixed_in),
        load(9, gate_w, gate_in),
        load(10, proj_w, proj_in),
        load(11, teacher, teacher_in),
    ]
    for one in weight_loads + block_loads[3] + block_loads[1] + block_loads[2] + block_loads[0] + incoming:
        one.start()
    greet((other_core, other_side))

    def forward_block(block):
        here = slice(block * count, (block + 1) * count)
        for one in block_loads[block]:
            one.wait()
        gate = right_dot(rows_in[here], held[0])
        upper = right_dot(rows_in[here], held[1])
        hidden = gated_product(gate, upper).astype(BF16)
        for side, values in zip(unit_sides, (gate, upper, hidden)):
            for step in range(steps):
                side[step, here] = values[:, step * units : (step + 1) * units]
        return own_in[here] + full_dot(hidden, held[2])

    def unit_store(kind, step):
        return pltpu.make_async_copy(
            unit_sides[kind].at[step], unit_outs[kind * steps + step], unit_stores.at[kind * steps + step]
        )

    def remote(src, dst, send, recv, peer):
        return pltpu.make_async_remote_copy(
            src_ref=src, dst_ref=dst, send_sem=send, recv_sem=recv, device_id=peer, device_id_type=MESH
        )

    def piece_of(at):
        return pl.ds(at * cut, cut)

    def core_copy(block, at):
        here = pl.ds(block * count + at * cut, cut)
        number = block * PARTS + at
        return remote(low.at[here], core_in.at[here], core_send.at[number], core_recv.at[number], other_core)

    def x_copy(at):
        here = piece_of(at)
        return remote(pair_low.at[here], x_in.at[here], x_send.at[at], x_recv.at[at], other_side)

    def out_copy(src, block, at, send, recv, peer):
        return remote(src, rows.at[pl.ds(block * count + at * cut, cut)], send.at[at], recv.at[at], peer)

    def across(at):
        return out_copy(grad_low.at[piece_of(at)], 1, at, y_send, y_recv, other_side)

    def near(at):
        return out_copy(grad_low.at[piece_of(at)], 2, at, near_send, near_recv, other_core)

    def far(at):
        return out_copy(rows.at[pl.ds(count + at * cut, cut)], 3, at, far_send, far_recv, other_core)

    def kept(number, at):
        here = piece_of(at)
        src, dst = ((result_out, result), (after_out, grad_after), (grad_low, rows))[number]
        return pltpu.make_async_copy(src.at[here], dst.at[here], stores.at[number, at])

    for one in weight_loads:
        one.wait()
    low[count:] = forward_block(3).astype(BF16)
    for at in range(PARTS):
        core_copy(1, at).start()
    own_in[count : 2 * count] = forward_block(1)
    for at in range(PARTS):
        there = pl.ds(count + at * cut, cut)
        core_copy(1, at).wait_recv()
        pair_low[piece_of(at)] = (own_in[there] + core_in[there].astype(F32)).astype(BF16)
        x_copy(at).start()
    low[:count] = forward_block(2).astype(BF16)
    for at in range(PARTS):
        core_copy(0, at).start()
    own_in[:count] = forward_block(0)
    for kind in range(3):
        for step in range(steps):
            unit_store(kind, step).start()
    for one in incoming:
        one.wait()
    gain_4, gain_5 = gains[4:5], gains[5:6]
    total = jnp.zeros((), F32)
    sum_4 = sum_5 = jnp.zeros((1, D), F32)
    for at in range(PARTS):
        here = piece_of(at)
        core_copy(0, at).wait_recv()
        x_copy(at).wait_recv()
        down = own_in[here] + core_in[here].astype(F32) + x_in[here].astype(F32)
        after = mixed_in[here] + down * inverse_rms(down) * gain_4
        low_here = after.astype(BF16)
        after_low[here] = low_here
        raw = full_dot(low_here, gate_in[...])
        act, act_back = jax.vjp(gelu_tanh, raw)
        layer = layer_in[here].astype(F32)
        mid = (act * layer).astype(BF16)
        mid_low[here] = mid
        out = full_dot(mid, proj_in[...])
        done = after + out * inverse_rms(out) * gain_5
        result_out[here] = done
        kept(0, at).start()
        errors = done - teacher_in[here].astype(F32)
        masked = mask[here][:, 0:1] * errors
        total += jnp.sum(masked * errors)
        grad_out = masked * scale[0:1, 0:1]
        back, term = norm_back(out, gain_5, grad_out)
        sum_5 += term
        back_low = back.astype(BF16)
        grad_pl[here] = back_low
        grad_mid = right_dot(back_low, proj_in[...])
        grad_layer[here] = grad_mid * act
        raw_low = act_back(grad_mid * layer)[0].astype(BF16)
        grad_raw[here] = raw_low
        grad_here = grad_out + right_dot(raw_low, gate_in[...])
        after_out[here] = grad_here
        kept(1, at).start()
        back, term = norm_back(down, gain_4, grad_here)
        sum_4 += term
        grad_low[here] = back.astype(BF16)
        across(at).start()
        near(at).start()
        kept(2, at).start()
    grad_gains[...] = jnp.concatenate([sum_4, sum_5, jnp.zeros((6, D), F32)], 0)
    squares[...] = jnp.broadcast_to(total, squares.shape)
    for at in range(PARTS // 2):
        across(at).wait_recv()
        far(at).start()
    grad_proj_w[...] = left_dot(mid_low[...], grad_pl[...]).astype(BF16)
    grad_gate_w[...] = left_dot(after_low[...], grad_raw[...]).astype(BF16)
    for at in range(PARTS // 2, PARTS):
        across(at).wait_recv()
        far(at).start()
    for at in range(PARTS):
        far(at).wait()
        near(at).wait()
        across(at).wait_send()
        x_copy(at).wait_send()
        for block in (0, 1):
            core_copy(block, at).wait_send()
        for number in range(3):
            kept(number, at).wait()
    for kind in range(3):
        for step in range(steps):
            unit_store(kind, step).wait()


def middle(weights, before, ffn_rows, mixed, layer_in, teacher, mask, scale, gains, gate_w, proj_w):
    count = mixed.shape[0]
    steps, units = len(weights) // 2, 2 * weights[0].shape[1]
    sides = [(4 * count, units)] * steps
    dma, vmem = pltpu.SemaphoreType.DMA, pltpu.VMEM
    anywhere, inside = pl.BlockSpec(memory_space=pl.ANY), pl.BlockSpec(memory_space=pltpu.VMEM)
    shape = jax.ShapeDtypeStruct
    outs = pl.pallas_call(
        functools.partial(middle_kernel, steps),
        out_shape=[
            shape((count, D), F32),
            shape((count, D), F32),
            shape((count, PLD), F32),
            shape((4 * count, D), BF16),
            shape((D, PLD), BF16),
            shape((PLD, D), BF16),
            shape((8, D), F32),
            shape((8, 128), F32),
        ]
        + [shape(side, F32) for side in sides * 2]
        + [shape(side, BF16) for side in sides],
        in_specs=[anywhere] * (2 * steps) + [anywhere, anywhere, anywhere, inside, anywhere, inside, inside, inside, anywhere, anywhere],
        out_specs=[anywhere, anywhere, inside, anywhere, inside, inside, inside, inside] + [anywhere] * (3 * steps),
        scratch_shapes=[
            vmem((4 * count, D), F32),
            vmem((count, D), F32),
            vmem((count, D), BF16),
            vmem((D, PLD), BF16),
            vmem((PLD, D), BF16),
            vmem((2 * count, D), BF16),
            vmem((count, D), BF16),
            vmem((count, D), BF16),
            vmem((count, D), F32),
            vmem((count, D), F32),
            vmem((count, D), BF16),
            vmem((count, PLD), BF16),
            vmem((count, D), BF16),
            vmem((count, PLD), BF16),
            vmem((count, D), BF16),
            vmem((4 * count, D), BF16),
            vmem((3, steps * units, D), BF16),
            vmem((2 * count, D), BF16),
            vmem((steps, 4 * count, units), F32),
            vmem((steps, 4 * count, units), F32),
            vmem((steps, 4 * count, units), BF16),
            dma((12,)),
            dma((3, PARTS)),
            dma((2 * PARTS,)),
            dma((2 * PARTS,)),
        ]
        + [dma((PARTS,)) for _ in range(8)]
        + [dma((2 * steps,)), dma((3 * steps,))],
        compiler_params=pltpu.CompilerParams(
            collective_id=3, has_side_effects=True, vmem_limit_bytes=VMEM_LIMIT
        ),
        cost_estimate=LITTLE,
        name="middle",
    )(*weights, before, ffn_rows, mixed, layer_in, teacher, mask, scale, gains, gate_w, proj_w)
    return refs_of((8, steps, steps, steps), outs)


def body(
    tokens,
    per_layer,
    teacher,
    cont_lengths,
    w_query,
    w_kv,
    w_out,
    laurel_left,
    laurel_right,
    pl_gate,
    pl_proj,
    norm_gains,
    head_gains,
    ffn_weight,
):
    row_count = tokens.shape[1]
    chips = lax.axis_size("zy")
    seq_count = 2 * chips
    group_count = lax.axis_size("fsdp")
    shards = seq_count * group_count
    chip = lax.axis_index("zy")
    core = lax.axis_index("core")
    seq_index = chip * 2 + core
    group_index = lax.axis_index("fsdp")
    half_point = seq_count // 2
    prompt_len = half_point * row_count
    cont_shards = CONT_LEN // row_count
    cont_count = prompt_len // CONT_LEN
    is_cont = seq_index >= half_point
    rel_index = seq_index - half_point
    local_shard = jnp.where(is_cont, rel_index % cont_shards, 0)
    cont_index = jnp.where(is_cont, rel_index // cont_shards, 0)
    first_place = jnp.where(is_cont, prompt_len + local_shard * row_count, seq_index * row_count)
    row_range = jnp.arange(row_count, dtype=jnp.int32)
    places = first_place + row_range
    group_lengths = jnp.sum(
        jnp.where(
            jnp.arange(group_count, dtype=jnp.int32)[:, None] == group_index, cont_lengths, 0
        ),
        axis=0,
    )
    my_length = jnp.sum(
        jnp.where(jnp.arange(cont_count, dtype=jnp.int32) == cont_index, group_lengths, 0)
    )
    valid = jnp.logical_or(
        jnp.logical_not(is_cont), local_shard * row_count + row_range < my_length
    )
    weight_mask = valid.astype(F32)
    count = F32(group_count * prompt_len) + jnp.sum(cont_lengths).astype(F32)
    total_slots = float(row_count * seq_count * group_count)
    shard_rows = w_query.shape[0]
    key_cols = KV_HEADS * HEAD
    proj_cols = pl_proj.shape[0] * D // shard_rows
    misc_cols = RANK
    head_part = head_gains.reshape(-1, 1)
    misc = jnp.concatenate(
        [
            norm_gains.T,
            jnp.pad(head_part, ((0, shard_rows - head_part.shape[0]), (0, 0))),
            jnp.zeros((shard_rows, misc_cols - 7), BF16),
        ],
        1,
    )
    pack = jnp.concatenate(
        [
            w_out,
            w_query,
            w_kv,
            pl_gate,
            pl_proj.reshape(shard_rows, proj_cols),
            laurel_left,
            misc,
            laurel_right.T,
            jnp.zeros((shard_rows, 128 - RANK), BF16),
        ],
        1,
    )

    units = ffn_weight.shape[0]
    half = units // 2
    by_kind = ffn_weight.transpose(1, 0, 2)
    ups, downs = [by_kind[:, :half]], [by_kind[:, half:]]
    stage_steps = shares(chips - 1, 7)

    def pass_on(stage):
        for _ in range(stage_steps[stage]):
            ups.append(ring(ups[-1], 1))
            downs.append(ring(downs[-1], -1))

    def stage_end(values):
        (ups[-1], downs[-1]), values = tie((ups[-1], downs[-1]), values)
        return values

    pass_on(0)
    full = gather_all(pack, chips)
    at = 2 * D + 2 * key_cols
    plg = full[:, at : at + PLD]
    plp = full[:, at + PLD : at + PLD + proj_cols].reshape(PLD, D)
    at += PLD + proj_cols + RANK
    misc_full = stage_end(full[:, at : at + misc_cols])
    pass_on(1)
    gains = jnp.pad(misc_full[:, :6].T.astype(F32), ((0, 2), (0, 0)))
    head_n = head_gains.shape[1]
    head_gain = (
        misc_full[:, 6]
        .reshape(shards, shard_rows)[:, : 2 * head_n]
        .reshape(shards, 2, head_n)
        .transpose(1, 0, 2)
        .reshape(2, HEAD)
        .astype(F32)
    )
    freqs = jnp.exp(
        jnp.arange(HEAD // 2, dtype=F32) * (-2.0 * math.log(ROPE_BASE) / HEAD)
    )
    angles = places.astype(F32)[:, None] * freqs
    cosine, sine = jnp.cos(angles), jnp.sin(angles)
    normed_low, qkv_raw, qkv = make_qkv(tokens[0], gains, head_gain, cosine, sine, full)
    qkv = stage_end(qkv)
    kv_own = qkv[:, D:]
    pass_on(2)

    mid = chips // 2
    chain = [(i, i + 1) for i in range(mid - 1)] + [(mid - 1, mid + 1)]
    kv_before = jnp.where(
        chip == mid,
        lax.ppermute(kv_own, "zy", [(mid - 1, mid)]),
        lax.ppermute(kv_own, "zy", chain),
    )
    spans = []
    span = 2
    while span < mid:
        spans.append(span)
        span *= 2
    for span in spans:
        moved = lax.ppermute(
            kv_before, "zy", [(mid + i, mid + i + span) for i in range(min(span, mid - span))]
        )
        fresh = jnp.logical_and(chip >= mid + span, chip < mid + 2 * span)
        kv_before = jnp.where(fresh, moved, kv_before)
    kv_other = swap(jnp.where(core == 0, kv_own, kv_before), "core")
    keys_all = jnp.concatenate([kv_before, kv_other, kv_own], 0)
    keys_all = stage_end(keys_all)
    pass_on(3)
    key_len = keys_all.shape[0]
    key_places = first_place - 2 * row_count + jnp.arange(key_len, dtype=jnp.int32)
    visible = (
        (key_places[None, :] <= places[:, None])
        & (places[:, None] - key_places[None, :] < WINDOW)
        & (key_places[None, :] >= 0)
    ).astype(F32)
    context_low, attn_raw, mixed, ffn_in, laurel_mid = attend(
        tokens[0], gains, normed_low, qkv, keys_all, visible, full
    )

    ffn_in = stage_end(ffn_in)
    pass_on(4)
    ffn_rows = stage_end(rows_of_four(ffn_in, 2))
    here = len(ups)
    pass_on(5)
    gates, uppers, hiddens = [], [], []

    def weights_of(steps):
        return [w for k in steps for w in (ups[k], downs[k])]

    def forward_part(running, first, end):
        running, gate, upper, hidden = ffn_forward(ffn_rows, running, weights_of(range(first, end)))
        gates.extend(gate)
        uppers.extend(upper)
        hiddens.extend(hidden)
        return running

    running = stage_end(forward_part(None, 0, here))
    then = len(ups)
    pass_on(6)
    running = stage_end(forward_part(running, here, then))
    outs, gate, upper, hidden = middle(
        weights_of(range(then, chips)),
        running,
        ffn_rows,
        mixed,
        per_layer[0],
        teacher[0],
        jnp.broadcast_to(weight_mask[:, None], (row_count, 128)),
        jnp.broadcast_to(total_slots / count, (8, 128)),
        gains,
        plg,
        plp,
    )
    result, grad_after, grad_layer_in, grad_down_rows, grad_plg, grad_plp, late_gains, squares = outs
    gates.extend(gate)
    uppers.extend(upper)
    hiddens.extend(hidden)
    grad_gates, grad_uppers = [None] * chips, [None] * chips

    def backward_part(steps, running, last=False):
        sums, grad_gate, grad_upper = ffn_backward(
            grad_down_rows, running, weights_of(steps), [gates[k] for k in steps], [uppers[k] for k in steps], last
        )
        for k, gg, gu in zip(steps, grad_gate, grad_upper):
            grad_gates[k], grad_uppers[k] = gg, gu
        return sums if last else sums[0]

    ready = {}

    def unit_grads(k):
        if k in ready:
            return ready[k]
        return unit_grads_of(grad_gates[k], grad_uppers[k], hiddens[k], ffn_rows, grad_down_rows)

    order = list(range(1, chips)) + [0]
    ring_steps = shares(chips - 2, 6)
    done = 0

    def beside(stage, work):
        nonlocal done, up_sum, down_sum
        values = None
        for step in range(ring_steps[stage]):
            up_in = ring(up_sum, 1)
            down_in = ring(down_sum, -1)
            if step == 0:
                values = work()
            done += 1
            terms = unit_grads(order[done])
            (up_in, down_in), terms, values = tie((up_in, down_in), terms, values)
            up_sum = (up_in.astype(F32) + terms[0].astype(F32)).astype(BF16)
            down_sum = (down_in.astype(F32) + terms[1].astype(F32)).astype(BF16)
        return work() if values is None else values

    first = ring_steps[0]
    then = first + 1 + ring_steps[0] + ring_steps[1]
    if first == 1 and units % 128 == 0:
        k = order[0]
        running, grad_gates[k], grad_uppers[k], up_sum, down_sum = first_backward(
            grad_down_rows, ffn_rows, weights_of([k]), gates[k], uppers[k], hiddens[k]
        )
    else:
        running = backward_part(order[:first], None)
        up_sum, down_sum = unit_grads(order[0])
    running = beside(0, lambda: backward_part(order[first:then], running))
    own_sum, low_sum = beside(1, lambda: backward_part(order[then:], running, True))

    def work():
        steps = order[done + ring_steps[2] :] if units % 128 == 0 else []
        total, grads = sum_of_four(
            own_sum,
            low_sum,
            5,
            [(grad_gates[k], grad_uppers[k], hiddens[k]) for k in steps],
            ffn_rows,
            grad_down_rows,
        )
        ready.update(zip(steps, grads))
        return total

    grad_ffn_in = beside(2, work)
    def work():
        *out, grad_keys, grad_values = attend_back(
            gains, grad_ffn_in, grad_after, mixed, attn_raw, laurel_mid, normed_low, full, context_low, qkv, keys_all,
            visible,
        )
        grad_kv = jnp.concatenate([grad_keys, grad_values], 1)
        grad_before = grad_kv[:row_count]
        grad_own = grad_kv[2 * row_count :]
        returned = swap(grad_kv[row_count : 2 * row_count].astype(BF16), "core").astype(F32)
        grad_own = grad_own + jnp.where(core == 0, returned, 0.0)
        grad_before = grad_before + jnp.where(core == 0, 0.0, returned)
        return out, grad_own, grad_before

    out, grad_own, grad_before = beside(3, work)
    (
        grad_scaled,
        grad_mid_low,
        grad_mid_gains,
        grad_lleft,
        grad_lright_t,
        grad_wo,
        grad_queries,
    ) = out

    def work():
        total = grad_before
        for span in reversed(spans):
            back = [(mid + i + span, mid + i) for i in range(min(span, mid - span))]
            total = total + lax.ppermute(total.astype(BF16), "zy", back).astype(F32)
        before_low = total.astype(BF16)
        return (
            grad_own
            + lax.ppermute(before_low, "zy", [(b, a) for a, b in chain]).astype(F32)
            + lax.ppermute(before_low, "zy", [(mid, mid - 1)]).astype(F32)
        ), query_back(grad_queries, qkv_raw, cosine, sine, head_gain, normed_low, full)

    grad_own, (grad_wq, grad_normed, grad_hq) = beside(4, work)

    def work():
        grad_wkv, grad_tokens, grad_hk, grad_g0 = key_back(
            grad_own, qkv_raw, cosine, sine, head_gain, normed_low, full, grad_normed, grad_scaled, grad_mid_low,
            tokens[0], gains,
        )
        head_back = jnp.concatenate([grad_hq, grad_hk], 0).reshape(2, shards, head_n).transpose(1, 0, 2)
        head_back = head_back.reshape(shards, 2 * head_n)
        head_back = jnp.pad(head_back, ((0, 0), (0, shard_rows - 2 * head_n))).reshape(1, D)
        misc_back = jnp.concatenate(
            [grad_g0, grad_mid_gains[:3], late_gains[:2], head_back, jnp.zeros((1, D), F32)], 0
        )
        return grad_wkv, grad_tokens, jnp.concatenate(
            [
                grad_plg,
                grad_plp.reshape(D, proj_cols),
                grad_lleft[:, :RANK].astype(BF16),
                jnp.pad(misc_back.T, ((0, 0), (0, misc_cols - 8))).astype(BF16),
                grad_lright_t.astype(BF16),
            ],
            1,
        )

    last_terms, (grad_wkv, grad_tokens, rest_back) = beside(5, lambda: (unit_grads(0), work()))
    sums_wq, sums_wkv, sums_wo, sums_rest, total, up_in, down_in = sum_all(
        [grad_wq, grad_wkv, grad_wo, rest_back],
        (D, 2 * key_cols, D - 512, 0),
        squares,
        up_sum,
        down_sum,
        chips,
    )
    grad_ffn = jnp.concatenate(
        [
            (arrived.astype(F32) + term.astype(F32)).transpose(1, 0, 2)
            for arrived, term in zip((up_in, down_in), last_terms)
        ],
        0,
    )
    at = 0
    rest = []
    for width in (PLD, proj_cols, RANK, misc_cols, RANK):
        rest.append(sums_rest[:, at : at + width])
        at += width

    match_loss = total[0, 0] / (2.0 * D * count)

    return (
        result[None],
        match_loss,
        grad_tokens[None],
        grad_layer_in[None],
        sums_wq,
        sums_wkv,
        sums_wo,
        rest[2],
        rest[4].T,
        rest[0],
        rest[1].reshape(pl_proj.shape),
        rest[3][:, :6].T,
        rest[3][: 2 * head_n, 6].reshape(2, head_n),
        grad_ffn,
    )


def solution(mesh):
    seq, fsdp = mesh.shape["seq"], mesh.shape["fsdp"]
    fine = Mesh(mesh.devices.reshape(seq // 2, 2, fsdp), ("zy", "core", "fsdp"))
    rows = P("fsdp", ("zy", "core"), None)
    split = ("zy", "core", "fsdp")
    weights = (
        P(split, None),
        P(split, None),
        P(split, None),
        P(split, None),
        P(None, split),
        P(split, None),
        P(split, None),
        P(None, split),
        P(None, split),
        P(split, None, None),
    )
    return jax.shard_map(
        body,
        mesh=fine,
        in_specs=(rows, rows, rows, P()) + weights,
        out_specs=(rows, P(), rows, rows) + weights,
        check_vma=False,
    )
```

```python
import functools
import math

import jax
import jax.numpy as jnp
from jax import lax
from jax.experimental import pallas as pl
from jax.experimental.pallas import tpu as pltpu
from jax.sharding import Mesh, PartitionSpec as P

D = 2048
HEADS = 8
KV_HEADS = 2
HEAD = 256
WINDOW = 512
CONT_LEN = 512
RANK = 64
PLD = 256

EPSILON = 1e-06
INV_SQRT2 = 0.7071067811865476
ROPE_BASE = 10000.0
BF16 = jnp.bfloat16
F32 = jnp.float32


def gelu_tanh(values):
    return jax.nn.gelu(values, approximate=True)


def gated_product(gate_in, up_in):
    return gelu_tanh(gate_in) * up_in


def full_dot(left, right):
    return jnp.dot(left, right, preferred_element_type=F32)


def left_dot(left, right):
    return lax.dot_general(left, right, (((0,), (0,)), ((), ())), preferred_element_type=F32)


def right_dot(left, right):
    return lax.dot_general(left, right, (((1,), (1,)), ((), ())), preferred_element_type=F32)


def ring_order(n):
    return list(range(0, n, 2)) + list(range(n - 1, 0, -2))


def ring_pairs(n, by):
    order = ring_order(n)
    return [(order[i], order[(i + by) % n]) for i in range(n)]


def ring(value, by):
    return lax.ppermute(value, "zy", ring_pairs(lax.axis_size("zy"), by))


def swap(value, axis):
    return lax.ppermute(value, axis, [(0, 1), (1, 0)])


MESH = pl.DeviceIdType.MESH


def ring_chip(spot, chips):
    spot = lax.rem(spot, chips)
    return jnp.where(spot < chips // 2, 2 * spot, 2 * (chips - 1 - spot) + 1)


def ring_spot(chip, chips):
    return jnp.where(lax.rem(chip, 2) == 0, chip // 2, chips - 1 - chip // 2)


def gather_kernel(chips, streams, shard, full, ring_send, ring_recv, x_send, x_recv, core_send, core_recv, own_sem):
    chip = lax.axis_index("zy")
    core = lax.axis_index("core")
    side = lax.axis_index("fsdp")
    spot = ring_spot(chip, chips)
    rows = shard.shape[0]

    def neighbour(by):
        return {"zy": ring_chip(spot + chips + by, chips)}

    other_core = {"core": 1 - core}
    other_side = {"fsdp": 1 - side}

    barrier = pltpu.get_barrier_semaphore()
    for peer in (neighbour(1), neighbour(-1), other_core, other_side):
        pl.semaphore_signal(barrier, inc=1, device_id=peer, device_id_type=MESH)
    pl.semaphore_wait(barrier, 4)

    def place(owner, its_core, its_side, stream):
        row = ((owner * 2 + its_core) * 2 + its_side) * rows
        return full.at[pl.ds(pl.multiple_of(row, rows), rows), pl.ds(stream[0], stream[1])]

    def owner_at(step, stream):
        return ring_chip(spot + chips - stream[2] * step, chips)

    def send(src, dst, sems, at, peer):
        return pltpu.make_async_remote_copy(
            src_ref=src,
            dst_ref=dst,
            send_sem=sems[0].at[at],
            recv_sem=sems[1].at[at],
            device_id=peer,
            device_id_type=MESH,
        )

    ring_sems, x_sems, core_sems = (ring_send, ring_recv), (x_send, x_recv), (core_send, core_recv)

    def ring_copy(number, away, step, src=None):
        stream = streams[number]
        its_side = 1 - side if away else side
        spot_ref = place(owner_at(step, stream), core, its_side, stream)
        return send(src if src is not None else spot_ref, spot_ref, ring_sems, (number, away, step), neighbour(stream[2]))

    def ring_arrival(number, away, step):
        stream = streams[number]
        its_side = 1 - side if away else side
        spot_ref = place(owner_at(step, stream), core, its_side, stream)
        return send(spot_ref, spot_ref, ring_sems, (number, away, step - 1), neighbour(stream[2]))

    def x_copy(number, step, its_side, src=None):
        stream = streams[number]
        spot_ref = place(owner_at(step, stream), core, its_side, stream)
        return send(src if src is not None else spot_ref, spot_ref, x_sems, (number, step), other_side)

    def core_copy(number, away, step, its_core, src=None):
        stream = streams[number]
        its_side = 1 - side if away else side
        spot_ref = place(owner_at(step, stream), its_core, its_side, stream)
        return send(src if src is not None else spot_ref, spot_ref, core_sems, (number, away, step), other_core)

    def cut(stream):
        return shard.at[:, pl.ds(stream[0], stream[1])]

    own_row = ((chip * 2 + core) * 2 + side) * rows
    own = pltpu.make_async_copy(
        shard, full.at[pl.ds(pl.multiple_of(own_row, rows), rows), :], own_sem
    )
    own.start()
    numbers = range(len(streams))
    for number in numbers:
        if streams[number][3]:
            x_copy(number, 0, side, cut(streams[number])).start()
    for number in numbers:
        ring_copy(number, 0, 0, cut(streams[number])).start()
    for number in numbers:
        if not streams[number][3]:
            x_copy(number, 0, side, cut(streams[number])).start()
    for number in numbers:
        core_copy(number, 0, 0, core, cut(streams[number])).start()
    for number in numbers:
        if streams[number][3]:
            x_copy(number, 0, 1 - side).wait_recv()
            ring_copy(number, 1, 0).start()
            core_copy(number, 1, 0, core).start()

    def turn(step, carry):
        for number in numbers:
            aways = (0, 1) if streams[number][3] else (0,)
            for away in aways:
                ring_arrival(number, away, step).wait_recv()

                @pl.when(step < chips - 1)
                def _(number=number, away=away):
                    ring_copy(number, away, step).start()

                core_copy(number, away, step, core).start()
            if not streams[number][3]:
                x_copy(number, step, side).start()
        for number in numbers:
            if not streams[number][3]:
                x_copy(number, step - 1, 1 - side).wait_recv()
                core_copy(number, 1, step - 1, core).start()
        return carry

    lax.fori_loop(1, chips, turn, 0)
    for number in numbers:
        if not streams[number][3]:
            x_copy(number, chips - 1, 1 - side).wait_recv()
            core_copy(number, 1, chips - 1, core).start()
    own.wait()

    def drain(step, carry):
        for number in numbers:
            first = streams[number][3]
            for away in (0, 1):
                core_copy(number, away, step, 1 - core).wait_recv()
                core_copy(number, away, step, core).wait_send()
                if first or not away:

                    @pl.when(step < chips - 1)
                    def _(number=number, away=away):
                        ring_copy(number, away, step).wait_send()

            if not first:
                x_copy(number, step, side).wait_send()
        return carry

    lax.fori_loop(0, chips, drain, 0)
    for number in numbers:
        if streams[number][3]:
            x_copy(number, 0, side).wait_send()


def gather_all(shard, chips):
    rows, cols = shard.shape
    tiles = cols // 128
    first = int(round(tiles * 0.43)) // 2 * 2
    rest = tiles - first
    bounds = [0, first // 2, first, first + rest // 2, tiles]
    streams = tuple(
        (128 * bounds[i], 128 * (bounds[i + 1] - bounds[i]), 1 if i % 2 == 0 else -1, i < 2)
        for i in range(4)
    )
    dma = pltpu.SemaphoreType.DMA
    return pl.pallas_call(
        functools.partial(gather_kernel, chips, streams),
        out_shape=jax.ShapeDtypeStruct((rows * 4 * chips, cols), shard.dtype),
        in_specs=[pl.BlockSpec(memory_space=pl.ANY)],
        out_specs=pl.BlockSpec(memory_space=pl.ANY),
        scratch_shapes=[
            dma((4, 2, chips)),
            dma((4, 2, chips)),
            dma((4, chips)),
            dma((4, chips)),
            dma((4, 2, chips)),
            dma((4, 2, chips)),
            dma,
        ],
        compiler_params=pltpu.CompilerParams(collective_id=0, has_side_effects=True),
        cost_estimate=pl.CostEstimate(
            flops=0, bytes_accessed=2 * rows * 4 * chips * cols * 2, transcendentals=0
        ),
        name="gather_all",
    )(shard)


def sum_kernel(chips, streams, counts, *refs):
    arrays, (tile, *unit_refs), outs, (tile_out, up_in, down_in), held, core_in, ring_in, x_in, tiles, sems = refs_of(counts, refs)
    load_sem, core_send, core_recv, ring_send, ring_recv, x_send, x_recv, tile_send, tile_recv, hop_send, hop_recv = sems
    tile_pairs, tile_ring, hop_sums, hop_terms = tiles
    chip = lax.axis_index("zy")
    core = lax.axis_index("core")
    side = lax.axis_index("fsdp")
    spot = ring_spot(chip, chips)
    far = 1 - side

    def neighbour(by):
        return {"zy": ring_chip(spot + chips + by, chips)}

    other_core = {"core": 1 - core}
    other_side = {"fsdp": 1 - side}
    barrier = pltpu.get_barrier_semaphore()
    for peer in (neighbour(1), neighbour(-1), other_core, other_side):
        pl.semaphore_signal(barrier, inc=1, device_id=peer, device_id_type=MESH)
    pl.semaphore_wait(barrier, 4)

    numbers = range(len(streams))

    def owner_at(number, turn):
        return ring_chip(spot + 2 * chips - streams[number][3] * turn, chips)

    def cols(number):
        return pl.ds(streams[number][1], streams[number][2])

    def remote(src, dst, send, recv, peer):
        return pltpu.make_async_remote_copy(
            src_ref=src, dst_ref=dst, send_sem=send, recv_sem=recv, device_id=peer, device_id_type=MESH
        )

    def core_copy(number, turn):
        owner = owner_at(number, turn)
        array = streams[number][0]
        return remote(
            arrays[array].at[owner, 1 - core, :, :, cols(number)],
            core_in[array].at[owner, :, :, cols(number)],
            core_send.at[number, turn - 1],
            core_recv.at[number, turn - 1],
            other_core,
        )

    def x_copy(number, turn):
        array = streams[number][0]
        first = streams[number][4]
        slot = turn - 1 if first else 0
        return remote(
            held[array].at[owner_at(number, turn), far, :, cols(number)],
            x_in[number].at[slot],
            x_send.at[number, slot],
            x_recv.at[number, slot],
            other_side,
        )

    def ring_copy(number, turn):
        array = streams[number][0]
        owner = owner_at(number, turn)
        if streams[number][4]:
            src = held[array].at[owner, pl.ds(side, 1), :, cols(number)]
        else:
            src = held[array].at[owner, :, :, cols(number)]
        return remote(
            src,
            ring_in[number].at[turn - 1],
            ring_send.at[number, turn - 1],
            ring_recv.at[number, turn - 1],
            neighbour(streams[number][3]),
        )

    loads = [
        pltpu.make_async_copy(arrays[i].at[:, core], held[i], load_sem.at[i])
        for i in range(len(arrays))
    ]

    loads += [
        pltpu.make_async_copy(ref, held_in.at[way], load_sem.at[len(arrays) + 2 * i + way])
        for i, held_in in enumerate((hop_sums, hop_terms))
        for way, ref in enumerate(unit_refs[2 * i : 2 * i + 2])
    ]

    def send_cores(turn, carry):
        for number in numbers:
            core_copy(number, turn).start()
        return carry

    def hop_copy(way, kind):
        return remote(
            hop_sums.at[way, kind],
            (up_in, down_in)[way].at[kind],
            hop_send.at[way, kind],
            hop_recv.at[way, kind],
            neighbour(1 - 2 * way),
        )

    def hop_on(kind):
        for way in range(2):
            hop_sums[way, kind] = (
                hop_sums[way, kind].astype(F32) + hop_terms[way, kind].astype(F32)
            ).astype(BF16)
            hop_copy(way, kind).start()

    def tile_copy(src, dst, number, peer):
        return remote(src, dst, tile_send.at[number], tile_recv.at[number], peer)

    def tile_turn(turn):
        spot_ref = tile_ring.at[ring_chip(spot + 2 * chips - turn + 1, chips)]
        return tile_copy(spot_ref, spot_ref, turn + 1, neighbour(1))

    def tile_arrival(turn):
        spot_ref = tile_ring.at[ring_chip(spot + 2 * chips - turn, chips)]
        return tile_copy(spot_ref, spot_ref, turn + 1, neighbour(1))

    tile_copy(tile, tile_pairs.at[0], 0, other_core).start()
    lax.fori_loop(1, 2, send_cores, 0)
    for load in loads:
        load.start()
    tile_copy(tile, tile_pairs.at[0], 0, other_core).wait()
    tile_pairs[1] = tile[...] + tile_pairs[0]
    tile_copy(tile_pairs.at[1], tile_pairs.at[2], 1, other_side).start()
    lax.fori_loop(2, chips + 1, send_cores, 0)
    for load in loads:
        load.wait()

    def add_cores(number, turn):
        array = streams[number][0]
        owner = owner_at(number, turn)
        core_copy(number, turn).wait_recv()
        for its_side in range(2):
            held[array][owner, its_side, :, cols(number)] = (
                held[array][owner, its_side, :, cols(number)].astype(F32)
                + core_in[array][owner, its_side, :, cols(number)].astype(F32)
            ).astype(BF16)

    def begin(turn):
        for number in numbers:
            if streams[number][4]:
                add_cores(number, turn)
                x_copy(number, turn).start()

    begin(1)
    tile_copy(tile_pairs.at[1], tile_pairs.at[2], 1, other_side).wait()
    tile_ring[chip] = tile_pairs[1] + tile_pairs[2]

    def round_trip(turn, carry):
        @pl.when(turn > 1)
        def _():
            tile_arrival(turn - 1).wait_recv()

        @pl.when(turn < chips)
        def _():
            tile_turn(turn).start()

        for kind in range(3):

            @pl.when(turn == 1 + kind)
            def _(kind=kind):
                hop_on(kind)

        @pl.when(turn < chips)
        def _():
            begin(turn + 1)

        for number in numbers:
            array = streams[number][0]
            owner = owner_at(number, turn)
            if not streams[number][4]:
                add_cores(number, turn)

                @pl.when(turn > 1)
                def _(number=number, array=array, owner=owner):
                    ring_copy(number, turn - 1).wait_recv()
                    for its_side in range(2):
                        held[array][owner, its_side, :, cols(number)] = (
                            held[array][owner, its_side, :, cols(number)].astype(F32)
                            + ring_in[number][turn - 2, its_side].astype(F32)
                        ).astype(BF16)

                @pl.when(turn < chips)
                def _(number=number):
                    ring_copy(number, turn).start()

        for number in numbers:
            array = streams[number][0]
            owner = owner_at(number, turn)
            if streams[number][4]:
                x_copy(number, turn).wait_recv()

                @pl.when(turn == 1)
                def _(number=number, array=array, owner=owner):
                    held[array][owner, side, :, cols(number)] = (
                        held[array][owner, side, :, cols(number)].astype(F32)
                        + x_in[number][turn - 1].astype(F32)
                    ).astype(BF16)

                @pl.when(turn > 1)
                def _(number=number, array=array, owner=owner):
                    ring_copy(number, turn - 1).wait_recv()
                    total = (
                        held[array][owner, side, :, cols(number)].astype(F32)
                        + x_in[number][turn - 1].astype(F32)
                        + ring_in[number][turn - 2, 0].astype(F32)
                    )
                    held[array][owner, side, :, cols(number)] = total.astype(BF16)

                    @pl.when(turn == chips)
                    def _():
                        outs[array][:, cols(number)] = total

                @pl.when(turn < chips)
                def _(number=number):
                    ring_copy(number, turn).start()

        return carry

    lax.fori_loop(1, chips + 1, round_trip, 0)
    for number in numbers:
        if not streams[number][4]:
            x_copy(number, chips).start()
    tile_out[...] = lax.fori_loop(1, chips, lambda i, total: total + tile_ring[i], tile_ring[0])
    for number in numbers:
        array = streams[number][0]
        if not streams[number][4]:
            x_copy(number, chips).wait_recv()
            outs[array][:, cols(number)] = held[array][chip, side, :, cols(number)].astype(
                F32
            ) + x_in[number][0].astype(F32)

    for kind in range(3):
        for way in range(2):
            hop_copy(way, kind).wait()

    def drain(turn, carry):
        for number in numbers:
            core_copy(number, turn).wait_send()
            if streams[number][4]:
                x_copy(number, turn).wait_send()

            @pl.when(turn < chips)
            def _(number=number):
                ring_copy(number, turn).wait_send()

        @pl.when(turn < chips)
        def _():
            tile_turn(turn).wait_send()

        return carry

    lax.fori_loop(1, chips + 1, drain, 0)
    for number in numbers:
        if not streams[number][4]:
            x_copy(number, chips).wait_send()


def refs_of(counts, refs):
    groups, at = [], 0
    for count in counts:
        groups.append(refs[at : at + count])
        at += count
    return groups


def sum_all(arrays, firsts, tile, arrived, terms, chips):
    rows = arrays[0].shape[0] // (4 * chips)
    streams = []
    for i, (array, first) in enumerate(zip(arrays, firsts)):
        for low, high, is_first in ((0, first, True), (first, array.shape[1], False)):
            left = (high - low) // 256 * 128
            if high > low:
                streams.append((i, low, left, 1, is_first))
                streams.append((i, low + left, high - low - left, -1, is_first))
    streams = tuple(sorted(streams, key=lambda stream: stream[4]))
    count, number = len(arrays), len(streams)
    dma = pltpu.SemaphoreType.DMA
    vmem = pltpu.VMEM
    scratch = (
        [vmem((chips, 2, rows, a.shape[1]), BF16) for a in arrays]
        + [vmem((chips, 2, rows, a.shape[1]), BF16) for a in arrays]
        + [vmem((chips - 1, 1 if first else 2, rows, width), BF16) for _, _, width, _, first in streams]
        + [vmem((chips if first else 1, rows, width), BF16) for _, _, width, _, first in streams]
        + [vmem((3, 8, 128), F32), vmem((chips, 8, 128), F32)]
        + [vmem((2,) + terms[0].shape, BF16)] * 2
        + [dma((count + 4,))]
        + [dma((number, chips)) for _ in range(6)]
        + [dma((chips + 1,)) for _ in range(2)]
        + [dma((2, 3)) for _ in range(2)]
    )
    return pl.pallas_call(
        functools.partial(
            sum_kernel, chips, streams, (count, 5, count, 3, count, count, number, number, 4, 11)
        ),
        out_shape=[jax.ShapeDtypeStruct((rows, a.shape[1]), F32) for a in arrays]
        + [jax.ShapeDtypeStruct((8, 128), F32)]
        + [jax.ShapeDtypeStruct(terms[0].shape, BF16)] * 2,
        in_specs=[pl.BlockSpec(memory_space=pl.ANY)] * count
        + [pl.BlockSpec(memory_space=pltpu.VMEM)]
        + [pl.BlockSpec(memory_space=pl.ANY)] * 4,
        out_specs=[pl.BlockSpec(memory_space=pltpu.VMEM)] * (count + 1) + [pl.BlockSpec(memory_space=pl.ANY)] * 2,
        scratch_shapes=scratch,
        compiler_params=pltpu.CompilerParams(
            collective_id=1, has_side_effects=True, vmem_limit_bytes=58 << 20
        ),
        cost_estimate=pl.CostEstimate(
            flops=0, bytes_accessed=sum(2 * a.size for a in arrays), transcendentals=0
        ),
        name="sum_all",
    )(*[a.reshape(chips, 2, 2, rows, a.shape[1]) for a in arrays], tile, *arrived, *terms)


LITTLE = pl.CostEstimate(flops=0, bytes_accessed=1024, transcendentals=0)
VMEM_LIMIT = 56 << 20


def whole(shape):
    return pl.BlockSpec(shape, lambda *_: (0,) * len(shape))


def piece(kernel, name, grid, in_specs, out_specs, out_shapes, scratch=()):
    return pl.pallas_call(
        kernel,
        grid=grid,
        in_specs=in_specs,
        out_specs=out_specs,
        out_shape=[jax.ShapeDtypeStruct(shape, dtype) for shape, dtype in out_shapes],
        scratch_shapes=list(scratch),
        compiler_params=pltpu.CompilerParams(vmem_limit_bytes=VMEM_LIMIT),
        cost_estimate=LITTLE,
        name=name,
    )


def inverse_rms(values):
    return lax.rsqrt(jnp.mean(values * values, axis=-1, keepdims=True) + EPSILON)


def norm_back(values, gain, grad):
    scale = inverse_rms(values)
    scaled = grad * gain
    mean = jnp.mean(values * scaled, axis=-1, keepdims=True)
    back = scale * scaled - values * (scale * scale * scale * mean)
    return back, jnp.sum(grad * (values * scale), axis=0, keepdims=True)


def qkv_kernel(tokens, gains, head_gain, cosine, sine, weight, low, raw, new):
    at = pl.program_id(0)

    @pl.when(at == 0)
    def _():
        states = tokens[...].astype(F32)
        low[...] = (states * inverse_rms(states) * gains[0:1]).astype(BF16)

    out = full_dot(low[...], weight[...])
    raw[...] = out
    plain = out * inverse_rms(out)
    values = plain * jnp.where(at < HEADS, head_gain[0:1], head_gain[1:2])
    half = HEAD // 2
    first, second = values[:, :half], values[:, half:]
    turned = jnp.concatenate(
        [first * cosine[...] - second * sine[...], second * cosine[...] + first * sine[...]], 1
    )
    new[...] = jnp.where(at < HEADS + KV_HEADS, turned, plain).astype(BF16)


def make_qkv(tokens, gains, head_gain, cosine, sine, full):
    rows = tokens.shape[0]
    heads = HEADS + 2 * KV_HEADS
    return piece(
        qkv_kernel,
        "make_qkv",
        (heads,),
        [
            whole((rows, D)),
            whole(gains.shape),
            whole((2, HEAD)),
            whole(cosine.shape),
            whole(sine.shape),
            pl.BlockSpec((D, HEAD), lambda i: (0, HEADS + i)),
        ],
        [
            whole((rows, D)),
            pl.BlockSpec((rows, HEAD), lambda i: (0, i)),
            pl.BlockSpec((rows, HEAD), lambda i: (0, i)),
        ],
        [((rows, D), BF16), ((rows, heads * HEAD), F32), ((rows, heads * HEAD), BF16)],
    )(tokens, gains, head_gain, cosine, sine, full)


def softmax_of(query, key, visible):
    scores = jnp.where(visible > 0.0, right_dot(query, key), -1e30)
    expo = jnp.exp(scores - jnp.max(scores, axis=-1, keepdims=True))
    return expo / jnp.sum(expo, axis=-1, keepdims=True)


def attend_kernel(
    tokens, gains, low, query, key, value, visible, w_out, lleft, lright,
    context, attn_raw, mixed, ffn_in, mid,
):
    at = pl.program_id(0)
    probs = softmax_of(query[...], key[...], visible[...]).astype(BF16)
    here = full_dot(probs, value[...]).astype(BF16)
    context[...] = here
    term = full_dot(here, w_out[...])

    @pl.when(at == 0)
    def _():
        attn_raw[...] = term

    @pl.when(at > 0)
    def _():
        attn_raw[...] += term

    @pl.when(at == HEADS - 1)
    def _():
        states = tokens[...].astype(F32)
        raw = attn_raw[...]
        total = states + raw * inverse_rms(raw) * gains[1:2]
        total = total + states * inverse_rms(states) * gains[0:1]
        mid[...] = full_dot(low[...], lleft[...]).astype(BF16)
        laurel = right_dot(mid[...], lright[...])
        total = (total + laurel * inverse_rms(laurel) * gains[2:3]) * INV_SQRT2
        mixed[...] = total
        ffn_in[...] = (total * inverse_rms(total) * gains[3:4]).astype(BF16)


def attend(tokens, gains, low, qkv, keys_all, visible, full):
    rows = tokens.shape[0]
    seen = keys_all.shape[0]
    group = HEADS // KV_HEADS
    side = 128
    left_at, right_at = full.shape[1] // side - 2, full.shape[1] // side - 1
    return piece(
        attend_kernel,
        "attend",
        (HEADS,),
        [
            whole((rows, D)),
            whole(gains.shape),
            whole((rows, D)),
            pl.BlockSpec((rows, HEAD), lambda i: (0, i)),
            pl.BlockSpec((seen, HEAD), lambda i: (0, i // group)),
            pl.BlockSpec((seen, HEAD), lambda i: (0, KV_HEADS + i // group)),
            whole((rows, seen)),
            pl.BlockSpec((HEAD, D), lambda i: (i, 0)),
            pl.BlockSpec((D, side), lambda i: (0, left_at)),
            pl.BlockSpec((D, side), lambda i: (0, right_at)),
        ],
        [
            pl.BlockSpec((rows, HEAD), lambda i: (0, i)),
            whole((rows, D)),
            whole((rows, D)),
            whole((rows, D)),
            whole((rows, side)),
        ],
        [
            ((rows, HEADS * HEAD), BF16),
            ((rows, D), F32),
            ((rows, D), F32),
            ((rows, D), BF16),
            ((rows, side), BF16),
        ],
    )(tokens, gains, low, qkv, keys_all, keys_all, visible, full, full, full)


def load_weights(weights, held, sems):
    copies, at = [], 0
    for number, ref in enumerate(weights):
        count = ref.shape[1]
        copies.append(pltpu.make_async_copy(ref, held.at[:, pl.ds(at, count)], sems.at[number]))
        at += count

    @pl.when(pl.program_id(0) == 0)
    def _():
        for copy in copies:
            copy.start()
        for copy in copies:
            copy.wait()


ROW_BLOCK = 256
UNIT_BLOCK = 512


def unit_blocks(steps, units):
    many = max(1, UNIT_BLOCK // units)
    return [range(first, min(first + many, steps)) for first in range(0, steps, many)]


def ffn_forward_kernel(steps, add, *refs):
    weights, refs = refs[: 2 * steps], refs[2 * steps :]
    if add:
        before, refs = refs[0], refs[1:]
    rows, total, refs = refs[0], refs[1], refs[2:]
    gates, uppers, hiddens, (held, sems) = refs_of((steps, steps, steps, 2), refs)
    load_weights(weights, held, sems)
    units = held.shape[1] // steps
    here = rows[...]
    running = before[...] if add else None
    for block in unit_blocks(steps, units):
        cut = slice(block[0] * units, (block[-1] + 1) * units)
        gate_in = right_dot(here, held[0, cut])
        upper_in = right_dot(here, held[1, cut])
        low = gated_product(gate_in, upper_in).astype(BF16)
        for i, step in enumerate(block):
            own = slice(i * units, (i + 1) * units)
            gates[step][...] = gate_in[:, own]
            uppers[step][...] = upper_in[:, own]
            hiddens[step][...] = low[:, own]
        term = full_dot(low, held[2, cut])
        running = term if running is None else running + term
    total[...] = running


def write_sum(running, total, low_total):
    if low_total is None:
        total[...] = running
        return
    half = pl.num_programs(0) // 2

    @pl.when(pl.program_id(0) < half)
    def _():
        low_total[...] = running.astype(BF16)

    @pl.when(pl.program_id(0) >= half)
    def _():
        total[...] = running


def sum_specs(many, last):
    blocks = many // ROW_BLOCK
    half = blocks // 2
    if not last:
        return (lambda i: i), [pl.BlockSpec((ROW_BLOCK, D), lambda i: (i, 0))], [((many, D), F32)]
    specs = [
        pl.BlockSpec((ROW_BLOCK, D), lambda i: (jnp.maximum(i - half, 0), 0)),
        pl.BlockSpec((ROW_BLOCK, D), lambda i: (jnp.minimum(i, half - 1), 0)),
    ]
    return (lambda i: lax.rem(i + half, blocks)), specs, [((many // 2, D), F32), ((many // 2, D), BF16)]


def ffn_forward(rows, before, weights):
    many = rows.shape[0]
    steps, units = len(weights) // 2, 2 * weights[0].shape[1]
    by_row = lambda width: pl.BlockSpec((ROW_BLOCK, width), lambda i: (i, 0))
    add = before is not None
    outs = piece(
        functools.partial(ffn_forward_kernel, steps, add),
        "ffn_forward",
        (many // ROW_BLOCK,),
        [pl.BlockSpec(memory_space=pl.ANY)] * len(weights) + [by_row(D)] * (1 + add),
        [by_row(D)] + [by_row(units)] * (3 * steps),
        [((many, D), F32)] + [((many, units), F32)] * (2 * steps) + [((many, units), BF16)] * steps,
        [pltpu.VMEM((3, steps * units, D), BF16), pltpu.SemaphoreType.DMA((len(weights),))],
    )(*weights, *([before] if add else []), rows)
    (total,), gate, upper, hidden = refs_of((1, steps, steps, steps), outs)
    return total, gate, upper, hidden


def ffn_backward_kernel(steps, add, last, *refs):
    weights, refs = refs[: 2 * steps], refs[2 * steps :]
    if add:
        before, refs = refs[0], refs[1:]
    (rows,), gates, uppers, totals, grad_gates, grad_uppers, (held, sems) = refs_of(
        (1, steps, steps, 1 + last, steps, steps, 2), refs
    )
    load_weights(weights, held, sems)
    units = held.shape[1] // steps
    here = rows[...]
    running = before[...] if add else None
    for block in unit_blocks(steps, units):
        cut = slice(block[0] * units, (block[-1] + 1) * units)
        grad_hidden = right_dot(here, held[2, cut])
        low_gates, low_uppers = [], []
        for i, step in enumerate(block):
            unused, act_back = jax.vjp(gated_product, gates[step][...], uppers[step][...])
            back_gate, back_upper = act_back(grad_hidden[:, i * units : (i + 1) * units])
            low_gates.append(back_gate.astype(BF16))
            low_uppers.append(back_upper.astype(BF16))
            grad_gates[step][...] = low_gates[-1]
            grad_uppers[step][...] = low_uppers[-1]
        term = full_dot(jnp.concatenate(low_gates, 1), held[0, cut])
        term = term + full_dot(jnp.concatenate(low_uppers, 1), held[1, cut])
        running = term if running is None else running + term
    write_sum(running, totals[0], totals[1] if last else None)


def ffn_backward(rows, before, weights, gates, uppers, last):
    many = rows.shape[0]
    steps, units = len(gates), gates[0].shape[1]
    at, sums, sum_shapes = sum_specs(many, last)
    by_row = lambda width: pl.BlockSpec((ROW_BLOCK, width), lambda i: (at(i), 0))
    add = before is not None
    outs = piece(
        functools.partial(ffn_backward_kernel, steps, add, last),
        "ffn_backward",
        (many // ROW_BLOCK,),
        [pl.BlockSpec(memory_space=pl.ANY)] * len(weights)
        + [by_row(D)] * (1 + add)
        + [by_row(units)] * (2 * steps),
        sums + [by_row(units)] * (2 * steps),
        sum_shapes + [((many, units), BF16)] * (2 * steps),
        [pltpu.VMEM((3, steps * units, D), BF16), pltpu.SemaphoreType.DMA((len(weights),))],
    )(*weights, *([before] if add else []), rows, *gates, *uppers)
    return refs_of((len(sums), steps, steps), outs)


def first_backward_kernel(
    up_w, down_w, down_rows, rows, gate, upper, hidden, total, grad_gate, grad_upper, up_out, down_out, held, sums, sems
):
    load_weights((up_w, down_w), held, sems)
    at = pl.program_id(0)
    unused, act_back = jax.vjp(gated_product, gate[...], upper[...])
    back_gate, back_upper = act_back(right_dot(down_rows[...], held[2]))
    low_gate, low_upper = back_gate.astype(BF16), back_upper.astype(BF16)
    grad_gate[...] = low_gate
    grad_upper[...] = low_upper
    total[...] = full_dot(low_gate, held[0]) + full_dot(low_upper, held[1])
    pairs = ((low_gate, rows), (low_upper, rows), (hidden[...], down_rows))

    @pl.when(at == 0)
    def _():
        for kind, (left, right) in enumerate(pairs):
            sums[kind] = left_dot(left, right[...])

    @pl.when(at > 0)
    def _():
        for kind, (left, right) in enumerate(pairs):
            sums[kind] += left_dot(left, right[...])

    @pl.when(at == pl.num_programs(0) - 1)
    def _():
        half = up_out.shape[1]
        up_out[...] = sums[:, :half].astype(BF16)
        down_out[...] = sums[:, half:].astype(BF16)


def first_backward(down_rows, rows, weights, gate, upper, hidden):
    many, units = gate.shape
    by_row = lambda width: pl.BlockSpec((ROW_BLOCK, width), lambda i: (i, 0))
    part = (3, units // 2, D)
    return piece(
        first_backward_kernel,
        "first_backward",
        (many // ROW_BLOCK,),
        [pl.BlockSpec(memory_space=pl.ANY)] * 2 + [by_row(D)] * 2 + [by_row(units)] * 3,
        [by_row(D)] + [by_row(units)] * 2 + [whole(part)] * 2,
        [((many, D), F32)] + [((many, units), BF16)] * 2 + [(part, BF16)] * 2,
        [pltpu.VMEM((3, units, D), BF16), pltpu.VMEM((3, units, D), F32), pltpu.SemaphoreType.DMA((2,))],
    )(*weights, down_rows, rows, gate, upper, hidden)


def unit_grads_kernel(grad_gate, grad_upper, hidden, rows, down_rows, up_out, down_out):
    half = up_out.shape[1]
    pairs = ((grad_gate, rows), (grad_upper, rows), (hidden, down_rows))
    for kind, (left, right) in enumerate(pairs):
        out = left_dot(left[...], right[...]).astype(BF16)
        up_out[kind] = out[:half]
        down_out[kind] = out[half:]


def unit_grads_of(grad_gate, grad_upper, hidden, rows, down_rows):
    many, units = hidden.shape
    width = 1024
    narrow = whole((many, units))
    wide = pl.BlockSpec((many, width), lambda i: (0, i))
    part = pl.BlockSpec((3, units // 2, width), lambda i: (0, 0, i))
    return piece(
        unit_grads_kernel,
        "unit_grads",
        (D // width,),
        [narrow, narrow, narrow, wide, wide],
        [part, part],
        [((3, units // 2, D), BF16)] * 2,
    )(grad_gate, grad_upper, hidden, rows, down_rows)


def attend_back_kernel(
    gains, grad_in, grad_after, mixed, attn_raw, mid, low, lleft, lright, w_out, context, query, key, value, visible,
    grad_mixed, grad_mid, grad_gains, grad_left, grad_right, grad_w_out, grad_query, grad_key, grad_value,
    grad_attn,
):
    at = pl.program_id(0)

    @pl.when(at == 0)
    def _():
        back, gain_3 = norm_back(mixed[...], gains[3:4], grad_in[...])
        total = (grad_after[...] + back) * INV_SQRT2
        grad_mixed[...] = total
        back, gain_2 = norm_back(right_dot(mid[...], lright[...]), gains[2:3], total)
        back_low = back.astype(BF16)
        grad_right[...] = left_dot(back_low, mid[...])
        mid_low = full_dot(back_low, lright[...]).astype(BF16)
        grad_mid[...] = mid_low
        grad_left[...] = left_dot(low[...], mid_low)
        back, gain_1 = norm_back(attn_raw[...], gains[1:2], total)
        grad_attn[...] = back.astype(BF16)
        grad_gains[...] = jnp.concatenate(
            [gain_1, gain_2, gain_3, jnp.zeros((5, D), F32)], 0
        )

    grad_context = right_dot(grad_attn[...], w_out[...]).astype(BF16)
    grad_w_out[...] = left_dot(context[...], grad_attn[...]).astype(BF16)
    probs = softmax_of(query[...], key[...], visible[...])
    grad_probs = right_dot(grad_context, value[...])
    inner = jnp.sum(probs * grad_probs, axis=-1, keepdims=True)
    grad_scores = (probs * (grad_probs - inner)).astype(BF16)
    grad_query[...] = full_dot(grad_scores, key[...])
    key_term = left_dot(grad_scores, query[...])
    value_term = left_dot(probs.astype(BF16), grad_context)
    group = HEADS // KV_HEADS

    @pl.when(lax.rem(at, group) == 0)
    def _():
        grad_key[...] = key_term
        grad_value[...] = value_term

    @pl.when(lax.rem(at, group) > 0)
    def _():
        grad_key[...] += key_term
        grad_value[...] += value_term


def attend_back(gains, grad_in, grad_after, mixed, attn_raw, mid, low, full, context, qkv, keys_all, visible):
    rows = low.shape[0]
    seen = keys_all.shape[0]
    group = HEADS // KV_HEADS
    side = 128
    left_at, right_at = full.shape[1] // side - 2, full.shape[1] // side - 1
    head = pl.BlockSpec((rows, HEAD), lambda i: (0, i))
    once = lambda shape: pl.BlockSpec(shape, lambda i: (0, 0), pipeline_mode=pl.Buffered(1))
    return piece(
        attend_back_kernel,
        "attend_back",
        (HEADS,),
        [
            whole(gains.shape),
            once((rows, D)),
            once((rows, D)),
            once((rows, D)),
            once((rows, D)),
            whole((rows, side)),
            whole((rows, D)),
            pl.BlockSpec((D, side), lambda i: (0, left_at)),
            pl.BlockSpec((D, side), lambda i: (0, right_at)),
            pl.BlockSpec((HEAD, D), lambda i: (i, 0)),
            head,
            head,
            pl.BlockSpec((seen, HEAD), lambda i: (0, i // group)),
            pl.BlockSpec((seen, HEAD), lambda i: (0, KV_HEADS + i // group)),
            whole((rows, seen)),
        ],
        [
            whole((rows, D)),
            whole((rows, side)),
            whole((8, D)),
            whole((D, side)),
            whole((D, side)),
            pl.BlockSpec((HEAD, D), lambda i: (i, 0)),
            head,
            pl.BlockSpec((seen, HEAD), lambda i: (0, i // group)),
            pl.BlockSpec((seen, HEAD), lambda i: (0, i // group)),
        ],
        [
            ((rows, D), F32),
            ((rows, side), BF16),
            ((8, D), F32),
            ((D, side), F32),
            ((D, side), F32),
            ((HEADS * HEAD, D), BF16),
            ((rows, HEADS * HEAD), F32),
            ((seen, KV_HEADS * HEAD), F32),
            ((seen, KV_HEADS * HEAD), F32),
        ],
        [pltpu.VMEM((rows, D), BF16)],
    )(
        gains, grad_in, grad_after, mixed, attn_raw, mid, low, full, full, full, context, qkv, keys_all, keys_all,
        visible,
    )


def turn_back(grad, cosine, sine):
    half = HEAD // 2
    first, second = grad[:, :half], grad[:, half:]
    return jnp.concatenate([first * cosine + second * sine, second * cosine - first * sine], 1)


def query_back_kernel(grad_query, raw, cosine, sine, head_gain, low, weight, grad_w, grad_low, grad_head):
    at = pl.program_id(0)
    turned = turn_back(grad_query[...], cosine[...], sine[...])
    back, gain = norm_back(raw[...], head_gain[0:1], turned)
    back_low = back.astype(BF16)
    grad_w[...] = left_dot(low[...], back_low).astype(BF16)
    term = right_dot(back_low, weight[...])

    @pl.when(at == 0)
    def _():
        grad_low[...] = term
        grad_head[...] = gain

    @pl.when(at > 0)
    def _():
        grad_low[...] += term
        grad_head[...] += gain


def query_back(grad_query, raw, cosine, sine, head_gain, low, full):
    rows = low.shape[0]
    head = pl.BlockSpec((rows, HEAD), lambda i: (0, i))
    return piece(
        query_back_kernel,
        "query_back",
        (HEADS,),
        [
            head,
            head,
            whole(cosine.shape),
            whole(sine.shape),
            whole((2, HEAD)),
            whole((rows, D)),
            pl.BlockSpec((D, HEAD), lambda i: (0, HEADS + i)),
        ],
        [pl.BlockSpec((D, HEAD), lambda i: (0, i)), whole((rows, D)), whole((1, HEAD))],
        [((D, HEADS * HEAD), BF16), ((rows, D), F32), ((1, HEAD), F32)],
    )(grad_query, raw, cosine, sine, head_gain, low, full)


def key_back_kernel(
    grad_kv, raw, cosine, sine, head_gain, low, weight, before, grad_mixed, grad_mid, lleft, tokens, gains,
    grad_w, grad_tokens, grad_head, grad_gain, total,
):
    at = pl.program_id(0)
    is_key = at < KV_HEADS
    grad = grad_kv[...]
    turned = jnp.where(is_key, turn_back(grad, cosine[...], sine[...]), grad)
    back, gain = norm_back(raw[...], jnp.where(is_key, head_gain[1:2], 1.0), turned)
    back_low = back.astype(BF16)
    grad_w[...] = left_dot(low[...], back_low).astype(BF16)
    term = right_dot(back_low, weight[...])

    @pl.when(at == 0)
    def _():
        total[...] = before[...] + term
        grad_head[...] = gain

    @pl.when(at > 0)
    def _():
        total[...] += term
        grad_head[...] += jnp.where(is_key, gain, 0.0)

    @pl.when(at == 2 * KV_HEADS - 1)
    def _():
        grad_normed = total[...] + grad_mixed[...] + right_dot(grad_mid[...], lleft[...])
        back, gain_0 = norm_back(tokens[...].astype(F32), gains[0:1], grad_normed)
        grad_tokens[...] = grad_mixed[...] + back
        grad_gain[...] = gain_0


def key_back(grad_kv, raw, cosine, sine, head_gain, low, full, before, grad_mixed, grad_mid, tokens, gains):
    rows = low.shape[0]
    side = 128
    left_at = full.shape[1] // side - 2
    return piece(
        key_back_kernel,
        "key_back",
        (2 * KV_HEADS,),
        [
            pl.BlockSpec((rows, HEAD), lambda i: (0, i)),
            pl.BlockSpec((rows, HEAD), lambda i: (0, HEADS + i)),
            whole(cosine.shape),
            whole(sine.shape),
            whole((2, HEAD)),
            whole((rows, D)),
            pl.BlockSpec((D, HEAD), lambda i: (0, 2 * HEADS + i)),
            whole((rows, D)),
            whole((rows, D)),
            whole((rows, side)),
            pl.BlockSpec((D, side), lambda i: (0, left_at)),
            whole((rows, D)),
            whole(gains.shape),
        ],
        [
            pl.BlockSpec((D, HEAD), lambda i: (0, i)),
            whole((rows, D)),
            whole((1, HEAD)),
            whole((1, D)),
        ],
        [
            ((D, 2 * KV_HEADS * HEAD), BF16),
            ((rows, D), F32),
            ((1, HEAD), F32),
            ((1, D), F32),
        ],
        [pltpu.VMEM((rows, D), F32)],
    )(grad_kv, raw, cosine, sine, head_gain, low, full, before, grad_mixed, grad_mid, full, tokens, gains)


def tie(*values):
    return lax.optimization_barrier(values)


def shares(total, count):
    return [total // count + (1 if i < total % count else 0) for i in range(count)]


def greet(peers):
    barrier = pltpu.get_barrier_semaphore()
    for peer in peers:
        pl.semaphore_signal(barrier, inc=1, device_id=peer, device_id_type=MESH)
    pl.semaphore_wait(barrier, len(peers))


def partners():
    return {"core": 1 - lax.axis_index("core")}, {"fsdp": 1 - lax.axis_index("fsdp")}


CUTS = 8
FLYING = 2


def spread_kernel(own, rows, x_send, x_recv, near_send, near_recv, far_send, far_recv, own_sem):
    count = own.shape[0]
    cut = count // CUTS
    other_core, other_side = partners()
    greet((other_core, other_side))

    def copy(src, block, at, send, recv, peer):
        return pltpu.make_async_remote_copy(
            src_ref=src,
            dst_ref=rows.at[pl.ds(block * count + at * cut, cut)],
            send_sem=send.at[at],
            recv_sem=recv.at[at],
            device_id=peer,
            device_id_type=MESH,
        )

    mine = [own.at[pl.ds(at * cut, cut)] for at in range(CUTS)]
    came = [rows.at[pl.ds(count + at * cut, cut)] for at in range(CUTS)]
    across = [copy(mine[at], 1, at, x_send, x_recv, other_side) for at in range(CUTS)]
    near = [copy(mine[at], 2, at, near_send, near_recv, other_core) for at in range(CUTS)]
    far = [copy(came[at], 3, at, far_send, far_recv, other_core) for at in range(CUTS)]
    for one in across[:FLYING] + near:
        one.start()
    keep = pltpu.make_async_copy(own, rows.at[pl.ds(0, count)], own_sem)
    keep.start()
    for at in range(CUTS):
        across[at].wait_send()
        if at + FLYING < CUTS:
            across[at + FLYING].start()
        across[at].wait_recv()
        far[at].start()
    for one in near + far:
        one.wait()
    keep.wait()


def rows_of_four(own, number):
    count = own.shape[0]
    dma = pltpu.SemaphoreType.DMA
    return pl.pallas_call(
        spread_kernel,
        out_shape=jax.ShapeDtypeStruct((4 * count, D), BF16),
        in_specs=[pl.BlockSpec(memory_space=pltpu.VMEM)],
        out_specs=pl.BlockSpec(memory_space=pl.ANY),
        scratch_shapes=[dma((CUTS,)) for _ in range(6)] + [dma],
        compiler_params=pltpu.CompilerParams(collective_id=number, has_side_effects=True),
        cost_estimate=LITTLE,
        name="spread_rows",
    )(own)


def gather_sum_kernel(steps, *refs):
    if steps:
        (own, low, rows, down_rows), sides, (out,), grads, more, held, sems = refs_of(
            (4, 3 * steps, 1, 2 * steps, 4 + 4, 3, 3), refs
        )
        core_in, pair_low, x_in, parts, *copy_sems = more
        core_send, core_recv, x_send, x_recv = copy_sems
        rows_in, down_in, more_out = held
        loads_sem, parts_sem, grads_sem = sems
        parts_out = more_out

        def store(step, way):
            return pltpu.make_async_copy(parts_out.at[step, way], grads[2 * step + way], grads_sem.at[step, way])

        loads = [
            pltpu.make_async_copy(rows, rows_in, loads_sem.at[0]),
            pltpu.make_async_copy(down_rows, down_in, loads_sem.at[1]),
        ]
        part_loads = [
            pltpu.make_async_copy(side, parts.at[number], parts_sem.at[number]) for number, side in enumerate(sides)
        ]
        for load in loads + part_loads:
            load.start()
    else:
        own, low, out, core_in, pair_low, x_in, core_send, core_recv, x_send, x_recv = refs
    count = out.shape[0]
    cut = count // CUTS
    other_core, other_side = partners()
    greet((other_core, other_side))

    def core_copy(block, at):
        here = pl.ds(block * count + at * cut, cut)
        number = block * CUTS + at
        return pltpu.make_async_remote_copy(
            src_ref=low.at[here],
            dst_ref=core_in.at[here],
            send_sem=core_send.at[number],
            recv_sem=core_recv.at[number],
            device_id=other_core,
            device_id_type=MESH,
        )

    def x_copy(at):
        here = pl.ds(at * cut, cut)
        return pltpu.make_async_remote_copy(
            src_ref=pair_low.at[here],
            dst_ref=x_in.at[here],
            send_sem=x_send.at[at],
            recv_sem=x_recv.at[at],
            device_id=other_side,
            device_id_type=MESH,
        )

    pieces = [(block, at) for block in (1, 0) for at in range(CUTS)]

    def next_piece(number):
        core_copy(*pieces[number]).wait_send()
        if number + FLYING < len(pieces):
            core_copy(*pieces[number + FLYING]).start()

    for one in pieces[:FLYING]:
        core_copy(*one).start()
    for at in range(CUTS):
        there = pl.ds(count + at * cut, cut)
        next_piece(at)
        core_copy(1, at).wait_recv()
        pair_low[pl.ds(at * cut, cut)] = (own[there] + core_in[there].astype(F32)).astype(BF16)
        x_copy(at).start()
    for at in range(CUTS):
        here = pl.ds(at * cut, cut)
        next_piece(CUTS + at)
        core_copy(0, at).wait_recv()
        out[here] = own[here] + core_in[here].astype(F32)
    if steps:
        for load in loads:
            load.wait()
        half = grads[0].shape[1]
        width = D // 2
        for step in range(steps):
            for kind in range(3):
                number = 3 * step + kind
                part_loads[number].wait()
                left, right = parts[number], down_in if kind == 2 else rows_in
                for first in range(0, D, width):
                    cols = slice(first, first + width)
                    term = left_dot(left, right[:, cols]).astype(BF16)
                    parts_out[step, 0, kind, :, cols] = term[:half]
                    parts_out[step, 1, kind, :, cols] = term[half:]
            for way in range(2):
                store(step, way).start()
    for at in range(CUTS):
        here = pl.ds(at * cut, cut)
        x_copy(at).wait_recv()
        out[here] += x_in[here].astype(F32)
    for at in range(CUTS):
        x_copy(at).wait_send()
    for step in range(steps):
        for way in range(2):
            store(step, way).wait()


def sum_of_four(own, low, number, units=(), rows=None, down_rows=None):
    count = own.shape[0] // 2
    steps = len(units)
    dma = pltpu.SemaphoreType.DMA
    vmem, anywhere = pltpu.VMEM, pl.BlockSpec(memory_space=pl.ANY)
    scratch = [vmem((2 * count, D), BF16), vmem((count, D), BF16), vmem((count, D), BF16)]
    copy_sems = [dma((2 * CUTS,)), dma((2 * CUTS,)), dma((CUTS,)), dma((CUTS,))]
    operands, shapes = [], []
    if steps:
        many, width = units[0][0].shape
        operands = [rows, down_rows] + [side for sides in units for side in sides]
        shapes = [jax.ShapeDtypeStruct((3, width // 2, D), BF16)] * (2 * steps)
        scratch += [vmem((3 * steps, many, width), BF16)]
        copy_sems += [vmem((many, D), BF16), vmem((many, D), BF16), vmem((steps, 2, 3, width // 2, D), BF16)]
        copy_sems += [dma((2,)), dma((3 * steps,)), dma((steps, 2))]
    total, *grads = pl.pallas_call(
        functools.partial(gather_sum_kernel, steps),
        out_shape=[jax.ShapeDtypeStruct((count, D), F32)] + shapes,
        in_specs=[pl.BlockSpec(memory_space=pltpu.VMEM), anywhere] + [anywhere] * len(operands),
        out_specs=[pl.BlockSpec(memory_space=pltpu.VMEM)] + [anywhere] * len(shapes),
        scratch_shapes=scratch + copy_sems,
        compiler_params=pltpu.CompilerParams(
            collective_id=number, has_side_effects=True, vmem_limit_bytes=VMEM_LIMIT
        ),
        cost_estimate=LITTLE,
        name="gather_sum",
    )(own, low, *operands)
    return total, [(grads[2 * i], grads[2 * i + 1]) for i in range(steps)]


PARTS = 4


def middle_kernel(steps, *refs):
    weights, inputs, outs, unit_outs, scratch, unit_scratch, sems = refs_of((2 * steps, 10, 8, 3 * steps, 15, 6, 14), refs)
    before, ffn_rows, mixed, layer_in, teacher, mask, scale, gains, gate_w, proj_w = inputs
    result, grad_after, grad_layer, rows, grad_gate_w, grad_proj_w, grad_gains, squares = outs
    (
        own_in, mixed_in, teacher_in, gate_in, proj_in, core_in, pair_low, x_in,
        result_out, after_out, after_low, mid_low, grad_pl, grad_raw, grad_low,
    ) = scratch
    rows_in, held, low, *unit_sides = unit_scratch
    (
        loads, stores, core_send, core_recv, x_send, x_recv, y_send, y_recv, near_send, near_recv, far_send, far_recv,
        unit_loads, unit_stores,
    ) = sems
    count = mixed.shape[0]
    cut = count // PARTS
    other_core, other_side = partners()

    def load(number, src, dst):
        return pltpu.make_async_copy(src, dst, loads.at[number])

    units = held.shape[1] // steps
    weight_loads = [
        pltpu.make_async_copy(ref, held.at[:, pl.ds(at * units // 2, units // 2)], unit_loads.at[at])
        for at, ref in enumerate(weights)
    ]
    block_loads = [
        [
            load(2 * block, ffn_rows.at[pl.ds(block * count, count)], rows_in.at[pl.ds(block * count, count)]),
            load(2 * block + 1, before.at[pl.ds(block * count, count)], own_in.at[pl.ds(block * count, count)]),
        ]
        for block in range(4)
    ]
    incoming = [
        load(8, mixed, mixed_in),
        load(9, gate_w, gate_in),
        load(10, proj_w, proj_in),
        load(11, teacher, teacher_in),
    ]
    for one in weight_loads + block_loads[3] + block_loads[1] + block_loads[2] + block_loads[0] + incoming:
        one.start()
    greet((other_core, other_side))

    def forward_block(block):
        here = slice(block * count, (block + 1) * count)
        for one in block_loads[block]:
            one.wait()
        gate = right_dot(rows_in[here], held[0])
        upper = right_dot(rows_in[here], held[1])
        hidden = gated_product(gate, upper).astype(BF16)
        for side, values in zip(unit_sides, (gate, upper, hidden)):
            for step in range(steps):
                side[step, here] = values[:, step * units : (step + 1) * units]
        return own_in[here] + full_dot(hidden, held[2])

    def unit_store(kind, step):
        return pltpu.make_async_copy(
            unit_sides[kind].at[step], unit_outs[kind * steps + step], unit_stores.at[kind * steps + step]
        )

    def remote(src, dst, send, recv, peer):
        return pltpu.make_async_remote_copy(
            src_ref=src, dst_ref=dst, send_sem=send, recv_sem=recv, device_id=peer, device_id_type=MESH
        )

    def piece_of(at):
        return pl.ds(at * cut, cut)

    def core_copy(block, at):
        here = pl.ds(block * count + at * cut, cut)
        number = block * PARTS + at
        return remote(low.at[here], core_in.at[here], core_send.at[number], core_recv.at[number], other_core)

    def x_copy(at):
        here = piece_of(at)
        return remote(pair_low.at[here], x_in.at[here], x_send.at[at], x_recv.at[at], other_side)

    def out_copy(src, block, at, send, recv, peer):
        return remote(src, rows.at[pl.ds(block * count + at * cut, cut)], send.at[at], recv.at[at], peer)

    def across(at):
        return out_copy(grad_low.at[piece_of(at)], 1, at, y_send, y_recv, other_side)

    def near(at):
        return out_copy(grad_low.at[piece_of(at)], 2, at, near_send, near_recv, other_core)

    def far(at):
        return out_copy(rows.at[pl.ds(count + at * cut, cut)], 3, at, far_send, far_recv, other_core)

    def kept(number, at):
        here = piece_of(at)
        src, dst = ((result_out, result), (after_out, grad_after), (grad_low, rows))[number]
        return pltpu.make_async_copy(src.at[here], dst.at[here], stores.at[number, at])

    for one in weight_loads:
        one.wait()
    low[count:] = forward_block(3).astype(BF16)
    for at in range(PARTS):
        core_copy(1, at).start()
    own_in[count : 2 * count] = forward_block(1)
    for at in range(PARTS):
        there = pl.ds(count + at * cut, cut)
        core_copy(1, at).wait_recv()
        pair_low[piece_of(at)] = (own_in[there] + core_in[there].astype(F32)).astype(BF16)
        x_copy(at).start()
    low[:count] = forward_block(2).astype(BF16)
    for at in range(PARTS):
        core_copy(0, at).start()
    own_in[:count] = forward_block(0)
    for kind in range(3):
        for step in range(steps):
            unit_store(kind, step).start()
    for one in incoming:
        one.wait()
    gain_4, gain_5 = gains[4:5], gains[5:6]
    total = jnp.zeros((), F32)
    sum_4 = sum_5 = jnp.zeros((1, D), F32)
    for at in range(PARTS):
        here = piece_of(at)
        core_copy(0, at).wait_recv()
        x_copy(at).wait_recv()
        down = own_in[here] + core_in[here].astype(F32) + x_in[here].astype(F32)
        after = mixed_in[here] + down * inverse_rms(down) * gain_4
        low_here = after.astype(BF16)
        after_low[here] = low_here
        raw = full_dot(low_here, gate_in[...])
        act, act_back = jax.vjp(gelu_tanh, raw)
        layer = layer_in[here].astype(F32)
        mid = (act * layer).astype(BF16)
        mid_low[here] = mid
        out = full_dot(mid, proj_in[...])
        done = after + out * inverse_rms(out) * gain_5
        result_out[here] = done
        kept(0, at).start()
        errors = done - teacher_in[here].astype(F32)
        masked = mask[here][:, 0:1] * errors
        total += jnp.sum(masked * errors)
        grad_out = masked * scale[0:1, 0:1]
        back, term = norm_back(out, gain_5, grad_out)
        sum_5 += term
        back_low = back.astype(BF16)
        grad_pl[here] = back_low
        grad_mid = right_dot(back_low, proj_in[...])
        grad_layer[here] = grad_mid * act
        raw_low = act_back(grad_mid * layer)[0].astype(BF16)
        grad_raw[here] = raw_low
        grad_here = grad_out + right_dot(raw_low, gate_in[...])
        after_out[here] = grad_here
        kept(1, at).start()
        back, term = norm_back(down, gain_4, grad_here)
        sum_4 += term
        grad_low[here] = back.astype(BF16)
        across(at).start()
        near(at).start()
        kept(2, at).start()
    grad_gains[...] = jnp.concatenate([sum_4, sum_5, jnp.zeros((6, D), F32)], 0)
    squares[...] = jnp.broadcast_to(total, squares.shape)
    for at in range(PARTS // 2):
        across(at).wait_recv()
        far(at).start()
    grad_proj_w[...] = left_dot(mid_low[...], grad_pl[...]).astype(BF16)
    grad_gate_w[...] = left_dot(after_low[...], grad_raw[...]).astype(BF16)
    for at in range(PARTS // 2, PARTS):
        across(at).wait_recv()
        far(at).start()
    for at in range(PARTS):
        far(at).wait()
        near(at).wait()
        across(at).wait_send()
        x_copy(at).wait_send()
        for block in (0, 1):
            core_copy(block, at).wait_send()
        for number in range(3):
            kept(number, at).wait()
    for kind in range(3):
        for step in range(steps):
            unit_store(kind, step).wait()


def middle(weights, before, ffn_rows, mixed, layer_in, teacher, mask, scale, gains, gate_w, proj_w):
    count = mixed.shape[0]
    steps, units = len(weights) // 2, 2 * weights[0].shape[1]
    sides = [(4 * count, units)] * steps
    dma, vmem = pltpu.SemaphoreType.DMA, pltpu.VMEM
    anywhere, inside = pl.BlockSpec(memory_space=pl.ANY), pl.BlockSpec(memory_space=pltpu.VMEM)
    shape = jax.ShapeDtypeStruct
    outs = pl.pallas_call(
        functools.partial(middle_kernel, steps),
        out_shape=[
            shape((count, D), F32),
            shape((count, D), F32),
            shape((count, PLD), F32),
            shape((4 * count, D), BF16),
            shape((D, PLD), BF16),
            shape((PLD, D), BF16),
            shape((8, D), F32),
            shape((8, 128), F32),
        ]
        + [shape(side, F32) for side in sides * 2]
        + [shape(side, BF16) for side in sides],
        in_specs=[anywhere] * (2 * steps) + [anywhere, anywhere, anywhere, inside, anywhere, inside, inside, inside, anywhere, anywhere],
        out_specs=[anywhere, anywhere, inside, anywhere, inside, inside, inside, inside] + [anywhere] * (3 * steps),
        scratch_shapes=[
            vmem((4 * count, D), F32),
            vmem((count, D), F32),
            vmem((count, D), BF16),
            vmem((D, PLD), BF16),
            vmem((PLD, D), BF16),
            vmem((2 * count, D), BF16),
            vmem((count, D), BF16),
            vmem((count, D), BF16),
            vmem((count, D), F32),
            vmem((count, D), F32),
            vmem((count, D), BF16),
            vmem((count, PLD), BF16),
            vmem((count, D), BF16),
            vmem((count, PLD), BF16),
            vmem((count, D), BF16),
            vmem((4 * count, D), BF16),
            vmem((3, steps * units, D), BF16),
            vmem((2 * count, D), BF16),
            vmem((steps, 4 * count, units), F32),
            vmem((steps, 4 * count, units), F32),
            vmem((steps, 4 * count, units), BF16),
            dma((12,)),
            dma((3, PARTS)),
            dma((2 * PARTS,)),
            dma((2 * PARTS,)),
        ]
        + [dma((PARTS,)) for _ in range(8)]
        + [dma((2 * steps,)), dma((3 * steps,))],
        compiler_params=pltpu.CompilerParams(
            collective_id=3, has_side_effects=True, vmem_limit_bytes=VMEM_LIMIT
        ),
        cost_estimate=LITTLE,
        name="middle",
    )(*weights, before, ffn_rows, mixed, layer_in, teacher, mask, scale, gains, gate_w, proj_w)
    return refs_of((8, steps, steps, steps), outs)


def body(
    tokens,
    per_layer,
    teacher,
    cont_lengths,
    w_query,
    w_kv,
    w_out,
    laurel_left,
    laurel_right,
    pl_gate,
    pl_proj,
    norm_gains,
    head_gains,
    ffn_weight,
):
    row_count = tokens.shape[1]
    chips = lax.axis_size("zy")
    seq_count = 2 * chips
    group_count = lax.axis_size("fsdp")
    shards = seq_count * group_count
    chip = lax.axis_index("zy")
    core = lax.axis_index("core")
    seq_index = chip * 2 + core
    group_index = lax.axis_index("fsdp")
    half_point = seq_count // 2
    prompt_len = half_point * row_count
    cont_shards = CONT_LEN // row_count
    cont_count = prompt_len // CONT_LEN
    is_cont = seq_index >= half_point
    rel_index = seq_index - half_point
    local_shard = jnp.where(is_cont, rel_index % cont_shards, 0)
    cont_index = jnp.where(is_cont, rel_index // cont_shards, 0)
    first_place = jnp.where(is_cont, prompt_len + local_shard * row_count, seq_index * row_count)
    row_range = jnp.arange(row_count, dtype=jnp.int32)
    places = first_place + row_range
    group_lengths = jnp.sum(
        jnp.where(
            jnp.arange(group_count, dtype=jnp.int32)[:, None] == group_index, cont_lengths, 0
        ),
        axis=0,
    )
    my_length = jnp.sum(
        jnp.where(jnp.arange(cont_count, dtype=jnp.int32) == cont_index, group_lengths, 0)
    )
    valid = jnp.logical_or(
        jnp.logical_not(is_cont), local_shard * row_count + row_range < my_length
    )
    weight_mask = valid.astype(F32)
    count = F32(group_count * prompt_len) + jnp.sum(cont_lengths).astype(F32)
    total_slots = float(row_count * seq_count * group_count)
    shard_rows = w_query.shape[0]
    key_cols = KV_HEADS * HEAD
    proj_cols = pl_proj.shape[0] * D // shard_rows
    misc_cols = RANK
    head_part = head_gains.reshape(-1, 1)
    misc = jnp.concatenate(
        [
            norm_gains.T,
            jnp.pad(head_part, ((0, shard_rows - head_part.shape[0]), (0, 0))),
            jnp.zeros((shard_rows, misc_cols - 7), BF16),
        ],
        1,
    )
    pack = jnp.concatenate(
        [
            w_out,
            w_query,
            w_kv,
            pl_gate,
            pl_proj.reshape(shard_rows, proj_cols),
            laurel_left,
            misc,
            laurel_right.T,
            jnp.zeros((shard_rows, 128 - RANK), BF16),
        ],
        1,
    )

    units = ffn_weight.shape[0]
    half = units // 2
    by_kind = ffn_weight.transpose(1, 0, 2)
    ups, downs = [by_kind[:, :half]], [by_kind[:, half:]]
    stage_steps = shares(chips - 1, 7)

    def pass_on(stage):
        for _ in range(stage_steps[stage]):
            ups.append(ring(ups[-1], 1))
            downs.append(ring(downs[-1], -1))

    def stage_end(values):
        (ups[-1], downs[-1]), values = tie((ups[-1], downs[-1]), values)
        return values

    pass_on(0)
    full = gather_all(pack, chips)
    at = 2 * D + 2 * key_cols
    plg = full[:, at : at + PLD]
    plp = full[:, at + PLD : at + PLD + proj_cols].reshape(PLD, D)
    at += PLD + proj_cols + RANK
    misc_full = stage_end(full[:, at : at + misc_cols])
    pass_on(1)
    gains = jnp.pad(misc_full[:, :6].T.astype(F32), ((0, 2), (0, 0)))
    head_n = head_gains.shape[1]
    head_gain = (
        misc_full[:, 6]
        .reshape(shards, shard_rows)[:, : 2 * head_n]
        .reshape(shards, 2, head_n)
        .transpose(1, 0, 2)
        .reshape(2, HEAD)
        .astype(F32)
    )
    freqs = jnp.exp(
        jnp.arange(HEAD // 2, dtype=F32) * (-2.0 * math.log(ROPE_BASE) / HEAD)
    )
    angles = places.astype(F32)[:, None] * freqs
    cosine, sine = jnp.cos(angles), jnp.sin(angles)
    normed_low, qkv_raw, qkv = make_qkv(tokens[0], gains, head_gain, cosine, sine, full)
    qkv = stage_end(qkv)
    kv_own = qkv[:, D:]
    pass_on(2)

    mid = chips // 2
    chain = [(i, i + 1) for i in range(mid - 1)] + [(mid - 1, mid + 1)]
    kv_before = jnp.where(
        chip == mid,
        lax.ppermute(kv_own, "zy", [(mid - 1, mid)]),
        lax.ppermute(kv_own, "zy", chain),
    )
    spans = []
    span = 2
    while span < mid:
        spans.append(span)
        span *= 2
    for span in spans:
        moved = lax.ppermute(
            kv_before, "zy", [(mid + i, mid + i + span) for i in range(min(span, mid - span))]
        )
        fresh = jnp.logical_and(chip >= mid + span, chip < mid + 2 * span)
        kv_before = jnp.where(fresh, moved, kv_before)
    kv_other = swap(jnp.where(core == 0, kv_own, kv_before), "core")
    keys_all = jnp.concatenate([kv_before, kv_other, kv_own], 0)
    keys_all = stage_end(keys_all)
    pass_on(3)
    key_len = keys_all.shape[0]
    key_places = first_place - 2 * row_count + jnp.arange(key_len, dtype=jnp.int32)
    visible = (
        (key_places[None, :] <= places[:, None])
        & (places[:, None] - key_places[None, :] < WINDOW)
        & (key_places[None, :] >= 0)
    ).astype(F32)
    context_low, attn_raw, mixed, ffn_in, laurel_mid = attend(
        tokens[0], gains, normed_low, qkv, keys_all, visible, full
    )

    ffn_in = stage_end(ffn_in)
    pass_on(4)
    ffn_rows = stage_end(rows_of_four(ffn_in, 2))
    here = len(ups)
    pass_on(5)
    gates, uppers, hiddens = [], [], []

    def weights_of(steps):
        return [w for k in steps for w in (ups[k], downs[k])]

    def forward_part(running, first, end):
        running, gate, upper, hidden = ffn_forward(ffn_rows, running, weights_of(range(first, end)))
        gates.extend(gate)
        uppers.extend(upper)
        hiddens.extend(hidden)
        return running

    running = stage_end(forward_part(None, 0, here))
    then = len(ups)
    pass_on(6)
    running = stage_end(forward_part(running, here, then))
    outs, gate, upper, hidden = middle(
        weights_of(range(then, chips)),
        running,
        ffn_rows,
        mixed,
        per_layer[0],
        teacher[0],
        jnp.broadcast_to(weight_mask[:, None], (row_count, 128)),
        jnp.broadcast_to(total_slots / count, (8, 128)),
        gains,
        plg,
        plp,
    )
    result, grad_after, grad_layer_in, grad_down_rows, grad_plg, grad_plp, late_gains, squares = outs
    gates.extend(gate)
    uppers.extend(upper)
    hiddens.extend(hidden)
    grad_gates, grad_uppers = [None] * chips, [None] * chips

    def backward_part(steps, running, last=False):
        sums, grad_gate, grad_upper = ffn_backward(
            grad_down_rows, running, weights_of(steps), [gates[k] for k in steps], [uppers[k] for k in steps], last
        )
        for k, gg, gu in zip(steps, grad_gate, grad_upper):
            grad_gates[k], grad_uppers[k] = gg, gu
        return sums if last else sums[0]

    ready = {}

    def unit_grads(k):
        if k in ready:
            return ready[k]
        return unit_grads_of(grad_gates[k], grad_uppers[k], hiddens[k], ffn_rows, grad_down_rows)

    order = list(range(1, chips)) + [0]
    ring_steps = shares(chips - 2, 6)
    done = 0
    last_sums = None

    def beside(stage, work):
        nonlocal done, up_sum, down_sum, last_sums
        values = None
        for step in range(ring_steps[stage]):
            up_in = ring(up_sum, 1)
            down_in = ring(down_sum, -1)
            if step == 0:
                values = work()
            done += 1
            terms = unit_grads(order[done])
            (up_in, down_in), terms, values = tie((up_in, down_in), terms, values)
            last_sums = (up_in, down_in), terms
            up_sum = (up_in.astype(F32) + terms[0].astype(F32)).astype(BF16)
            down_sum = (down_in.astype(F32) + terms[1].astype(F32)).astype(BF16)
        return work() if values is None else values

    first = ring_steps[0]
    then = first + 1 + ring_steps[0] + ring_steps[1]
    if first == 1 and units % 128 == 0:
        k = order[0]
        running, grad_gates[k], grad_uppers[k], up_sum, down_sum = first_backward(
            grad_down_rows, ffn_rows, weights_of([k]), gates[k], uppers[k], hiddens[k]
        )
    else:
        running = backward_part(order[:first], None)
        up_sum, down_sum = unit_grads(order[0])
    running = beside(0, lambda: backward_part(order[first:then], running))
    own_sum, low_sum = beside(1, lambda: backward_part(order[then:], running, True))

    def work():
        steps = order[done + ring_steps[2] :] if units % 128 == 0 else []
        total, grads = sum_of_four(
            own_sum,
            low_sum,
            5,
            [(grad_gates[k], grad_uppers[k], hiddens[k]) for k in steps],
            ffn_rows,
            grad_down_rows,
        )
        ready.update(zip(steps, grads))
        return total

    grad_ffn_in = beside(2, work)
    def work():
        *out, grad_keys, grad_values = attend_back(
            gains, grad_ffn_in, grad_after, mixed, attn_raw, laurel_mid, normed_low, full, context_low, qkv, keys_all,
            visible,
        )
        grad_kv = jnp.concatenate([grad_keys, grad_values], 1)
        grad_before = grad_kv[:row_count]
        grad_own = grad_kv[2 * row_count :]
        returned = swap(grad_kv[row_count : 2 * row_count].astype(BF16), "core").astype(F32)
        grad_own = grad_own + jnp.where(core == 0, returned, 0.0)
        grad_before = grad_before + jnp.where(core == 0, 0.0, returned)
        return out, grad_own, grad_before

    out, grad_own, grad_before = beside(3, work)
    (
        grad_scaled,
        grad_mid_low,
        grad_mid_gains,
        grad_lleft,
        grad_lright_t,
        grad_wo,
        grad_queries,
    ) = out

    def work():
        total = grad_before
        for span in reversed(spans):
            back = [(mid + i + span, mid + i) for i in range(min(span, mid - span))]
            total = total + lax.ppermute(total.astype(BF16), "zy", back).astype(F32)
        before_low = total.astype(BF16)
        return (
            grad_own
            + lax.ppermute(before_low, "zy", [(b, a) for a, b in chain]).astype(F32)
            + lax.ppermute(before_low, "zy", [(mid, mid - 1)]).astype(F32)
        ), query_back(grad_queries, qkv_raw, cosine, sine, head_gain, normed_low, full)

    grad_own, (grad_wq, grad_normed, grad_hq) = beside(4, work)

    def work():
        grad_wkv, grad_tokens, grad_hk, grad_g0 = key_back(
            grad_own, qkv_raw, cosine, sine, head_gain, normed_low, full, grad_normed, grad_scaled, grad_mid_low,
            tokens[0], gains,
        )
        head_back = jnp.concatenate([grad_hq, grad_hk], 0).reshape(2, shards, head_n).transpose(1, 0, 2)
        head_back = head_back.reshape(shards, 2 * head_n)
        head_back = jnp.pad(head_back, ((0, 0), (0, shard_rows - 2 * head_n))).reshape(1, D)
        misc_back = jnp.concatenate(
            [grad_g0, grad_mid_gains[:3], late_gains[:2], head_back, jnp.zeros((1, D), F32)], 0
        )
        return grad_wkv, grad_tokens, jnp.concatenate(
            [
                grad_plg,
                grad_plp.reshape(D, proj_cols),
                grad_lleft[:, :RANK].astype(BF16),
                jnp.pad(misc_back.T, ((0, 0), (0, misc_cols - 8))).astype(BF16),
                grad_lright_t.astype(BF16),
            ],
            1,
        )

    last_terms, (grad_wkv, grad_tokens, rest_back) = beside(5, lambda: (unit_grads(0), work()))
    sums_wq, sums_wkv, sums_wo, sums_rest, total, up_in, down_in = sum_all(
        [grad_wq, grad_wkv, grad_wo, rest_back],
        (D, 2 * key_cols, D - 512, 0),
        squares,
        *last_sums,
        chips,
    )
    grad_ffn = jnp.concatenate(
        [
            (arrived.astype(F32) + term.astype(F32)).transpose(1, 0, 2)
            for arrived, term in zip((up_in, down_in), last_terms)
        ],
        0,
    )
    at = 0
    rest = []
    for width in (PLD, proj_cols, RANK, misc_cols, RANK):
        rest.append(sums_rest[:, at : at + width])
        at += width

    match_loss = total[0, 0] / (2.0 * D * count)

    return (
        result[None],
        match_loss,
        grad_tokens[None],
        grad_layer_in[None],
        sums_wq,
        sums_wkv,
        sums_wo,
        rest[2],
        rest[4].T,
        rest[0],
        rest[1].reshape(pl_proj.shape),
        rest[3][:, :6].T,
        rest[3][: 2 * head_n, 6].reshape(2, head_n),
        grad_ffn,
    )


def solution(mesh):
    seq, fsdp = mesh.shape["seq"], mesh.shape["fsdp"]
    fine = Mesh(mesh.devices.reshape(seq // 2, 2, fsdp), ("zy", "core", "fsdp"))
    rows = P("fsdp", ("zy", "core"), None)
    split = ("zy", "core", "fsdp")
    weights = (
        P(split, None),
        P(split, None),
        P(split, None),
        P(split, None),
        P(None, split),
        P(split, None),
        P(split, None),
        P(None, split),
        P(None, split),
        P(split, None, None),
    )
    return jax.shard_map(
        body,
        mesh=fine,
        in_specs=(rows, rows, rows, P()) + weights,
        out_specs=(rows, P(), rows, rows) + weights,
        check_vma=False,
    )
```

```python
import functools
import math

import jax
import jax.numpy as jnp
from jax import lax
from jax.experimental import pallas as pl
from jax.experimental.pallas import tpu as pltpu
from jax.sharding import Mesh, PartitionSpec as P

D = 2048
HEADS = 8
KV_HEADS = 2
HEAD = 256
WINDOW = 512
CONT_LEN = 512
RANK = 64
PLD = 256

EPSILON = 1e-06
INV_SQRT2 = 0.7071067811865476
ROPE_BASE = 10000.0
BF16 = jnp.bfloat16
F32 = jnp.float32


def gelu_tanh(values):
    return jax.nn.gelu(values, approximate=True)


def gated_product(gate_in, up_in):
    return gelu_tanh(gate_in) * up_in


def full_dot(left, right):
    return jnp.dot(left, right, preferred_element_type=F32)


def left_dot(left, right):
    return lax.dot_general(left, right, (((0,), (0,)), ((), ())), preferred_element_type=F32)


def right_dot(left, right):
    return lax.dot_general(left, right, (((1,), (1,)), ((), ())), preferred_element_type=F32)


def ring_order(n):
    return list(range(0, n, 2)) + list(range(n - 1, 0, -2))


def ring_pairs(n, by):
    order = ring_order(n)
    return [(order[i], order[(i + by) % n]) for i in range(n)]


def ring(value, by):
    return lax.ppermute(value, "zy", ring_pairs(lax.axis_size("zy"), by))


def swap(value, axis):
    return lax.ppermute(value, axis, [(0, 1), (1, 0)])


MESH = pl.DeviceIdType.MESH


def ring_chip(spot, chips):
    spot = lax.rem(spot, chips)
    return jnp.where(spot < chips // 2, 2 * spot, 2 * (chips - 1 - spot) + 1)


def ring_spot(chip, chips):
    return jnp.where(lax.rem(chip, 2) == 0, chip // 2, chips - 1 - chip // 2)


def gather_kernel(chips, streams, shard, full, ring_send, ring_recv, x_send, x_recv, core_send, core_recv, own_sem):
    chip = lax.axis_index("zy")
    core = lax.axis_index("core")
    side = lax.axis_index("fsdp")
    spot = ring_spot(chip, chips)
    rows = shard.shape[0]

    def neighbour(by):
        return {"zy": ring_chip(spot + chips + by, chips)}

    other_core = {"core": 1 - core}
    other_side = {"fsdp": 1 - side}

    barrier = pltpu.get_barrier_semaphore()
    for peer in (neighbour(1), neighbour(-1), other_core, other_side):
        pl.semaphore_signal(barrier, inc=1, device_id=peer, device_id_type=MESH)
    pl.semaphore_wait(barrier, 4)

    def place(owner, its_core, its_side, stream):
        row = ((owner * 2 + its_core) * 2 + its_side) * rows
        return full.at[pl.ds(pl.multiple_of(row, rows), rows), pl.ds(stream[0], stream[1])]

    def owner_at(step, stream):
        return ring_chip(spot + chips - stream[2] * step, chips)

    def send(src, dst, sems, at, peer):
        return pltpu.make_async_remote_copy(
            src_ref=src,
            dst_ref=dst,
            send_sem=sems[0].at[at],
            recv_sem=sems[1].at[at],
            device_id=peer,
            device_id_type=MESH,
        )

    ring_sems, x_sems, core_sems = (ring_send, ring_recv), (x_send, x_recv), (core_send, core_recv)

    def ring_copy(number, away, step, src=None):
        stream = streams[number]
        its_side = 1 - side if away else side
        spot_ref = place(owner_at(step, stream), core, its_side, stream)
        return send(src if src is not None else spot_ref, spot_ref, ring_sems, (number, away, step), neighbour(stream[2]))

    def ring_arrival(number, away, step):
        stream = streams[number]
        its_side = 1 - side if away else side
        spot_ref = place(owner_at(step, stream), core, its_side, stream)
        return send(spot_ref, spot_ref, ring_sems, (number, away, step - 1), neighbour(stream[2]))

    def x_copy(number, step, its_side, src=None):
        stream = streams[number]
        spot_ref = place(owner_at(step, stream), core, its_side, stream)
        return send(src if src is not None else spot_ref, spot_ref, x_sems, (number, step), other_side)

    def core_copy(number, away, step, its_core, src=None):
        stream = streams[number]
        its_side = 1 - side if away else side
        spot_ref = place(owner_at(step, stream), its_core, its_side, stream)
        return send(src if src is not None else spot_ref, spot_ref, core_sems, (number, away, step), other_core)

    def cut(stream):
        return shard.at[:, pl.ds(stream[0], stream[1])]

    own_row = ((chip * 2 + core) * 2 + side) * rows
    own = pltpu.make_async_copy(
        shard, full.at[pl.ds(pl.multiple_of(own_row, rows), rows), :], own_sem
    )
    own.start()
    numbers = range(len(streams))
    for number in numbers:
        if streams[number][3]:
            x_copy(number, 0, side, cut(streams[number])).start()
    for number in numbers:
        ring_copy(number, 0, 0, cut(streams[number])).start()
    for number in numbers:
        if not streams[number][3]:
            x_copy(number, 0, side, cut(streams[number])).start()
    for number in numbers:
        core_copy(number, 0, 0, core, cut(streams[number])).start()
    for number in numbers:
        if streams[number][3]:
            x_copy(number, 0, 1 - side).wait_recv()
            ring_copy(number, 1, 0).start()
            core_copy(number, 1, 0, core).start()

    def turn(step, carry):
        for number in numbers:
            aways = (0, 1) if streams[number][3] else (0,)
            for away in aways:
                ring_arrival(number, away, step).wait_recv()

                @pl.when(step < chips - 1)
                def _(number=number, away=away):
                    ring_copy(number, away, step).start()

                core_copy(number, away, step, core).start()
            if not streams[number][3]:
                x_copy(number, step, side).start()
        for number in numbers:
            if not streams[number][3]:
                x_copy(number, step - 1, 1 - side).wait_recv()
                core_copy(number, 1, step - 1, core).start()
        return carry

    lax.fori_loop(1, chips, turn, 0)
    for number in numbers:
        if not streams[number][3]:
            x_copy(number, chips - 1, 1 - side).wait_recv()
            core_copy(number, 1, chips - 1, core).start()
    own.wait()

    def drain(step, carry):
        for number in numbers:
            first = streams[number][3]
            for away in (0, 1):
                core_copy(number, away, step, 1 - core).wait_recv()
                core_copy(number, away, step, core).wait_send()
                if first or not away:

                    @pl.when(step < chips - 1)
                    def _(number=number, away=away):
                        ring_copy(number, away, step).wait_send()

            if not first:
                x_copy(number, step, side).wait_send()
        return carry

    lax.fori_loop(0, chips, drain, 0)
    for number in numbers:
        if streams[number][3]:
            x_copy(number, 0, side).wait_send()


def gather_all(shard, chips):
    rows, cols = shard.shape
    tiles = cols // 128
    first = int(round(tiles * 0.43)) // 2 * 2
    rest = tiles - first
    bounds = [0, first // 2, first, first + rest // 2, tiles]
    streams = tuple(
        (128 * bounds[i], 128 * (bounds[i + 1] - bounds[i]), 1 if i % 2 == 0 else -1, i < 2)
        for i in range(4)
    )
    dma = pltpu.SemaphoreType.DMA
    return pl.pallas_call(
        functools.partial(gather_kernel, chips, streams),
        out_shape=jax.ShapeDtypeStruct((rows * 4 * chips, cols), shard.dtype),
        in_specs=[pl.BlockSpec(memory_space=pl.ANY)],
        out_specs=pl.BlockSpec(memory_space=pl.ANY),
        scratch_shapes=[
            dma((4, 2, chips)),
            dma((4, 2, chips)),
            dma((4, chips)),
            dma((4, chips)),
            dma((4, 2, chips)),
            dma((4, 2, chips)),
            dma,
        ],
        compiler_params=pltpu.CompilerParams(collective_id=0, has_side_effects=True),
        cost_estimate=pl.CostEstimate(
            flops=0, bytes_accessed=2 * rows * 4 * chips * cols * 2, transcendentals=0
        ),
        name="gather_all",
    )(shard)


def sum_kernel(chips, streams, counts, *refs):
    arrays, (tile, *unit_refs), outs, (tile_out, up_in, down_in), held, core_in, ring_in, x_in, tiles, sems = refs_of(counts, refs)
    load_sem, core_send, core_recv, ring_send, ring_recv, x_send, x_recv, tile_send, tile_recv, hop_send, hop_recv = sems
    tile_pairs, tile_ring, hop_sums, hop_terms = tiles
    chip = lax.axis_index("zy")
    core = lax.axis_index("core")
    side = lax.axis_index("fsdp")
    spot = ring_spot(chip, chips)
    far = 1 - side

    def neighbour(by):
        return {"zy": ring_chip(spot + chips + by, chips)}

    other_core = {"core": 1 - core}
    other_side = {"fsdp": 1 - side}
    barrier = pltpu.get_barrier_semaphore()
    for peer in (neighbour(1), neighbour(-1), other_core, other_side):
        pl.semaphore_signal(barrier, inc=1, device_id=peer, device_id_type=MESH)
    pl.semaphore_wait(barrier, 4)

    numbers = range(len(streams))

    def owner_at(number, turn):
        return ring_chip(spot + 2 * chips - streams[number][3] * turn, chips)

    def cols(number):
        return pl.ds(streams[number][1], streams[number][2])

    def remote(src, dst, send, recv, peer):
        return pltpu.make_async_remote_copy(
            src_ref=src, dst_ref=dst, send_sem=send, recv_sem=recv, device_id=peer, device_id_type=MESH
        )

    def core_copy(number, turn):
        owner = owner_at(number, turn)
        array = streams[number][0]
        return remote(
            arrays[array].at[owner, 1 - core, :, :, cols(number)],
            core_in[array].at[owner, :, :, cols(number)],
            core_send.at[number, turn - 1],
            core_recv.at[number, turn - 1],
            other_core,
        )

    def x_copy(number, turn):
        array = streams[number][0]
        first = streams[number][4]
        slot = turn - 1 if first else 0
        return remote(
            held[array].at[owner_at(number, turn), far, :, cols(number)],
            x_in[number].at[slot],
            x_send.at[number, slot],
            x_recv.at[number, slot],
            other_side,
        )

    def ring_copy(number, turn):
        array = streams[number][0]
        owner = owner_at(number, turn)
        if streams[number][4]:
            src = held[array].at[owner, pl.ds(side, 1), :, cols(number)]
        else:
            src = held[array].at[owner, :, :, cols(number)]
        return remote(
            src,
            ring_in[number].at[turn - 1],
            ring_send.at[number, turn - 1],
            ring_recv.at[number, turn - 1],
            neighbour(streams[number][3]),
        )

    loads = [
        pltpu.make_async_copy(arrays[i].at[:, core], held[i], load_sem.at[i])
        for i in range(len(arrays))
    ]

    loads += [
        pltpu.make_async_copy(ref, held_in.at[way], load_sem.at[len(arrays) + 2 * i + way])
        for i, held_in in enumerate((hop_sums, hop_terms))
        for way, ref in enumerate(unit_refs[2 * i : 2 * i + 2])
    ]

    def send_cores(turn, carry):
        for number in numbers:
            core_copy(number, turn).start()
        return carry

    def hop_copy(way, kind):
        return remote(
            hop_sums.at[way, kind],
            (up_in, down_in)[way].at[kind],
            hop_send.at[way, kind],
            hop_recv.at[way, kind],
            neighbour(1 - 2 * way),
        )

    def hop_on(kind):
        for way in range(2):
            hop_sums[way, kind] = (
                hop_sums[way, kind].astype(F32) + hop_terms[way, kind].astype(F32)
            ).astype(BF16)
            hop_copy(way, kind).start()

    def tile_copy(src, dst, number, peer):
        return remote(src, dst, tile_send.at[number], tile_recv.at[number], peer)

    def tile_turn(turn):
        spot_ref = tile_ring.at[ring_chip(spot + 2 * chips - turn + 1, chips)]
        return tile_copy(spot_ref, spot_ref, turn + 1, neighbour(1))

    def tile_arrival(turn):
        spot_ref = tile_ring.at[ring_chip(spot + 2 * chips - turn, chips)]
        return tile_copy(spot_ref, spot_ref, turn + 1, neighbour(1))

    tile_copy(tile, tile_pairs.at[0], 0, other_core).start()
    lax.fori_loop(1, 2, send_cores, 0)
    for load in loads:
        load.start()
    tile_copy(tile, tile_pairs.at[0], 0, other_core).wait()
    tile_pairs[1] = tile[...] + tile_pairs[0]
    tile_copy(tile_pairs.at[1], tile_pairs.at[2], 1, other_side).start()
    lax.fori_loop(2, chips + 1, send_cores, 0)
    for load in loads:
        load.wait()

    def add_cores(number, turn):
        array = streams[number][0]
        owner = owner_at(number, turn)
        core_copy(number, turn).wait_recv()
        for its_side in range(2):
            held[array][owner, its_side, :, cols(number)] = (
                held[array][owner, its_side, :, cols(number)].astype(F32)
                + core_in[array][owner, its_side, :, cols(number)].astype(F32)
            ).astype(BF16)

    def begin(turn):
        for number in numbers:
            if streams[number][4]:
                add_cores(number, turn)
                x_copy(number, turn).start()

    begin(1)
    tile_copy(tile_pairs.at[1], tile_pairs.at[2], 1, other_side).wait()
    tile_ring[chip] = tile_pairs[1] + tile_pairs[2]

    def round_trip(turn, carry):
        @pl.when(turn > 1)
        def _():
            tile_arrival(turn - 1).wait_recv()

        @pl.when(turn < chips)
        def _():
            tile_turn(turn).start()

        for kind in range(3):

            @pl.when(turn == 1 + kind)
            def _(kind=kind):
                hop_on(kind)

        @pl.when(turn < chips)
        def _():
            begin(turn + 1)

        for number in numbers:
            array = streams[number][0]
            owner = owner_at(number, turn)
            if not streams[number][4]:
                add_cores(number, turn)

                @pl.when(turn > 1)
                def _(number=number, array=array, owner=owner):
                    ring_copy(number, turn - 1).wait_recv()
                    for its_side in range(2):
                        held[array][owner, its_side, :, cols(number)] = (
                            held[array][owner, its_side, :, cols(number)].astype(F32)
                            + ring_in[number][turn - 2, its_side].astype(F32)
                        ).astype(BF16)

                @pl.when(turn < chips)
                def _(number=number):
                    ring_copy(number, turn).start()

        for number in numbers:
            array = streams[number][0]
            owner = owner_at(number, turn)
            if streams[number][4]:
                x_copy(number, turn).wait_recv()

                @pl.when(turn == 1)
                def _(number=number, array=array, owner=owner):
                    held[array][owner, side, :, cols(number)] = (
                        held[array][owner, side, :, cols(number)].astype(F32)
                        + x_in[number][turn - 1].astype(F32)
                    ).astype(BF16)

                @pl.when(turn > 1)
                def _(number=number, array=array, owner=owner):
                    ring_copy(number, turn - 1).wait_recv()
                    total = (
                        held[array][owner, side, :, cols(number)].astype(F32)
                        + x_in[number][turn - 1].astype(F32)
                        + ring_in[number][turn - 2, 0].astype(F32)
                    )
                    held[array][owner, side, :, cols(number)] = total.astype(BF16)

                    @pl.when(turn == chips)
                    def _():
                        outs[array][:, cols(number)] = total

                @pl.when(turn < chips)
                def _(number=number):
                    ring_copy(number, turn).start()

        return carry

    lax.fori_loop(1, chips + 1, round_trip, 0)
    for number in numbers:
        if not streams[number][4]:
            x_copy(number, chips).start()
    tile_out[...] = lax.fori_loop(1, chips, lambda i, total: total + tile_ring[i], tile_ring[0])
    for number in numbers:
        array = streams[number][0]
        if not streams[number][4]:
            x_copy(number, chips).wait_recv()
            outs[array][:, cols(number)] = held[array][chip, side, :, cols(number)].astype(
                F32
            ) + x_in[number][0].astype(F32)

    for kind in range(3):
        for way in range(2):
            hop_copy(way, kind).wait()

    def drain(turn, carry):
        for number in numbers:
            core_copy(number, turn).wait_send()
            if streams[number][4]:
                x_copy(number, turn).wait_send()

            @pl.when(turn < chips)
            def _(number=number):
                ring_copy(number, turn).wait_send()

        @pl.when(turn < chips)
        def _():
            tile_turn(turn).wait_send()

        return carry

    lax.fori_loop(1, chips + 1, drain, 0)
    for number in numbers:
        if not streams[number][4]:
            x_copy(number, chips).wait_send()


def refs_of(counts, refs):
    groups, at = [], 0
    for count in counts:
        groups.append(refs[at : at + count])
        at += count
    return groups


def sum_all(arrays, firsts, tile, arrived, terms, chips):
    rows = arrays[0].shape[0] // (4 * chips)
    streams = []
    for i, (array, first) in enumerate(zip(arrays, firsts)):
        for low, high, is_first in ((0, first, True), (first, array.shape[1], False)):
            left = (high - low) // 256 * 128
            if high > low:
                streams.append((i, low, left, 1, is_first))
                streams.append((i, low + left, high - low - left, -1, is_first))
    streams = tuple(sorted(streams, key=lambda stream: stream[4]))
    count, number = len(arrays), len(streams)
    dma = pltpu.SemaphoreType.DMA
    vmem = pltpu.VMEM
    scratch = (
        [vmem((chips, 2, rows, a.shape[1]), BF16) for a in arrays]
        + [vmem((chips, 2, rows, a.shape[1]), BF16) for a in arrays]
        + [vmem((chips - 1, 1 if first else 2, rows, width), BF16) for _, _, width, _, first in streams]
        + [vmem((chips if first else 1, rows, width), BF16) for _, _, width, _, first in streams]
        + [vmem((3, 8, 128), F32), vmem((chips, 8, 128), F32)]
        + [vmem((2,) + terms[0].shape, BF16)] * 2
        + [dma((count + 4,))]
        + [dma((number, chips)) for _ in range(6)]
        + [dma((chips + 1,)) for _ in range(2)]
        + [dma((2, 3)) for _ in range(2)]
    )
    return pl.pallas_call(
        functools.partial(
            sum_kernel, chips, streams, (count, 5, count, 3, count, count, number, number, 4, 11)
        ),
        out_shape=[jax.ShapeDtypeStruct((rows, a.shape[1]), F32) for a in arrays]
        + [jax.ShapeDtypeStruct((8, 128), F32)]
        + [jax.ShapeDtypeStruct(terms[0].shape, BF16)] * 2,
        in_specs=[pl.BlockSpec(memory_space=pl.ANY)] * count
        + [pl.BlockSpec(memory_space=pltpu.VMEM)]
        + [pl.BlockSpec(memory_space=pl.ANY)] * 4,
        out_specs=[pl.BlockSpec(memory_space=pltpu.VMEM)] * (count + 1) + [pl.BlockSpec(memory_space=pl.ANY)] * 2,
        scratch_shapes=scratch,
        compiler_params=pltpu.CompilerParams(
            collective_id=1, has_side_effects=True, vmem_limit_bytes=58 << 20
        ),
        cost_estimate=pl.CostEstimate(
            flops=0, bytes_accessed=sum(2 * a.size for a in arrays), transcendentals=0
        ),
        name="sum_all",
    )(*[a.reshape(chips, 2, 2, rows, a.shape[1]) for a in arrays], tile, *arrived, *terms)


LITTLE = pl.CostEstimate(flops=0, bytes_accessed=1024, transcendentals=0)
VMEM_LIMIT = 56 << 20


def whole(shape):
    return pl.BlockSpec(shape, lambda *_: (0,) * len(shape))


def piece(kernel, name, grid, in_specs, out_specs, out_shapes, scratch=()):
    return pl.pallas_call(
        kernel,
        grid=grid,
        in_specs=in_specs,
        out_specs=out_specs,
        out_shape=[jax.ShapeDtypeStruct(shape, dtype) for shape, dtype in out_shapes],
        scratch_shapes=list(scratch),
        compiler_params=pltpu.CompilerParams(vmem_limit_bytes=VMEM_LIMIT),
        cost_estimate=LITTLE,
        name=name,
    )


def inverse_rms(values):
    return lax.rsqrt(jnp.mean(values * values, axis=-1, keepdims=True) + EPSILON)


def norm_back(values, gain, grad):
    scale = inverse_rms(values)
    scaled = grad * gain
    mean = jnp.mean(values * scaled, axis=-1, keepdims=True)
    back = scale * scaled - values * (scale * scale * scale * mean)
    return back, jnp.sum(grad * (values * scale), axis=0, keepdims=True)


def qkv_kernel(tokens, gains, head_gain, cosine, sine, weight, low, raw, new):
    at = pl.program_id(0)

    @pl.when(at == 0)
    def _():
        states = tokens[...].astype(F32)
        low[...] = (states * inverse_rms(states) * gains[0:1]).astype(BF16)

    out = full_dot(low[...], weight[...])
    raw[...] = out
    plain = out * inverse_rms(out)
    values = plain * jnp.where(at < HEADS, head_gain[0:1], head_gain[1:2])
    half = HEAD // 2
    first, second = values[:, :half], values[:, half:]
    turned = jnp.concatenate(
        [first * cosine[...] - second * sine[...], second * cosine[...] + first * sine[...]], 1
    )
    new[...] = jnp.where(at < HEADS + KV_HEADS, turned, plain).astype(BF16)


def make_qkv(tokens, gains, head_gain, cosine, sine, full):
    rows = tokens.shape[0]
    heads = HEADS + 2 * KV_HEADS
    return piece(
        qkv_kernel,
        "make_qkv",
        (heads,),
        [
            whole((rows, D)),
            whole(gains.shape),
            whole((2, HEAD)),
            whole(cosine.shape),
            whole(sine.shape),
            pl.BlockSpec((D, HEAD), lambda i: (0, HEADS + i)),
        ],
        [
            whole((rows, D)),
            pl.BlockSpec((rows, HEAD), lambda i: (0, i)),
            pl.BlockSpec((rows, HEAD), lambda i: (0, i)),
        ],
        [((rows, D), BF16), ((rows, heads * HEAD), F32), ((rows, heads * HEAD), BF16)],
    )(tokens, gains, head_gain, cosine, sine, full)


def softmax_of(query, key, visible):
    scores = jnp.where(visible > 0.0, right_dot(query, key), -1e30)
    expo = jnp.exp(scores - jnp.max(scores, axis=-1, keepdims=True))
    return expo / jnp.sum(expo, axis=-1, keepdims=True)


def attend_kernel(
    tokens, gains, low, query, key, value, visible, w_out, lleft, lright,
    context, attn_raw, mixed, ffn_in, mid,
):
    at = pl.program_id(0)
    probs = softmax_of(query[...], key[...], visible[...]).astype(BF16)
    here = full_dot(probs, value[...]).astype(BF16)
    context[...] = here
    term = full_dot(here, w_out[...])

    @pl.when(at == 0)
    def _():
        attn_raw[...] = term

    @pl.when(at > 0)
    def _():
        attn_raw[...] += term

    @pl.when(at == HEADS - 1)
    def _():
        states = tokens[...].astype(F32)
        raw = attn_raw[...]
        total = states + raw * inverse_rms(raw) * gains[1:2]
        total = total + states * inverse_rms(states) * gains[0:1]
        mid[...] = full_dot(low[...], lleft[...]).astype(BF16)
        laurel = right_dot(mid[...], lright[...])
        total = (total + laurel * inverse_rms(laurel) * gains[2:3]) * INV_SQRT2
        mixed[...] = total
        ffn_in[...] = (total * inverse_rms(total) * gains[3:4]).astype(BF16)


def attend(tokens, gains, low, qkv, keys_all, visible, full):
    rows = tokens.shape[0]
    seen = keys_all.shape[0]
    group = HEADS // KV_HEADS
    side = 128
    left_at, right_at = full.shape[1] // side - 2, full.shape[1] // side - 1
    return piece(
        attend_kernel,
        "attend",
        (HEADS,),
        [
            whole((rows, D)),
            whole(gains.shape),
            whole((rows, D)),
            pl.BlockSpec((rows, HEAD), lambda i: (0, i)),
            pl.BlockSpec((seen, HEAD), lambda i: (0, i // group)),
            pl.BlockSpec((seen, HEAD), lambda i: (0, KV_HEADS + i // group)),
            whole((rows, seen)),
            pl.BlockSpec((HEAD, D), lambda i: (i, 0)),
            pl.BlockSpec((D, side), lambda i: (0, left_at)),
            pl.BlockSpec((D, side), lambda i: (0, right_at)),
        ],
        [
            pl.BlockSpec((rows, HEAD), lambda i: (0, i)),
            whole((rows, D)),
            whole((rows, D)),
            whole((rows, D)),
            whole((rows, side)),
        ],
        [
            ((rows, HEADS * HEAD), BF16),
            ((rows, D), F32),
            ((rows, D), F32),
            ((rows, D), BF16),
            ((rows, side), BF16),
        ],
    )(tokens, gains, low, qkv, keys_all, keys_all, visible, full, full, full)


def load_weights(weights, held, sems):
    copies, at = [], 0
    for number, ref in enumerate(weights):
        count = ref.shape[1]
        copies.append(pltpu.make_async_copy(ref, held.at[:, pl.ds(at, count)], sems.at[number]))
        at += count

    @pl.when(pl.program_id(0) == 0)
    def _():
        for copy in copies:
            copy.start()
        for copy in copies:
            copy.wait()


ROW_BLOCK = 256
UNIT_BLOCK = 512


def unit_blocks(steps, units):
    many = max(1, UNIT_BLOCK // units)
    return [range(first, min(first + many, steps)) for first in range(0, steps, many)]


def ffn_forward_kernel(steps, add, *refs):
    weights, refs = refs[: 2 * steps], refs[2 * steps :]
    if add:
        before, refs = refs[0], refs[1:]
    rows, total, refs = refs[0], refs[1], refs[2:]
    gates, uppers, hiddens, (held, sems) = refs_of((steps, steps, steps, 2), refs)
    load_weights(weights, held, sems)
    units = held.shape[1] // steps
    here = rows[...]
    running = before[...] if add else None
    for block in unit_blocks(steps, units):
        cut = slice(block[0] * units, (block[-1] + 1) * units)
        gate_in = right_dot(here, held[0, cut])
        upper_in = right_dot(here, held[1, cut])
        low = gated_product(gate_in, upper_in).astype(BF16)
        for i, step in enumerate(block):
            own = slice(i * units, (i + 1) * units)
            gates[step][...] = gate_in[:, own]
            uppers[step][...] = upper_in[:, own]
            hiddens[step][...] = low[:, own]
        term = full_dot(low, held[2, cut])
        running = term if running is None else running + term
    total[...] = running


def write_sum(running, total, low_total):
    if low_total is None:
        total[...] = running
        return
    half = pl.num_programs(0) // 2

    @pl.when(pl.program_id(0) < half)
    def _():
        low_total[...] = running.astype(BF16)

    @pl.when(pl.program_id(0) >= half)
    def _():
        total[...] = running


def sum_specs(many, last):
    blocks = many // ROW_BLOCK
    half = blocks // 2
    if not last:
        return (lambda i: i), [pl.BlockSpec((ROW_BLOCK, D), lambda i: (i, 0))], [((many, D), F32)]
    specs = [
        pl.BlockSpec((ROW_BLOCK, D), lambda i: (jnp.maximum(i - half, 0), 0)),
        pl.BlockSpec((ROW_BLOCK, D), lambda i: (jnp.minimum(i, half - 1), 0)),
    ]
    return (lambda i: lax.rem(i + half, blocks)), specs, [((many // 2, D), F32), ((many // 2, D), BF16)]


def ffn_forward(rows, before, weights):
    many = rows.shape[0]
    steps, units = len(weights) // 2, 2 * weights[0].shape[1]
    by_row = lambda width: pl.BlockSpec((ROW_BLOCK, width), lambda i: (i, 0))
    add = before is not None
    outs = piece(
        functools.partial(ffn_forward_kernel, steps, add),
        "ffn_forward",
        (many // ROW_BLOCK,),
        [pl.BlockSpec(memory_space=pl.ANY)] * len(weights) + [by_row(D)] * (1 + add),
        [by_row(D)] + [by_row(units)] * (3 * steps),
        [((many, D), F32)] + [((many, units), F32)] * (2 * steps) + [((many, units), BF16)] * steps,
        [pltpu.VMEM((3, steps * units, D), BF16), pltpu.SemaphoreType.DMA((len(weights),))],
    )(*weights, *([before] if add else []), rows)
    (total,), gate, upper, hidden = refs_of((1, steps, steps, steps), outs)
    return total, gate, upper, hidden


def ffn_backward_kernel(steps, add, last, *refs):
    weights, refs = refs[: 2 * steps], refs[2 * steps :]
    if add:
        before, refs = refs[0], refs[1:]
    (rows,), gates, uppers, totals, grad_gates, grad_uppers, (held, sems) = refs_of(
        (1, steps, steps, 1 + last, steps, steps, 2), refs
    )
    load_weights(weights, held, sems)
    units = held.shape[1] // steps
    here = rows[...]
    running = before[...] if add else None
    for block in unit_blocks(steps, units):
        cut = slice(block[0] * units, (block[-1] + 1) * units)
        grad_hidden = right_dot(here, held[2, cut])
        low_gates, low_uppers = [], []
        for i, step in enumerate(block):
            unused, act_back = jax.vjp(gated_product, gates[step][...], uppers[step][...])
            back_gate, back_upper = act_back(grad_hidden[:, i * units : (i + 1) * units])
            low_gates.append(back_gate.astype(BF16))
            low_uppers.append(back_upper.astype(BF16))
            grad_gates[step][...] = low_gates[-1]
            grad_uppers[step][...] = low_uppers[-1]
        term = full_dot(jnp.concatenate(low_gates, 1), held[0, cut])
        term = term + full_dot(jnp.concatenate(low_uppers, 1), held[1, cut])
        running = term if running is None else running + term
    write_sum(running, totals[0], totals[1] if last else None)


def ffn_backward(rows, before, weights, gates, uppers, last):
    many = rows.shape[0]
    steps, units = len(gates), gates[0].shape[1]
    at, sums, sum_shapes = sum_specs(many, last)
    by_row = lambda width: pl.BlockSpec((ROW_BLOCK, width), lambda i: (at(i), 0))
    add = before is not None
    outs = piece(
        functools.partial(ffn_backward_kernel, steps, add, last),
        "ffn_backward",
        (many // ROW_BLOCK,),
        [pl.BlockSpec(memory_space=pl.ANY)] * len(weights)
        + [by_row(D)] * (1 + add)
        + [by_row(units)] * (2 * steps),
        sums + [by_row(units)] * (2 * steps),
        sum_shapes + [((many, units), BF16)] * (2 * steps),
        [pltpu.VMEM((3, steps * units, D), BF16), pltpu.SemaphoreType.DMA((len(weights),))],
    )(*weights, *([before] if add else []), rows, *gates, *uppers)
    return refs_of((len(sums), steps, steps), outs)


def first_backward_kernel(
    up_w, down_w, down_rows, rows, gate, upper, hidden, total, grad_gate, grad_upper, up_out, down_out, held, sums, sems
):
    load_weights((up_w, down_w), held, sems)
    at = pl.program_id(0)
    unused, act_back = jax.vjp(gated_product, gate[...], upper[...])
    back_gate, back_upper = act_back(right_dot(down_rows[...], held[2]))
    low_gate, low_upper = back_gate.astype(BF16), back_upper.astype(BF16)
    grad_gate[...] = low_gate
    grad_upper[...] = low_upper
    total[...] = full_dot(low_gate, held[0]) + full_dot(low_upper, held[1])
    pairs = ((low_gate, rows), (low_upper, rows), (hidden[...], down_rows))

    @pl.when(at == 0)
    def _():
        for kind, (left, right) in enumerate(pairs):
            sums[kind] = left_dot(left, right[...])

    @pl.when(at > 0)
    def _():
        for kind, (left, right) in enumerate(pairs):
            sums[kind] += left_dot(left, right[...])

    @pl.when(at == pl.num_programs(0) - 1)
    def _():
        half = up_out.shape[1]
        up_out[...] = sums[:, :half].astype(BF16)
        down_out[...] = sums[:, half:].astype(BF16)


def first_backward(down_rows, rows, weights, gate, upper, hidden):
    many, units = gate.shape
    by_row = lambda width: pl.BlockSpec((ROW_BLOCK, width), lambda i: (i, 0))
    part = (3, units // 2, D)
    return piece(
        first_backward_kernel,
        "first_backward",
        (many // ROW_BLOCK,),
        [pl.BlockSpec(memory_space=pl.ANY)] * 2 + [by_row(D)] * 2 + [by_row(units)] * 3,
        [by_row(D)] + [by_row(units)] * 2 + [whole(part)] * 2,
        [((many, D), F32)] + [((many, units), BF16)] * 2 + [(part, BF16)] * 2,
        [pltpu.VMEM((3, units, D), BF16), pltpu.VMEM((3, units, D), F32), pltpu.SemaphoreType.DMA((2,))],
    )(*weights, down_rows, rows, gate, upper, hidden)


def unit_grads_kernel(grad_gate, grad_upper, hidden, rows, down_rows, up_out, down_out):
    half = up_out.shape[1]
    pairs = ((grad_gate, rows), (grad_upper, rows), (hidden, down_rows))
    for kind, (left, right) in enumerate(pairs):
        out = left_dot(left[...], right[...]).astype(BF16)
        up_out[kind] = out[:half]
        down_out[kind] = out[half:]


def unit_grads_of(grad_gate, grad_upper, hidden, rows, down_rows):
    many, units = hidden.shape
    width = 1024
    narrow = whole((many, units))
    wide = pl.BlockSpec((many, width), lambda i: (0, i))
    part = pl.BlockSpec((3, units // 2, width), lambda i: (0, 0, i))
    return piece(
        unit_grads_kernel,
        "unit_grads",
        (D // width,),
        [narrow, narrow, narrow, wide, wide],
        [part, part],
        [((3, units // 2, D), BF16)] * 2,
    )(grad_gate, grad_upper, hidden, rows, down_rows)


def attend_back_kernel(
    gains, grad_in, grad_after, mixed, attn_raw, mid, low, lleft, lright, w_out, context, query, key, value, visible,
    grad_mixed, grad_mid, grad_gains, grad_left, grad_right, grad_w_out, grad_query, grad_key, grad_value,
    grad_attn,
):
    at = pl.program_id(0)

    @pl.when(at == 0)
    def _():
        back, gain_3 = norm_back(mixed[...], gains[3:4], grad_in[...])
        total = (grad_after[...] + back) * INV_SQRT2
        grad_mixed[...] = total
        back, gain_2 = norm_back(right_dot(mid[...], lright[...]), gains[2:3], total)
        back_low = back.astype(BF16)
        grad_right[...] = left_dot(back_low, mid[...])
        mid_low = full_dot(back_low, lright[...]).astype(BF16)
        grad_mid[...] = mid_low
        grad_left[...] = left_dot(low[...], mid_low)
        back, gain_1 = norm_back(attn_raw[...], gains[1:2], total)
        grad_attn[...] = back.astype(BF16)
        grad_gains[...] = jnp.concatenate(
            [gain_1, gain_2, gain_3, jnp.zeros((5, D), F32)], 0
        )

    grad_context = right_dot(grad_attn[...], w_out[...]).astype(BF16)
    grad_w_out[...] = left_dot(context[...], grad_attn[...]).astype(BF16)
    probs = softmax_of(query[...], key[...], visible[...])
    grad_probs = right_dot(grad_context, value[...])
    inner = jnp.sum(probs * grad_probs, axis=-1, keepdims=True)
    grad_scores = (probs * (grad_probs - inner)).astype(BF16)
    grad_query[...] = full_dot(grad_scores, key[...])
    key_term = left_dot(grad_scores, query[...])
    value_term = left_dot(probs.astype(BF16), grad_context)
    group = HEADS // KV_HEADS

    @pl.when(lax.rem(at, group) == 0)
    def _():
        grad_key[...] = key_term
        grad_value[...] = value_term

    @pl.when(lax.rem(at, group) > 0)
    def _():
        grad_key[...] += key_term
        grad_value[...] += value_term


def attend_back(gains, grad_in, grad_after, mixed, attn_raw, mid, low, full, context, qkv, keys_all, visible):
    rows = low.shape[0]
    seen = keys_all.shape[0]
    group = HEADS // KV_HEADS
    side = 128
    left_at, right_at = full.shape[1] // side - 2, full.shape[1] // side - 1
    head = pl.BlockSpec((rows, HEAD), lambda i: (0, i))
    once = lambda shape: pl.BlockSpec(shape, lambda i: (0, 0), pipeline_mode=pl.Buffered(1))
    return piece(
        attend_back_kernel,
        "attend_back",
        (HEADS,),
        [
            whole(gains.shape),
            once((rows, D)),
            once((rows, D)),
            once((rows, D)),
            once((rows, D)),
            whole((rows, side)),
            whole((rows, D)),
            pl.BlockSpec((D, side), lambda i: (0, left_at)),
            pl.BlockSpec((D, side), lambda i: (0, right_at)),
            pl.BlockSpec((HEAD, D), lambda i: (i, 0)),
            head,
            head,
            pl.BlockSpec((seen, HEAD), lambda i: (0, i // group)),
            pl.BlockSpec((seen, HEAD), lambda i: (0, KV_HEADS + i // group)),
            whole((rows, seen)),
        ],
        [
            whole((rows, D)),
            whole((rows, side)),
            whole((8, D)),
            whole((D, side)),
            whole((D, side)),
            pl.BlockSpec((HEAD, D), lambda i: (i, 0)),
            head,
            pl.BlockSpec((seen, HEAD), lambda i: (0, i // group)),
            pl.BlockSpec((seen, HEAD), lambda i: (0, i // group)),
        ],
        [
            ((rows, D), F32),
            ((rows, side), BF16),
            ((8, D), F32),
            ((D, side), F32),
            ((D, side), F32),
            ((HEADS * HEAD, D), BF16),
            ((rows, HEADS * HEAD), F32),
            ((seen, KV_HEADS * HEAD), F32),
            ((seen, KV_HEADS * HEAD), F32),
        ],
        [pltpu.VMEM((rows, D), BF16)],
    )(
        gains, grad_in, grad_after, mixed, attn_raw, mid, low, full, full, full, context, qkv, keys_all, keys_all,
        visible,
    )


def turn_back(grad, cosine, sine):
    half = HEAD // 2
    first, second = grad[:, :half], grad[:, half:]
    return jnp.concatenate([first * cosine + second * sine, second * cosine - first * sine], 1)


def query_back_kernel(grad_query, raw, cosine, sine, head_gain, low, weight, grad_w, grad_low, grad_head):
    at = pl.program_id(0)
    turned = turn_back(grad_query[...], cosine[...], sine[...])
    back, gain = norm_back(raw[...], head_gain[0:1], turned)
    back_low = back.astype(BF16)
    grad_w[...] = left_dot(low[...], back_low).astype(BF16)
    term = right_dot(back_low, weight[...])

    @pl.when(at == 0)
    def _():
        grad_low[...] = term
        grad_head[...] = gain

    @pl.when(at > 0)
    def _():
        grad_low[...] += term
        grad_head[...] += gain


def query_back(grad_query, raw, cosine, sine, head_gain, low, full):
    rows = low.shape[0]
    head = pl.BlockSpec((rows, HEAD), lambda i: (0, i))
    return piece(
        query_back_kernel,
        "query_back",
        (HEADS,),
        [
            head,
            head,
            whole(cosine.shape),
            whole(sine.shape),
            whole((2, HEAD)),
            whole((rows, D)),
            pl.BlockSpec((D, HEAD), lambda i: (0, HEADS + i)),
        ],
        [pl.BlockSpec((D, HEAD), lambda i: (0, i)), whole((rows, D)), whole((1, HEAD))],
        [((D, HEADS * HEAD), BF16), ((rows, D), F32), ((1, HEAD), F32)],
    )(grad_query, raw, cosine, sine, head_gain, low, full)


def key_back_kernel(
    grad_kv, raw, cosine, sine, head_gain, low, weight, before, grad_mixed, grad_mid, lleft, tokens, gains,
    grad_w, grad_tokens, grad_head, grad_gain, total,
):
    at = pl.program_id(0)
    is_key = at < KV_HEADS
    grad = grad_kv[...]
    turned = jnp.where(is_key, turn_back(grad, cosine[...], sine[...]), grad)
    back, gain = norm_back(raw[...], jnp.where(is_key, head_gain[1:2], 1.0), turned)
    back_low = back.astype(BF16)
    grad_w[...] = left_dot(low[...], back_low).astype(BF16)
    term = right_dot(back_low, weight[...])

    @pl.when(at == 0)
    def _():
        total[...] = before[...] + term
        grad_head[...] = gain

    @pl.when(at > 0)
    def _():
        total[...] += term
        grad_head[...] += jnp.where(is_key, gain, 0.0)

    @pl.when(at == 2 * KV_HEADS - 1)
    def _():
        grad_normed = total[...] + grad_mixed[...] + right_dot(grad_mid[...], lleft[...])
        back, gain_0 = norm_back(tokens[...].astype(F32), gains[0:1], grad_normed)
        grad_tokens[...] = grad_mixed[...] + back
        grad_gain[...] = gain_0


def key_back(grad_kv, raw, cosine, sine, head_gain, low, full, before, grad_mixed, grad_mid, tokens, gains):
    rows = low.shape[0]
    side = 128
    left_at = full.shape[1] // side - 2
    return piece(
        key_back_kernel,
        "key_back",
        (2 * KV_HEADS,),
        [
            pl.BlockSpec((rows, HEAD), lambda i: (0, i)),
            pl.BlockSpec((rows, HEAD), lambda i: (0, HEADS + i)),
            whole(cosine.shape),
            whole(sine.shape),
            whole((2, HEAD)),
            whole((rows, D)),
            pl.BlockSpec((D, HEAD), lambda i: (0, 2 * HEADS + i)),
            whole((rows, D)),
            whole((rows, D)),
            whole((rows, side)),
            pl.BlockSpec((D, side), lambda i: (0, left_at)),
            whole((rows, D)),
            whole(gains.shape),
        ],
        [
            pl.BlockSpec((D, HEAD), lambda i: (0, i)),
            whole((rows, D)),
            whole((1, HEAD)),
            whole((1, D)),
        ],
        [
            ((D, 2 * KV_HEADS * HEAD), BF16),
            ((rows, D), F32),
            ((1, HEAD), F32),
            ((1, D), F32),
        ],
        [pltpu.VMEM((rows, D), F32)],
    )(grad_kv, raw, cosine, sine, head_gain, low, full, before, grad_mixed, grad_mid, full, tokens, gains)


def tie(*values):
    return lax.optimization_barrier(values)


def shares(total, count):
    return [total // count + (1 if i < total % count else 0) for i in range(count)]


def greet(peers):
    barrier = pltpu.get_barrier_semaphore()
    for peer in peers:
        pl.semaphore_signal(barrier, inc=1, device_id=peer, device_id_type=MESH)
    pl.semaphore_wait(barrier, len(peers))


def partners():
    return {"core": 1 - lax.axis_index("core")}, {"fsdp": 1 - lax.axis_index("fsdp")}


CUTS = 8
FLYING = 2


def spread_kernel(own, rows, x_send, x_recv, near_send, near_recv, far_send, far_recv, own_sem):
    count = own.shape[0]
    cut = count // CUTS
    other_core, other_side = partners()
    greet((other_core, other_side))

    def copy(src, block, at, send, recv, peer):
        return pltpu.make_async_remote_copy(
            src_ref=src,
            dst_ref=rows.at[pl.ds(block * count + at * cut, cut)],
            send_sem=send.at[at],
            recv_sem=recv.at[at],
            device_id=peer,
            device_id_type=MESH,
        )

    mine = [own.at[pl.ds(at * cut, cut)] for at in range(CUTS)]
    came = [rows.at[pl.ds(count + at * cut, cut)] for at in range(CUTS)]
    across = [copy(mine[at], 1, at, x_send, x_recv, other_side) for at in range(CUTS)]
    near = [copy(mine[at], 2, at, near_send, near_recv, other_core) for at in range(CUTS)]
    far = [copy(came[at], 3, at, far_send, far_recv, other_core) for at in range(CUTS)]
    for one in across[:FLYING] + near:
        one.start()
    keep = pltpu.make_async_copy(own, rows.at[pl.ds(0, count)], own_sem)
    keep.start()
    for at in range(CUTS):
        across[at].wait_send()
        if at + FLYING < CUTS:
            across[at + FLYING].start()
        across[at].wait_recv()
        far[at].start()
    for one in near + far:
        one.wait()
    keep.wait()


def rows_of_four(own, number):
    count = own.shape[0]
    dma = pltpu.SemaphoreType.DMA
    return pl.pallas_call(
        spread_kernel,
        out_shape=jax.ShapeDtypeStruct((4 * count, D), BF16),
        in_specs=[pl.BlockSpec(memory_space=pltpu.VMEM)],
        out_specs=pl.BlockSpec(memory_space=pl.ANY),
        scratch_shapes=[dma((CUTS,)) for _ in range(6)] + [dma],
        compiler_params=pltpu.CompilerParams(collective_id=number, has_side_effects=True),
        cost_estimate=LITTLE,
        name="spread_rows",
    )(own)


def gather_sum_kernel(steps, *refs):
    if steps:
        (own, low, rows, down_rows), sides, (out,), grads, more, held, sems = refs_of(
            (4, 3 * steps, 1, 2 * steps, 4 + 4, 3, 3), refs
        )
        core_in, pair_low, x_in, parts, *copy_sems = more
        core_send, core_recv, x_send, x_recv = copy_sems
        rows_in, down_in, more_out = held
        loads_sem, parts_sem, grads_sem = sems
        parts_out = more_out

        def store(step, way):
            return pltpu.make_async_copy(parts_out.at[step, way], grads[2 * step + way], grads_sem.at[step, way])

        loads = [
            pltpu.make_async_copy(rows, rows_in, loads_sem.at[0]),
            pltpu.make_async_copy(down_rows, down_in, loads_sem.at[1]),
        ]
        part_loads = [
            pltpu.make_async_copy(side, parts.at[number], parts_sem.at[number]) for number, side in enumerate(sides)
        ]
        for load in loads + part_loads:
            load.start()
    else:
        own, low, out, core_in, pair_low, x_in, core_send, core_recv, x_send, x_recv = refs
    count = out.shape[0]
    cut = count // CUTS
    other_core, other_side = partners()
    greet((other_core, other_side))

    def core_copy(block, at):
        here = pl.ds(block * count + at * cut, cut)
        number = block * CUTS + at
        return pltpu.make_async_remote_copy(
            src_ref=low.at[here],
            dst_ref=core_in.at[here],
            send_sem=core_send.at[number],
            recv_sem=core_recv.at[number],
            device_id=other_core,
            device_id_type=MESH,
        )

    def x_copy(at):
        here = pl.ds(at * cut, cut)
        return pltpu.make_async_remote_copy(
            src_ref=pair_low.at[here],
            dst_ref=x_in.at[here],
            send_sem=x_send.at[at],
            recv_sem=x_recv.at[at],
            device_id=other_side,
            device_id_type=MESH,
        )

    pieces = [(block, at) for block in (1, 0) for at in range(CUTS)]

    def next_piece(number):
        core_copy(*pieces[number]).wait_send()
        if number + FLYING < len(pieces):
            core_copy(*pieces[number + FLYING]).start()

    for one in pieces[:FLYING]:
        core_copy(*one).start()
    for at in range(CUTS):
        there = pl.ds(count + at * cut, cut)
        next_piece(at)
        core_copy(1, at).wait_recv()
        pair_low[pl.ds(at * cut, cut)] = (own[there] + core_in[there].astype(F32)).astype(BF16)
        x_copy(at).start()
    for number in range(CUTS + FLYING, 2 * CUTS):
        core_copy(*pieces[number]).start()
    if steps:
        for load in loads:
            load.wait()
        half = grads[0].shape[1]
        width = D // 2
        for step in range(steps):
            for kind in range(3):
                number = 3 * step + kind
                part_loads[number].wait()
                left, right = parts[number], down_in if kind == 2 else rows_in
                for first in range(0, D, width):
                    cols = slice(first, first + width)
                    term = left_dot(left, right[:, cols]).astype(BF16)
                    parts_out[step, 0, kind, :, cols] = term[:half]
                    parts_out[step, 1, kind, :, cols] = term[half:]
            for way in range(2):
                store(step, way).start()
    for at in range(CUTS):
        here = pl.ds(at * cut, cut)
        core_copy(0, at).wait_recv()
        x_copy(at).wait_recv()
        out[here] = own[here] + core_in[here].astype(F32) + x_in[here].astype(F32)
    for at in range(CUTS):
        x_copy(at).wait_send()
        core_copy(0, at).wait_send()
    for step in range(steps):
        for way in range(2):
            store(step, way).wait()


def sum_of_four(own, low, number, units=(), rows=None, down_rows=None):
    count = own.shape[0] // 2
    steps = len(units)
    dma = pltpu.SemaphoreType.DMA
    vmem, anywhere = pltpu.VMEM, pl.BlockSpec(memory_space=pl.ANY)
    scratch = [vmem((2 * count, D), BF16), vmem((count, D), BF16), vmem((count, D), BF16)]
    copy_sems = [dma((2 * CUTS,)), dma((2 * CUTS,)), dma((CUTS,)), dma((CUTS,))]
    operands, shapes = [], []
    if steps:
        many, width = units[0][0].shape
        operands = [rows, down_rows] + [side for sides in units for side in sides]
        shapes = [jax.ShapeDtypeStruct((3, width // 2, D), BF16)] * (2 * steps)
        scratch += [vmem((3 * steps, many, width), BF16)]
        copy_sems += [vmem((many, D), BF16), vmem((many, D), BF16), vmem((steps, 2, 3, width // 2, D), BF16)]
        copy_sems += [dma((2,)), dma((3 * steps,)), dma((steps, 2))]
    total, *grads = pl.pallas_call(
        functools.partial(gather_sum_kernel, steps),
        out_shape=[jax.ShapeDtypeStruct((count, D), F32)] + shapes,
        in_specs=[pl.BlockSpec(memory_space=pltpu.VMEM), anywhere] + [anywhere] * len(operands),
        out_specs=[pl.BlockSpec(memory_space=pltpu.VMEM)] + [anywhere] * len(shapes),
        scratch_shapes=scratch + copy_sems,
        compiler_params=pltpu.CompilerParams(
            collective_id=number, has_side_effects=True, vmem_limit_bytes=VMEM_LIMIT
        ),
        cost_estimate=LITTLE,
        name="gather_sum",
    )(own, low, *operands)
    return total, [(grads[2 * i], grads[2 * i + 1]) for i in range(steps)]


PARTS = 4


def middle_kernel(steps, *refs):
    weights, inputs, outs, unit_outs, scratch, unit_scratch, sems = refs_of((2 * steps, 10, 8, 3 * steps, 15, 6, 14), refs)
    before, ffn_rows, mixed, layer_in, teacher, mask, scale, gains, gate_w, proj_w = inputs
    result, grad_after, grad_layer, rows, grad_gate_w, grad_proj_w, grad_gains, squares = outs
    (
        own_in, mixed_in, teacher_in, gate_in, proj_in, core_in, pair_low, x_in,
        result_out, after_out, after_low, mid_low, grad_pl, grad_raw, grad_low,
    ) = scratch
    rows_in, held, low, *unit_sides = unit_scratch
    (
        loads, stores, core_send, core_recv, x_send, x_recv, y_send, y_recv, near_send, near_recv, far_send, far_recv,
        unit_loads, unit_stores,
    ) = sems
    count = mixed.shape[0]
    cut = count // PARTS
    other_core, other_side = partners()

    def load(number, src, dst):
        return pltpu.make_async_copy(src, dst, loads.at[number])

    units = held.shape[1] // steps
    weight_loads = [
        pltpu.make_async_copy(ref, held.at[:, pl.ds(at * units // 2, units // 2)], unit_loads.at[at])
        for at, ref in enumerate(weights)
    ]
    block_loads = [
        [
            load(2 * block, ffn_rows.at[pl.ds(block * count, count)], rows_in.at[pl.ds(block * count, count)]),
            load(2 * block + 1, before.at[pl.ds(block * count, count)], own_in.at[pl.ds(block * count, count)]),
        ]
        for block in range(4)
    ]
    incoming = [
        load(8, mixed, mixed_in),
        load(9, gate_w, gate_in),
        load(10, proj_w, proj_in),
        load(11, teacher, teacher_in),
    ]
    for one in weight_loads + block_loads[3] + block_loads[1] + block_loads[2] + block_loads[0] + incoming:
        one.start()
    greet((other_core, other_side))

    def forward_block(block):
        here = slice(block * count, (block + 1) * count)
        for one in block_loads[block]:
            one.wait()
        gate = right_dot(rows_in[here], held[0])
        upper = right_dot(rows_in[here], held[1])
        hidden = gated_product(gate, upper).astype(BF16)
        for side, values in zip(unit_sides, (gate, upper, hidden)):
            for step in range(steps):
                side[step, here] = values[:, step * units : (step + 1) * units]
        return own_in[here] + full_dot(hidden, held[2])

    def unit_store(kind, step):
        return pltpu.make_async_copy(
            unit_sides[kind].at[step], unit_outs[kind * steps + step], unit_stores.at[kind * steps + step]
        )

    def remote(src, dst, send, recv, peer):
        return pltpu.make_async_remote_copy(
            src_ref=src, dst_ref=dst, send_sem=send, recv_sem=recv, device_id=peer, device_id_type=MESH
        )

    def piece_of(at):
        return pl.ds(at * cut, cut)

    def core_copy(block, at):
        here = pl.ds(block * count + at * cut, cut)
        number = block * PARTS + at
        return remote(low.at[here], core_in.at[here], core_send.at[number], core_recv.at[number], other_core)

    def x_copy(at):
        here = piece_of(at)
        return remote(pair_low.at[here], x_in.at[here], x_send.at[at], x_recv.at[at], other_side)

    def out_copy(src, block, at, send, recv, peer):
        return remote(src, rows.at[pl.ds(block * count + at * cut, cut)], send.at[at], recv.at[at], peer)

    def across(at):
        return out_copy(grad_low.at[piece_of(at)], 1, at, y_send, y_recv, other_side)

    def near(at):
        return out_copy(grad_low.at[piece_of(at)], 2, at, near_send, near_recv, other_core)

    def far(at):
        return out_copy(rows.at[pl.ds(count + at * cut, cut)], 3, at, far_send, far_recv, other_core)

    def kept(number, at):
        here = piece_of(at)
        src, dst = ((result_out, result), (after_out, grad_after), (grad_low, rows))[number]
        return pltpu.make_async_copy(src.at[here], dst.at[here], stores.at[number, at])

    for one in weight_loads:
        one.wait()
    low[count:] = forward_block(3).astype(BF16)
    for at in range(PARTS):
        core_copy(1, at).start()
    own_in[count : 2 * count] = forward_block(1)
    for at in range(PARTS):
        there = pl.ds(count + at * cut, cut)
        core_copy(1, at).wait_recv()
        pair_low[piece_of(at)] = (own_in[there] + core_in[there].astype(F32)).astype(BF16)
        x_copy(at).start()
    low[:count] = forward_block(2).astype(BF16)
    for at in range(PARTS):
        core_copy(0, at).start()
    own_in[:count] = forward_block(0)
    for kind in range(3):
        for step in range(steps):
            unit_store(kind, step).start()
    for one in incoming:
        one.wait()
    gain_4, gain_5 = gains[4:5], gains[5:6]
    total = jnp.zeros((), F32)
    sum_4 = sum_5 = jnp.zeros((1, D), F32)
    for at in range(PARTS):
        here = piece_of(at)
        core_copy(0, at).wait_recv()
        x_copy(at).wait_recv()
        down = own_in[here] + core_in[here].astype(F32) + x_in[here].astype(F32)
        after = mixed_in[here] + down * inverse_rms(down) * gain_4
        low_here = after.astype(BF16)
        after_low[here] = low_here
        raw = full_dot(low_here, gate_in[...])
        act, act_back = jax.vjp(gelu_tanh, raw)
        layer = layer_in[here].astype(F32)
        mid = (act * layer).astype(BF16)
        mid_low[here] = mid
        out = full_dot(mid, proj_in[...])
        done = after + out * inverse_rms(out) * gain_5
        result_out[here] = done
        kept(0, at).start()
        errors = done - teacher_in[here].astype(F32)
        masked = mask[here][:, 0:1] * errors
        total += jnp.sum(masked * errors)
        grad_out = masked * scale[0:1, 0:1]
        back, term = norm_back(out, gain_5, grad_out)
        sum_5 += term
        back_low = back.astype(BF16)
        grad_pl[here] = back_low
        grad_mid = right_dot(back_low, proj_in[...])
        grad_layer[here] = grad_mid * act
        raw_low = act_back(grad_mid * layer)[0].astype(BF16)
        grad_raw[here] = raw_low
        grad_here = grad_out + right_dot(raw_low, gate_in[...])
        after_out[here] = grad_here
        kept(1, at).start()
        back, term = norm_back(down, gain_4, grad_here)
        sum_4 += term
        grad_low[here] = back.astype(BF16)
        across(at).start()
        near(at).start()
        kept(2, at).start()
    grad_gains[...] = jnp.concatenate([sum_4, sum_5, jnp.zeros((6, D), F32)], 0)
    squares[...] = jnp.broadcast_to(total, squares.shape)
    for at in range(PARTS // 2):
        across(at).wait_recv()
        far(at).start()
    grad_proj_w[...] = left_dot(mid_low[...], grad_pl[...]).astype(BF16)
    grad_gate_w[...] = left_dot(after_low[...], grad_raw[...]).astype(BF16)
    for at in range(PARTS // 2, PARTS):
        across(at).wait_recv()
        far(at).start()
    for at in range(PARTS):
        far(at).wait()
        near(at).wait()
        across(at).wait_send()
        x_copy(at).wait_send()
        for block in (0, 1):
            core_copy(block, at).wait_send()
        for number in range(3):
            kept(number, at).wait()
    for kind in range(3):
        for step in range(steps):
            unit_store(kind, step).wait()


def middle(weights, before, ffn_rows, mixed, layer_in, teacher, mask, scale, gains, gate_w, proj_w):
    count = mixed.shape[0]
    steps, units = len(weights) // 2, 2 * weights[0].shape[1]
    sides = [(4 * count, units)] * steps
    dma, vmem = pltpu.SemaphoreType.DMA, pltpu.VMEM
    anywhere, inside = pl.BlockSpec(memory_space=pl.ANY), pl.BlockSpec(memory_space=pltpu.VMEM)
    shape = jax.ShapeDtypeStruct
    outs = pl.pallas_call(
        functools.partial(middle_kernel, steps),
        out_shape=[
            shape((count, D), F32),
            shape((count, D), F32),
            shape((count, PLD), F32),
            shape((4 * count, D), BF16),
            shape((D, PLD), BF16),
            shape((PLD, D), BF16),
            shape((8, D), F32),
            shape((8, 128), F32),
        ]
        + [shape(side, F32) for side in sides * 2]
        + [shape(side, BF16) for side in sides],
        in_specs=[anywhere] * (2 * steps) + [anywhere, anywhere, anywhere, inside, anywhere, inside, inside, inside, anywhere, anywhere],
        out_specs=[anywhere, anywhere, inside, anywhere, inside, inside, inside, inside] + [anywhere] * (3 * steps),
        scratch_shapes=[
            vmem((4 * count, D), F32),
            vmem((count, D), F32),
            vmem((count, D), BF16),
            vmem((D, PLD), BF16),
            vmem((PLD, D), BF16),
            vmem((2 * count, D), BF16),
            vmem((count, D), BF16),
            vmem((count, D), BF16),
            vmem((count, D), F32),
            vmem((count, D), F32),
            vmem((count, D), BF16),
            vmem((count, PLD), BF16),
            vmem((count, D), BF16),
            vmem((count, PLD), BF16),
            vmem((count, D), BF16),
            vmem((4 * count, D), BF16),
            vmem((3, steps * units, D), BF16),
            vmem((2 * count, D), BF16),
            vmem((steps, 4 * count, units), F32),
            vmem((steps, 4 * count, units), F32),
            vmem((steps, 4 * count, units), BF16),
            dma((12,)),
            dma((3, PARTS)),
            dma((2 * PARTS,)),
            dma((2 * PARTS,)),
        ]
        + [dma((PARTS,)) for _ in range(8)]
        + [dma((2 * steps,)), dma((3 * steps,))],
        compiler_params=pltpu.CompilerParams(
            collective_id=3, has_side_effects=True, vmem_limit_bytes=VMEM_LIMIT
        ),
        cost_estimate=LITTLE,
        name="middle",
    )(*weights, before, ffn_rows, mixed, layer_in, teacher, mask, scale, gains, gate_w, proj_w)
    return refs_of((8, steps, steps, steps), outs)


def body(
    tokens,
    per_layer,
    teacher,
    cont_lengths,
    w_query,
    w_kv,
    w_out,
    laurel_left,
    laurel_right,
    pl_gate,
    pl_proj,
    norm_gains,
    head_gains,
    ffn_weight,
):
    row_count = tokens.shape[1]
    chips = lax.axis_size("zy")
    seq_count = 2 * chips
    group_count = lax.axis_size("fsdp")
    shards = seq_count * group_count
    chip = lax.axis_index("zy")
    core = lax.axis_index("core")
    seq_index = chip * 2 + core
    group_index = lax.axis_index("fsdp")
    half_point = seq_count // 2
    prompt_len = half_point * row_count
    cont_shards = CONT_LEN // row_count
    cont_count = prompt_len // CONT_LEN
    is_cont = seq_index >= half_point
    rel_index = seq_index - half_point
    local_shard = jnp.where(is_cont, rel_index % cont_shards, 0)
    cont_index = jnp.where(is_cont, rel_index // cont_shards, 0)
    first_place = jnp.where(is_cont, prompt_len + local_shard * row_count, seq_index * row_count)
    row_range = jnp.arange(row_count, dtype=jnp.int32)
    places = first_place + row_range
    group_lengths = jnp.sum(
        jnp.where(
            jnp.arange(group_count, dtype=jnp.int32)[:, None] == group_index, cont_lengths, 0
        ),
        axis=0,
    )
    my_length = jnp.sum(
        jnp.where(jnp.arange(cont_count, dtype=jnp.int32) == cont_index, group_lengths, 0)
    )
    valid = jnp.logical_or(
        jnp.logical_not(is_cont), local_shard * row_count + row_range < my_length
    )
    weight_mask = valid.astype(F32)
    count = F32(group_count * prompt_len) + jnp.sum(cont_lengths).astype(F32)
    total_slots = float(row_count * seq_count * group_count)
    shard_rows = w_query.shape[0]
    key_cols = KV_HEADS * HEAD
    proj_cols = pl_proj.shape[0] * D // shard_rows
    misc_cols = RANK
    head_part = head_gains.reshape(-1, 1)
    misc = jnp.concatenate(
        [
            norm_gains.T,
            jnp.pad(head_part, ((0, shard_rows - head_part.shape[0]), (0, 0))),
            jnp.zeros((shard_rows, misc_cols - 7), BF16),
        ],
        1,
    )
    pack = jnp.concatenate(
        [
            w_out,
            w_query,
            w_kv,
            pl_gate,
            pl_proj.reshape(shard_rows, proj_cols),
            laurel_left,
            misc,
            laurel_right.T,
            jnp.zeros((shard_rows, 128 - RANK), BF16),
        ],
        1,
    )

    units = ffn_weight.shape[0]
    half = units // 2
    by_kind = ffn_weight.transpose(1, 0, 2)
    ups, downs = [by_kind[:, :half]], [by_kind[:, half:]]
    stage_steps = shares(chips - 1, 7)

    def pass_on(stage):
        for _ in range(stage_steps[stage]):
            ups.append(ring(ups[-1], 1))
            downs.append(ring(downs[-1], -1))

    def stage_end(values):
        (ups[-1], downs[-1]), values = tie((ups[-1], downs[-1]), values)
        return values

    pass_on(0)
    full = gather_all(pack, chips)
    at = 2 * D + 2 * key_cols
    plg = full[:, at : at + PLD]
    plp = full[:, at + PLD : at + PLD + proj_cols].reshape(PLD, D)
    at += PLD + proj_cols + RANK
    misc_full = stage_end(full[:, at : at + misc_cols])
    pass_on(1)
    gains = jnp.pad(misc_full[:, :6].T.astype(F32), ((0, 2), (0, 0)))
    head_n = head_gains.shape[1]
    head_gain = (
        misc_full[:, 6]
        .reshape(shards, shard_rows)[:, : 2 * head_n]
        .reshape(shards, 2, head_n)
        .transpose(1, 0, 2)
        .reshape(2, HEAD)
        .astype(F32)
    )
    freqs = jnp.exp(
        jnp.arange(HEAD // 2, dtype=F32) * (-2.0 * math.log(ROPE_BASE) / HEAD)
    )
    angles = places.astype(F32)[:, None] * freqs
    cosine, sine = jnp.cos(angles), jnp.sin(angles)
    normed_low, qkv_raw, qkv = make_qkv(tokens[0], gains, head_gain, cosine, sine, full)
    qkv = stage_end(qkv)
    kv_own = qkv[:, D:]
    pass_on(2)

    mid = chips // 2
    chain = [(i, i + 1) for i in range(mid - 1)] + [(mid - 1, mid + 1)]
    kv_before = jnp.where(
        chip == mid,
        lax.ppermute(kv_own, "zy", [(mid - 1, mid)]),
        lax.ppermute(kv_own, "zy", chain),
    )
    spans = []
    span = 2
    while span < mid:
        spans.append(span)
        span *= 2
    for span in spans:
        moved = lax.ppermute(
            kv_before, "zy", [(mid + i, mid + i + span) for i in range(min(span, mid - span))]
        )
        fresh = jnp.logical_and(chip >= mid + span, chip < mid + 2 * span)
        kv_before = jnp.where(fresh, moved, kv_before)
    kv_other = swap(jnp.where(core == 0, kv_own, kv_before), "core")
    keys_all = jnp.concatenate([kv_before, kv_other, kv_own], 0)
    keys_all = stage_end(keys_all)
    pass_on(3)
    key_len = keys_all.shape[0]
    key_places = first_place - 2 * row_count + jnp.arange(key_len, dtype=jnp.int32)
    visible = (
        (key_places[None, :] <= places[:, None])
        & (places[:, None] - key_places[None, :] < WINDOW)
        & (key_places[None, :] >= 0)
    ).astype(F32)
    context_low, attn_raw, mixed, ffn_in, laurel_mid = attend(
        tokens[0], gains, normed_low, qkv, keys_all, visible, full
    )

    ffn_in = stage_end(ffn_in)
    pass_on(4)
    ffn_rows = stage_end(rows_of_four(ffn_in, 2))
    here = len(ups)
    pass_on(5)
    gates, uppers, hiddens = [], [], []

    def weights_of(steps):
        return [w for k in steps for w in (ups[k], downs[k])]

    def forward_part(running, first, end):
        running, gate, upper, hidden = ffn_forward(ffn_rows, running, weights_of(range(first, end)))
        gates.extend(gate)
        uppers.extend(upper)
        hiddens.extend(hidden)
        return running

    running = stage_end(forward_part(None, 0, here))
    then = len(ups)
    pass_on(6)
    running = stage_end(forward_part(running, here, then))
    outs, gate, upper, hidden = middle(
        weights_of(range(then, chips)),
        running,
        ffn_rows,
        mixed,
        per_layer[0],
        teacher[0],
        jnp.broadcast_to(weight_mask[:, None], (row_count, 128)),
        jnp.broadcast_to(total_slots / count, (8, 128)),
        gains,
        plg,
        plp,
    )
    result, grad_after, grad_layer_in, grad_down_rows, grad_plg, grad_plp, late_gains, squares = outs
    gates.extend(gate)
    uppers.extend(upper)
    hiddens.extend(hidden)
    grad_gates, grad_uppers = [None] * chips, [None] * chips

    def backward_part(steps, running, last=False):
        sums, grad_gate, grad_upper = ffn_backward(
            grad_down_rows, running, weights_of(steps), [gates[k] for k in steps], [uppers[k] for k in steps], last
        )
        for k, gg, gu in zip(steps, grad_gate, grad_upper):
            grad_gates[k], grad_uppers[k] = gg, gu
        return sums if last else sums[0]

    ready = {}

    def unit_grads(k):
        if k in ready:
            return ready[k]
        return unit_grads_of(grad_gates[k], grad_uppers[k], hiddens[k], ffn_rows, grad_down_rows)

    order = list(range(1, chips)) + [0]
    ring_steps = shares(chips - 2, 6)
    done = 0
    last_sums = None

    def beside(stage, work):
        nonlocal done, up_sum, down_sum, last_sums
        values = None
        for step in range(ring_steps[stage]):
            up_in = ring(up_sum, 1)
            down_in = ring(down_sum, -1)
            if step == 0:
                values = work()
            done += 1
            terms = unit_grads(order[done])
            (up_in, down_in), terms, values = tie((up_in, down_in), terms, values)
            last_sums = (up_in, down_in), terms
            up_sum = (up_in.astype(F32) + terms[0].astype(F32)).astype(BF16)
            down_sum = (down_in.astype(F32) + terms[1].astype(F32)).astype(BF16)
        return work() if values is None else values

    first = ring_steps[0]
    then = first + 1 + ring_steps[0] + ring_steps[1]
    if first == 1 and units % 128 == 0:
        k = order[0]
        running, grad_gates[k], grad_uppers[k], up_sum, down_sum = first_backward(
            grad_down_rows, ffn_rows, weights_of([k]), gates[k], uppers[k], hiddens[k]
        )
    else:
        running = backward_part(order[:first], None)
        up_sum, down_sum = unit_grads(order[0])
    running = beside(0, lambda: backward_part(order[first:then], running))
    own_sum, low_sum = beside(1, lambda: backward_part(order[then:], running, True))

    def work():
        steps = order[done + ring_steps[2] :] if units % 128 == 0 else []
        total, grads = sum_of_four(
            own_sum,
            low_sum,
            5,
            [(grad_gates[k], grad_uppers[k], hiddens[k]) for k in steps],
            ffn_rows,
            grad_down_rows,
        )
        ready.update(zip(steps, grads))
        return total

    grad_ffn_in = beside(2, work)
    def work():
        *out, grad_keys, grad_values = attend_back(
            gains, grad_ffn_in, grad_after, mixed, attn_raw, laurel_mid, normed_low, full, context_low, qkv, keys_all,
            visible,
        )
        grad_kv = jnp.concatenate([grad_keys, grad_values], 1)
        grad_before = grad_kv[:row_count]
        grad_own = grad_kv[2 * row_count :]
        returned = swap(grad_kv[row_count : 2 * row_count].astype(BF16), "core").astype(F32)
        grad_own = grad_own + jnp.where(core == 0, returned, 0.0)
        grad_before = grad_before + jnp.where(core == 0, 0.0, returned)
        return out, grad_own, grad_before

    out, grad_own, grad_before = beside(3, work)
    (
        grad_scaled,
        grad_mid_low,
        grad_mid_gains,
        grad_lleft,
        grad_lright_t,
        grad_wo,
        grad_queries,
    ) = out

    def work():
        total = grad_before
        for span in reversed(spans):
            back = [(mid + i + span, mid + i) for i in range(min(span, mid - span))]
            total = total + lax.ppermute(total.astype(BF16), "zy", back).astype(F32)
        before_low = total.astype(BF16)
        return (
            grad_own
            + lax.ppermute(before_low, "zy", [(b, a) for a, b in chain]).astype(F32)
            + lax.ppermute(before_low, "zy", [(mid, mid - 1)]).astype(F32)
        ), query_back(grad_queries, qkv_raw, cosine, sine, head_gain, normed_low, full)

    grad_own, (grad_wq, grad_normed, grad_hq) = beside(4, work)

    def work():
        grad_wkv, grad_tokens, grad_hk, grad_g0 = key_back(
            grad_own, qkv_raw, cosine, sine, head_gain, normed_low, full, grad_normed, grad_scaled, grad_mid_low,
            tokens[0], gains,
        )
        head_back = jnp.concatenate([grad_hq, grad_hk], 0).reshape(2, shards, head_n).transpose(1, 0, 2)
        head_back = head_back.reshape(shards, 2 * head_n)
        head_back = jnp.pad(head_back, ((0, 0), (0, shard_rows - 2 * head_n))).reshape(1, D)
        misc_back = jnp.concatenate(
            [grad_g0, grad_mid_gains[:3], late_gains[:2], head_back, jnp.zeros((1, D), F32)], 0
        )
        return grad_wkv, grad_tokens, jnp.concatenate(
            [
                grad_plg,
                grad_plp.reshape(D, proj_cols),
                grad_lleft[:, :RANK].astype(BF16),
                jnp.pad(misc_back.T, ((0, 0), (0, misc_cols - 8))).astype(BF16),
                grad_lright_t.astype(BF16),
            ],
            1,
        )

    last_terms, (grad_wkv, grad_tokens, rest_back) = beside(5, lambda: (unit_grads(0), work()))
    sums_wq, sums_wkv, sums_wo, sums_rest, total, up_in, down_in = sum_all(
        [grad_wq, grad_wkv, grad_wo, rest_back],
        (D, 2 * key_cols, D - 512, 0),
        squares,
        *last_sums,
        chips,
    )
    grad_ffn = jnp.concatenate(
        [
            (arrived.astype(F32) + term.astype(F32)).transpose(1, 0, 2)
            for arrived, term in zip((up_in, down_in), last_terms)
        ],
        0,
    )
    at = 0
    rest = []
    for width in (PLD, proj_cols, RANK, misc_cols, RANK):
        rest.append(sums_rest[:, at : at + width])
        at += width

    match_loss = total[0, 0] / (2.0 * D * count)

    return (
        result[None],
        match_loss,
        grad_tokens[None],
        grad_layer_in[None],
        sums_wq,
        sums_wkv,
        sums_wo,
        rest[2],
        rest[4].T,
        rest[0],
        rest[1].reshape(pl_proj.shape),
        rest[3][:, :6].T,
        rest[3][: 2 * head_n, 6].reshape(2, head_n),
        grad_ffn,
    )


def solution(mesh):
    seq, fsdp = mesh.shape["seq"], mesh.shape["fsdp"]
    fine = Mesh(mesh.devices.reshape(seq // 2, 2, fsdp), ("zy", "core", "fsdp"))
    rows = P("fsdp", ("zy", "core"), None)
    split = ("zy", "core", "fsdp")
    weights = (
        P(split, None),
        P(split, None),
        P(split, None),
        P(split, None),
        P(None, split),
        P(split, None),
        P(split, None),
        P(None, split),
        P(None, split),
        P(split, None, None),
    )
    return jax.shard_map(
        body,
        mesh=fine,
        in_specs=(rows, rows, rows, P()) + weights,
        out_specs=(rows, P(), rows, rows) + weights,
        check_vma=False,
    )
```
